32 devices in a mesh: dp: 16 (over z, y, core), fsdp: 2 (over x).
Axes of the slice: x: 2, y: 2, z: 4, core: 2. Of those that a mesh axis runs over, the one named last changes fastest.
Arguments:
- pixels: bfloat16 [32768, 640], P(('dp', 'fsdp')), may hold values from -6 to 6
- wave_table: float32 [16], replicated, may hold values from 0.4 to 2.5
- band_count: int32 [7], replicated, may hold values from 3 to 10, as said below
- wave_index: int32 [7, 10], replicated, may hold values from 0 to 15
- group_sensor: int32 [16], replicated, may hold values from 0 to 6
- chip_kind: int32 [32], P(('dp', 'fsdp')), may hold values from 0 to 1
- chip_gsd: int32 [32, 4], P(('dp', 'fsdp')), may hold values from 1 to 30
- time_loc: float32 [32, 4, 8], P(('dp', 'fsdp')), may hold values from -1 to 1
- gen_in: bfloat16 [128, 128], replicated, may hold values from -0.5 to 0.5
- gen_bias: bfloat16 [128], replicated, may hold values from -3 to 3
- gen_out: bfloat16 [128, 49920], P(None, ('dp', 'fsdp')), may hold values from -0.0390625 to 0.0390625
- meta_weight: bfloat16 [9, 768], replicated, may hold values from -3 to 3
- w_qkv: bfloat16 [768, 2304], P('dp', 'fsdp'), may hold values from -0.21875 to 0.21875
- w_out: bfloat16 [768, 768], P('dp', 'fsdp'), may hold values from -0.875 to 0.875
- w_up: bfloat16 [768, 3072], P('dp', 'fsdp'), may hold values from -0.21875 to 0.21875
- w_down: bfloat16 [3072, 768], P('dp', 'fsdp'), may hold values from -0.109375 to 0.109375
- vectors: bfloat16 [768, 6], P('dp')
- b_up: bfloat16 [3072], P('dp'), may hold values from -2 to 2
- cotangent: bfloat16 [33024, 768], P(('dp', 'fsdp')), may hold values from -6 to 6
Outputs:
- layer_out: bfloat16 [33024, 768], P(('dp', 'fsdp'))
- pixel_grad: float32 [32768, 640], P(('dp', 'fsdp'))
- gen_in_grad: float32 [128, 128], replicated
- gen_bias_grad: float32 [128], replicated
- gen_out_grad: float32 [128, 49920], P(None, ('dp', 'fsdp'))
- meta_grad: float32 [9, 768], replicated
- w_qkv_grad: float32 [768, 2304], P('dp', 'fsdp')
- w_out_grad: float32 [768, 768], P('dp', 'fsdp')
- w_up_grad: float32 [768, 3072], P('dp', 'fsdp')
- w_down_grad: float32 [3072, 768], P('dp', 'fsdp')
- vectors_grad: float32 [768, 6], P('dp')
- b_up_grad: float32 [3072], P('dp')
The draws below stay inside these ranges and needn't reach their ends.
Inputs may be any that keep to these rules, and one draw needn't show every extreme that they name: `band_count`: one sensor has exactly 10 bands.
All inputs are finite; a program needn't handle non-finite values.
Results may differ from the reference program's by a relative error of at most 0.019.
Values may be sent and summed in bfloat16 or wider, within the bound.
A program may use at most 320 MiB of HBM per device.

```python
import math
import jax
import jax.numpy as jnp
from jax import lax

D = 768
HEADS = 12
HEAD = 64
FF = 3072
GEN = 128
PIX = 64
MAXB = 10
SENSORS = 7
WAVES = 16
TLOC = 8
TOK_DEV = 1024
SLOTS = 4
GENOUT = 49920
BLOCKS = 32
TOKENS = 32768
ROWS = 33024
N_DP = 16
N_FSDP = 2


def draw_band_count(key, part):
    key = jax.random.fold_in(key, 11)
    first, second = jax.random.split(key)
    counts = jax.random.randint(first, (SENSORS,), 3, MAXB + 1)
    chosen = jax.random.randint(second, (), 0, SENSORS)
    return jnp.where(jnp.arange(SENSORS) == chosen, MAXB, counts).astype(jnp.int32)


def draw_vectors(key, part):
    key = jax.random.fold_in(key, 23)
    centre = jnp.array([1.0, 0.0, 0.0, 1.0, 0.0, 0.0], jnp.float32)
    noise = 0.2 * jax.random.normal(key, (D, 6), jnp.float32)
    return (centre[None, :] + noise).astype(jnp.bfloat16)


def set_ends(entries, stream_key, low, largest):
    longest = entries.shape.index(max(entries.shape))
    spots = []
    for shift in (0, 1):
        where = [jax.random.randint(jax.random.fold_in(stream_key, axis), (), 0, length) for axis, length in enumerate(entries.shape)]
        where[longest] = (where[longest] + shift) % entries.shape[longest]
        spots.append(tuple(where))
    return entries.at[spots[0]].set(low).at[spots[1]].set(largest)


def block_levels(rng, dims, cuts, low, high):
    level, own = 1.0, jax.random.fold_in(rng, 6)
    for axis_at, parts in cuts:
        draws = jnp.exp(jax.random.uniform(jax.random.fold_in(own, axis_at), (parts,), jnp.float32, low / len(cuts), high / len(cuts)))
        level = level * jnp.repeat(draws, dims[axis_at] // parts).reshape([-1 if axis == axis_at else 1 for axis in range(len(dims))])
    return level


def gaussian(own_key, dims, spread, reach, cuts=(), kind=jnp.bfloat16):
    values = spread * jax.random.normal(own_key, dims, jnp.float32)
    if cuts:
        values = values * block_levels(own_key, dims, cuts, -0.22, 0.18)
    return jnp.clip(values, -reach, reach).astype(kind)


def setup_inputs(seed: int = 0) -> dict:
    key_list = jax.random.split(jax.random.key(seed), 20)
    pixels = gaussian(key_list[0], (TOKENS, MAXB * PIX), 1.0, 6.0, ((0, 32),))
    wave_table = jnp.clip(jnp.exp(jax.random.uniform(key_list[1], (WAVES,), jnp.float32, math.log(0.4), math.log(2.5))), 0.4, 2.5)
    band_count = draw_band_count(jax.random.fold_in(key_list[19], 71), 0)
    wave_index = set_ends(jax.random.randint(key_list[3], (SENSORS, MAXB), 0, WAVES), jax.random.fold_in(key_list[3], 1), 0, WAVES - 1).astype(jnp.int32)
    group_sensor = set_ends(jax.random.randint(key_list[4], (N_DP,), 0, SENSORS), jax.random.fold_in(key_list[4], 1), 0, SENSORS - 1).astype(jnp.int32)
    chip_kind = set_ends(jax.random.randint(key_list[5], (BLOCKS,), 0, 2), jax.random.fold_in(key_list[5], 1), 0, 1).astype(jnp.int32)
    chip_gsd = set_ends(jax.random.randint(key_list[6], (BLOCKS, SLOTS), 1, 31), jax.random.fold_in(key_list[6], 1), 1, 30).astype(jnp.int32)
    time_loc = jnp.clip(jax.random.uniform(key_list[7], (BLOCKS, SLOTS, TLOC), jnp.float32, -1.0, 1.0) * block_levels(key_list[7], (BLOCKS, SLOTS, TLOC), ((0, 32),), -0.4, 0.0), -1.0, 1.0)
    gen_in = gaussian(key_list[8], (GEN, GEN), GEN ** -0.5, 0.5)
    gen_bias = gaussian(key_list[9], (GEN,), 0.5, 3.0)
    gen_out = gaussian(key_list[10], (GEN, GENOUT), (GEN * MAXB * 16) ** -0.5, 0.0390625, ((1, 32),))
    meta_weight = gaussian(key_list[11], (1 + TLOC, D), 0.5, 3.0)
    w_qkv = gaussian(key_list[12], (D, 3 * D), D ** -0.5, 0.21875, ((0, 16), (1, 2)))
    w_out = gaussian(key_list[13], (D, D), (D // 16) ** -0.5, 0.875, ((0, 16), (1, 2)))
    w_up = gaussian(key_list[14], (D, FF), D ** -0.5, 0.21875, ((0, 16), (1, 2)))
    w_down = gaussian(key_list[15], (FF, D), FF ** -0.5, 0.109375, ((0, 16), (1, 2)))
    vectors = draw_vectors(jax.random.fold_in(key_list[19], 71), 0)
    b_up = gaussian(key_list[17], (FF,), 0.3, 2.0, ((0, 16),))
    cotangent = gaussian(key_list[18], (ROWS, D), 1.0, 6.0, ((0, 32),))
    return dict(pixels=pixels, wave_table=wave_table, band_count=band_count, wave_index=wave_index, group_sensor=group_sensor, chip_kind=chip_kind, chip_gsd=chip_gsd, time_loc=time_loc, gen_in=gen_in, gen_bias=gen_bias, gen_out=gen_out, meta_weight=meta_weight, w_qkv=w_qkv, w_out=w_out, w_up=w_up, w_down=w_down, vectors=vectors, b_up=b_up, cotangent=cotangent)


@jax.custom_vjp
def low(v):
    return lax.optimization_barrier(v.astype(jnp.bfloat16)).astype(jnp.float32)

@jax.custom_vjp
def low_back(v):
    return v

def low_keep(v):
    return (low(v), None)

def low_pass(kept, grad):
    return (grad,)

def back_keep(v):
    return (v, None)

def back_low(kept, grad):
    return (low(grad),)
low.defvjp(low_keep, low_pass)
low_back.defvjp(back_keep, back_low)

def exact_dot(left, right):
    return jnp.dot(left, right, precision=lax.Precision.HIGHEST)

def wave_code(wavelengths):
    half = GEN // 2
    omega = 1.0 / 10000.0 ** (jnp.arange(half, dtype=jnp.float32) / half)
    angle = (wavelengths * 1000.0)[:, None] * omega[None, :]
    return jnp.concatenate([jnp.sin(angle), jnp.cos(angle)], axis=1)

def place_code(kind_one, gsd_one):
    small = TOK_DEV // SLOTS
    index = jnp.arange(TOK_DEV, dtype=jnp.int32)
    within = jnp.where(kind_one == 1, index, index % small)
    side = jnp.where(kind_one == 1, math.isqrt(TOK_DEV), math.isqrt(small)).astype(jnp.int32)
    across = (within // side).astype(jnp.float32)
    along = (within % side).astype(jnp.float32)
    holder = jnp.where(kind_one == 1, 0, index // small)
    ground = lax.optimization_barrier(jnp.sum(jnp.where(holder[:, None] == jnp.arange(SLOTS, dtype=jnp.int32)[None, :], gsd_one[None, :], 0), axis=1)).astype(jnp.float32) / 10.0
    quarter = D // 4
    omega = 1.0 / 10000.0 ** (jnp.arange(quarter, dtype=jnp.float32) / (quarter - 1))
    first = (across * ground)[:, None] * omega[None, :]
    second = (along * ground)[:, None] * omega[None, :]
    return jnp.concatenate([jnp.sin(first), jnp.cos(first), jnp.sin(second), jnp.cos(second)], axis=1)

def segment_ids(kind_one):
    index = jnp.arange(TOK_DEV, dtype=jnp.int32)
    patches = jnp.where(kind_one == 1, 0, index // (TOK_DEV // SLOTS))
    extra = jnp.arange(2 * SLOTS, dtype=jnp.int32) // 2
    return jnp.concatenate([patches, extra])

def layer_norm(values, gain, shift):
    centred = values - lax.optimization_barrier(jnp.mean(values, axis=-1, keepdims=True))
    scale = lax.rsqrt(lax.optimization_barrier(jnp.mean(centred * centred, axis=-1, keepdims=True)) + 1e-05)
    return centred * scale * gain + shift

def block_rows(params, pixel, kind_one, gsd_one, stamp_one, sensor, wave_table, band_count, wave_index):
    gen_in, gen_bias, gen_out, meta_weight, w_qkv, w_out, w_up, w_down, vectors, b_up = params
    band_total = band_count[sensor]
    wavelengths = wave_table[wave_index[sensor]]
    before = exact_dot(wave_code(wavelengths), gen_in) + gen_bias
    hidden = low(jax.nn.gelu(before, approximate=False))
    generated = low_back(low(exact_dot(hidden, gen_out)))
    live_band = (jnp.arange(MAXB, dtype=jnp.int32) < band_total).astype(jnp.float32)[:, None]
    kernel = (generated[:, :PIX * D] * live_band).reshape(MAXB * PIX, D)
    embed_bias = lax.optimization_barrier(jnp.sum(generated[:, PIX * D:] * live_band, axis=0)) / band_total.astype(jnp.float32)
    patches = exact_dot(pixel, kernel) + embed_bias + place_code(kind_one, gsd_one)
    stamps = exact_dot(stamp_one, meta_weight[1:])
    classes = jnp.broadcast_to(meta_weight[0], stamps.shape)
    extra = jnp.stack([classes, stamps], axis=1).reshape(2 * SLOTS, D)
    tokens_in = low_back(jnp.concatenate([patches, extra], axis=0))
    total_rows = tokens_in.shape[0]
    first = low(layer_norm(tokens_in, vectors[:, 0], vectors[:, 1]))
    qkv = low_back(low(exact_dot(first, w_qkv)))
    query = qkv[:, :D].reshape(total_rows, HEADS, HEAD)
    keys = qkv[:, D:2 * D].reshape(total_rows, HEADS, HEAD)
    values = qkv[:, 2 * D:].reshape(total_rows, HEADS, HEAD)
    scores = low_back(jnp.einsum('qhd,khd->hqk', query, keys, precision=lax.Precision.HIGHEST) * HEAD ** (-0.5))
    segment = segment_ids(kind_one)
    same = (segment[:, None] == segment[None, :])[None]
    scores = jnp.where(same, scores, -1e+30)
    peak = lax.optimization_barrier(jnp.max(scores, axis=-1, keepdims=True))
    expo = jnp.exp(scores - peak)
    prob = low(expo / lax.optimization_barrier(jnp.sum(expo, axis=-1, keepdims=True)))
    mixed = low_back(low(jnp.einsum('hqk,khd->qhd', prob, values, precision=lax.Precision.HIGHEST).reshape(total_rows, D)))
    after = tokens_in + low_back(exact_dot(mixed, w_out) + vectors[:, 2])
    second = low(layer_norm(after, vectors[:, 3], vectors[:, 4]))
    upper = low_back(exact_dot(second, w_up) + b_up)
    active = low(jax.nn.gelu(upper, approximate=False))
    return after + exact_dot(active, w_down) + vectors[:, 5]

def reference(pixels, wave_table, band_count, wave_index, group_sensor, chip_kind, chip_gsd, time_loc, gen_in, gen_bias, gen_out, meta_weight, w_qkv, w_out, w_up, w_down, vectors, b_up, cotangent):
    weights = tuple((member.astype(jnp.float32) for member in (gen_in, gen_bias, gen_out, meta_weight, w_qkv, w_out, w_up, w_down, vectors, b_up)))
    block_sensor = group_sensor[jnp.arange(N_DP * N_FSDP, dtype=jnp.int32) // N_FSDP]
    pixel_blocks = pixels.astype(jnp.float32).reshape(N_DP * N_FSDP, TOK_DEV, MAXB * PIX)

    def forward(params, pixel_all):

        def one_block(member):
            pixel, kind_one, gsd_one, stamp_one, sensor = member
            return block_rows(params, pixel, kind_one, gsd_one, stamp_one, sensor, wave_table, band_count, wave_index)
        return lax.map(jax.checkpoint(one_block), (pixel_all, chip_kind, chip_gsd, time_loc, block_sensor))
    result, pullback = jax.vjp(forward, weights, pixel_blocks)
    grads, pixel_grad = pullback(cotangent.astype(jnp.float32).reshape(result.shape))
    layer_out = result.reshape(-1, D).astype(jnp.bfloat16)
    pixel_grad = pixel_grad.reshape(-1, MAXB * PIX)
    return (layer_out, pixel_grad, grads[0], grads[1], grads[2], grads[3], grads[4], grads[5], grads[6], grads[7], grads[8], grads[9])
```

```python
import math

import jax
import jax.numpy as jnp
from jax import lax
from jax.experimental import pallas as pl
from jax.experimental.pallas import tpu as pltpu
from jax.sharding import PartitionSpec as P

D = 768
HEADS = 12
HEAD = 64
GEN = 128
PIX = 64
MAXB = 10
SENSORS = 7
TOK_DEV = 1024
SLOTS = 4
GENOUT = 49920


def exact_dot(left, right):
    return jnp.dot(left, right, precision=lax.Precision.HIGHEST)


def inner_dot(left, right):
    return lax.dot_general(
        left, right, (((0,), (0,)), ((), ())), preferred_element_type=jnp.float32
    )


def outer_dot(left, right):
    return lax.dot_general(
        left, right, (((1,), (1,)), ((), ())), preferred_element_type=jnp.float32
    )


def gelu_exact(values):
    return jax.nn.gelu(values, approximate=False)


def gelu_slope(values, upstream):
    return jax.vjp(gelu_exact, values)[1](upstream)[0]


def table_lookup(indices, table):
    return jnp.sum(
        jnp.where(
            indices[:, None] == jnp.arange(table.shape[0], dtype=jnp.int32)[None, :],
            table[None, :],
            0.0,
        ),
        axis=1,
    )


def wave_code(wavelengths):
    half = GEN // 2
    omega = 1.0 / 10000.0 ** (jnp.arange(half, dtype=jnp.float32) / half)
    angle = (wavelengths * 1000.0)[:, None] * omega[None, :]
    return jnp.concatenate([jnp.sin(angle), jnp.cos(angle)], axis=1)


def place_code(kind_one, gsd_one):
    small = TOK_DEV // SLOTS
    index = jnp.arange(TOK_DEV, dtype=jnp.int32)
    within = jnp.where(kind_one == 1, index, index % small)
    side = jnp.where(kind_one == 1, math.isqrt(TOK_DEV), math.isqrt(small)).astype(jnp.int32)
    across = (within // side).astype(jnp.float32)
    along = (within % side).astype(jnp.float32)
    holder = jnp.where(kind_one == 1, 0, index // small)
    ground = (
        jnp.sum(
            jnp.where(
                holder[:, None] == jnp.arange(SLOTS, dtype=jnp.int32)[None, :], gsd_one[None, :], 0
            ),
            axis=1,
        ).astype(jnp.float32)
        / 10.0
    )
    quarter = D // 4
    omega = 1.0 / 10000.0 ** (jnp.arange(quarter, dtype=jnp.float32) / (quarter - 1))
    first = (across * ground)[:, None] * omega[None, :]
    second = (along * ground)[:, None] * omega[None, :]
    return jnp.concatenate(
        [jnp.sin(first), jnp.cos(first), jnp.sin(second), jnp.cos(second)], axis=1
    )


def segment_ids(kind_one):
    index = jnp.arange(TOK_DEV, dtype=jnp.int32)
    patches = jnp.where(kind_one == 1, 0, index // (TOK_DEV // SLOTS))
    extra = jnp.arange(2 * SLOTS, dtype=jnp.int32) // 2
    return jnp.concatenate([patches, extra])


def layer_norm(values, gain, shift):
    centred = values - jnp.mean(values, axis=-1, keepdims=True)
    scale = lax.rsqrt(jnp.mean(centred * centred, axis=-1, keepdims=True) + 1e-05)
    normed = centred * scale
    return (normed * gain + shift, normed, scale)


def norm_back(upstream, normed, scale, gain):
    gain_grad = jnp.sum(upstream * normed, axis=0)
    shift_grad = jnp.sum(upstream, axis=0)
    scaled = upstream * gain
    inside = (
        scaled
        - jnp.mean(scaled, axis=-1, keepdims=True)
        - normed * jnp.mean(scaled * normed, axis=-1, keepdims=True)
    )
    return (scale * inside, gain_grad, shift_grad)


def body_general(
    pixels,
    wave_table,
    band_count,
    wave_index,
    group_sensor,
    chip_kind,
    chip_gsd,
    time_loc,
    gen_in,
    gen_bias,
    gen_out,
    meta_weight,
    w_qkv,
    w_out,
    w_up,
    w_down,
    vectors,
    b_up,
    cotangent,
):
    half_type = jnp.bfloat16
    group = lax.axis_index("dp")
    sensor = jnp.sum(
        jnp.where(jnp.arange(group_sensor.shape[0], dtype=jnp.int32) == group, group_sensor, 0)
    )
    chosen_sensor = jnp.arange(SENSORS, dtype=jnp.int32) == sensor
    band_total = jnp.sum(jnp.where(chosen_sensor, band_count, 0))
    gen_in_full = gen_in.astype(jnp.float32)
    gen_bias_full = gen_bias.astype(jnp.float32)
    codes = wave_code(table_lookup(wave_index.reshape(-1), wave_table))
    before = exact_dot(codes, gen_in_full) + gen_bias_full
    hidden = gelu_exact(before).astype(half_type)
    shard_made = jnp.dot(hidden, gen_out, preferred_element_type=jnp.float32).astype(half_type)
    all_made = lax.all_gather(shard_made, ("dp", "fsdp"), axis=1, tiled=True)
    generated = lax.dynamic_slice_in_dim(all_made, sensor * MAXB, MAXB, 0)
    live_band = (jnp.arange(MAXB, dtype=jnp.int32) < band_total)[:, None]
    kernel = jnp.where(live_band, generated[:, : PIX * D], jnp.zeros((), half_type)).reshape(
        MAXB * PIX, D
    )
    band_float = band_total.astype(jnp.float32)
    embed_bias = (
        jnp.sum(jnp.where(live_band, generated[:, PIX * D :].astype(jnp.float32), 0.0), axis=0)
        / band_float
    )
    kind_one = chip_kind[0]
    patches = (
        jnp.dot(pixels, kernel, preferred_element_type=jnp.float32)
        + embed_bias
        + place_code(kind_one, chip_gsd[0])
    )
    meta_full = meta_weight.astype(jnp.float32)
    stamps = exact_dot(time_loc[0], meta_full[1:])
    classes = jnp.broadcast_to(meta_full[0], stamps.shape)
    extra = jnp.stack([classes, stamps], axis=1).reshape(2 * SLOTS, D)
    tokens_in = jnp.concatenate([patches, extra], axis=0)
    total_rows = tokens_in.shape[0]
    qkv_rows, out_rows, up_rows, down_rows, vectors_all, b_up_all = (
        lax.all_gather(w_qkv, "dp", axis=0, tiled=True),
        lax.all_gather(w_out, "dp", axis=0, tiled=True),
        lax.all_gather(w_up, "dp", axis=0, tiled=True),
        lax.all_gather(w_down, "dp", axis=0, tiled=True),
        lax.all_gather(vectors, "dp", axis=0, tiled=True),
        lax.all_gather(b_up, "dp", axis=0, tiled=True),
    )
    w_qkv_all, w_out_all, w_up_all, w_down_all = (
        lax.all_gather(qkv_rows, "fsdp", axis=1, tiled=True),
        lax.all_gather(out_rows, "fsdp", axis=1, tiled=True),
        lax.all_gather(up_rows, "fsdp", axis=1, tiled=True),
        lax.all_gather(down_rows, "fsdp", axis=1, tiled=True),
    )
    vector_full = vectors_all.astype(jnp.float32)
    b_up_full = b_up_all.astype(jnp.float32)
    first_norm, normed_one, scale_one = layer_norm(tokens_in, vector_full[:, 0], vector_full[:, 1])
    first = first_norm.astype(half_type)
    qkv = jnp.dot(first, w_qkv_all, preferred_element_type=jnp.float32).astype(half_type)
    query = qkv[:, :D].reshape(total_rows, HEADS, HEAD)
    keys = qkv[:, D : 2 * D].reshape(total_rows, HEADS, HEAD)
    values = qkv[:, 2 * D :].reshape(total_rows, HEADS, HEAD)
    segment = segment_ids(kind_one)
    same = (segment[:, None] == segment[None, :])[None]
    scores = jnp.einsum("qhd,khd->hqk", query, keys, preferred_element_type=jnp.float32) * HEAD ** (
        -0.5
    )
    scores = jnp.where(same, scores, -1e30)
    peak = jnp.max(scores, axis=-1, keepdims=True)
    expo = jnp.exp(scores - peak)
    totals = jnp.sum(expo, axis=-1, keepdims=True)
    prob_half = (expo / totals).astype(half_type)
    mixed = (
        jnp.einsum("hqk,khd->qhd", prob_half, values, preferred_element_type=jnp.float32)
        .reshape(total_rows, D)
        .astype(half_type)
    )
    after = tokens_in + (
        jnp.dot(mixed, w_out_all, preferred_element_type=jnp.float32) + vector_full[:, 2]
    )
    second_norm, normed_two, scale_two = layer_norm(after, vector_full[:, 3], vector_full[:, 4])
    second = second_norm.astype(half_type)
    upper = jnp.dot(second, w_up_all, preferred_element_type=jnp.float32) + b_up_full
    active = gelu_exact(upper).astype(half_type)
    layer_out = (
        after + jnp.dot(active, w_down_all, preferred_element_type=jnp.float32) + vector_full[:, 5]
    ).astype(half_type)
    grad_top = cotangent.astype(jnp.float32)
    w_down_grad = inner_dot(active, cotangent)
    down_bias_grad = jnp.sum(grad_top, axis=0)
    d_active = outer_dot(cotangent, w_down_all)
    d_upper = gelu_slope(upper, d_active).astype(half_type)
    w_up_grad = inner_dot(second, d_upper)
    b_up_grad = jnp.sum(d_upper.astype(jnp.float32), axis=0)
    d_second = outer_dot(d_upper, w_up_all)
    d_after_norm, gain_two_grad, shift_two_grad = norm_back(
        d_second, normed_two, scale_two, vector_full[:, 3]
    )
    d_after = grad_top + d_after_norm
    d_proj = d_after.astype(half_type)
    w_out_grad = inner_dot(mixed, d_proj)
    out_bias_grad = jnp.sum(d_proj.astype(jnp.float32), axis=0)
    d_mixed = outer_dot(d_proj, w_out_all).astype(half_type).reshape(total_rows, HEADS, HEAD)
    again = jnp.einsum("qhd,khd->hqk", query, keys, preferred_element_type=jnp.float32) * HEAD ** (
        -0.5
    )
    again = jnp.where(same, again, -1e30)
    prob_full = jnp.exp(again - peak) / totals
    recalled = prob_full.astype(half_type)
    d_values = jnp.einsum("hqk,qhd->khd", recalled, d_mixed, preferred_element_type=jnp.float32)
    d_prob = jnp.einsum("qhd,khd->hqk", d_mixed, values, preferred_element_type=jnp.float32)
    d_scores = prob_full * (d_prob - jnp.sum(d_prob * prob_full, axis=-1, keepdims=True))
    d_scores = jnp.where(same, d_scores, 0.0).astype(half_type)
    d_query = jnp.einsum(
        "hqk,khd->qhd", d_scores, keys, preferred_element_type=jnp.float32
    ) * HEAD ** (-0.5)
    d_keys = jnp.einsum(
        "hqk,qhd->khd", d_scores, query, preferred_element_type=jnp.float32
    ) * HEAD ** (-0.5)
    d_qkv = jnp.concatenate(
        [
            d_query.reshape(total_rows, D),
            d_keys.reshape(total_rows, D),
            d_values.reshape(total_rows, D),
        ],
        axis=1,
    ).astype(half_type)
    w_qkv_grad = inner_dot(first, d_qkv)
    d_first = outer_dot(d_qkv, w_qkv_all)
    d_tokens_norm, gain_one_grad, shift_one_grad = norm_back(
        d_first, normed_one, scale_one, vector_full[:, 0]
    )
    d_tokens = (d_after + d_tokens_norm).astype(half_type)
    vectors_grad = jnp.stack(
        [
            gain_one_grad,
            shift_one_grad,
            out_bias_grad,
            gain_two_grad,
            shift_two_grad,
            down_bias_grad,
        ],
        axis=1,
    )
    d_patches = d_tokens[:TOK_DEV]
    d_extra = d_tokens[TOK_DEV:].astype(jnp.float32).reshape(SLOTS, 2, D)
    pixel_grad = outer_dot(d_patches, kernel)
    class_grad = jnp.sum(d_extra[:, 0], axis=0)
    stamp_grad = exact_dot(time_loc[0].T, d_extra[:, 1])
    meta_part = jnp.concatenate([class_grad[None, :], stamp_grad], axis=0)
    d_kernel = inner_dot(pixels, d_patches).reshape(MAXB, PIX * D)
    d_kernel = jnp.where(live_band, d_kernel, 0.0)
    d_bias = jnp.sum(d_patches.astype(jnp.float32), axis=0) / band_float
    d_bias_rows = jnp.where(live_band, d_bias[None, :], 0.0)
    d_generated = jnp.concatenate([d_kernel, d_bias_rows], axis=1).astype(half_type)
    placed = jnp.where(
        chosen_sensor[:, None, None], d_generated.astype(jnp.float32)[None], 0.0
    ).reshape(SENSORS * MAXB, GENOUT)
    columns = lax.psum_scatter(placed, ("dp", "fsdp"), scatter_dimension=1, tiled=True)
    gen_out_grad = exact_dot(hidden.astype(jnp.float32).T, columns)
    d_hidden = exact_dot(columns, gen_out.astype(jnp.float32).T)
    d_before = gelu_slope(before, d_hidden)
    gen_in_part = exact_dot(codes.T, d_before)
    gen_bias_part = jnp.sum(d_before, axis=0)
    meta_grad, gen_in_grad, gen_bias_grad = lax.psum(
        (meta_part, gen_in_part, gen_bias_part), ("dp", "fsdp")
    )
    qkv_cols, out_cols, up_cols, down_cols = (
        lax.psum_scatter(
            w_qkv_grad.astype(jnp.bfloat16), "fsdp", scatter_dimension=1, tiled=True
        ).astype(jnp.float32),
        lax.psum_scatter(
            w_out_grad.astype(jnp.bfloat16), "fsdp", scatter_dimension=1, tiled=True
        ).astype(jnp.float32),
        lax.psum_scatter(
            w_up_grad.astype(jnp.bfloat16), "fsdp", scatter_dimension=1, tiled=True
        ).astype(jnp.float32),
        lax.psum_scatter(
            w_down_grad.astype(jnp.bfloat16), "fsdp", scatter_dimension=1, tiled=True
        ).astype(jnp.float32),
    )
    vectors_group, b_up_group = lax.psum((vectors_grad, b_up_grad), "fsdp")
    w_qkv_out, w_out_out, w_up_out, w_down_out, vectors_out, b_up_out = (
        lax.psum_scatter(
            qkv_cols.astype(jnp.bfloat16), "dp", scatter_dimension=0, tiled=True
        ).astype(jnp.float32),
        lax.psum_scatter(
            out_cols.astype(jnp.bfloat16), "dp", scatter_dimension=0, tiled=True
        ).astype(jnp.float32),
        lax.psum_scatter(
            up_cols.astype(jnp.bfloat16), "dp", scatter_dimension=0, tiled=True
        ).astype(jnp.float32),
        lax.psum_scatter(
            down_cols.astype(jnp.bfloat16), "dp", scatter_dimension=0, tiled=True
        ).astype(jnp.float32),
        lax.psum_scatter(
            vectors_group.astype(jnp.bfloat16), "dp", scatter_dimension=0, tiled=True
        ).astype(jnp.float32),
        lax.psum_scatter(
            b_up_group.astype(jnp.bfloat16), "dp", scatter_dimension=0, tiled=True
        ).astype(jnp.float32),
    )
    return (
        layer_out,
        pixel_grad,
        gen_in_grad,
        gen_bias_grad,
        gen_out_grad,
        meta_grad,
        w_qkv_out,
        w_out_out,
        w_up_out,
        w_down_out,
        vectors_out,
        b_up_out,
    )


LIVE = 1032
ROWS = 1040
TILE = 208
TILES = 5
NZ = 4
GROUPS = 16
PIECE = 144
COVER = 14
VMEM_ASK = 60 * 1024 * 1024
BF = jnp.bfloat16
F32 = jnp.float32


def nt_dot(left, right):
    return lax.dot_general(left, right, (((1,), (1,)), ((), ())), preferred_element_type=F32)


def nn_dot(left, right):
    return lax.dot_general(left, right, (((1,), (0,)), ((), ())), preferred_element_type=F32)


def spot():
    group = lax.axis_index("dp")
    return group // 4, (group // 2) % 2, group % 2, lax.axis_index("fsdp")


def device(z, y, c, x):
    return {"dp": z * 4 + y * 2 + c, "fsdp": x}


def remote(source, target, sems, slot, where):
    return pltpu.make_async_remote_copy(
        src_ref=source,
        dst_ref=target,
        send_sem=sems[0].at[slot],
        recv_sem=sems[1].at[slot],
        device_id=where,
        device_id_type=pl.DeviceIdType.MESH,
    )


def greet(others):
    barrier = pltpu.get_barrier_semaphore()
    for where in others:
        pl.semaphore_signal(
            barrier, inc=1, device_id=where, device_id_type=pl.DeviceIdType.MESH
        )
    pl.semaphore_wait(barrier, len(others))


def columns(ref, x):
    width = ref.shape[-1] // 2
    return pl.ds(pl.multiple_of(x * width, 128), width)


def group_peers(z, y, c, x):
    return [
        ((dz, dy, dc), device((z + dz) % NZ, (y + dy) % 2, (c + dc) % 2, x))
        for dz in range(NZ)
        for dy in range(2)
        for dc in range(2)
        if dz + dy + dc
    ]


def first_hop(shard, whole, sems, first, local, here):
    z, y, c, x = here
    target = whole.at[z, y, c, :, columns(whole, x)]
    return pltpu.make_async_copy(shard, target, local), [
        remote(shard, target, sems, first + k - 1, device((z + k) % NZ, y, c, x))
        for k in range(1, NZ)
    ]


CHUNK = 768
BANDS = ((0, 256), (256, 256), (512, 256), (768, 256), (1024, 8))


def gelu_parts(values):
    bell = jnp.exp(values * values * (-0.5))
    step = 1.0 / (1.0 + (0.3275911 * math.sqrt(0.5)) * jnp.abs(values))
    poly = 0.5 * 1.061405429 * step - 0.5 * 1.453152027
    poly = poly * step + 0.5 * 1.421413741
    poly = poly * step - 0.5 * 0.284496736
    poly = poly * step + 0.5 * 0.254829592
    tail = poly * step * bell
    below = jnp.where(values < 0.0, tail, 1.0 - tail)
    return values * below, below + values * bell * (1.0 / math.sqrt(2.0 * math.pi))


def standard(values):
    centred = values - jnp.mean(values, axis=-1, keepdims=True)
    scale = lax.rsqrt(jnp.mean(centred * centred, axis=-1, keepdims=True) + 1e-05)
    return centred * scale, scale


def column_sum(values):
    return jnp.sum(values, axis=0, keepdims=True)


def put_rows(target, first, count, values):
    if count % 16:
        values = jnp.concatenate(
            [values, jnp.zeros((16 - count % 16, values.shape[1]), values.dtype)], axis=0
        )
    target[first : first + values.shape[0], :] = values


class Gather:
    def __init__(self, whole, sems, first, here):
        z, y, c, x = here
        mine, other = columns(whole, x), columns(whole, 1 - x)
        block = whole.at[:, y, c, :, mine]
        from_x = whole.at[:, y, c, :, other]
        from_y = whole.at[:, 1 - y, c, :, mine]
        far_low = whole.at[0:2, 1 - y, c, :, other]
        far_high = whole.at[2:4, 1 - y, c, :, other]
        across, beside, twin = device(z, y, c, 1 - x), device(z, 1 - y, c, x), device(z, y, 1 - c, x)
        self.to_x = remote(block, block, sems, first, across)
        self.to_y = remote(block, block, sems, first + 1, beside)
        self.core = [remote(block, block, sems, first + 2, twin)]
        low = whole.at[0:2, y, c, :, other]
        high = whole.at[2:4, 1 - y, c, :, mine]
        self.far_y = remote(low, low, sems, first + 3, beside)
        self.far_x = remote(high, high, sems, first + 4, across)
        for step, part in enumerate((from_x, from_y, far_low, far_high)):
            self.core.append(remote(part, part, sems, first + 5 + step, twin))

    def stage_b(self):
        self.to_x.start()
        self.to_y.start()
        self.core[0].start()

    def stage_c(self, receive=True):
        if receive:
            self.to_x.wait_recv()
        self.far_y.start()
        self.core[1].start()
        if receive:
            self.to_y.wait_recv()
        self.far_x.start()
        self.core[2].start()

    def stage_d(self):
        self.far_y.wait_recv()
        self.core[3].start()
        self.far_x.wait_recv()
        self.core[4].start()

    def finish(self, receive=True, began=True):
        skip = 0 if began else 1
        if receive:
            for copy in self.core[skip:]:
                copy.wait_recv()
        if began:
            self.to_x.wait_send()
            self.to_y.wait_send()
        for copy in (self.far_y, self.far_x, *self.core[skip:]):
            copy.wait_send()


def open_kernel(
    wq, wo, wu, wd, small, made, pixels, table, places, meta, bands,
    full_q, full_o, full_u, full_d, params, kernel, tokens, first, qkv,
    taken, full_small, flat, wide,
    a_send, a_recv, b_send, b_recv, local_sem, s_send, s_recv, g_send, g_recv,
):
    here = z, y, c, x = spot()
    peers = group_peers(z, y, c, x)
    across = device(z, y, c, 1 - x)
    greet([where for _, where in peers] + [across])
    pairs = ((wq, full_q), (wo, full_o), (wu, full_u), (wd, full_d))
    hops = [
        first_hop(shard, whole, (a_send, a_recv), 3 * step, local_sem.at[step], here)
        for step, (shard, whole) in enumerate(pairs)
    ]
    q, o, u = [
        Gather(whole, (b_send, b_recv), 9 * step, here) for step, (_, whole) in enumerate(pairs[:3])
    ]

    def start_hop(local, along):
        local.start()
        for copy in along:
            copy.start()

    def end_hop(local, along):
        local.wait()
        for copy in along:
            copy.wait_recv()

    s_sems = (s_send, s_recv)
    g_sems = (g_send, g_recv)
    own_made = pltpu.make_async_copy(
        made.at[z, y, c], taken.at[z, y, c, x], local_sem.at[4]
    )
    own_made.start()
    sends = {}
    for (dz, dy, dc), where in peers:
        copy = remote(
            made.at[(z + dz) % NZ, (y + dy) % 2, (c + dc) % 2],
            taken.at[z, y, c, x],
            g_sems,
            dz * 4 + dy * 2 + dc,
            where,
        )
        copy.start()
        sends[dz, dy, dc] = copy
    start_hop(*hops[0])
    own_small = pltpu.make_async_copy(small, full_small.at[z, y, c], local_sem.at[5])
    own_small.start()
    small_z = [
        remote(small, full_small.at[z, y, c], s_sems, k - 1, device((z + k) % NZ, y, c, x))
        for k in range(1, NZ)
    ]
    for copy in small_z:
        copy.start()
    for hop in hops[1:]:
        start_hop(*hop)
    own_made.wait()
    swaps = []
    for dz in range(NZ):
        for dy in range(2):
            for dc in range(2):
                if dz + dy + dc:
                    sends[dz, dy, dc].wait_recv()
        part = taken.at[(z + NZ - dz) % NZ, :, :, x]
        swap = remote(part, part, g_sems, 16 + dz, across)
        swap.start()
        swaps.append(swap)
    end_hop(*hops[0])
    q.stage_b()
    own_small.wait()
    for copy in small_z:
        copy.wait_recv()
    part = full_small.at[:, y, c]
    small_y = remote(part, part, s_sems, 3, device(z, 1 - y, c, x))
    small_y.start()
    for swap in swaps:
        swap.wait_recv()
    unpack(taken, flat, wide, kernel)
    end_hop(*hops[1])
    q.stage_c()
    o.stage_b()
    small_y.wait_recv()
    part = full_small.at[:, :, c]
    small_c = remote(part, part, s_sems, 4, device(z, y, 1 - c, x))
    small_c.start()
    bias = jnp.concatenate(
        [
            column_sum(flat[(PIX * 6 + part) * MAXB : (PIX * 6 + part + 1) * MAXB, :])
            for part in range(6)
        ],
        axis=1,
    ) / bands[0:1, 0:1]
    for start, count in BANDS[:-1]:
        band = slice(start, start + count)
        made_rows = nn_dot(pixels[band, :], kernel[...])
        spread = [nn_dot(places[band, way * 256 : (way + 1) * 256], table[...]) for way in range(2)]
        tokens[band, :] = made_rows + bias + jnp.concatenate(spread, axis=1)
        if start == 256:
            q.stage_d()
    small_c.wait_recv()
    end_hop(*hops[2])
    o.stage_c()
    u.stage_b()
    params[...] = jnp.zeros_like(params)
    for n in range(GROUPS):
        params[...] += full_small[n // 4, (n // 2) % 2, n % 2].astype(F32)
    tokens[TOK_DEV:LIVE, :] = meta[...]
    for start, count in BANDS:
        band = slice(start, start + count)
        normed, _ = standard(tokens[band, :])
        first[band, :] = (normed * params[0:1, :] + params[1:2, :]).astype(BF)
    for copy in q.core:
        copy.wait_recv()
    for start, count in BANDS:
        band = slice(start, start + count)
        for third in range(3):
            part = slice(third * D, (third + 1) * D)
            qkv[band, part] = nn_dot(
                first[band, :], full_q[:, :, :, :, part].reshape(D, D)
            ).astype(BF)
    o.stage_d()
    end_hop(*hops[3])
    for gather in (q, o):
        gather.finish(gather is not q)
    for copy in (u.to_x, u.to_y, u.core[0]):
        copy.wait()
    for copy in (*small_z, small_y, small_c, *sends.values(), *swaps):
        copy.wait_send()
    for _, along in hops:
        for copy in along:
            copy.wait_send()


def opening(w_qkv, w_out, w_up, w_down, small, made, pixels, table, places, meta, bands):
    anywhere = pl.BlockSpec(memory_space=pl.ANY)
    vmem = pl.BlockSpec(memory_space=pltpu.VMEM)
    shards = (w_qkv, w_out, w_up, w_down)
    outs = [
        jax.ShapeDtypeStruct((NZ, 2, 2, shard.shape[0], 2 * shard.shape[1]), BF) for shard in shards
    ]
    outs += [
        jax.ShapeDtypeStruct((16, D), F32),
        jax.ShapeDtypeStruct((MAXB * PIX, D), BF),
        jax.ShapeDtypeStruct((LIVE, D), F32),
        jax.ShapeDtypeStruct((LIVE, D), BF),
        jax.ShapeDtypeStruct((LIVE, 3 * D), BF),
    ]
    return pl.pallas_call(
        open_kernel,
        out_shape=outs,
        in_specs=[anywhere] * 6 + [vmem] * 5,
        out_specs=[vmem] + [anywhere] * 3 + [vmem] * 5,
        scratch_shapes=[
            pltpu.VMEM((NZ, 2, 2, 2) + made.shape[3:], BF),
            pltpu.VMEM((NZ, 2, 2, 16, D), BF),
            pltpu.VMEM((FLAT, 128), F32),
            pltpu.VMEM((6, MAXB * PIX, 128), F32),
        ]
        + [pltpu.SemaphoreType.DMA((count,)) for count in (12, 12, 27, 27, 6, 5, 5, 20, 20)],
        compiler_params=pltpu.CompilerParams(
            collective_id=0, has_side_effects=True, vmem_limit_bytes=VMEM_ASK
        ),
    )(*shards, small, made, pixels, table, places, meta, bands)


class Scatter:
    def __init__(self, whole, own, came, low, high, side_x, side_y, last, out, sems, first, here):
        z, y, c, x = here
        self.here, self.own, self.came, self.out = here, own, came, out
        self.low, self.high, self.side_x, self.side_y, self.last = low, high, side_x, side_y, last
        self.mine, self.other = columns(own, x), columns(own, 1 - x)
        mine, other = self.mine, self.other
        across, beside, twin = device(z, y, c, 1 - x), device(z, 1 - y, c, x), device(z, y, 1 - c, x)
        self.local = pltpu.make_async_copy(whole.at[:, :, c], own, sems[2].at[first // 8])
        self.core = remote(whole.at[:, :, 1 - c], came, sems, first, twin)
        self.far_y = remote(own.at[0:2, 1 - y, :, other], low, sems, first + 1, beside)
        self.far_x = remote(own.at[2:4, 1 - y, :, other], high, sems, first + 2, across)
        self.to_x = remote(own.at[:, y, :, other], side_x, sems, first + 3, across)
        self.to_y = remote(own.at[:, 1 - y, :, mine], side_y, sems, first + 4, beside)
        self.along = [
            remote(
                own.at[(z + k) % NZ, y, :, mine], last.at[k - 1], sems, first + 4 + k,
                device((z + k) % NZ, y, c, x),
            )
            for k in range(1, NZ)
        ]

    def stage_a(self):
        self.local.start()
        self.core.start()

    def stage_b(self):
        self.local.wait()
        self.core.wait_recv()
        for at_z in range(NZ):
            for at_y in range(2):
                self.own[at_z, at_y] = (
                    self.own[at_z, at_y].astype(F32) + self.came[at_z, at_y].astype(F32)
                ).astype(BF)
        self.far_y.start()
        self.far_x.start()

    def stage_c(self):
        _, y, _, _ = self.here
        self.far_y.wait_recv()
        for k in range(2):
            self.own[k, y, :, self.other] = (
                self.own[k, y, :, self.other].astype(F32) + self.low[k].astype(F32)
            ).astype(BF)
        self.to_x.start()
        self.far_x.wait_recv()
        for k in range(2):
            self.own[2 + k, 1 - y, :, self.mine] = (
                self.own[2 + k, 1 - y, :, self.mine].astype(F32) + self.high[k].astype(F32)
            ).astype(BF)
        self.to_y.start()

    def stage_d(self):
        _, y, _, _ = self.here
        self.to_x.wait_recv()
        self.to_y.wait_recv()
        for k in range(NZ):
            self.own[k, y, :, self.mine] = (
                self.own[k, y, :, self.mine].astype(F32)
                + self.side_x[k].astype(F32)
                + self.side_y[k].astype(F32)
            ).astype(BF)
        for copy in self.along:
            copy.start()

    def stage_e(self):
        z, y, _, _ = self.here
        for copy in self.along:
            copy.wait_recv()
        self.out[...] = (
            self.own[z, y, :, self.mine].astype(F32)
            + self.last[0].astype(F32)
            + self.last[1].astype(F32)
            + self.last[2].astype(F32)
        )
        for copy in (self.core, self.far_y, self.far_x, self.to_x, self.to_y, *self.along):
            copy.wait_send()


class Total:
    def __init__(self, source, out, held, came, slots, send_sem, recv_sem, here):
        z, y, c, x = here
        sems = (send_sem, recv_sem)
        self.source, self.held, self.came, self.slots, self.out = source, held, came, slots, out
        self.z = z
        where = (device(z, y, 1 - c, x), device(z, y, c, 1 - x), device(z, 1 - y, c, x))
        self.steps = [
            remote(source if step == 0 else held.at[step - 1], came.at[step], sems, step, where[step])
            for step in range(3)
        ]
        self.along = [
            remote(held.at[2], slots.at[z], sems, 2 + k, device((z + k) % NZ, y, c, x))
            for k in range(1, NZ)
        ]

    def begin(self):
        self.steps[0].start()

    def turn(self, step):
        self.steps[step].wait_recv()
        before = self.source[...] if step == 0 else self.held[step - 1]
        self.held[step] = before + self.came[step]
        if step < 2:
            self.steps[step + 1].start()
        else:
            self.slots[self.z] = self.held[2]
            for copy in self.along:
                copy.start()

    def finish(self):
        for copy in self.along:
            copy.wait_recv()
        self.out[...] = self.slots[0] + self.slots[1] + self.slots[2] + self.slots[3]
        for copy in (*self.steps, *self.along):
            copy.wait_send()


def near(z, y, c, x):
    return [
        device(z, y, c, 1 - x),
        device(z, 1 - y, c, x),
        device(z, y, 1 - c, x),
        *[device((z + k) % NZ, y, c, x) for k in range(1, NZ)],
    ]


def scatter_scratch(rows, width):
    half = width // 2
    return [
        pltpu.VMEM((NZ, 2, rows, width), BF),
        pltpu.VMEM((NZ, 2, rows, width), BF),
        pltpu.VMEM((2, rows, half), BF),
        pltpu.VMEM((2, rows, half), BF),
        pltpu.VMEM((NZ, rows, half), BF),
        pltpu.VMEM((NZ, rows, half), BF),
        pltpu.VMEM((3, rows, half), BF),
    ]


def total_scratch(shape):
    return [
        pltpu.VMEM((3,) + shape, F32),
        pltpu.VMEM((3,) + shape, F32),
        pltpu.VMEM((NZ,) + shape, F32),
        pltpu.SemaphoreType.DMA((6,)),
        pltpu.SemaphoreType.DMA((6,)),
    ]


def piece_start(owner):
    return (owner * (GENOUT // 32)) // 128


def make_kernel(hidden, gen_out, pieces, gen_shift, rows, wide):
    wide[...] = jnp.zeros_like(wide)
    wide[:, : gen_out.shape[1]] = gen_out[...].astype(F32)
    owner = lax.axis_index("dp") * 2 + lax.axis_index("fsdp")
    gen_shift[...] = pltpu.roll(wide[...], (owner * gen_out.shape[1]) % 128, 1).astype(BF)
    rows[:, COVER * MAXB :, :] = jnp.zeros((GROUPS, PIECE - COVER * MAXB, 128), F32)
    for at in range(COVER):
        made = nn_dot(hidden[...], gen_shift[:, at * 128 : (at + 1) * 128])
        for group in range(GROUPS):
            rows[group, at * MAXB : (at + 1) * MAXB, :] = made[group * MAXB : (group + 1) * MAXB]
    pieces[...] = rows[...].astype(BF)


def make_pieces(hidden, gen_out):
    return pl.pallas_call(
        make_kernel,
        out_shape=[
            jax.ShapeDtypeStruct((GROUPS, PIECE, 128), BF),
            jax.ShapeDtypeStruct((GEN, COVER * 128), BF),
        ],
        scratch_shapes=[
            pltpu.VMEM((GROUPS, PIECE, 128), F32),
            pltpu.VMEM((GEN, COVER * 128), F32),
        ],
        compiler_params=pltpu.CompilerParams(vmem_limit_bytes=VMEM_ASK),
    )(hidden, gen_out)


FLAT = (GENOUT // 128) * MAXB


def unpack(taken, flat, wide, kernel):
    flat[...] = jnp.zeros_like(flat)
    used = COVER * MAXB
    for owner in range(32):
        first = piece_start(owner) * MAXB
        count = min(used, FLAT - first)
        piece = taken[owner // 8, (owner // 4) % 2, (owner // 2) % 2, owner % 2]
        flat[first : first + count, :] += piece.astype(F32)[:count]
    for pixel in range(PIX):
        for part in range(6):
            first = (pixel * 6 + part) * MAXB
            wide[part, pl.ds(pixel, MAXB, stride=PIX), :] = flat[first : first + MAXB, :]
    for part in range(6):
        kernel[:, part * 128 : (part + 1) * 128] = wide[part].astype(BF)


def pack(d_kernel, bias, pieces, wide, flat):
    for part in range(6):
        wide[part] = d_kernel[:, part * 128 : (part + 1) * 128]
        first = (PIX * 6 + part) * MAXB
        flat[first : first + MAXB, :] = bias[0:MAXB, part * 128 : (part + 1) * 128]
    flat[FLAT:, :] = jnp.zeros((flat.shape[0] - FLAT, 128), F32)
    for pixel in range(PIX):
        for part in range(6):
            first = (pixel * 6 + part) * MAXB
            flat[first : first + MAXB, :] = wide[part, pl.ds(pixel, MAXB, stride=PIX), :]
    for owner in range(32):
        first = piece_start(owner) * MAXB
        pieces[owner // 8, (owner // 4) % 2, (owner // 2) % 2, owner % 2] = flat[
            first : first + PIECE, :
        ].astype(BF)


def norm_rows_back(value, upstream, gain):
    normed, scale = standard(value)
    scaled = upstream * gain
    inside = (
        scaled
        - jnp.mean(scaled, axis=-1, keepdims=True)
        - normed * jnp.mean(scaled * normed, axis=-1, keepdims=True)
    )
    return scale * inside, column_sum(upstream * normed), column_sum(upstream)


def close_kernel(
    d_qkv, first, w_qkv, tokens, d_after, params, pixels, kernel, meta_mix, late, b_grad, live,
    hidden, gen_shift, slope, codes,
    out_grad, in_grad, out_q, out_early, pixel_grad,
    d_tokens, grad_q, pieces, taken, flat, wide, rows, source, early,
    send_sem, recv_sem, local_sem, q_send, q_recv, *rest,
):
    here = z, y, c, x = spot()
    peers = [
        ((dz, dy, dc, dx), ((z + dz) % NZ, (y + dy) % 2, (c + dc) % 2, (x + dx) % 2))
        for dz in range(NZ)
        for dy in range(2)
        for dc in range(2)
        for dx in range(2)
        if dz + dy + dc + dx
    ]
    greet([device(*where) for _, where in peers])
    scatter = Scatter(
        grad_q, *rest[10:17], out_q, (q_send, q_recv, local_sem), 0, here
    )
    begin = Total(early, out_early, *rest[0:5], here)
    for third in range(3):
        part = slice(third * D, (third + 1) * D)
        grad_q[:, :, :, :, part] = (
            inner_dot(first[...], d_qkv[:, part]).astype(BF).reshape(NZ, 2, 2, -1, D)
        )
    scatter.stage_a()
    gain = shift = jnp.zeros((1, D), F32)
    for start, count in BANDS:
        band = slice(start, start + count)
        upstream = nt_dot(d_qkv[band, :], w_qkv[...].reshape(D, 3 * D))
        d_norm, gain_part, shift_part = norm_rows_back(tokens[band, :], upstream, params[0:1, :])
        gain += gain_part
        shift += shift_part
        d_tokens[band, :] = (d_after[band, :] + d_norm).astype(BF)
    scatter.stage_b()
    patches = d_tokens[0:TOK_DEV, :]
    d_kernel = inner_dot(pixels[...], patches)
    sums = column_sum(patches.astype(F32))
    pack(d_kernel, live[...] * sums, pieces, wide, flat)
    own = pltpu.make_async_copy(pieces.at[z, y, c, x], taken.at[z, y, c, x], local_sem.at[1])
    own.start()
    sends = []
    for (dz, dy, dc, dx), where in peers:
        copy = remote(
            pieces.at[where],
            taken.at[z, y, c, x],
            (send_sem, recv_sem),
            dz * 8 + dy * 4 + dc * 2 + dx,
            device(*where),
        )
        copy.start()
        sends.append(copy)
    early[0:16, :] = lax.dot_general(
        meta_mix[...],
        d_tokens[TOK_DEV:LIVE, :].astype(F32),
        (((1,), (0,)), ((), ())),
        precision=lax.Precision.HIGHEST,
        preferred_element_type=F32,
    )
    early[16:24, :] = late[...]
    early[16:17, :] = gain
    early[17:18, :] = shift
    early[24:32, :] = b_grad[...]
    begin.begin()
    scatter.stage_c()
    begin.turn(0)
    for start, count in BANDS[:-1]:
        band = slice(start, start + count)
        pixel_grad[band, :] = nt_dot(d_tokens[band, :], kernel[...])
    begin.turn(1)
    scatter.stage_d()
    begin.turn(2)
    own.wait()
    for copy in sends:
        copy.wait_recv()
    for n in range(32):
        block = taken[n // 8, (n // 4) % 2, (n // 2) % 2, n % 2].astype(F32)
        for at in range(COVER):
            rows[at, n * MAXB : (n + 1) * MAXB, :] = block[at * MAXB : (at + 1) * MAXB]
    d_hidden = jnp.zeros((32 * MAXB, GEN), F32)
    for at in range(COVER):
        d_hidden += nt_dot(rows[at].astype(BF), gen_shift[:, at * 128 : (at + 1) * 128])
    d_before = d_hidden * slope[...]
    source[0:GEN, :] = lax.dot_general(
        codes[...],
        d_before,
        (((1,), (0,)), ((), ())),
        precision=lax.Precision.HIGHEST,
        preferred_element_type=F32,
    )
    source[GEN : GEN + 8, :] = jnp.broadcast_to(column_sum(d_before), (8, GEN))
    total = Total(source, in_grad, *rest[5:10], here)
    total.begin()
    for at in range(COVER):
        out_grad[:, at * 128 : (at + 1) * 128] = nn_dot(hidden[...], rows[at].astype(BF))
    scatter.stage_e()
    begin.finish()
    for step in range(3):
        total.turn(step)
    total.finish()
    for copy in sends:
        copy.wait_send()


def closing(
    d_qkv, first, w_qkv, tokens, d_after, params, pixels, kernel, meta_mix, late, b_grad, live,
    hidden, gen_shift, slope, codes,
):
    vmem = pl.BlockSpec(memory_space=pltpu.VMEM)
    small, early = (GEN + 8, GEN), (32, D)
    held = (NZ, 2, 2, 2, PIECE, 128)
    _, _, _, rows, width = w_qkv.shape
    return pl.pallas_call(
        close_kernel,
        in_specs=[vmem] * 16,
        out_specs=[vmem] * 5,
        out_shape=[
            jax.ShapeDtypeStruct((GEN, COVER * 128), F32),
            jax.ShapeDtypeStruct(small, F32),
            jax.ShapeDtypeStruct((rows, width // 2), F32),
            jax.ShapeDtypeStruct(early, F32),
            jax.ShapeDtypeStruct(pixels.shape, F32),
        ],
        scratch_shapes=[
            pltpu.VMEM((LIVE, D), BF),
            pltpu.VMEM(w_qkv.shape, BF),
            pltpu.VMEM(held, BF),
            pltpu.VMEM(held, BF),
            pltpu.VMEM((FLAT + 64, 128), F32),
            pltpu.VMEM((6, MAXB * PIX, 128), F32),
            pltpu.VMEM((COVER, 32 * MAXB, 128), F32),
            pltpu.VMEM(small, F32),
            pltpu.VMEM(early, F32),
            pltpu.SemaphoreType.DMA((32,)),
            pltpu.SemaphoreType.DMA((32,)),
            pltpu.SemaphoreType.DMA((2,)),
            pltpu.SemaphoreType.DMA((8,)),
            pltpu.SemaphoreType.DMA((8,)),
            *total_scratch(early),
            *total_scratch(small),
            *scatter_scratch(rows, width),
        ],
        compiler_params=pltpu.CompilerParams(
            collective_id=2, has_side_effects=True, vmem_limit_bytes=VMEM_ASK
        ),
    )(
        d_qkv, first, w_qkv, tokens, d_after, params, pixels, kernel, meta_mix, late, b_grad, live,
        hidden, gen_shift, slope, codes,
    )


def mask_lanes(kind):
    row = lax.broadcasted_iota(jnp.int32, (ROWS, 128), 0)
    lane = lax.broadcasted_iota(jnp.int32, (ROWS, 128), 1)
    patch = jnp.where(kind == 1, 0, row // (TOK_DEV // SLOTS))
    segment = jnp.where(row < TOK_DEV, patch, (row - TOK_DEV) // 2)
    hot = (lane == segment) & (row < LIVE)
    for_query = jnp.where(hot, 1.0, 0.0)
    for_key = jnp.where(
        lane < SLOTS, jnp.where(hot, 0.0, -1e30), jnp.where(lane < SLOTS + 3, 1.0, 0.0)
    )
    return for_query.astype(BF), for_key.astype(BF)


def pad_into(target, source):
    target[0:TOK_DEV, 0:128] = source[0:TOK_DEV, :]
    target[TOK_DEV:ROWS, 0:128] = jnp.concatenate(
        [source[TOK_DEV:LIVE, :], jnp.zeros((ROWS - LIVE, 128), BF)], axis=0
    )


def tile_rows(source, first):
    if first + TILE <= LIVE:
        return source[first : first + TILE, :]
    part = source[first:LIVE, :]
    return jnp.concatenate([part, jnp.zeros((first + TILE - LIVE, 128), part.dtype)], axis=0)


def attend_kernel(
    q_ref, k_ref, v_ref, mask_q, mask_k, _u, _d, mixed, log_sum, full_u, full_d,
    keys, values, send_sem, recv_sem,
):
    step = pl.program_id(0)
    here = spot()
    u, d = [
        Gather(whole, (send_sem, recv_sem), 9 * at, here)
        for at, whole in enumerate((full_u, full_d))
    ]

    @pl.when(step == 0)
    def _():
        greet(near(*here))
        u.stage_c(False)
        d.stage_b()

    @pl.when(step == 3)
    def _():
        u.stage_d()
        d.stage_c()

    lane = lax.broadcasted_iota(jnp.int32, (TILE, 128), 1)
    pad_into(keys, k_ref)
    keys[:, 128:256] = mask_k[...]
    pad_into(values, v_ref)
    values[:, 128:256] = jnp.ones((ROWS, 128), BF)
    for tile in range(TILES):
        first = tile * TILE
        both = tile_rows(q_ref, first) * BF(0.125)
        results, sums = [], []
        for head in range(2):
            query = jnp.where((lane < HEAD) == (head == 0), both, BF(0))
            scores = nt_dot(
                jnp.concatenate([query, mask_q[first : first + TILE, :]], axis=1), keys[...]
            )
            peak = jnp.max(scores, axis=1, keepdims=True)
            expo = jnp.exp(scores - peak).astype(BF)
            made = nn_dot(expo, values[...])
            totals = made[:, 128:256]
            results.append(made[:, 0:128] / totals)
            sums.append(peak + jnp.log(totals))
        count = min(TILE, LIVE - first)
        mixed[first : first + count, :] = jnp.where(lane < HEAD, *results)[:count].astype(BF)
        log_sum[0, first : first + count, :] = jnp.where(lane < HEAD, *sums)[:count]

    @pl.when(step == HEADS // 2 - 1)
    def _():
        d.stage_d()
        u.finish(True, False)
        d.finish()


def attend(qkv, mask_q, mask_k, wholes):
    def band(first):
        return pl.BlockSpec((LIVE, 128), lambda pair: (0, first + pair))

    full = pl.BlockSpec((ROWS, 128), lambda pair: (0, 0))
    anywhere = pl.BlockSpec(memory_space=pl.ANY)
    return pl.pallas_call(
        attend_kernel,
        grid=(HEADS // 2,),
        in_specs=[band(0), band(6), band(12), full, full] + [anywhere] * 2,
        out_specs=[band(0), pl.BlockSpec((1, LIVE, 128), lambda pair: (pair, 0, 0))]
        + [anywhere] * 2,
        out_shape=[
            jax.ShapeDtypeStruct((LIVE, D), BF),
            jax.ShapeDtypeStruct((HEADS // 2, LIVE, 128), F32),
            *[jax.ShapeDtypeStruct(whole.shape, BF) for whole in wholes],
        ],
        input_output_aliases={5: 2, 6: 3},
        scratch_shapes=[pltpu.VMEM((ROWS, 256), BF)] * 2 + [pltpu.SemaphoreType.DMA((18,))] * 2,
        compiler_params=pltpu.CompilerParams(
            collective_id=1, has_side_effects=True, vmem_limit_bytes=VMEM_ASK
        ),
    )(qkv, qkv, qkv, mask_q, mask_k, *wholes)


def feed_kernel(
    tokens, mixed, top, w_out, vectors, w_up, w_down,
    layer_out, d_after, d_mixed, out_grad, rows, up_grad, down_grad, b_grad,
    second, second_turned, top_full, after, sum_out, sum_second, active, d_upper, proj,
):
    step = pl.program_id(0)

    @pl.when(step == 0)
    def _():
        for first, count in BANDS:
            band = slice(first, first + count)
            value = tokens[band, :] + (nn_dot(mixed[band, :], w_out[...]) + vectors[2:3, :])
            after[band, :] = value
            normed, _ = standard(value)
            put_rows(
                second, first, count, (normed * vectors[3:4, :] + vectors[4:5, :]).astype(BF)
            )
            put_rows(top_full, first, count, top[band, :])
        second_turned[...] = second[...].T
        sum_out[...] = jnp.zeros_like(sum_out)
        b_grad[...] = jnp.zeros_like(b_grad)
        sum_second[...] = jnp.zeros_like(sum_second)

    total = jnp.zeros((1, CHUNK), F32)
    for first, count in BANDS:
        count = -(-count // 16) * 16
        band = slice(first, first + count)
        upper = nn_dot(second[band, :], w_up[...]) + vectors[pl.ds(6 + step, 1), :]
        made, slope = gelu_parts(upper)
        made = made.astype(BF)
        active[band, :] = made
        back = (nt_dot(top_full[band, :], w_down[...]) * slope).astype(BF)
        d_upper[band, :] = back
        total += column_sum(back.astype(F32))
    b_grad[pl.ds(step, 1), :] = total
    sum_out[...] += nn_dot(active[...], w_down[...])
    sum_second[...] += nt_dot(d_upper[...], w_up[...])
    down_grad[...] = inner_dot(active[...], top_full[...]).astype(BF)
    up_grad[...] = nn_dot(second_turned[...], d_upper[...]).astype(BF)

    @pl.when(step == pl.num_programs(0) - 1)
    def _():
        gain = shift = bias = last = jnp.zeros((1, D), F32)
        for first, count in BANDS:
            band = slice(first, first + count)
            value = after[band, :]
            layer_out[band, :] = (value + sum_out[band, :] + vectors[5:6, :]).astype(BF)
            normed, scale = standard(value)
            upstream = sum_second[band, :]
            gain += column_sum(upstream * normed)
            shift += column_sum(upstream)
            scaled = upstream * vectors[3:4, :]
            inside = (
                scaled
                - jnp.mean(scaled, axis=-1, keepdims=True)
                - normed * jnp.mean(scaled * normed, axis=-1, keepdims=True)
            )
            grad_top = top[band, :].astype(F32)
            last += column_sum(grad_top)
            result = grad_top + scale * inside
            d_after[band, :] = result
            low = result.astype(BF)
            bias += column_sum(low.astype(F32))
            put_rows(proj, first, count, low)
            d_mixed[band, :] = nt_dot(low, w_out[...]).astype(BF)
        out_grad[...] = inner_dot(mixed[...], proj[0:LIVE, :]).astype(BF)
        rows[...] = jnp.concatenate([jnp.zeros((2, D), F32), bias, gain, shift, last, jnp.zeros((2, D), F32)], axis=0)


def feed(tokens, mixed, top, w_out, vectors, w_up, w_down):
    width = w_up.shape[1]

    def whole(*shape):
        return pl.BlockSpec(shape, lambda step: (0, 0))

    across = pl.BlockSpec((D, CHUNK), lambda step: (0, step))
    down = pl.BlockSpec((CHUNK, D), lambda step: (step, 0))
    block = whole(LIVE, D)
    return pl.pallas_call(
        feed_kernel,
        grid=(width // CHUNK,),
        in_specs=[block, block, block, whole(D, D), whole(16, D), across, down],
        out_specs=[block, block, block, whole(D, D), whole(8, D), across, down, whole(8, D)],
        out_shape=[
            jax.ShapeDtypeStruct((LIVE, D), BF),
            jax.ShapeDtypeStruct((LIVE, D), F32),
            jax.ShapeDtypeStruct((LIVE, D), BF),
            jax.ShapeDtypeStruct((D, D), BF),
            jax.ShapeDtypeStruct((8, D), F32),
            jax.ShapeDtypeStruct((D, width), BF),
            jax.ShapeDtypeStruct((width, D), BF),
            jax.ShapeDtypeStruct((8, D), F32),
        ],
        scratch_shapes=[
            pltpu.VMEM((ROWS, D), BF),
            pltpu.VMEM((D, ROWS), BF),
            pltpu.VMEM((ROWS, D), BF),
            pltpu.VMEM((LIVE, D), F32),
            pltpu.VMEM((ROWS, D), F32),
            pltpu.VMEM((ROWS, D), F32),
            pltpu.VMEM((ROWS, CHUNK), BF),
            pltpu.VMEM((ROWS, CHUNK), BF),
            pltpu.VMEM((ROWS, D), BF),
        ],
        compiler_params=pltpu.CompilerParams(vmem_limit_bytes=VMEM_ASK),
    )(tokens, mixed, top, w_out, vectors, w_up, w_down)


def three_parts(exact):
    high = exact.astype(BF)
    left = exact - high.astype(F32)
    middle = left.astype(BF)
    return high, middle, (left - middle.astype(F32)).astype(BF)


def attend_back_kernel(
    q_ref, k_ref, v_ref, d_mixed, mixed, log_sum, mask_q, mask_k, go, gu, gd,
    out, out_o, out_u, out_d,
    keys, values, keys_turned, d_query, d_keys, d_values, send_sem, recv_sem, local_sem, *rest,
):
    pair, part = pl.program_id(0), pl.program_id(1)
    here = spot()
    o, u, d = [
        Scatter(
            whole, *rest[7 * at : 7 * at + 7], result, (send_sem, recv_sem, local_sem), 8 * at, here
        )
        for at, (whole, result) in enumerate(((go, out_o), (gu, out_u), (gd, out_d)))
    ]

    @pl.when((pair == 0) & (part == 0))
    def _():
        greet(near(*here))
        d.stage_a()
        u.stage_a()
        o.stage_a()

    @pl.when((pair == 0) & (part == 1))
    def _():
        d.stage_b()

    @pl.when((pair == 1) & (part == 1))
    def _():
        u.stage_b()
        d.stage_c()

    @pl.when((pair == 2) & (part == 1))
    def _():
        o.stage_b()
        u.stage_c()

    @pl.when((pair == 3) & (part == 1))
    def _():
        d.stage_d()
        o.stage_c()

    @pl.when((pair == 4) & (part == 1))
    def _():
        u.stage_d()

    @pl.when((pair == 5) & (part == 1))
    def _():
        d.stage_e()
        o.stage_d()

    @pl.when((pair == 5) & (part == 2))
    def _():
        u.stage_e()
        o.stage_e()

    lane = lax.broadcasted_iota(jnp.int32, (TILE, 128), 1)
    sub = lax.broadcasted_iota(jnp.int32, (128, TILE), 0)

    def with_parts(exact, rest):
        a, b, c = three_parts(exact)
        return jnp.where(
            lane == SLOTS,
            a,
            jnp.where(lane == SLOTS + 1, b, jnp.where(lane == SLOTS + 2, c, rest)),
        )

    @pl.when(part == 0)
    def _():
        pad_into(keys, k_ref)
        keys[:, 128:256] = mask_k[...]
        pad_into(values, v_ref)
        values[:, 128:256] = mask_k[...]
        keys_turned[...] = keys[:, 0:128].T
        d_keys[...] = jnp.zeros_like(d_keys)
        d_values[...] = jnp.zeros_like(d_values)
        for tile in range(TILES):
            first = tile * TILE
            both = tile_rows(q_ref, first) * BF(0.125)
            up = tile_rows(d_mixed, first)
            logs = tile_rows(log_sum.at[0], first)
            product = up.astype(F32) * tile_rows(mixed, first).astype(F32)
            marks = mask_q[first : first + TILE, :]
            turned = []
            for head in range(2):
                chosen = (lane < HEAD) == (head == 0)
                query = jnp.where(chosen, both, BF(0))
                upstream = jnp.where(chosen, up, BF(0))
                inside = jnp.sum(jnp.where(chosen, product, 0.0), axis=1, keepdims=True)
                wide_query = jnp.concatenate(
                    [query, with_parts(-logs[:, head * HEAD : head * HEAD + 1], marks)], axis=1
                )
                wide_up = jnp.concatenate(
                    [upstream, with_parts(-inside, jnp.zeros_like(marks))], axis=1
                )
                prob = jnp.exp(nt_dot(keys[...], wide_query))
                d_scores = (prob * nt_dot(values[...], wide_up)).astype(BF)
                d_values[...] += nn_dot(prob.astype(BF), upstream)
                d_keys[...] += nn_dot(d_scores, query)
                turned.append(nn_dot(keys_turned[...], d_scores))
            d_query[first : first + TILE, :] = (
                (jnp.where(sub < HEAD, *turned) * 0.125).T.astype(BF)
            )
        out[...] = d_query[0:LIVE, :]

    @pl.when(part == 1)
    def _():
        out[...] = d_keys[0:LIVE, :].astype(BF)

    @pl.when(part == 2)
    def _():
        out[...] = d_values[0:LIVE, :].astype(BF)


def attend_back(qkv, d_mixed, mixed, log_sum, mask_q, mask_k, grads):
    def band(first):
        return pl.BlockSpec((LIVE, 128), lambda pair, part: (0, first + pair))

    full = pl.BlockSpec((ROWS, 128), lambda pair, part: (0, 0))
    shapes = [grad.shape[3:] for grad in grads]
    outs = [(rows, width // 2) for rows, width in shapes]
    return pl.pallas_call(
        attend_back_kernel,
        grid=(HEADS // 2, 3),
        in_specs=[
            band(0), band(6), band(12), band(0), band(0),
            pl.BlockSpec((1, LIVE, 128), lambda pair, part: (pair, 0, 0)), full, full,
        ]
        + [pl.BlockSpec(memory_space=pl.ANY)] * 3,
        out_specs=[pl.BlockSpec((LIVE, 128), lambda pair, part: (0, part * 6 + pair))]
        + [pl.BlockSpec(shape, lambda pair, part: (0, 0)) for shape in outs],
        out_shape=[
            jax.ShapeDtypeStruct((LIVE, 3 * D), BF),
            *[jax.ShapeDtypeStruct(shape, F32) for shape in outs],
        ],
        scratch_shapes=[
            pltpu.VMEM((ROWS, 256), BF),
            pltpu.VMEM((ROWS, 256), BF),
            pltpu.VMEM((128, ROWS), BF),
            pltpu.VMEM((ROWS, 128), BF),
            pltpu.VMEM((ROWS, 128), F32),
            pltpu.VMEM((ROWS, 128), F32),
            pltpu.SemaphoreType.DMA((24,)),
            pltpu.SemaphoreType.DMA((24,)),
            pltpu.SemaphoreType.DMA((3,)),
            *[entry for shape in shapes for entry in scatter_scratch(*shape)],
        ],
        compiler_params=pltpu.CompilerParams(
            collective_id=3, has_side_effects=True, vmem_limit_bytes=VMEM_ASK
        ),
    )(qkv, qkv, qkv, d_mixed, mixed, log_sum, mask_q, mask_k, *grads)


def place_table(kind, ground):
    quarter = D // 4
    entry = jnp.arange(64, dtype=jnp.int32)
    chip = jnp.where(kind == 1, 0, entry // 16)
    step = jnp.where(kind == 1, entry, entry % 16).astype(F32)
    scale = (
        jnp.sum(
            jnp.where(
                chip[:, None] == jnp.arange(SLOTS, dtype=jnp.int32)[None, :], ground[None, :], 0
            ),
            axis=1,
        ).astype(F32)
        / 10.0
    )
    omega = 1.0 / 10000.0 ** (jnp.arange(quarter, dtype=F32) / (quarter - 1))
    angle = (step * scale)[:, None] * omega[None, :]
    exact = jnp.concatenate([jnp.sin(angle), jnp.cos(angle)], axis=1)
    table = jnp.concatenate([*three_parts(exact), jnp.zeros((64, 2 * quarter), BF)], axis=0)
    index = jnp.arange(TOK_DEV, dtype=jnp.int32)[:, None]
    lane = jnp.arange(512, dtype=jnp.int32)[None, :]
    across = jnp.where(kind == 1, index // 32, index // 16)
    along = jnp.where(kind == 1, index % 32, index // 256 * 16 + index % 16)
    spots = jnp.where(lane < 256, across, along)
    hot = (lane % 64 == spots) & (lane % 256 < 192)
    return table, jnp.where(hot, 1.0, 0.0).astype(BF)


def body_block(
    pixels,
    wave_table,
    band_count,
    wave_index,
    group_sensor,
    chip_kind,
    chip_gsd,
    time_loc,
    gen_in,
    gen_bias,
    gen_out,
    meta_weight,
    w_qkv,
    w_out,
    w_up,
    w_down,
    vectors,
    b_up,
    cotangent,
):
    group = lax.axis_index("dp")
    owner = group * 2 + lax.axis_index("fsdp")
    is_sensor = group_sensor[:, None] == jnp.arange(SENSORS, dtype=jnp.int32)[None, :]
    bands_of = jnp.sum(jnp.where(is_sensor, band_count[None, :], 0), axis=1)
    waves_of = jnp.sum(jnp.where(is_sensor[:, :, None], wave_index[None], 0), axis=1)
    band_total = jnp.sum(jnp.where(jnp.arange(GROUPS, dtype=jnp.int32) == group, bands_of, 0))
    live = (jnp.arange(MAXB, dtype=jnp.int32)[None, :] < bands_of[:, None]).reshape(-1, 1)
    codes = wave_code(table_lookup(waves_of.reshape(-1), wave_table))
    before = exact_dot(codes, gen_in.astype(F32)) + gen_bias.astype(F32)
    hidden = jnp.where(live, gelu_exact(before), 0.0).astype(BF)
    slope = jnp.where(live, gelu_slope(before, jnp.ones_like(before)), 0.0)
    made, gen_shift = make_pieces(hidden, gen_out)
    width, rows, up_rows = gen_out.shape[1], vectors.shape[0], b_up.shape[0]
    lane = jnp.arange(D, dtype=jnp.int32)
    row = jnp.arange(10, dtype=jnp.int32)[:, None]
    per_row = D // up_rows
    small = jnp.where(
        row < 6,
        jnp.where(
            (lane // rows == group)[None, :],
            jnp.concatenate([jnp.tile(vectors.T, (1, GROUPS)), jnp.zeros((4, D), BF)], axis=0),
            BF(0),
        ),
        jnp.where(
            (row == 6 + group // per_row) & (lane // up_rows == group % per_row)[None, :],
            jnp.tile(b_up, per_row)[None, :],
            BF(0),
        ),
    )
    small = jnp.pad(small, ((0, 6), (0, 0)))
    kind_one = chip_kind[0]
    band_float = band_total.astype(F32)
    table, places = place_table(kind_one, chip_gsd[0])
    meta_mix = jnp.concatenate(
        [
            jnp.stack([jnp.ones((SLOTS,), F32), jnp.zeros((SLOTS,), F32)], axis=1).reshape(1, -1),
            jnp.stack([jnp.zeros_like(time_loc[0]), time_loc[0]], axis=1).reshape(
                2 * SLOTS, -1
            ).T,
            jnp.zeros((7, 2 * SLOTS), F32),
        ],
        axis=0,
    )
    meta_rows = exact_dot(
        meta_mix.T, jnp.pad(meta_weight.astype(F32), ((0, 7), (0, 0)))
    )
    full_q, full_o, part_u, part_d, params, kernel, tokens_in, first, qkv = opening(
        w_qkv,
        w_out,
        w_up,
        w_down,
        small,
        made.reshape(NZ, 2, 2, PIECE, 128),
        pixels,
        table,
        places,
        meta_rows,
        jnp.broadcast_to(band_float, (8, 128)),
    )
    mask_q, mask_k = mask_lanes(kind_one)
    mixed, log_sum, full_u, full_d = attend(qkv, mask_q, mask_k, [part_u, part_d])
    w_out_all = full_o.reshape(D, D)
    w_up_all = full_u.reshape(D, -1)
    w_down_all = full_d.reshape(-1, D)
    layer_out, d_after, d_mixed, w_out_grad, late, w_up_grad, w_down_grad, b_grad = feed(
        tokens_in, mixed, cotangent, w_out_all, params, w_up_all, w_down_all
    )
    d_qkv, w_out_out, w_up_out, w_down_out = attend_back(
        qkv,
        d_mixed,
        mixed,
        log_sum,
        mask_q,
        mask_k,
        [
            grad.reshape(NZ, 2, 2, -1, grad.shape[1])
            for grad in (w_out_grad, w_up_grad, w_down_grad)
        ],
    )

    def by_block(rows_of):
        return jnp.broadcast_to(
            rows_of.reshape(GROUPS, 1, MAXB, GEN), (GROUPS, 2, MAXB, GEN)
        ).reshape(32 * MAXB, GEN)

    own_live = (jnp.arange(16, dtype=jnp.int32) < band_total)[:, None]
    gen_out_wide, gen_small, w_qkv_out, summed, pixel_grad = closing(
        d_qkv,
        first,
        full_q,
        tokens_in,
        d_after,
        params,
        pixels,
        kernel,
        meta_mix,
        late,
        b_grad,
        jnp.where(own_live, 1.0 / band_float, 0.0),
        by_block(hidden).T,
        gen_shift,
        by_block(slope),
        by_block(codes).T,
    )
    gen_out_grad = lax.dynamic_slice(gen_out_wide, (0, (owner * width) % 128), (GEN, width))
    vectors_out = lax.dynamic_slice(summed, (16, group * rows), (6, rows)).T
    b_up_out = lax.dynamic_slice(
        summed[24:28].reshape(-1), (group * up_rows,), (up_rows,)
    )
    return (
        layer_out,
        pixel_grad,
        gen_small[:GEN],
        gen_small[GEN],
        gen_out_grad,
        summed[:9],
        w_qkv_out,
        w_out_out,
        w_up_out,
        w_down_out,
        vectors_out,
        b_up_out,
    )


def solution(mesh):
    fits = dict(mesh.shape) == {"dp": 16, "fsdp": 2}
    body = body_block if fits else body_general
    placed = (
        P(("dp", "fsdp"), None),
        P(),
        P(),
        P(),
        P(),
        P(("dp", "fsdp")),
        P(("dp", "fsdp"), None),
        P(("dp", "fsdp"), None, None),
        P(),
        P(),
        P(None, ("dp", "fsdp")),
        P(),
        P("dp", "fsdp"),
        P("dp", "fsdp"),
        P("dp", "fsdp"),
        P("dp", "fsdp"),
        P("dp", None),
        P("dp"),
        P(("dp", "fsdp"), None),
    )
    return jax.shard_map(
        body,
        mesh=mesh,
        in_specs=placed,
        out_specs=(
            P(("dp", "fsdp"), None),
            P(("dp", "fsdp"), None),
            P(),
            P(),
            P(None, ("dp", "fsdp")),
            P(),
            P("dp", "fsdp"),
            P("dp", "fsdp"),
            P("dp", "fsdp"),
            P("dp", "fsdp"),
            P("dp", None),
            P("dp"),
        ),
        check_vma=False,
    )
```

```python
import math

import jax
import jax.numpy as jnp
from jax import lax
from jax.experimental import pallas as pl
from jax.experimental.pallas import tpu as pltpu
from jax.sharding import PartitionSpec as P

D = 768
HEADS = 12
HEAD = 64
GEN = 128
PIX = 64
MAXB = 10
SENSORS = 7
TOK_DEV = 1024
SLOTS = 4
GENOUT = 49920


def exact_dot(left, right):
    return jnp.dot(left, right, precision=lax.Precision.HIGHEST)


def inner_dot(left, right):
    return lax.dot_general(
        left, right, (((0,), (0,)), ((), ())), preferred_element_type=jnp.float32
    )


def outer_dot(left, right):
    return lax.dot_general(
        left, right, (((1,), (1,)), ((), ())), preferred_element_type=jnp.float32
    )


def gelu_exact(values):
    return jax.nn.gelu(values, approximate=False)


def gelu_slope(values, upstream):
    return jax.vjp(gelu_exact, values)[1](upstream)[0]


def table_lookup(indices, table):
    return jnp.sum(
        jnp.where(
            indices[:, None] == jnp.arange(table.shape[0], dtype=jnp.int32)[None, :],
            table[None, :],
            0.0,
        ),
        axis=1,
    )


def wave_code(wavelengths):
    half = GEN // 2
    omega = 1.0 / 10000.0 ** (jnp.arange(half, dtype=jnp.float32) / half)
    angle = (wavelengths * 1000.0)[:, None] * omega[None, :]
    return jnp.concatenate([jnp.sin(angle), jnp.cos(angle)], axis=1)


def place_code(kind_one, gsd_one):
    small = TOK_DEV // SLOTS
    index = jnp.arange(TOK_DEV, dtype=jnp.int32)
    within = jnp.where(kind_one == 1, index, index % small)
    side = jnp.where(kind_one == 1, math.isqrt(TOK_DEV), math.isqrt(small)).astype(jnp.int32)
    across = (within // side).astype(jnp.float32)
    along = (within % side).astype(jnp.float32)
    holder = jnp.where(kind_one == 1, 0, index // small)
    ground = (
        jnp.sum(
            jnp.where(
                holder[:, None] == jnp.arange(SLOTS, dtype=jnp.int32)[None, :], gsd_one[None, :], 0
            ),
            axis=1,
        ).astype(jnp.float32)
        / 10.0
    )
    quarter = D // 4
    omega = 1.0 / 10000.0 ** (jnp.arange(quarter, dtype=jnp.float32) / (quarter - 1))
    first = (across * ground)[:, None] * omega[None, :]
    second = (along * ground)[:, None] * omega[None, :]
    return jnp.concatenate(
        [jnp.sin(first), jnp.cos(first), jnp.sin(second), jnp.cos(second)], axis=1
    )


def segment_ids(kind_one):
    index = jnp.arange(TOK_DEV, dtype=jnp.int32)
    patches = jnp.where(kind_one == 1, 0, index // (TOK_DEV // SLOTS))
    extra = jnp.arange(2 * SLOTS, dtype=jnp.int32) // 2
    return jnp.concatenate([patches, extra])


def layer_norm(values, gain, shift):
    centred = values - jnp.mean(values, axis=-1, keepdims=True)
    scale = lax.rsqrt(jnp.mean(centred * centred, axis=-1, keepdims=True) + 1e-05)
    normed = centred * scale
    return (normed * gain + shift, normed, scale)


def norm_back(upstream, normed, scale, gain):
    gain_grad = jnp.sum(upstream * normed, axis=0)
    shift_grad = jnp.sum(upstream, axis=0)
    scaled = upstream * gain
    inside = (
        scaled
        - jnp.mean(scaled, axis=-1, keepdims=True)
        - normed * jnp.mean(scaled * normed, axis=-1, keepdims=True)
    )
    return (scale * inside, gain_grad, shift_grad)


def body_general(
    pixels,
    wave_table,
    band_count,
    wave_index,
    group_sensor,
    chip_kind,
    chip_gsd,
    time_loc,
    gen_in,
    gen_bias,
    gen_out,
    meta_weight,
    w_qkv,
    w_out,
    w_up,
    w_down,
    vectors,
    b_up,
    cotangent,
):
    half_type = jnp.bfloat16
    group = lax.axis_index("dp")
    sensor = jnp.sum(
        jnp.where(jnp.arange(group_sensor.shape[0], dtype=jnp.int32) == group, group_sensor, 0)
    )
    chosen_sensor = jnp.arange(SENSORS, dtype=jnp.int32) == sensor
    band_total = jnp.sum(jnp.where(chosen_sensor, band_count, 0))
    gen_in_full = gen_in.astype(jnp.float32)
    gen_bias_full = gen_bias.astype(jnp.float32)
    codes = wave_code(table_lookup(wave_index.reshape(-1), wave_table))
    before = exact_dot(codes, gen_in_full) + gen_bias_full
    hidden = gelu_exact(before).astype(half_type)
    shard_made = jnp.dot(hidden, gen_out, preferred_element_type=jnp.float32).astype(half_type)
    all_made = lax.all_gather(shard_made, ("dp", "fsdp"), axis=1, tiled=True)
    generated = lax.dynamic_slice_in_dim(all_made, sensor * MAXB, MAXB, 0)
    live_band = (jnp.arange(MAXB, dtype=jnp.int32) < band_total)[:, None]
    kernel = jnp.where(live_band, generated[:, : PIX * D], jnp.zeros((), half_type)).reshape(
        MAXB * PIX, D
    )
    band_float = band_total.astype(jnp.float32)
    embed_bias = (
        jnp.sum(jnp.where(live_band, generated[:, PIX * D :].astype(jnp.float32), 0.0), axis=0)
        / band_float
    )
    kind_one = chip_kind[0]
    patches = (
        jnp.dot(pixels, kernel, preferred_element_type=jnp.float32)
        + embed_bias
        + place_code(kind_one, chip_gsd[0])
    )
    meta_full = meta_weight.astype(jnp.float32)
    stamps = exact_dot(time_loc[0], meta_full[1:])
    classes = jnp.broadcast_to(meta_full[0], stamps.shape)
    extra = jnp.stack([classes, stamps], axis=1).reshape(2 * SLOTS, D)
    tokens_in = jnp.concatenate([patches, extra], axis=0)
    total_rows = tokens_in.shape[0]
    qkv_rows, out_rows, up_rows, down_rows, vectors_all, b_up_all = (
        lax.all_gather(w_qkv, "dp", axis=0, tiled=True),
        lax.all_gather(w_out, "dp", axis=0, tiled=True),
        lax.all_gather(w_up, "dp", axis=0, tiled=True),
        lax.all_gather(w_down, "dp", axis=0, tiled=True),
        lax.all_gather(vectors, "dp", axis=0, tiled=True),
        lax.all_gather(b_up, "dp", axis=0, tiled=True),
    )
    w_qkv_all, w_out_all, w_up_all, w_down_all = (
        lax.all_gather(qkv_rows, "fsdp", axis=1, tiled=True),
        lax.all_gather(out_rows, "fsdp", axis=1, tiled=True),
        lax.all_gather(up_rows, "fsdp", axis=1, tiled=True),
        lax.all_gather(down_rows, "fsdp", axis=1, tiled=True),
    )
    vector_full = vectors_all.astype(jnp.float32)
    b_up_full = b_up_all.astype(jnp.float32)
    first_norm, normed_one, scale_one = layer_norm(tokens_in, vector_full[:, 0], vector_full[:, 1])
    first = first_norm.astype(half_type)
    qkv = jnp.dot(first, w_qkv_all, preferred_element_type=jnp.float32).astype(half_type)
    query = qkv[:, :D].reshape(total_rows, HEADS, HEAD)
    keys = qkv[:, D : 2 * D].reshape(total_rows, HEADS, HEAD)
    values = qkv[:, 2 * D :].reshape(total_rows, HEADS, HEAD)
    segment = segment_ids(kind_one)
    same = (segment[:, None] == segment[None, :])[None]
    scores = jnp.einsum("qhd,khd->hqk", query, keys, preferred_element_type=jnp.float32) * HEAD ** (
        -0.5
    )
    scores = jnp.where(same, scores, -1e30)
    peak = jnp.max(scores, axis=-1, keepdims=True)
    expo = jnp.exp(scores - peak)
    totals = jnp.sum(expo, axis=-1, keepdims=True)
    prob_half = (expo / totals).astype(half_type)
    mixed = (
        jnp.einsum("hqk,khd->qhd", prob_half, values, preferred_element_type=jnp.float32)
        .reshape(total_rows, D)
        .astype(half_type)
    )
    after = tokens_in + (
        jnp.dot(mixed, w_out_all, preferred_element_type=jnp.float32) + vector_full[:, 2]
    )
    second_norm, normed_two, scale_two = layer_norm(after, vector_full[:, 3], vector_full[:, 4])
    second = second_norm.astype(half_type)
    upper = jnp.dot(second, w_up_all, preferred_element_type=jnp.float32) + b_up_full
    active = gelu_exact(upper).astype(half_type)
    layer_out = (
        after + jnp.dot(active, w_down_all, preferred_element_type=jnp.float32) + vector_full[:, 5]
    ).astype(half_type)
    grad_top = cotangent.astype(jnp.float32)
    w_down_grad = inner_dot(active, cotangent)
    down_bias_grad = jnp.sum(grad_top, axis=0)
    d_active = outer_dot(cotangent, w_down_all)
    d_upper = gelu_slope(upper, d_active).astype(half_type)
    w_up_grad = inner_dot(second, d_upper)
    b_up_grad = jnp.sum(d_upper.astype(jnp.float32), axis=0)
    d_second = outer_dot(d_upper, w_up_all)
    d_after_norm, gain_two_grad, shift_two_grad = norm_back(
        d_second, normed_two, scale_two, vector_full[:, 3]
    )
    d_after = grad_top + d_after_norm
    d_proj = d_after.astype(half_type)
    w_out_grad = inner_dot(mixed, d_proj)
    out_bias_grad = jnp.sum(d_proj.astype(jnp.float32), axis=0)
    d_mixed = outer_dot(d_proj, w_out_all).astype(half_type).reshape(total_rows, HEADS, HEAD)
    again = jnp.einsum("qhd,khd->hqk", query, keys, preferred_element_type=jnp.float32) * HEAD ** (
        -0.5
    )
    again = jnp.where(same, again, -1e30)
    prob_full = jnp.exp(again - peak) / totals
    recalled = prob_full.astype(half_type)
    d_values = jnp.einsum("hqk,qhd->khd", recalled, d_mixed, preferred_element_type=jnp.float32)
    d_prob = jnp.einsum("qhd,khd->hqk", d_mixed, values, preferred_element_type=jnp.float32)
    d_scores = prob_full * (d_prob - jnp.sum(d_prob * prob_full, axis=-1, keepdims=True))
    d_scores = jnp.where(same, d_scores, 0.0).astype(half_type)
    d_query = jnp.einsum(
        "hqk,khd->qhd", d_scores, keys, preferred_element_type=jnp.float32
    ) * HEAD ** (-0.5)
    d_keys = jnp.einsum(
        "hqk,qhd->khd", d_scores, query, preferred_element_type=jnp.float32
    ) * HEAD ** (-0.5)
    d_qkv = jnp.concatenate(
        [
            d_query.reshape(total_rows, D),
            d_keys.reshape(total_rows, D),
            d_values.reshape(total_rows, D),
        ],
        axis=1,
    ).astype(half_type)
    w_qkv_grad = inner_dot(first, d_qkv)
    d_first = outer_dot(d_qkv, w_qkv_all)
    d_tokens_norm, gain_one_grad, shift_one_grad = norm_back(
        d_first, normed_one, scale_one, vector_full[:, 0]
    )
    d_tokens = (d_after + d_tokens_norm).astype(half_type)
    vectors_grad = jnp.stack(
        [
            gain_one_grad,
            shift_one_grad,
            out_bias_grad,
            gain_two_grad,
            shift_two_grad,
            down_bias_grad,
        ],
        axis=1,
    )
    d_patches = d_tokens[:TOK_DEV]
    d_extra = d_tokens[TOK_DEV:].astype(jnp.float32).reshape(SLOTS, 2, D)
    pixel_grad = outer_dot(d_patches, kernel)
    class_grad = jnp.sum(d_extra[:, 0], axis=0)
    stamp_grad = exact_dot(time_loc[0].T, d_extra[:, 1])
    meta_part = jnp.concatenate([class_grad[None, :], stamp_grad], axis=0)
    d_kernel = inner_dot(pixels, d_patches).reshape(MAXB, PIX * D)
    d_kernel = jnp.where(live_band, d_kernel, 0.0)
    d_bias = jnp.sum(d_patches.astype(jnp.float32), axis=0) / band_float
    d_bias_rows = jnp.where(live_band, d_bias[None, :], 0.0)
    d_generated = jnp.concatenate([d_kernel, d_bias_rows], axis=1).astype(half_type)
    placed = jnp.where(
        chosen_sensor[:, None, None], d_generated.astype(jnp.float32)[None], 0.0
    ).reshape(SENSORS * MAXB, GENOUT)
    columns = lax.psum_scatter(placed, ("dp", "fsdp"), scatter_dimension=1, tiled=True)
    gen_out_grad = exact_dot(hidden.astype(jnp.float32).T, columns)
    d_hidden = exact_dot(columns, gen_out.astype(jnp.float32).T)
    d_before = gelu_slope(before, d_hidden)
    gen_in_part = exact_dot(codes.T, d_before)
    gen_bias_part = jnp.sum(d_before, axis=0)
    meta_grad, gen_in_grad, gen_bias_grad = lax.psum(
        (meta_part, gen_in_part, gen_bias_part), ("dp", "fsdp")
    )
    qkv_cols, out_cols, up_cols, down_cols = (
        lax.psum_scatter(
            w_qkv_grad.astype(jnp.bfloat16), "fsdp", scatter_dimension=1, tiled=True
        ).astype(jnp.float32),
        lax.psum_scatter(
            w_out_grad.astype(jnp.bfloat16), "fsdp", scatter_dimension=1, tiled=True
        ).astype(jnp.float32),
        lax.psum_scatter(
            w_up_grad.astype(jnp.bfloat16), "fsdp", scatter_dimension=1, tiled=True
        ).astype(jnp.float32),
        lax.psum_scatter(
            w_down_grad.astype(jnp.bfloat16), "fsdp", scatter_dimension=1, tiled=True
        ).astype(jnp.float32),
    )
    vectors_group, b_up_group = lax.psum((vectors_grad, b_up_grad), "fsdp")
    w_qkv_out, w_out_out, w_up_out, w_down_out, vectors_out, b_up_out = (
        lax.psum_scatter(
            qkv_cols.astype(jnp.bfloat16), "dp", scatter_dimension=0, tiled=True
        ).astype(jnp.float32),
        lax.psum_scatter(
            out_cols.astype(jnp.bfloat16), "dp", scatter_dimension=0, tiled=True
        ).astype(jnp.float32),
        lax.psum_scatter(
            up_cols.astype(jnp.bfloat16), "dp", scatter_dimension=0, tiled=True
        ).astype(jnp.float32),
        lax.psum_scatter(
            down_cols.astype(jnp.bfloat16), "dp", scatter_dimension=0, tiled=True
        ).astype(jnp.float32),
        lax.psum_scatter(
            vectors_group.astype(jnp.bfloat16), "dp", scatter_dimension=0, tiled=True
        ).astype(jnp.float32),
        lax.psum_scatter(
            b_up_group.astype(jnp.bfloat16), "dp", scatter_dimension=0, tiled=True
        ).astype(jnp.float32),
    )
    return (
        layer_out,
        pixel_grad,
        gen_in_grad,
        gen_bias_grad,
        gen_out_grad,
        meta_grad,
        w_qkv_out,
        w_out_out,
        w_up_out,
        w_down_out,
        vectors_out,
        b_up_out,
    )


LIVE = 1032
ROWS = 1040
TILE = 208
TILES = 5
NZ = 4
GROUPS = 16
PIECE = 144
COVER = 14
VMEM_ASK = 60 * 1024 * 1024
BF = jnp.bfloat16
F32 = jnp.float32


def nt_dot(left, right):
    return lax.dot_general(left, right, (((1,), (1,)), ((), ())), preferred_element_type=F32)


def nn_dot(left, right):
    return lax.dot_general(left, right, (((1,), (0,)), ((), ())), preferred_element_type=F32)


def spot():
    group = lax.axis_index("dp")
    return group // 4, (group // 2) % 2, group % 2, lax.axis_index("fsdp")


def device(z, y, c, x):
    return {"dp": z * 4 + y * 2 + c, "fsdp": x}


def remote(source, target, sems, slot, where):
    return pltpu.make_async_remote_copy(
        src_ref=source,
        dst_ref=target,
        send_sem=sems[0].at[slot],
        recv_sem=sems[1].at[slot],
        device_id=where,
        device_id_type=pl.DeviceIdType.MESH,
    )


def greet(others):
    barrier = pltpu.get_barrier_semaphore()
    for where in others:
        pl.semaphore_signal(
            barrier, inc=1, device_id=where, device_id_type=pl.DeviceIdType.MESH
        )
    pl.semaphore_wait(barrier, len(others))


def columns(ref, x):
    width = ref.shape[-1] // 2
    return pl.ds(pl.multiple_of(x * width, 128), width)


def group_peers(z, y, c, x):
    return [
        ((dz, dy, dc), device((z + dz) % NZ, (y + dy) % 2, (c + dc) % 2, x))
        for dz in range(NZ)
        for dy in range(2)
        for dc in range(2)
        if dz + dy + dc
    ]


CHUNK = 768
BANDS = ((0, 256), (256, 256), (512, 256), (768, 256), (1024, 8))


def gelu_parts(values):
    bell = jnp.exp(values * values * (-0.5))
    step = 1.0 / (1.0 + (0.3275911 * math.sqrt(0.5)) * jnp.abs(values))
    poly = 0.5 * 1.061405429 * step - 0.5 * 1.453152027
    poly = poly * step + 0.5 * 1.421413741
    poly = poly * step - 0.5 * 0.284496736
    poly = poly * step + 0.5 * 0.254829592
    tail = poly * step * bell
    below = jnp.where(values < 0.0, tail, 1.0 - tail)
    return values * below, below + values * bell * (1.0 / math.sqrt(2.0 * math.pi))


def standard(values):
    centred = values - jnp.mean(values, axis=-1, keepdims=True)
    scale = lax.rsqrt(jnp.mean(centred * centred, axis=-1, keepdims=True) + 1e-05)
    return centred * scale, scale


def column_sum(values):
    return jnp.sum(values, axis=0, keepdims=True)


def put_rows(target, first, count, values):
    if count % 16:
        values = jnp.concatenate(
            [values, jnp.zeros((16 - count % 16, values.shape[1]), values.dtype)], axis=0
        )
    target[first : first + values.shape[0], :] = values


class Gather:
    COPIES = 19

    def __init__(self, shard, whole, sems, local, first, lean, here):
        z, y, c, x = here
        self.lean = lean
        mine, other = columns(whole, x), columns(whole, 1 - x)
        across, beside, twin = device(z, y, c, 1 - x), device(z, 1 - y, c, x), device(z, y, 1 - c, x)
        target = whole.at[z, y, c, :, mine]
        self.local = pltpu.make_async_copy(shard, target, local)
        self.along = [
            remote(shard, target, sems, first + k - 1, device((z + k) % NZ, y, c, x))
            for k in range(1, NZ)
        ]
        self.to_x, self.to_y, self.far = [], [], []
        for k in range(NZ):
            at = (z + NZ - k) % NZ
            place = whole.at[at, y, c, :, mine]
            source = place if k else shard
            self.to_x.append(remote(source, place, sems, first + 3 + k, across))
            self.to_y.append(remote(source, place, sems, first + 7 + k, beside))
            if k < lean:
                place = whole.at[at, y, c, :, other]
                self.far.append(remote(place, place, sems, first + 11 + k, beside))
            else:
                place = whole.at[at, 1 - y, c, :, mine]
                self.far.append(remote(place, place, sems, first + 11 + k, across))
        self.core = []
        for step, part in enumerate(
            (
                whole.at[:, y, c, :, mine],
                whole.at[:, y, c, :, other],
                whole.at[:, 1 - y, c, :, mine],
                whole.at[:, 1 - y, c, :, other],
            )
        ):
            self.core.append(remote(part, part, sems, first + 15 + step, twin))

    def send_z(self):
        self.local.start()
        for copy in self.along:
            copy.start()

    def send_own(self):
        self.to_x[0].start()
        self.to_y[0].start()

    def pass_on(self):
        for k in range(1, NZ):
            self.along[k - 1].wait_recv()
            self.to_x[k].start()
            self.to_y[k].start()
        self.local.wait()
        self.core[0].start()

    def turn_corner(self):
        for k in range(NZ):
            (self.to_x if k < self.lean else self.to_y)[k].wait_recv()
            self.far[k].start()
        for k in range(self.lean, NZ):
            self.to_x[k].wait_recv()
        self.core[1].start()
        for k in range(self.lean):
            self.to_y[k].wait_recv()
        self.core[2].start()

    def share(self):
        for copy in self.far:
            copy.wait_recv()
        self.core[3].start()

    def receive(self):
        for copy in self.core:
            copy.wait_recv()

    def finish(self):
        for copy in (*self.along, *self.to_x, *self.to_y, *self.far, *self.core):
            copy.wait_send()


def make_pieces(
    groups, bands, waves, wave_code_rows, gen_in, gen_bias, gen_out, gen_shift, hidden, slope, codes,
    made, code_rows, rows, wide,
):
    sensors = code_rows.shape[0]
    for sensor in range(SENSORS):
        for band in range(MAXB):
            code_rows[sensor, band : band + 1, :] = wave_code_rows[
                pl.ds(waves[sensor, band], 1), :
            ]
        code_rows[sensor, MAXB:16, :] = jnp.zeros((16 - MAXB, GEN), F32)
    flat = code_rows[:, 0:16, :].reshape(sensors * 16, GEN)
    before = exact_dot(flat, gen_in[...].astype(F32)) + gen_bias[...].astype(F32)
    values, slopes = gelu_parts(before)
    band_at = lax.broadcasted_iota(jnp.int32, (16, GEN), 0)
    wide[0:GEN, :] = jnp.zeros((GEN, COVER * 128), F32)
    wide[0:GEN, : gen_out.shape[1]] = gen_out[...].astype(F32)
    owner = lax.axis_index("dp") * 2 + lax.axis_index("fsdp")
    gen_shift[...] = pltpu.roll(wide[...], (owner * gen_out.shape[1]) % 128, 1).astype(BF)
    kept, steep = [], []
    for sensor in range(SENSORS):
        part = slice(sensor * 16, sensor * 16 + 16)
        live = band_at < bands[sensor]
        kept.append(jnp.where(live, values[part], 0.0))
        steep.append(jnp.where(live, slopes[part], 0.0))
        code_rows[sensor, 16:32, :] = kept[-1].astype(BF).astype(F32)
        code_rows[sensor, 32:48, :] = steep[-1]
    lower = jnp.concatenate(kept, axis=0).astype(BF)
    for at in range(COVER):
        product = nn_dot(lower, gen_shift[:, at * 128 : (at + 1) * 128])
        for sensor in range(SENSORS):
            rows[sensor, at * MAXB : (at + 1) * MAXB, :] = product[
                sensor * 16 : sensor * 16 + MAXB
            ]
    rows[:, COVER * MAXB :, :] = jnp.zeros((SENSORS, PIECE - COVER * MAXB, 128), F32)
    for group in range(GROUPS):
        made[group // 4, (group // 2) % 2, group % 2] = rows[groups[group]].astype(BF)
    for group in range(GROUPS):
        own = code_rows[groups[group]]
        for twin in range(2):
            first = (group * 2 + twin) * MAXB
            codes[first : first + MAXB, :] = own[0:MAXB]
            hidden[first : first + MAXB, :] = own[16 : 16 + MAXB]
            slope[first : first + MAXB, :] = own[32 : 32 + MAXB]


def mask_rows(kind, for_query, for_key):
    row = lax.broadcasted_iota(jnp.int32, (ROWS, 128), 0)
    lane = lax.broadcasted_iota(jnp.int32, (ROWS, 128), 1)
    patch = jnp.where(kind == 1, 0, row // (TOK_DEV // SLOTS))
    segment = jnp.where(row < TOK_DEV, patch, (row - TOK_DEV) // 2)
    hot = (lane == segment) & (row < LIVE)
    for_query[...] = jnp.where(hot, 1.0, 0.0).astype(BF)
    for_key[...] = jnp.where(
        lane < SLOTS, jnp.where(hot, 0.0, -1e30), jnp.where(lane < SLOTS + 3, 1.0, 0.0)
    ).astype(BF)


def attend_pair(pair, qkv, mask_q, mask_k, keys, values, mixed, log_sum):
    lane = lax.broadcasted_iota(jnp.int32, (TILE, 128), 1)
    lanes = pl.ds(pl.multiple_of(pair * 128, 128), 128)
    keys[:, 0:128] = qkv[6 + pair]
    keys[:, 128:256] = mask_k[...]
    values[:, 0:128] = qkv[12 + pair]
    for tile in range(TILES):
        first = tile * TILE
        both = qkv[pair, first : first + TILE, :] * BF(0.125)
        results, sums = [], []
        for head in range(2):
            query = jnp.where((lane < HEAD) == (head == 0), both, BF(0))
            scores = nt_dot(
                jnp.concatenate([query, mask_q[first : first + TILE, :]], axis=1), keys[...]
            )
            peak = jnp.max(scores, axis=1, keepdims=True)
            expo = jnp.exp(scores - peak).astype(BF)
            made = nn_dot(expo, values[...])
            totals = made[:, 128:256]
            results.append(made[:, 0:128] / totals)
            sums.append(peak + jnp.log(totals))
        count = min(TILE, LIVE - first)
        mixed[first : first + count, lanes] = jnp.where(lane < HEAD, *results)[:count].astype(BF)
        log_sum[pair, first : first + TILE, :] = jnp.where(lane < HEAD, *sums)


def forward_kernel(
    wq, wo, wu, wd, small, pixels, table, meta, groups, bands, own, waves, wave_code_rows,
    gen_in, gen_bias, gen_out,
    full_q, full_o, full_u, full_d, params, kernel, tokens, first, qkv, mixed, log_sum,
    gen_shift, hidden, slope, codes,
    made, code_rows, rows, roll, taken, full_small, flat, wide, keys, values, mask_q, mask_k,
    w_send, w_recv, local_sem, s_send, s_recv, g_send, g_recv,
):
    here = z, y, c, x = spot()
    peers = group_peers(z, y, c, x)
    across = device(z, y, c, 1 - x)
    greet([where for _, where in peers] + [across])
    gathers = q, o, u, d = [
        Gather(shard, whole, (w_send, w_recv), local_sem.at[step], Gather.COPIES * step, lean, here)
        for step, (shard, whole, lean) in enumerate(
            ((wq, full_q, 3), (wo, full_o, 2), (wu, full_u, 3), (wd, full_d, 2))
        )
    ]
    s_sems = (s_send, s_recv)
    g_sems = (g_send, g_recv)
    q.send_z()
    q.send_own()
    make_pieces(
        groups, bands, waves, wave_code_rows, gen_in, gen_bias, gen_out,
        gen_shift, hidden, slope, codes, made, code_rows, rows, roll,
    )
    own_made = pltpu.make_async_copy(
        made.at[z, y, c], taken.at[z, y, c, x], local_sem.at[4]
    )
    own_made.start()
    sends = {}
    for (dz, dy, dc), where in peers:
        copy = remote(
            made.at[(z + dz) % NZ, (y + dy) % 2, (c + dc) % 2],
            taken.at[z, y, c, x],
            g_sems,
            dz * 4 + dy * 2 + dc,
            where,
        )
        copy.start()
        sends[dz, dy, dc] = copy
    own_small = pltpu.make_async_copy(small, full_small.at[z, y, c], local_sem.at[5])
    own_small.start()
    small_z = [
        remote(small, full_small.at[z, y, c], s_sems, k - 1, device((z + k) % NZ, y, c, x))
        for k in range(1, NZ)
    ]
    for copy in small_z:
        copy.start()
    o.send_own()
    q.pass_on()
    o.send_z()
    own_made.wait()
    swaps = []
    for dz in range(NZ):
        for dy in range(2):
            for dc in range(2):
                if dz + dy + dc:
                    sends[dz, dy, dc].wait_recv()
        part = taken.at[(z + NZ - dz) % NZ, :, :, x]
        swap = remote(part, part, g_sems, 16 + dz, across)
        swap.start()
        swaps.append(swap)
    u.send_z()
    u.send_own()
    own_small.wait()
    for copy in small_z:
        copy.wait_recv()
    part = full_small.at[:, y, c]
    small_y = remote(part, part, s_sems, 3, device(z, 1 - y, c, x))
    small_y.start()
    mask_rows(own[0], mask_q, mask_k)
    values[:, 128:256] = jnp.ones((ROWS, 128), BF)
    q.turn_corner()
    o.pass_on()
    for swap in swaps:
        swap.wait_recv()
    small_y.wait_recv()
    part = full_small.at[:, :, c]
    small_c = remote(part, part, s_sems, 4, device(z, y, 1 - c, x))
    small_c.start()
    unpack(taken, flat, wide, kernel)
    d.send_z()
    q.share()
    u.pass_on()
    bias = jnp.concatenate(
        [
            column_sum(flat[(PIX * 6 + part) * MAXB : (PIX * 6 + part + 1) * MAXB, :])
            for part in range(6)
        ],
        axis=1,
    ) / own[1].astype(F32)
    single = own[0] == 1
    for start, count in BANDS[:-1]:
        band = slice(start, start + count)
        made_rows = nn_dot(pixels[band, :], kernel[...])
        index = start + lax.broadcasted_iota(jnp.int32, (count, 256), 0)
        lane = lax.broadcasted_iota(jnp.int32, (count, 256), 1)
        spread = []
        for spots in (
            jnp.where(single, index // 32, index // 16),
            jnp.where(single, index % 32, index // 256 * 16 + index % 16),
        ):
            hot = (lane % 64 == spots) & (lane < 192)
            spread.append(nn_dot(jnp.where(hot, 1.0, 0.0).astype(BF), table[...]))
        tokens[band, :] = made_rows + bias + jnp.concatenate(spread, axis=1)
    small_c.wait_recv()
    params[...] = jnp.zeros_like(params)
    for n in range(GROUPS):
        params[...] += full_small[n // 4, (n // 2) % 2, n % 2].astype(F32)
    tokens[TOK_DEV:LIVE, :] = meta[...]
    for start, count in BANDS:
        band = slice(start, start + count)
        normed, _ = standard(tokens[band, :])
        first[band, :] = (normed * params[0:1, :] + params[1:2, :]).astype(BF)
    d.send_own()
    q.receive()
    for start, count in BANDS:
        band = slice(start, start + count)
        for third in range(3):
            part = slice(third * D, (third + 1) * D)
            made_rows = nn_dot(
                first[band, :], full_q[:, :, :, :, part].reshape(D, D)
            ).astype(BF)
            for block in range(6):
                put_rows(
                    qkv.at[third * 6 + block],
                    start,
                    count,
                    made_rows[:, block * 128 : (block + 1) * 128],
                )
        if start == 256:
            o.turn_corner()

    d.pass_on()

    def one_pair(pair, carry):
        @pl.when(pair == 1)
        def _():
            u.turn_corner()
            o.share()

        @pl.when(pair == 2)
        def _():
            d.turn_corner()
            u.share()

        @pl.when(pair == 4)
        def _():
            d.share()

        attend_pair(pair, qkv, mask_q, mask_k, keys, values, mixed, log_sum)
        return carry

    lax.fori_loop(0, HEADS // 2, one_pair, 0)
    for gather in (o, u, d):
        gather.receive()
    for gather in gathers:
        gather.finish()
    for copy in (*small_z, small_y, small_c, *sends.values(), *swaps):
        copy.wait_send()


def forward(w_qkv, w_out, w_up, w_down, small, pixels, table, meta, groups, bands, own, waves, rest):
    anywhere = pl.BlockSpec(memory_space=pl.ANY)
    vmem = pl.BlockSpec(memory_space=pltpu.VMEM)
    smem = pl.BlockSpec(memory_space=pltpu.SMEM)
    shards = (w_qkv, w_out, w_up, w_down)
    blocks = 32 * MAXB
    outs = [
        jax.ShapeDtypeStruct((NZ, 2, 2, shard.shape[0], 2 * shard.shape[1]), BF) for shard in shards
    ]
    outs += [
        jax.ShapeDtypeStruct((16, D), F32),
        jax.ShapeDtypeStruct((MAXB * PIX, D), BF),
        jax.ShapeDtypeStruct((LIVE, D), F32),
        jax.ShapeDtypeStruct((LIVE, D), BF),
        jax.ShapeDtypeStruct((18, ROWS, 128), BF),
        jax.ShapeDtypeStruct((LIVE, D), BF),
        jax.ShapeDtypeStruct((HEADS // 2, ROWS, 128), F32),
        jax.ShapeDtypeStruct((GEN, COVER * 128), BF),
        jax.ShapeDtypeStruct((blocks, GEN), F32),
        jax.ShapeDtypeStruct((blocks, GEN), F32),
        jax.ShapeDtypeStruct((blocks, GEN), F32),
    ]
    return pl.pallas_call(
        forward_kernel,
        out_shape=outs,
        in_specs=[anywhere] * 4 + [vmem] * 4 + [smem] * 4 + [vmem] * 4,
        out_specs=[vmem] + [anywhere] * 3 + [vmem] * 11,
        scratch_shapes=[
            pltpu.VMEM((NZ, 2, 2, PIECE, 128), BF),
            pltpu.VMEM((SENSORS, 48, GEN), F32),
            pltpu.VMEM((SENSORS, PIECE, 128), F32),
            pltpu.VMEM((GEN, COVER * 128), F32),
            pltpu.VMEM((NZ, 2, 2, 2, PIECE, 128), BF),
            pltpu.VMEM((NZ, 2, 2, 16, D), BF),
            pltpu.VMEM((FLAT, 128), F32),
            pltpu.VMEM((6, MAXB * PIX, 128), F32),
            pltpu.VMEM((ROWS, 256), BF),
            pltpu.VMEM((ROWS, 256), BF),
            pltpu.VMEM((ROWS, 128), BF),
            pltpu.VMEM((ROWS, 128), BF),
        ]
        + [pltpu.SemaphoreType.DMA((count,)) for count in (76, 76, 6, 5, 5, 20, 20)],
        compiler_params=pltpu.CompilerParams(
            collective_id=0, has_side_effects=True, vmem_limit_bytes=VMEM_ASK
        ),
    )(*shards, small, pixels, table, meta, groups, bands, own, waves, *rest)


class Scatter:
    def __init__(self, whole, own, came, low, high, side_x, side_y, last, out, sems, first, here):
        z, y, c, x = here
        self.here, self.own, self.came, self.out = here, own, came, out
        self.low, self.high, self.side_x, self.side_y, self.last = low, high, side_x, side_y, last
        self.mine, self.other = columns(own, x), columns(own, 1 - x)
        mine, other = self.mine, self.other
        across, beside, twin = device(z, y, c, 1 - x), device(z, 1 - y, c, x), device(z, y, 1 - c, x)
        self.local = pltpu.make_async_copy(whole.at[:, :, c], own, sems[2].at[first // 8])
        self.core = remote(whole.at[:, :, 1 - c], came, sems, first, twin)
        self.far_y = remote(own.at[0:2, 1 - y, :, other], low, sems, first + 1, beside)
        self.far_x = remote(own.at[2:4, 1 - y, :, other], high, sems, first + 2, across)
        self.to_x = remote(own.at[:, y, :, other], side_x, sems, first + 3, across)
        self.to_y = remote(own.at[:, 1 - y, :, mine], side_y, sems, first + 4, beside)
        self.along = [
            remote(
                own.at[(z + k) % NZ, y, :, mine], last.at[k - 1], sems, first + 4 + k,
                device((z + k) % NZ, y, c, x),
            )
            for k in range(1, NZ)
        ]

    def stage_a(self):
        self.local.start()
        self.core.start()

    def stage_b(self):
        self.local.wait()
        self.core.wait_recv()
        for at_z in range(NZ):
            for at_y in range(2):
                self.own[at_z, at_y] = (
                    self.own[at_z, at_y].astype(F32) + self.came[at_z, at_y].astype(F32)
                ).astype(BF)
        self.far_y.start()
        self.far_x.start()

    def stage_c(self):
        _, y, _, _ = self.here
        self.far_y.wait_recv()
        for k in range(2):
            self.own[k, y, :, self.other] = (
                self.own[k, y, :, self.other].astype(F32) + self.low[k].astype(F32)
            ).astype(BF)
        self.to_x.start()
        self.far_x.wait_recv()
        for k in range(2):
            self.own[2 + k, 1 - y, :, self.mine] = (
                self.own[2 + k, 1 - y, :, self.mine].astype(F32) + self.high[k].astype(F32)
            ).astype(BF)
        self.to_y.start()

    def stage_d(self):
        _, y, _, _ = self.here
        self.to_x.wait_recv()
        self.to_y.wait_recv()
        for k in range(NZ):
            self.own[k, y, :, self.mine] = (
                self.own[k, y, :, self.mine].astype(F32)
                + self.side_x[k].astype(F32)
                + self.side_y[k].astype(F32)
            ).astype(BF)
        for copy in self.along:
            copy.start()

    def stage_e(self):
        z, y, _, _ = self.here
        for copy in self.along:
            copy.wait_recv()
        self.out[...] = (
            self.own[z, y, :, self.mine].astype(F32)
            + self.last[0].astype(F32)
            + self.last[1].astype(F32)
            + self.last[2].astype(F32)
        )
        for copy in (self.core, self.far_y, self.far_x, self.to_x, self.to_y, *self.along):
            copy.wait_send()


class Total:
    def __init__(self, source, out, held, came, slots, send_sem, recv_sem, here):
        z, y, c, x = here
        sems = (send_sem, recv_sem)
        self.source, self.held, self.came, self.slots, self.out = source, held, came, slots, out
        self.z = z
        where = (device(z, y, 1 - c, x), device(z, y, c, 1 - x), device(z, 1 - y, c, x))
        self.steps = [
            remote(source if step == 0 else held.at[step - 1], came.at[step], sems, step, where[step])
            for step in range(3)
        ]
        self.along = [
            remote(held.at[2], slots.at[z], sems, 2 + k, device((z + k) % NZ, y, c, x))
            for k in range(1, NZ)
        ]

    def begin(self):
        self.steps[0].start()

    def turn(self, step):
        self.steps[step].wait_recv()
        before = self.source[...] if step == 0 else self.held[step - 1]
        self.held[step] = before + self.came[step]
        if step < 2:
            self.steps[step + 1].start()
        else:
            self.slots[self.z] = self.held[2]
            for copy in self.along:
                copy.start()

    def finish(self):
        for copy in self.along:
            copy.wait_recv()
        self.out[...] = self.slots[0] + self.slots[1] + self.slots[2] + self.slots[3]
        for copy in (*self.steps, *self.along):
            copy.wait_send()


def near(z, y, c, x):
    return [
        device(z, y, c, 1 - x),
        device(z, 1 - y, c, x),
        device(z, y, 1 - c, x),
        *[device((z + k) % NZ, y, c, x) for k in range(1, NZ)],
    ]


def scatter_scratch(rows, width):
    half = width // 2
    return [
        pltpu.VMEM((NZ, 2, rows, width), BF),
        pltpu.VMEM((NZ, 2, rows, width), BF),
        pltpu.VMEM((2, rows, half), BF),
        pltpu.VMEM((2, rows, half), BF),
        pltpu.VMEM((NZ, rows, half), BF),
        pltpu.VMEM((NZ, rows, half), BF),
        pltpu.VMEM((3, rows, half), BF),
    ]


def total_scratch(shape):
    return [
        pltpu.VMEM((3,) + shape, F32),
        pltpu.VMEM((3,) + shape, F32),
        pltpu.VMEM((NZ,) + shape, F32),
        pltpu.SemaphoreType.DMA((6,)),
        pltpu.SemaphoreType.DMA((6,)),
    ]


def piece_start(owner):
    return (owner * (GENOUT // 32)) // 128


FLAT = (GENOUT // 128) * MAXB


def unpack(taken, flat, wide, kernel):
    flat[...] = jnp.zeros_like(flat)
    used = COVER * MAXB
    for owner in range(32):
        first = piece_start(owner) * MAXB
        count = min(used, FLAT - first)
        piece = taken[owner // 8, (owner // 4) % 2, (owner // 2) % 2, owner % 2]
        flat[first : first + count, :] += piece.astype(F32)[:count]
    for pixel in range(PIX):
        for part in range(6):
            first = (pixel * 6 + part) * MAXB
            wide[part, pl.ds(pixel, MAXB, stride=PIX), :] = flat[first : first + MAXB, :]
    for part in range(6):
        kernel[:, part * 128 : (part + 1) * 128] = wide[part].astype(BF)


def pack(d_kernel, bias, pieces, wide, flat):
    for part in range(6):
        wide[part] = d_kernel[:, part * 128 : (part + 1) * 128]
        first = (PIX * 6 + part) * MAXB
        flat[first : first + MAXB, :] = bias[0:MAXB, part * 128 : (part + 1) * 128]
    flat[FLAT:, :] = jnp.zeros((flat.shape[0] - FLAT, 128), F32)
    for pixel in range(PIX):
        for part in range(6):
            first = (pixel * 6 + part) * MAXB
            flat[first : first + MAXB, :] = wide[part, pl.ds(pixel, MAXB, stride=PIX), :]
    for owner in range(32):
        first = piece_start(owner) * MAXB
        pieces[owner // 8, (owner // 4) % 2, (owner // 2) % 2, owner % 2] = flat[
            first : first + PIECE, :
        ].astype(BF)


def norm_rows_back(value, upstream, gain):
    normed, scale = standard(value)
    scaled = upstream * gain
    inside = (
        scaled
        - jnp.mean(scaled, axis=-1, keepdims=True)
        - normed * jnp.mean(scaled * normed, axis=-1, keepdims=True)
    )
    return scale * inside, column_sum(upstream * normed), column_sum(upstream)


def close_kernel(
    d_qkv, first, w_qkv, tokens, d_after, params, pixels, kernel, meta_mix, late, b_grad, live,
    hidden, gen_shift, slope, codes,
    out_grad, in_grad, out_q, out_early, pixel_grad,
    d_tokens, grad_q, pieces, taken, flat, wide, rows, source, early,
    send_sem, recv_sem, local_sem, q_send, q_recv, *rest,
):
    here = z, y, c, x = spot()
    peers = [
        ((dz, dy, dc, dx), ((z + dz) % NZ, (y + dy) % 2, (c + dc) % 2, (x + dx) % 2))
        for dz in range(NZ)
        for dy in range(2)
        for dc in range(2)
        for dx in range(2)
        if dz + dy + dc + dx
    ]
    greet([device(*where) for _, where in peers])
    scatter = Scatter(
        grad_q, *rest[10:17], out_q, (q_send, q_recv, local_sem), 0, here
    )
    begin = Total(early, out_early, *rest[0:5], here)
    for third in range(3):
        part = slice(third * D, (third + 1) * D)
        grad_q[:, :, :, :, part] = (
            inner_dot(first[...], d_qkv[:, part]).astype(BF).reshape(NZ, 2, 2, -1, D)
        )
    scatter.stage_a()
    gain = shift = jnp.zeros((1, D), F32)
    for start, count in BANDS:
        band = slice(start, start + count)
        upstream = nt_dot(d_qkv[band, :], w_qkv[...].reshape(D, 3 * D))
        d_norm, gain_part, shift_part = norm_rows_back(tokens[band, :], upstream, params[0:1, :])
        gain += gain_part
        shift += shift_part
        d_tokens[band, :] = (d_after[band, :] + d_norm).astype(BF)
    scatter.stage_b()
    patches = d_tokens[0:TOK_DEV, :]
    d_kernel = inner_dot(pixels[...], patches)
    sums = column_sum(patches.astype(F32))
    pack(d_kernel, live[...] * sums, pieces, wide, flat)
    own = pltpu.make_async_copy(pieces.at[z, y, c, x], taken.at[z, y, c, x], local_sem.at[1])
    own.start()
    sends = []
    for (dz, dy, dc, dx), where in peers:
        copy = remote(
            pieces.at[where],
            taken.at[z, y, c, x],
            (send_sem, recv_sem),
            dz * 8 + dy * 4 + dc * 2 + dx,
            device(*where),
        )
        copy.start()
        sends.append(copy)
    early[0:16, :] = lax.dot_general(
        meta_mix[...],
        d_tokens[TOK_DEV:LIVE, :].astype(F32),
        (((1,), (0,)), ((), ())),
        precision=lax.Precision.HIGHEST,
        preferred_element_type=F32,
    )
    early[16:24, :] = late[...]
    early[16:17, :] = gain
    early[17:18, :] = shift
    early[24:32, :] = b_grad[...]
    begin.begin()
    scatter.stage_c()
    begin.turn(0)
    for start, count in BANDS[:-1]:
        band = slice(start, start + count)
        pixel_grad[band, :] = nt_dot(d_tokens[band, :], kernel[...])
    begin.turn(1)
    scatter.stage_d()
    begin.turn(2)
    own.wait()
    for copy in sends:
        copy.wait_recv()
    for n in range(32):
        block = taken[n // 8, (n // 4) % 2, (n // 2) % 2, n % 2].astype(F32)
        for at in range(COVER):
            rows[at, n * MAXB : (n + 1) * MAXB, :] = block[at * MAXB : (at + 1) * MAXB]
    d_hidden = jnp.zeros((32 * MAXB, GEN), F32)
    for at in range(COVER):
        d_hidden += nt_dot(rows[at].astype(BF), gen_shift[:, at * 128 : (at + 1) * 128])
    d_before = d_hidden * slope[...]
    source[0:GEN, :] = lax.dot_general(
        codes[...],
        d_before,
        (((0,), (0,)), ((), ())),
        precision=lax.Precision.HIGHEST,
        preferred_element_type=F32,
    )
    source[GEN : GEN + 8, :] = jnp.broadcast_to(column_sum(d_before), (8, GEN))
    total = Total(source, in_grad, *rest[5:10], here)
    total.begin()
    for at in range(COVER):
        out_grad[:, at * 128 : (at + 1) * 128] = inner_dot(
            hidden[...].astype(BF), rows[at].astype(BF)
        )
    scatter.stage_e()
    begin.finish()
    for step in range(3):
        total.turn(step)
    total.finish()
    for copy in sends:
        copy.wait_send()


def closing(
    d_qkv, first, w_qkv, tokens, d_after, params, pixels, kernel, meta_mix, late, b_grad, live,
    hidden, gen_shift, slope, codes,
):
    vmem = pl.BlockSpec(memory_space=pltpu.VMEM)
    small, early = (GEN + 8, GEN), (32, D)
    held = (NZ, 2, 2, 2, PIECE, 128)
    _, _, _, rows, width = w_qkv.shape
    return pl.pallas_call(
        close_kernel,
        in_specs=[vmem] * 16,
        out_specs=[vmem] * 5,
        out_shape=[
            jax.ShapeDtypeStruct((GEN, COVER * 128), F32),
            jax.ShapeDtypeStruct(small, F32),
            jax.ShapeDtypeStruct((rows, width // 2), F32),
            jax.ShapeDtypeStruct(early, F32),
            jax.ShapeDtypeStruct(pixels.shape, F32),
        ],
        scratch_shapes=[
            pltpu.VMEM((LIVE, D), BF),
            pltpu.VMEM(w_qkv.shape, BF),
            pltpu.VMEM(held, BF),
            pltpu.VMEM(held, BF),
            pltpu.VMEM((FLAT + 64, 128), F32),
            pltpu.VMEM((6, MAXB * PIX, 128), F32),
            pltpu.VMEM((COVER, 32 * MAXB, 128), F32),
            pltpu.VMEM(small, F32),
            pltpu.VMEM(early, F32),
            pltpu.SemaphoreType.DMA((32,)),
            pltpu.SemaphoreType.DMA((32,)),
            pltpu.SemaphoreType.DMA((2,)),
            pltpu.SemaphoreType.DMA((8,)),
            pltpu.SemaphoreType.DMA((8,)),
            *total_scratch(early),
            *total_scratch(small),
            *scatter_scratch(rows, width),
        ],
        compiler_params=pltpu.CompilerParams(
            collective_id=2, has_side_effects=True, vmem_limit_bytes=VMEM_ASK
        ),
    )(
        d_qkv, first, w_qkv, tokens, d_after, params, pixels, kernel, meta_mix, late, b_grad, live,
        hidden, gen_shift, slope, codes,
    )


def tile_rows(source, first):
    if first + TILE <= LIVE:
        return source[first : first + TILE, :]
    part = source[first:LIVE, :]
    return jnp.concatenate([part, jnp.zeros((first + TILE - LIVE, 128), part.dtype)], axis=0)


def feed_kernel(
    tokens, mixed, top, w_out, vectors, w_up, w_down,
    layer_out, d_after, d_mixed, out_grad, rows, up_grad, down_grad, b_grad,
    second, second_turned, top_full, after, sum_out, sum_second, active, d_upper, proj,
):
    step = pl.program_id(0)

    @pl.when(step == 0)
    def _():
        for first, count in BANDS:
            band = slice(first, first + count)
            value = tokens[band, :] + (nn_dot(mixed[band, :], w_out[...]) + vectors[2:3, :])
            after[band, :] = value
            normed, _ = standard(value)
            put_rows(
                second, first, count, (normed * vectors[3:4, :] + vectors[4:5, :]).astype(BF)
            )
            put_rows(top_full, first, count, top[band, :])
        second_turned[...] = second[...].T
        sum_out[...] = jnp.zeros_like(sum_out)
        b_grad[...] = jnp.zeros_like(b_grad)
        sum_second[...] = jnp.zeros_like(sum_second)

    total = jnp.zeros((1, CHUNK), F32)
    for first, count in BANDS:
        count = -(-count // 16) * 16
        band = slice(first, first + count)
        upper = nn_dot(second[band, :], w_up[...]) + vectors[pl.ds(6 + step, 1), :]
        made, slope = gelu_parts(upper)
        made = made.astype(BF)
        active[band, :] = made
        back = (nt_dot(top_full[band, :], w_down[...]) * slope).astype(BF)
        d_upper[band, :] = back
        total += column_sum(back.astype(F32))
    b_grad[pl.ds(step, 1), :] = total
    sum_out[...] += nn_dot(active[...], w_down[...])
    sum_second[...] += nt_dot(d_upper[...], w_up[...])
    down_grad[...] = inner_dot(active[...], top_full[...]).astype(BF)
    up_grad[...] = nn_dot(second_turned[...], d_upper[...]).astype(BF)

    @pl.when(step == pl.num_programs(0) - 1)
    def _():
        gain = shift = bias = last = jnp.zeros((1, D), F32)
        for first, count in BANDS:
            band = slice(first, first + count)
            value = after[band, :]
            layer_out[band, :] = (value + sum_out[band, :] + vectors[5:6, :]).astype(BF)
            normed, scale = standard(value)
            upstream = sum_second[band, :]
            gain += column_sum(upstream * normed)
            shift += column_sum(upstream)
            scaled = upstream * vectors[3:4, :]
            inside = (
                scaled
                - jnp.mean(scaled, axis=-1, keepdims=True)
                - normed * jnp.mean(scaled * normed, axis=-1, keepdims=True)
            )
            grad_top = top[band, :].astype(F32)
            last += column_sum(grad_top)
            result = grad_top + scale * inside
            d_after[band, :] = result
            low = result.astype(BF)
            bias += column_sum(low.astype(F32))
            put_rows(proj, first, count, low)
            d_mixed[band, :] = nt_dot(low, w_out[...]).astype(BF)
        out_grad[...] = inner_dot(mixed[...], proj[0:LIVE, :]).astype(BF)
        rows[...] = jnp.concatenate([jnp.zeros((2, D), F32), bias, gain, shift, last, jnp.zeros((2, D), F32)], axis=0)


def feed(tokens, mixed, top, w_out, vectors, w_up, w_down):
    width = w_up.shape[1]

    def whole(*shape):
        return pl.BlockSpec(shape, lambda step: (0, 0))

    across = pl.BlockSpec((D, CHUNK), lambda step: (0, step))
    down = pl.BlockSpec((CHUNK, D), lambda step: (step, 0))
    block = whole(LIVE, D)
    return pl.pallas_call(
        feed_kernel,
        grid=(width // CHUNK,),
        in_specs=[block, block, block, whole(D, D), whole(16, D), across, down],
        out_specs=[block, block, block, whole(D, D), whole(8, D), across, down, whole(8, D)],
        out_shape=[
            jax.ShapeDtypeStruct((LIVE, D), BF),
            jax.ShapeDtypeStruct((LIVE, D), F32),
            jax.ShapeDtypeStruct((LIVE, D), BF),
            jax.ShapeDtypeStruct((D, D), BF),
            jax.ShapeDtypeStruct((8, D), F32),
            jax.ShapeDtypeStruct((D, width), BF),
            jax.ShapeDtypeStruct((width, D), BF),
            jax.ShapeDtypeStruct((8, D), F32),
        ],
        scratch_shapes=[
            pltpu.VMEM((ROWS, D), BF),
            pltpu.VMEM((D, ROWS), BF),
            pltpu.VMEM((ROWS, D), BF),
            pltpu.VMEM((LIVE, D), F32),
            pltpu.VMEM((ROWS, D), F32),
            pltpu.VMEM((ROWS, D), F32),
            pltpu.VMEM((ROWS, CHUNK), BF),
            pltpu.VMEM((ROWS, CHUNK), BF),
            pltpu.VMEM((ROWS, D), BF),
        ],
        compiler_params=pltpu.CompilerParams(vmem_limit_bytes=VMEM_ASK),
    )(tokens, mixed, top, w_out, vectors, w_up, w_down)


def three_parts(exact):
    high = exact.astype(BF)
    left = exact - high.astype(F32)
    middle = left.astype(BF)
    return high, middle, (left - middle.astype(F32)).astype(BF)


def attend_back_kernel(
    own, q_ref, k_ref, v_ref, d_mixed, mixed, log_sum, go, gu, gd,
    out, out_o, out_u, out_d,
    mask_q, mask_k, keys, values, keys_turned, d_query, d_keys, d_values, send_sem, recv_sem, local_sem, *rest,
):
    pair, part = pl.program_id(0), pl.program_id(1)
    here = spot()
    o, u, d = [
        Scatter(
            whole, *rest[7 * at : 7 * at + 7], result, (send_sem, recv_sem, local_sem), 8 * at, here
        )
        for at, (whole, result) in enumerate(((go, out_o), (gu, out_u), (gd, out_d)))
    ]

    @pl.when((pair == 0) & (part == 0))
    def _():
        greet(near(*here))
        d.stage_a()
        u.stage_a()
        o.stage_a()

    @pl.when((pair == 0) & (part == 1))
    def _():
        d.stage_b()

    @pl.when((pair == 1) & (part == 1))
    def _():
        u.stage_b()
        d.stage_c()

    @pl.when((pair == 2) & (part == 1))
    def _():
        o.stage_b()
        u.stage_c()

    @pl.when((pair == 3) & (part == 1))
    def _():
        d.stage_d()
        o.stage_c()

    @pl.when((pair == 4) & (part == 1))
    def _():
        u.stage_d()

    @pl.when((pair == 5) & (part == 1))
    def _():
        d.stage_e()
        o.stage_d()

    @pl.when((pair == 5) & (part == 2))
    def _():
        u.stage_e()
        o.stage_e()

    lane = lax.broadcasted_iota(jnp.int32, (TILE, 128), 1)
    sub = lax.broadcasted_iota(jnp.int32, (128, TILE), 0)

    def with_parts(exact, rest):
        a, b, c = three_parts(exact)
        return jnp.where(
            lane == SLOTS,
            a,
            jnp.where(lane == SLOTS + 1, b, jnp.where(lane == SLOTS + 2, c, rest)),
        )

    @pl.when(part == 0)
    def _():
        @pl.when(pair == 0)
        def _():
            mask_rows(own[0], mask_q, mask_k)
            keys[:, 128:256] = mask_k[...]
            values[:, 128:256] = mask_k[...]

        keys[:, 0:128] = k_ref[0]
        values[:, 0:128] = v_ref[0]
        keys_turned[...] = keys[:, 0:128].T
        d_keys[...] = jnp.zeros_like(d_keys)
        d_values[...] = jnp.zeros_like(d_values)
        for tile in range(TILES):
            first = tile * TILE
            both = q_ref[0, first : first + TILE, :] * BF(0.125)
            up = tile_rows(d_mixed, first)
            logs = log_sum[0, first : first + TILE, :]
            product = up.astype(F32) * tile_rows(mixed, first).astype(F32)
            marks = mask_q[first : first + TILE, :]
            turned = []
            for head in range(2):
                chosen = (lane < HEAD) == (head == 0)
                query = jnp.where(chosen, both, BF(0))
                upstream = jnp.where(chosen, up, BF(0))
                inside = jnp.sum(jnp.where(chosen, product, 0.0), axis=1, keepdims=True)
                wide_query = jnp.concatenate(
                    [query, with_parts(-logs[:, head * HEAD : head * HEAD + 1], marks)], axis=1
                )
                wide_up = jnp.concatenate(
                    [upstream, with_parts(-inside, jnp.zeros_like(marks))], axis=1
                )
                prob = jnp.exp(nt_dot(keys[...], wide_query))
                d_scores = (prob * nt_dot(values[...], wide_up)).astype(BF)
                d_values[...] += nn_dot(prob.astype(BF), upstream)
                d_keys[...] += nn_dot(d_scores, query)
                turned.append(nn_dot(keys_turned[...], d_scores))
            d_query[first : first + TILE, :] = (
                (jnp.where(sub < HEAD, *turned) * 0.125).T.astype(BF)
            )
        out[...] = d_query[0:LIVE, :]

    @pl.when(part == 1)
    def _():
        out[...] = d_keys[0:LIVE, :].astype(BF)

    @pl.when(part == 2)
    def _():
        out[...] = d_values[0:LIVE, :].astype(BF)


def attend_back(own, qkv, d_mixed, mixed, log_sum, grads):
    def band(first):
        return pl.BlockSpec((LIVE, 128), lambda pair, part: (0, first + pair))

    def head(first):
        return pl.BlockSpec((1, ROWS, 128), lambda pair, part: (first + pair, 0, 0))

    shapes = [grad.shape[3:] for grad in grads]
    outs = [(rows, width // 2) for rows, width in shapes]
    return pl.pallas_call(
        attend_back_kernel,
        grid=(HEADS // 2, 3),
        in_specs=[
            pl.BlockSpec(memory_space=pltpu.SMEM),
            head(0), head(6), head(12), band(0), band(0), head(0),
        ]
        + [pl.BlockSpec(memory_space=pl.ANY)] * 3,
        out_specs=[pl.BlockSpec((LIVE, 128), lambda pair, part: (0, part * 6 + pair))]
        + [pl.BlockSpec(shape, lambda pair, part: (0, 0)) for shape in outs],
        out_shape=[
            jax.ShapeDtypeStruct((LIVE, 3 * D), BF),
            *[jax.ShapeDtypeStruct(shape, F32) for shape in outs],
        ],
        scratch_shapes=[
            pltpu.VMEM((ROWS, 128), BF),
            pltpu.VMEM((ROWS, 128), BF),
            pltpu.VMEM((ROWS, 256), BF),
            pltpu.VMEM((ROWS, 256), BF),
            pltpu.VMEM((128, ROWS), BF),
            pltpu.VMEM((ROWS, 128), BF),
            pltpu.VMEM((ROWS, 128), F32),
            pltpu.VMEM((ROWS, 128), F32),
            pltpu.SemaphoreType.DMA((24,)),
            pltpu.SemaphoreType.DMA((24,)),
            pltpu.SemaphoreType.DMA((3,)),
            *[entry for shape in shapes for entry in scatter_scratch(*shape)],
        ],
        compiler_params=pltpu.CompilerParams(
            collective_id=3, has_side_effects=True, vmem_limit_bytes=VMEM_ASK
        ),
    )(own, qkv, qkv, qkv, d_mixed, mixed, log_sum, *grads)


def place_table(kind, ground):
    quarter = D // 4
    entry = jnp.arange(64, dtype=jnp.int32)
    chip = jnp.where(kind == 1, 0, entry // 16)
    step = jnp.where(kind == 1, entry, entry % 16).astype(F32)
    scale = (
        jnp.sum(
            jnp.where(
                chip[:, None] == jnp.arange(SLOTS, dtype=jnp.int32)[None, :], ground[None, :], 0
            ),
            axis=1,
        ).astype(F32)
        / 10.0
    )
    omega = 1.0 / 10000.0 ** (jnp.arange(quarter, dtype=F32) / (quarter - 1))
    angle = (step * scale)[:, None] * omega[None, :]
    exact = jnp.concatenate([jnp.sin(angle), jnp.cos(angle)], axis=1)
    table = jnp.concatenate([*three_parts(exact), jnp.zeros((64, 2 * quarter), BF)], axis=0)
    return table


def body_block(
    pixels,
    wave_table,
    band_count,
    wave_index,
    group_sensor,
    chip_kind,
    chip_gsd,
    time_loc,
    gen_in,
    gen_bias,
    gen_out,
    meta_weight,
    w_qkv,
    w_out,
    w_up,
    w_down,
    vectors,
    b_up,
    cotangent,
):
    group = lax.axis_index("dp")
    owner = group * 2 + lax.axis_index("fsdp")
    sensor = jnp.sum(jnp.where(jnp.arange(GROUPS, dtype=jnp.int32) == group, group_sensor, 0))
    band_total = jnp.sum(
        jnp.where(jnp.arange(SENSORS, dtype=jnp.int32) == sensor, band_count, 0)
    )
    width, rows, up_rows = gen_out.shape[1], vectors.shape[0], b_up.shape[0]
    lane = jnp.arange(D, dtype=jnp.int32)
    row = jnp.arange(10, dtype=jnp.int32)[:, None]
    per_row = D // up_rows
    small = jnp.where(
        row < 6,
        jnp.where(
            (lane // rows == group)[None, :],
            jnp.concatenate([jnp.tile(vectors.T, (1, GROUPS)), jnp.zeros((4, D), BF)], axis=0),
            BF(0),
        ),
        jnp.where(
            (row == 6 + group // per_row) & (lane // up_rows == group % per_row)[None, :],
            jnp.tile(b_up, per_row)[None, :],
            BF(0),
        ),
    )
    small = jnp.pad(small, ((0, 6), (0, 0)))
    kind_one = chip_kind[0]
    band_float = band_total.astype(F32)
    table = place_table(kind_one, chip_gsd[0])
    own = jnp.stack([kind_one, band_total])
    meta_mix = jnp.concatenate(
        [
            jnp.stack([jnp.ones((SLOTS,), F32), jnp.zeros((SLOTS,), F32)], axis=1).reshape(1, -1),
            jnp.stack([jnp.zeros_like(time_loc[0]), time_loc[0]], axis=1).reshape(
                2 * SLOTS, -1
            ).T,
            jnp.zeros((7, 2 * SLOTS), F32),
        ],
        axis=0,
    )
    meta_rows = exact_dot(
        meta_mix.T, jnp.pad(meta_weight.astype(F32), ((0, 7), (0, 0)))
    )
    (
        full_q, full_o, full_u, full_d, params, kernel, tokens_in, first, qkv, mixed, log_sum,
        gen_shift, hidden, slope, codes,
    ) = forward(
        w_qkv,
        w_out,
        w_up,
        w_down,
        small,
        pixels,
        table,
        meta_rows,
        group_sensor,
        band_count,
        own,
        wave_index,
        (wave_code(wave_table), gen_in, gen_bias.reshape(1, -1), gen_out),
    )
    w_out_all = full_o.reshape(D, D)
    w_up_all = full_u.reshape(D, -1)
    w_down_all = full_d.reshape(-1, D)
    layer_out, d_after, d_mixed, w_out_grad, late, w_up_grad, w_down_grad, b_grad = feed(
        tokens_in, mixed, cotangent, w_out_all, params, w_up_all, w_down_all
    )
    d_qkv, w_out_out, w_up_out, w_down_out = attend_back(
        own,
        qkv,
        d_mixed,
        mixed,
        log_sum,
        [
            grad.reshape(NZ, 2, 2, -1, grad.shape[1])
            for grad in (w_out_grad, w_up_grad, w_down_grad)
        ],
    )

    own_live = (jnp.arange(16, dtype=jnp.int32) < band_total)[:, None]
    gen_out_wide, gen_small, w_qkv_out, summed, pixel_grad = closing(
        d_qkv,
        first,
        full_q,
        tokens_in,
        d_after,
        params,
        pixels,
        kernel,
        meta_mix,
        late,
        b_grad,
        jnp.where(own_live, 1.0 / band_float, 0.0),
        hidden,
        gen_shift,
        slope,
        codes,
    )
    gen_out_grad = lax.dynamic_slice(gen_out_wide, (0, (owner * width) % 128), (GEN, width))
    vectors_out = lax.dynamic_slice(summed, (16, group * rows), (6, rows)).T
    b_up_out = lax.dynamic_slice(
        summed[24:28].reshape(-1), (group * up_rows,), (up_rows,)
    )
    return (
        layer_out,
        pixel_grad,
        gen_small[:GEN],
        gen_small[GEN],
        gen_out_grad,
        summed[:9],
        w_qkv_out,
        w_out_out,
        w_up_out,
        w_down_out,
        vectors_out,
        b_up_out,
    )


def solution(mesh):
    fits = dict(mesh.shape) == {"dp": 16, "fsdp": 2}
    body = body_block if fits else body_general
    placed = (
        P(("dp", "fsdp"), None),
        P(),
        P(),
        P(),
        P(),
        P(("dp", "fsdp")),
        P(("dp", "fsdp"), None),
        P(("dp", "fsdp"), None, None),
        P(),
        P(),
        P(None, ("dp", "fsdp")),
        P(),
        P("dp", "fsdp"),
        P("dp", "fsdp"),
        P("dp", "fsdp"),
        P("dp", "fsdp"),
        P("dp", None),
        P("dp"),
        P(("dp", "fsdp"), None),
    )
    return jax.shard_map(
        body,
        mesh=mesh,
        in_specs=placed,
        out_specs=(
            P(("dp", "fsdp"), None),
            P(("dp", "fsdp"), None),
            P(),
            P(),
            P(None, ("dp", "fsdp")),
            P(),
            P("dp", "fsdp"),
            P("dp", "fsdp"),
            P("dp", "fsdp"),
            P("dp", "fsdp"),
            P("dp", None),
            P("dp"),
        ),
        check_vma=False,
    )
```

```python
import math

import jax
import jax.numpy as jnp
import numpy as np
from jax import lax
from jax.experimental import pallas as pl
from jax.experimental.pallas import tpu as pltpu
from jax.sharding import PartitionSpec as P

D = 768
HEADS = 12
HEAD = 64
GEN = 128
PIX = 64
MAXB = 10
SENSORS = 7
TOK_DEV = 1024
SLOTS = 4
GENOUT = 49920


def exact_dot(left, right):
    return jnp.dot(left, right, precision=lax.Precision.HIGHEST)


def inner_dot(left, right):
    return lax.dot_general(
        left, right, (((0,), (0,)), ((), ())), preferred_element_type=jnp.float32
    )


def outer_dot(left, right):
    return lax.dot_general(
        left, right, (((1,), (1,)), ((), ())), preferred_element_type=jnp.float32
    )


def gelu_exact(values):
    return jax.nn.gelu(values, approximate=False)


def gelu_slope(values, upstream):
    return jax.vjp(gelu_exact, values)[1](upstream)[0]


def table_lookup(indices, table):
    return jnp.sum(
        jnp.where(
            indices[:, None] == jnp.arange(table.shape[0], dtype=jnp.int32)[None, :],
            table[None, :],
            0.0,
        ),
        axis=1,
    )


def wave_code(wavelengths):
    half = GEN // 2
    omega = 1.0 / 10000.0 ** (jnp.arange(half, dtype=jnp.float32) / half)
    angle = (wavelengths * 1000.0)[:, None] * omega[None, :]
    return jnp.concatenate([jnp.sin(angle), jnp.cos(angle)], axis=1)


def place_code(kind_one, gsd_one):
    small = TOK_DEV // SLOTS
    index = jnp.arange(TOK_DEV, dtype=jnp.int32)
    within = jnp.where(kind_one == 1, index, index % small)
    side = jnp.where(kind_one == 1, math.isqrt(TOK_DEV), math.isqrt(small)).astype(jnp.int32)
    across = (within // side).astype(jnp.float32)
    along = (within % side).astype(jnp.float32)
    holder = jnp.where(kind_one == 1, 0, index // small)
    ground = (
        jnp.sum(
            jnp.where(
                holder[:, None] == jnp.arange(SLOTS, dtype=jnp.int32)[None, :], gsd_one[None, :], 0
            ),
            axis=1,
        ).astype(jnp.float32)
        / 10.0
    )
    quarter = D // 4
    omega = 1.0 / 10000.0 ** (jnp.arange(quarter, dtype=jnp.float32) / (quarter - 1))
    first = (across * ground)[:, None] * omega[None, :]
    second = (along * ground)[:, None] * omega[None, :]
    return jnp.concatenate(
        [jnp.sin(first), jnp.cos(first), jnp.sin(second), jnp.cos(second)], axis=1
    )


def segment_ids(kind_one):
    index = jnp.arange(TOK_DEV, dtype=jnp.int32)
    patches = jnp.where(kind_one == 1, 0, index // (TOK_DEV // SLOTS))
    extra = jnp.arange(2 * SLOTS, dtype=jnp.int32) // 2
    return jnp.concatenate([patches, extra])


def layer_norm(values, gain, shift):
    centred = values - jnp.mean(values, axis=-1, keepdims=True)
    scale = lax.rsqrt(jnp.mean(centred * centred, axis=-1, keepdims=True) + 1e-05)
    normed = centred * scale
    return (normed * gain + shift, normed, scale)


def norm_back(upstream, normed, scale, gain):
    gain_grad = jnp.sum(upstream * normed, axis=0)
    shift_grad = jnp.sum(upstream, axis=0)
    scaled = upstream * gain
    inside = (
        scaled
        - jnp.mean(scaled, axis=-1, keepdims=True)
        - normed * jnp.mean(scaled * normed, axis=-1, keepdims=True)
    )
    return (scale * inside, gain_grad, shift_grad)


def body_general(
    pixels,
    wave_table,
    band_count,
    wave_index,
    group_sensor,
    chip_kind,
    chip_gsd,
    time_loc,
    gen_in,
    gen_bias,
    gen_out,
    meta_weight,
    w_qkv,
    w_out,
    w_up,
    w_down,
    vectors,
    b_up,
    cotangent,
):
    half_type = jnp.bfloat16
    group = lax.axis_index("dp")
    sensor = jnp.sum(
        jnp.where(jnp.arange(group_sensor.shape[0], dtype=jnp.int32) == group, group_sensor, 0)
    )
    chosen_sensor = jnp.arange(SENSORS, dtype=jnp.int32) == sensor
    band_total = jnp.sum(jnp.where(chosen_sensor, band_count, 0))
    gen_in_full = gen_in.astype(jnp.float32)
    gen_bias_full = gen_bias.astype(jnp.float32)
    codes = wave_code(table_lookup(wave_index.reshape(-1), wave_table))
    before = exact_dot(codes, gen_in_full) + gen_bias_full
    hidden = gelu_exact(before).astype(half_type)
    shard_made = jnp.dot(hidden, gen_out, preferred_element_type=jnp.float32).astype(half_type)
    all_made = lax.all_gather(shard_made, ("dp", "fsdp"), axis=1, tiled=True)
    generated = lax.dynamic_slice_in_dim(all_made, sensor * MAXB, MAXB, 0)
    live_band = (jnp.arange(MAXB, dtype=jnp.int32) < band_total)[:, None]
    kernel = jnp.where(live_band, generated[:, : PIX * D], jnp.zeros((), half_type)).reshape(
        MAXB * PIX, D
    )
    band_float = band_total.astype(jnp.float32)
    embed_bias = (
        jnp.sum(jnp.where(live_band, generated[:, PIX * D :].astype(jnp.float32), 0.0), axis=0)
        / band_float
    )
    kind_one = chip_kind[0]
    patches = (
        jnp.dot(pixels, kernel, preferred_element_type=jnp.float32)
        + embed_bias
        + place_code(kind_one, chip_gsd[0])
    )
    meta_full = meta_weight.astype(jnp.float32)
    stamps = exact_dot(time_loc[0], meta_full[1:])
    classes = jnp.broadcast_to(meta_full[0], stamps.shape)
    extra = jnp.stack([classes, stamps], axis=1).reshape(2 * SLOTS, D)
    tokens_in = jnp.concatenate([patches, extra], axis=0)
    total_rows = tokens_in.shape[0]
    qkv_rows, out_rows, up_rows, down_rows, vectors_all, b_up_all = (
        lax.all_gather(w_qkv, "dp", axis=0, tiled=True),
        lax.all_gather(w_out, "dp", axis=0, tiled=True),
        lax.all_gather(w_up, "dp", axis=0, tiled=True),
        lax.all_gather(w_down, "dp", axis=0, tiled=True),
        lax.all_gather(vectors, "dp", axis=0, tiled=True),
        lax.all_gather(b_up, "dp", axis=0, tiled=True),
    )
    w_qkv_all, w_out_all, w_up_all, w_down_all = (
        lax.all_gather(qkv_rows, "fsdp", axis=1, tiled=True),
        lax.all_gather(out_rows, "fsdp", axis=1, tiled=True),
        lax.all_gather(up_rows, "fsdp", axis=1, tiled=True),
        lax.all_gather(down_rows, "fsdp", axis=1, tiled=True),
    )
    vector_full = vectors_all.astype(jnp.float32)
    b_up_full = b_up_all.astype(jnp.float32)
    first_norm, normed_one, scale_one = layer_norm(tokens_in, vector_full[:, 0], vector_full[:, 1])
    first = first_norm.astype(half_type)
    qkv = jnp.dot(first, w_qkv_all, preferred_element_type=jnp.float32).astype(half_type)
    query = qkv[:, :D].reshape(total_rows, HEADS, HEAD)
    keys = qkv[:, D : 2 * D].reshape(total_rows, HEADS, HEAD)
    values = qkv[:, 2 * D :].reshape(total_rows, HEADS, HEAD)
    segment = segment_ids(kind_one)
    same = (segment[:, None] == segment[None, :])[None]
    scores = jnp.einsum("qhd,khd->hqk", query, keys, preferred_element_type=jnp.float32) * HEAD ** (
        -0.5
    )
    scores = jnp.where(same, scores, -1e30)
    peak = jnp.max(scores, axis=-1, keepdims=True)
    expo = jnp.exp(scores - peak)
    totals = jnp.sum(expo, axis=-1, keepdims=True)
    prob_half = (expo / totals).astype(half_type)
    mixed = (
        jnp.einsum("hqk,khd->qhd", prob_half, values, preferred_element_type=jnp.float32)
        .reshape(total_rows, D)
        .astype(half_type)
    )
    after = tokens_in + (
        jnp.dot(mixed, w_out_all, preferred_element_type=jnp.float32) + vector_full[:, 2]
    )
    second_norm, normed_two, scale_two = layer_norm(after, vector_full[:, 3], vector_full[:, 4])
    second = second_norm.astype(half_type)
    upper = jnp.dot(second, w_up_all, preferred_element_type=jnp.float32) + b_up_full
    active = gelu_exact(upper).astype(half_type)
    layer_out = (
        after + jnp.dot(active, w_down_all, preferred_element_type=jnp.float32) + vector_full[:, 5]
    ).astype(half_type)
    grad_top = cotangent.astype(jnp.float32)
    w_down_grad = inner_dot(active, cotangent)
    down_bias_grad = jnp.sum(grad_top, axis=0)
    d_active = outer_dot(cotangent, w_down_all)
    d_upper = gelu_slope(upper, d_active).astype(half_type)
    w_up_grad = inner_dot(second, d_upper)
    b_up_grad = jnp.sum(d_upper.astype(jnp.float32), axis=0)
    d_second = outer_dot(d_upper, w_up_all)
    d_after_norm, gain_two_grad, shift_two_grad = norm_back(
        d_second, normed_two, scale_two, vector_full[:, 3]
    )
    d_after = grad_top + d_after_norm
    d_proj = d_after.astype(half_type)
    w_out_grad = inner_dot(mixed, d_proj)
    out_bias_grad = jnp.sum(d_proj.astype(jnp.float32), axis=0)
    d_mixed = outer_dot(d_proj, w_out_all).astype(half_type).reshape(total_rows, HEADS, HEAD)
    again = jnp.einsum("qhd,khd->hqk", query, keys, preferred_element_type=jnp.float32) * HEAD ** (
        -0.5
    )
    again = jnp.where(same, again, -1e30)
    prob_full = jnp.exp(again - peak) / totals
    recalled = prob_full.astype(half_type)
    d_values = jnp.einsum("hqk,qhd->khd", recalled, d_mixed, preferred_element_type=jnp.float32)
    d_prob = jnp.einsum("qhd,khd->hqk", d_mixed, values, preferred_element_type=jnp.float32)
    d_scores = prob_full * (d_prob - jnp.sum(d_prob * prob_full, axis=-1, keepdims=True))
    d_scores = jnp.where(same, d_scores, 0.0).astype(half_type)
    d_query = jnp.einsum(
        "hqk,khd->qhd", d_scores, keys, preferred_element_type=jnp.float32
    ) * HEAD ** (-0.5)
    d_keys = jnp.einsum(
        "hqk,qhd->khd", d_scores, query, preferred_element_type=jnp.float32
    ) * HEAD ** (-0.5)
    d_qkv = jnp.concatenate(
        [
            d_query.reshape(total_rows, D),
            d_keys.reshape(total_rows, D),
            d_values.reshape(total_rows, D),
        ],
        axis=1,
    ).astype(half_type)
    w_qkv_grad = inner_dot(first, d_qkv)
    d_first = outer_dot(d_qkv, w_qkv_all)
    d_tokens_norm, gain_one_grad, shift_one_grad = norm_back(
        d_first, normed_one, scale_one, vector_full[:, 0]
    )
    d_tokens = (d_after + d_tokens_norm).astype(half_type)
    vectors_grad = jnp.stack(
        [
            gain_one_grad,
            shift_one_grad,
            out_bias_grad,
            gain_two_grad,
            shift_two_grad,
            down_bias_grad,
        ],
        axis=1,
    )
    d_patches = d_tokens[:TOK_DEV]
    d_extra = d_tokens[TOK_DEV:].astype(jnp.float32).reshape(SLOTS, 2, D)
    pixel_grad = outer_dot(d_patches, kernel)
    class_grad = jnp.sum(d_extra[:, 0], axis=0)
    stamp_grad = exact_dot(time_loc[0].T, d_extra[:, 1])
    meta_part = jnp.concatenate([class_grad[None, :], stamp_grad], axis=0)
    d_kernel = inner_dot(pixels, d_patches).reshape(MAXB, PIX * D)
    d_kernel = jnp.where(live_band, d_kernel, 0.0)
    d_bias = jnp.sum(d_patches.astype(jnp.float32), axis=0) / band_float
    d_bias_rows = jnp.where(live_band, d_bias[None, :], 0.0)
    d_generated = jnp.concatenate([d_kernel, d_bias_rows], axis=1).astype(half_type)
    placed = jnp.where(
        chosen_sensor[:, None, None], d_generated.astype(jnp.float32)[None], 0.0
    ).reshape(SENSORS * MAXB, GENOUT)
    columns = lax.psum_scatter(placed, ("dp", "fsdp"), scatter_dimension=1, tiled=True)
    gen_out_grad = exact_dot(hidden.astype(jnp.float32).T, columns)
    d_hidden = exact_dot(columns, gen_out.astype(jnp.float32).T)
    d_before = gelu_slope(before, d_hidden)
    gen_in_part = exact_dot(codes.T, d_before)
    gen_bias_part = jnp.sum(d_before, axis=0)
    meta_grad, gen_in_grad, gen_bias_grad = lax.psum(
        (meta_part, gen_in_part, gen_bias_part), ("dp", "fsdp")
    )
    qkv_cols, out_cols, up_cols, down_cols = (
        lax.psum_scatter(
            w_qkv_grad.astype(jnp.bfloat16), "fsdp", scatter_dimension=1, tiled=True
        ).astype(jnp.float32),
        lax.psum_scatter(
            w_out_grad.astype(jnp.bfloat16), "fsdp", scatter_dimension=1, tiled=True
        ).astype(jnp.float32),
        lax.psum_scatter(
            w_up_grad.astype(jnp.bfloat16), "fsdp", scatter_dimension=1, tiled=True
        ).astype(jnp.float32),
        lax.psum_scatter(
            w_down_grad.astype(jnp.bfloat16), "fsdp", scatter_dimension=1, tiled=True
        ).astype(jnp.float32),
    )
    vectors_group, b_up_group = lax.psum((vectors_grad, b_up_grad), "fsdp")
    w_qkv_out, w_out_out, w_up_out, w_down_out, vectors_out, b_up_out = (
        lax.psum_scatter(
            qkv_cols.astype(jnp.bfloat16), "dp", scatter_dimension=0, tiled=True
        ).astype(jnp.float32),
        lax.psum_scatter(
            out_cols.astype(jnp.bfloat16), "dp", scatter_dimension=0, tiled=True
        ).astype(jnp.float32),
        lax.psum_scatter(
            up_cols.astype(jnp.bfloat16), "dp", scatter_dimension=0, tiled=True
        ).astype(jnp.float32),
        lax.psum_scatter(
            down_cols.astype(jnp.bfloat16), "dp", scatter_dimension=0, tiled=True
        ).astype(jnp.float32),
        lax.psum_scatter(
            vectors_group.astype(jnp.bfloat16), "dp", scatter_dimension=0, tiled=True
        ).astype(jnp.float32),
        lax.psum_scatter(
            b_up_group.astype(jnp.bfloat16), "dp", scatter_dimension=0, tiled=True
        ).astype(jnp.float32),
    )
    return (
        layer_out,
        pixel_grad,
        gen_in_grad,
        gen_bias_grad,
        gen_out_grad,
        meta_grad,
        w_qkv_out,
        w_out_out,
        w_up_out,
        w_down_out,
        vectors_out,
        b_up_out,
    )


LIVE = 1032
ROWS = 1040
TILE = 208
TILES = 5
NZ = 4
GROUPS = 16
PIECE = 144
COVER = 14
VMEM_ASK = 60 * 1024 * 1024
BF = jnp.bfloat16
F32 = jnp.float32


def nt_dot(left, right):
    return lax.dot_general(left, right, (((1,), (1,)), ((), ())), preferred_element_type=F32)


def nn_dot(left, right):
    return lax.dot_general(left, right, (((1,), (0,)), ((), ())), preferred_element_type=F32)


def spot():
    group = lax.axis_index("dp")
    return group // 4, (group // 2) % 2, group % 2, lax.axis_index("fsdp")


def device(z, y, c, x):
    return {"dp": z * 4 + y * 2 + c, "fsdp": x}


def remote(source, target, sems, slot, where):
    return pltpu.make_async_remote_copy(
        src_ref=source,
        dst_ref=target,
        send_sem=sems[0].at[slot],
        recv_sem=sems[1].at[slot],
        device_id=where,
        device_id_type=pl.DeviceIdType.MESH,
    )


def greet(others):
    barrier = pltpu.get_barrier_semaphore()
    for where in others:
        pl.semaphore_signal(
            barrier, inc=1, device_id=where, device_id_type=pl.DeviceIdType.MESH
        )
    pl.semaphore_wait(barrier, len(others))


def columns(ref, x):
    width = ref.shape[-1] // 2
    return pl.ds(pl.multiple_of(x * width, 128), width)


def group_peers(z, y, c, x):
    return [
        ((dz, dy, dc), device((z + dz) % NZ, (y + dy) % 2, (c + dc) % 2, x))
        for dz in range(NZ)
        for dy in range(2)
        for dc in range(2)
        if dz + dy + dc
    ]


CHUNK = 768
BANDS = ((0, 256), (256, 256), (512, 256), (768, 256), (1024, 8))


def gelu_parts(values):
    bell = jnp.exp(values * values * (-0.5))
    step = 1.0 / (1.0 + (0.3275911 * math.sqrt(0.5)) * jnp.abs(values))
    poly = 0.5 * 1.061405429 * step - 0.5 * 1.453152027
    poly = poly * step + 0.5 * 1.421413741
    poly = poly * step - 0.5 * 0.284496736
    poly = poly * step + 0.5 * 0.254829592
    tail = poly * step * bell
    below = jnp.where(values < 0.0, tail, 1.0 - tail)
    return values * below, below + values * bell * (1.0 / math.sqrt(2.0 * math.pi))


def standard(values):
    centred = values - jnp.mean(values, axis=-1, keepdims=True)
    scale = lax.rsqrt(jnp.mean(centred * centred, axis=-1, keepdims=True) + 1e-05)
    return centred * scale, scale


def column_sum(values):
    return jnp.sum(values, axis=0, keepdims=True)


def put_rows(target, first, count, values):
    if count % 16:
        values = jnp.concatenate(
            [values, jnp.zeros((16 - count % 16, values.shape[1]), values.dtype)], axis=0
        )
    target[first : first + values.shape[0], :] = values


class Gather:
    COPIES = 19

    def __init__(self, shard, whole, sems, local, first, lean, here):
        z, y, c, x = here
        self.lean = lean
        mine, other = columns(whole, x), columns(whole, 1 - x)
        across, beside, twin = device(z, y, c, 1 - x), device(z, 1 - y, c, x), device(z, y, 1 - c, x)
        target = whole.at[z, y, c, :, mine]
        self.local = pltpu.make_async_copy(shard, target, local)
        self.along = [
            remote(shard, target, sems, first + k - 1, device((z + k) % NZ, y, c, x))
            for k in range(1, NZ)
        ]
        self.to_x, self.to_y, self.far = [], [], []
        for k in range(NZ):
            at = (z + NZ - k) % NZ
            place = whole.at[at, y, c, :, mine]
            source = place if k else shard
            self.to_x.append(remote(source, place, sems, first + 3 + k, across))
            self.to_y.append(remote(source, place, sems, first + 7 + k, beside))
            if k < lean:
                place = whole.at[at, y, c, :, other]
                self.far.append(remote(place, place, sems, first + 11 + k, beside))
            else:
                place = whole.at[at, 1 - y, c, :, mine]
                self.far.append(remote(place, place, sems, first + 11 + k, across))
        self.core = []
        for step, part in enumerate(
            (
                whole.at[:, y, c, :, mine],
                whole.at[:, y, c, :, other],
                whole.at[:, 1 - y, c, :, mine],
                whole.at[:, 1 - y, c, :, other],
            )
        ):
            self.core.append(remote(part, part, sems, first + 15 + step, twin))

    def send_z(self):
        self.local.start()
        for copy in self.along:
            copy.start()

    def send_own(self):
        self.to_x[0].start()
        self.to_y[0].start()

    def pass_on(self):
        for k in range(1, NZ):
            self.along[k - 1].wait_recv()
            self.to_x[k].start()
            self.to_y[k].start()
        self.local.wait()
        self.core[0].start()

    def turn_corner(self):
        for k in range(NZ):
            (self.to_x if k < self.lean else self.to_y)[k].wait_recv()
            self.far[k].start()
        for k in range(self.lean, NZ):
            self.to_x[k].wait_recv()
        self.core[1].start()
        for k in range(self.lean):
            self.to_y[k].wait_recv()
        self.core[2].start()

    def share(self):
        for copy in self.far:
            copy.wait_recv()
        self.core[3].start()

    def receive(self):
        for copy in self.core:
            copy.wait_recv()

    def finish(self):
        for copy in (*self.along, *self.to_x, *self.to_y, *self.far, *self.core):
            copy.wait_send()


def make_small(vectors, b_up, held, small):
    group = lax.axis_index("dp")
    count, up_count = vectors.shape[1], b_up.shape[1]
    per_row = D // up_count
    held[...] = jnp.zeros_like(held)
    held[0:6, 0:count] = vectors[...].astype(F32)
    held[8:9, 0:up_count] = b_up[...].astype(F32)
    rows = pltpu.roll(held[0:8, :], group * count, 1)
    bias = pltpu.roll(held[8:16, :], (group % per_row) * up_count, 1)[0:1]
    row = lax.broadcasted_iota(jnp.int32, (8, D), 0)
    spot_at = 6 + group // per_row
    top = jnp.where(row < 6, rows, jnp.where(row == spot_at, bias, 0.0))
    small[...] = jnp.concatenate(
        [top, jnp.where(row + 8 == spot_at, bias, 0.0)], axis=0
    ).astype(BF)


def make_table(kind, ground, steps, table):
    wide = steps.shape[1]
    entry = lax.broadcasted_iota(jnp.int32, (64, wide), 0)
    lane = lax.broadcasted_iota(jnp.int32, (64, wide), 1)
    single = kind == 1
    chip = jnp.where(single, 0, entry // 16)
    step = jnp.where(single, entry, entry % 16).astype(F32)
    distance = jnp.zeros((64, wide), F32)
    for slot in range(SLOTS):
        distance = jnp.where(chip == slot, ground[0, slot].astype(F32), distance)
    angle = (step * (distance / 10.0)) * steps[0:1, :]
    exact = jnp.where(lane < wide // 2, jnp.sin(angle), jnp.cos(angle))
    for at, part in enumerate(three_parts(exact)):
        table[at * 64 : (at + 1) * 64, :] = part
    table[192:256, :] = jnp.zeros((64, wide), BF)


def make_pieces(
    groups, bands, waves, wave_table, steps, gen_in, gen_bias, gen_out,
    gen_shift, hidden, slope, codes, made, code_rows, rows, wide, angles,
):
    for wave in range(angles.shape[0]):
        angles[wave : wave + 1, :] = (wave_table[wave] * 1000.0) * steps[0:1, :]
    lane = lax.broadcasted_iota(jnp.int32, angles.shape, 1)
    angle = angles[...]
    angles[...] = jnp.where(lane < GEN // 2, jnp.sin(angle), jnp.cos(angle))
    for sensor in range(SENSORS):
        for band in range(MAXB):
            code_rows[sensor, band : band + 1, :] = angles[pl.ds(waves[sensor, band], 1), :]
        code_rows[sensor, MAXB:16, :] = jnp.zeros((16 - MAXB, GEN), F32)
    flat = code_rows[:, 0:16, :].reshape(SENSORS * 16, GEN)
    before = exact_dot(flat, gen_in[...].astype(F32)) + gen_bias[...].astype(F32)
    values, slopes = gelu_parts(before)
    band_at = lax.broadcasted_iota(jnp.int32, (16, GEN), 0)
    width = gen_out.shape[0]
    owner = lax.axis_index("dp") * 2 + lax.axis_index("fsdp")
    wide[...] = jnp.zeros_like(wide)
    wide[pl.ds(pl.multiple_of((owner * width) % 128, 8), width), :] = gen_out[...].astype(F32)
    gen_shift[...] = wide[...].astype(BF)
    kept = []
    for sensor in range(SENSORS):
        part = slice(sensor * 16, sensor * 16 + 16)
        live = band_at < bands[sensor]
        kept.append(jnp.where(live, values[part], 0.0))
        code_rows[sensor, 16:32, :] = kept[-1].astype(BF).astype(F32)
        code_rows[sensor, 32:48, :] = jnp.where(live, slopes[part], 0.0)
    lower = jnp.concatenate(kept, axis=0).astype(BF)
    for at in range(COVER):
        product = nt_dot(lower, gen_shift[at * 128 : (at + 1) * 128, :])
        for sensor in range(SENSORS):
            rows[sensor, at * MAXB : (at + 1) * MAXB, :] = product[
                sensor * 16 : sensor * 16 + MAXB
            ]
    rows[:, COVER * MAXB :, :] = jnp.zeros((SENSORS, PIECE - COVER * MAXB, 128), F32)
    for group in range(GROUPS):
        made[group // 4, (group // 2) % 2, group % 2] = rows[groups[group]].astype(BF)
    for group in range(GROUPS):
        own = code_rows[groups[group]]
        first = group * MAXB
        codes[first : first + MAXB, :] = own[0:MAXB]
        hidden[first : first + MAXB, :] = own[16 : 16 + MAXB]
        slope[first : first + MAXB, :] = own[32 : 32 + MAXB]


def mask_rows(kind, for_query, for_key):
    row = lax.broadcasted_iota(jnp.int32, (ROWS, 128), 0)
    lane = lax.broadcasted_iota(jnp.int32, (ROWS, 128), 1)
    patch = jnp.where(kind == 1, 0, row // (TOK_DEV // SLOTS))
    segment = jnp.where(row < TOK_DEV, patch, (row - TOK_DEV) // 2)
    hot = (lane == segment) & (row < LIVE)
    for_query[...] = jnp.where(hot, 1.0, 0.0).astype(BF)
    for_key[...] = jnp.where(
        lane < SLOTS, jnp.where(hot, 0.0, -1e30), jnp.where(lane < SLOTS + 3, 1.0, 0.0)
    ).astype(BF)


def attend_pair(pair, qkv, mask_q, mask_k, keys, values, mixed, log_sum):
    lane = lax.broadcasted_iota(jnp.int32, (TILE, 128), 1)
    lanes = pl.ds(pl.multiple_of(pair * 128, 128), 128)
    keys[:, 0:128] = qkv[6 + pair]
    keys[:, 128:256] = mask_k[...]
    values[:, 0:128] = qkv[12 + pair]
    for tile in range(TILES):
        first = tile * TILE
        both = qkv[pair, first : first + TILE, :] * BF(0.125)
        results, sums = [], []
        for head in range(2):
            query = jnp.where((lane < HEAD) == (head == 0), both, BF(0))
            scores = nt_dot(
                jnp.concatenate([query, mask_q[first : first + TILE, :]], axis=1), keys[...]
            )
            peak = jnp.max(scores, axis=1, keepdims=True)
            expo = jnp.exp(scores - peak).astype(BF)
            made = nn_dot(expo, values[...])
            totals = made[:, 128:256]
            results.append(made[:, 0:128] / totals)
            sums.append(peak + jnp.log(totals))
        count = min(TILE, LIVE - first)
        mixed[first : first + count, lanes] = jnp.where(lane < HEAD, *results)[:count].astype(BF)
        log_sum[pair, first : first + TILE, :] = jnp.where(lane < HEAD, *sums)


def forward_kernel(
    wq, wo, wu, wd, pixels, vectors, b_up, meta_weight, time_loc, gen_in, gen_bias, gen_out,
    wave_steps, place_steps,
    groups, bands, waves, wave_table, kind, ground,
    full_q, full_o, full_u, full_d, params, kernel, tokens, first, qkv, mixed, log_sum,
    gen_shift, hidden, slope, codes,
    made, code_rows, rows, roll, angles, small_held, small, table,
    taken, full_small, flat, wide, keys, values, mask_q, mask_k,
    w_send, w_recv, local_sem, s_send, s_recv, g_send, g_recv,
):
    here = z, y, c, x = spot()
    peers = group_peers(z, y, c, x)
    across = device(z, y, c, 1 - x)
    greet([where for _, where in peers] + [across])
    gathers = q, o, u, d = [
        Gather(shard, whole, (w_send, w_recv), local_sem.at[step], Gather.COPIES * step, lean, here)
        for step, (shard, whole, lean) in enumerate(
            ((wq, full_q, 3), (wo, full_o, 2), (wu, full_u, 3), (wd, full_d, 2))
        )
    ]
    s_sems = (s_send, s_recv)
    g_sems = (g_send, g_recv)
    q.send_z()
    for gather in gathers:
        gather.send_own()
    make_pieces(
        groups, bands, waves, wave_table, wave_steps, gen_in, gen_bias, gen_out,
        gen_shift, hidden, slope, codes, made, code_rows, rows, roll, angles,
    )
    make_small(vectors, b_up, small_held, small)
    mask_rows(kind[0], mask_q, mask_k)
    make_table(kind[0], ground, place_steps, table)
    values[:, 128:256] = jnp.ones((ROWS, 128), BF)
    q.pass_on()
    own_made = pltpu.make_async_copy(
        made.at[z, y, c], taken.at[z, y, c, x], local_sem.at[4]
    )
    own_made.start()
    sends = {}
    for (dz, dy, dc), where in peers:
        copy = remote(
            made.at[(z + dz) % NZ, (y + dy) % 2, (c + dc) % 2],
            taken.at[z, y, c, x],
            g_sems,
            dz * 4 + dy * 2 + dc,
            where,
        )
        copy.start()
        sends[dz, dy, dc] = copy
    own_small = pltpu.make_async_copy(small, full_small.at[z, y, c], local_sem.at[5])
    own_small.start()
    small_z = [
        remote(small, full_small.at[z, y, c], s_sems, k - 1, device((z + k) % NZ, y, c, x))
        for k in range(1, NZ)
    ]
    for copy in small_z:
        copy.start()
    q.turn_corner()
    own_made.wait()
    swaps = []
    for dz in range(NZ):
        for dy in range(2):
            for dc in range(2):
                if dz + dy + dc:
                    sends[dz, dy, dc].wait_recv()
        part = taken.at[(z + NZ - dz) % NZ, :, :, x]
        swap = remote(part, part, g_sems, 16 + dz, across)
        swap.start()
        swaps.append(swap)
    u.send_z()
    own_small.wait()
    for copy in small_z:
        copy.wait_recv()
    part = full_small.at[:, y, c]
    small_y = remote(part, part, s_sems, 3, device(z, 1 - y, c, x))
    small_y.start()
    q.share()
    for swap in swaps:
        swap.wait_recv()
    small_y.wait_recv()
    part = full_small.at[:, :, c]
    small_c = remote(part, part, s_sems, 4, device(z, y, 1 - c, x))
    small_c.start()
    unpack(taken, flat, wide, kernel)
    bias = jnp.concatenate(
        [
            column_sum(flat[(PIX * 6 + part) * MAXB : (PIX * 6 + part + 1) * MAXB, :])
            for part in range(6)
        ],
        axis=1,
    ) / bands[groups[lax.axis_index("dp")]].astype(F32)
    single = kind[0] == 1
    for start, count in BANDS[:-1]:
        band = slice(start, start + count)
        made_rows = nn_dot(pixels[band, :], kernel[...])
        index = start + lax.broadcasted_iota(jnp.int32, (count, 256), 0)
        lane = lax.broadcasted_iota(jnp.int32, (count, 256), 1)
        spread = []
        for spots in (
            jnp.where(single, index // 32, index // 16),
            jnp.where(single, index % 32, index // 256 * 16 + index % 16),
        ):
            hot = (lane % 64 == spots) & (lane < 192)
            spread.append(nn_dot(jnp.where(hot, 1.0, 0.0).astype(BF), table[...]))
        tokens[band, :] = made_rows + bias + jnp.concatenate(spread, axis=1)
    u.pass_on()
    d.send_z()
    small_c.wait_recv()
    params[...] = jnp.zeros_like(params)
    for n in range(GROUPS):
        params[...] += full_small[n // 4, (n // 2) % 2, n % 2].astype(F32)
    meta = meta_weight[...].astype(F32)
    stamps = exact_dot(time_loc[0], meta[1:])
    for slot in range(SLOTS):
        at = TOK_DEV + 2 * slot
        tokens[at : at + 1, :] = meta[0:1]
        tokens[at + 1 : at + 2, :] = stamps[slot : slot + 1]
    for start, count in BANDS:
        band = slice(start, start + count)
        normed, _ = standard(tokens[band, :])
        first[band, :] = (normed * params[0:1, :] + params[1:2, :]).astype(BF)
    q.receive()
    for start, count in BANDS:
        band = slice(start, start + count)
        for third in range(3):
            part = slice(third * D, (third + 1) * D)
            made_rows = nn_dot(
                first[band, :], full_q[:, :, :, :, part].reshape(D, D)
            ).astype(BF)
            for block in range(6):
                put_rows(
                    qkv.at[third * 6 + block],
                    start,
                    count,
                    made_rows[:, block * 128 : (block + 1) * 128],
                )

    def one_pair(pair, carry):
        @pl.when(pair == 1)
        def _():
            d.pass_on()
            o.send_z()
            u.turn_corner()

        @pl.when(pair == 2)
        def _():
            o.pass_on()

        @pl.when(pair == 3)
        def _():
            d.turn_corner()
            u.share()

        @pl.when(pair == 4)
        def _():
            o.turn_corner()
            d.share()

        @pl.when(pair == 5)
        def _():
            o.share()

        attend_pair(pair, qkv, mask_q, mask_k, keys, values, mixed, log_sum)
        return carry

    lax.fori_loop(0, HEADS // 2, one_pair, 0)
    for gather in (o, u, d):
        gather.receive()
    for gather in gathers:
        gather.finish()
    for copy in (*small_z, small_y, small_c, *sends.values(), *swaps):
        copy.wait_send()


def forward(shards, operands, scalars):
    anywhere = pl.BlockSpec(memory_space=pl.ANY)
    vmem = pl.BlockSpec(memory_space=pltpu.VMEM)
    smem = pl.BlockSpec(memory_space=pltpu.SMEM)
    blocks = GROUPS * MAXB
    outs = [
        jax.ShapeDtypeStruct((NZ, 2, 2, shard.shape[0], 2 * shard.shape[1]), BF) for shard in shards
    ]
    outs += [
        jax.ShapeDtypeStruct((16, D), F32),
        jax.ShapeDtypeStruct((MAXB * PIX, D), BF),
        jax.ShapeDtypeStruct((LIVE, D), F32),
        jax.ShapeDtypeStruct((LIVE, D), BF),
        jax.ShapeDtypeStruct((18, ROWS, 128), BF),
        jax.ShapeDtypeStruct((LIVE, D), BF),
        jax.ShapeDtypeStruct((HEADS // 2, ROWS, 128), F32),
        jax.ShapeDtypeStruct((COVER * 128, GEN), BF),
        jax.ShapeDtypeStruct((blocks, GEN), F32),
        jax.ShapeDtypeStruct((blocks, GEN), F32),
        jax.ShapeDtypeStruct((blocks, GEN), F32),
    ]
    return pl.pallas_call(
        forward_kernel,
        out_shape=outs,
        in_specs=[anywhere] * 4 + [vmem] * len(operands) + [smem] * len(scalars),
        out_specs=[vmem] + [anywhere] * 3 + [vmem] * 11,
        scratch_shapes=[
            pltpu.VMEM((NZ, 2, 2, PIECE, 128), BF),
            pltpu.VMEM((SENSORS, 48, GEN), F32),
            pltpu.VMEM((SENSORS, PIECE, 128), F32),
            pltpu.VMEM((COVER * 128, GEN), F32),
            pltpu.VMEM((scalars[3].shape[0], GEN), F32),
            pltpu.VMEM((16, D), F32),
            pltpu.VMEM((16, D), BF),
            pltpu.VMEM((256, D // 2), BF),
            pltpu.VMEM((NZ, 2, 2, 2, PIECE, 128), BF),
            pltpu.VMEM((NZ, 2, 2, 16, D), BF),
            pltpu.VMEM((FLAT, 128), F32),
            pltpu.VMEM((6, MAXB * PIX, 128), F32),
            pltpu.VMEM((ROWS, 256), BF),
            pltpu.VMEM((ROWS, 256), BF),
            pltpu.VMEM((ROWS, 128), BF),
            pltpu.VMEM((ROWS, 128), BF),
        ]
        + [pltpu.SemaphoreType.DMA((count,)) for count in (76, 76, 6, 5, 5, 20, 20)],
        compiler_params=pltpu.CompilerParams(
            collective_id=0, has_side_effects=True, vmem_limit_bytes=VMEM_ASK
        ),
    )(*shards, *operands, *scalars)


class Scatter:
    def __init__(self, whole, own, came, low, high, side_x, side_y, last, out, sems, first, here):
        z, y, c, x = here
        self.here, self.own, self.came, self.out = here, own, came, out
        self.low, self.high, self.side_x, self.side_y, self.last = low, high, side_x, side_y, last
        self.mine, self.other = columns(own, x), columns(own, 1 - x)
        mine, other = self.mine, self.other
        across, beside, twin = device(z, y, c, 1 - x), device(z, 1 - y, c, x), device(z, y, 1 - c, x)
        self.local = pltpu.make_async_copy(whole.at[:, :, c], own, sems[2].at[first // 8])
        self.core = remote(whole.at[:, :, 1 - c], came, sems, first, twin)
        self.far_y = remote(own.at[0:2, 1 - y, :, other], low, sems, first + 1, beside)
        self.far_x = remote(own.at[2:4, 1 - y, :, other], high, sems, first + 2, across)
        self.to_x = remote(own.at[:, y, :, other], side_x, sems, first + 3, across)
        self.to_y = remote(own.at[:, 1 - y, :, mine], side_y, sems, first + 4, beside)
        self.along = [
            remote(
                own.at[(z + k) % NZ, y, :, mine], last.at[k - 1], sems, first + 4 + k,
                device((z + k) % NZ, y, c, x),
            )
            for k in range(1, NZ)
        ]

    def stage_a(self):
        self.local.start()
        self.core.start()

    def stage_b(self):
        self.local.wait()
        self.core.wait_recv()
        for at_z in range(NZ):
            for at_y in range(2):
                self.own[at_z, at_y] = (
                    self.own[at_z, at_y].astype(F32) + self.came[at_z, at_y].astype(F32)
                ).astype(BF)
        self.far_y.start()
        self.far_x.start()

    def stage_c(self):
        _, y, _, _ = self.here
        self.far_y.wait_recv()
        for k in range(2):
            self.own[k, y, :, self.other] = (
                self.own[k, y, :, self.other].astype(F32) + self.low[k].astype(F32)
            ).astype(BF)
        self.to_x.start()
        self.far_x.wait_recv()
        for k in range(2):
            self.own[2 + k, 1 - y, :, self.mine] = (
                self.own[2 + k, 1 - y, :, self.mine].astype(F32) + self.high[k].astype(F32)
            ).astype(BF)
        self.to_y.start()

    def stage_d(self):
        _, y, _, _ = self.here
        self.to_x.wait_recv()
        self.to_y.wait_recv()
        for k in range(NZ):
            self.own[k, y, :, self.mine] = (
                self.own[k, y, :, self.mine].astype(F32)
                + self.side_x[k].astype(F32)
                + self.side_y[k].astype(F32)
            ).astype(BF)
        for copy in self.along:
            copy.start()

    def stage_e(self):
        z, y, _, _ = self.here
        for copy in self.along:
            copy.wait_recv()
        self.out[...] = (
            self.own[z, y, :, self.mine].astype(F32)
            + self.last[0].astype(F32)
            + self.last[1].astype(F32)
            + self.last[2].astype(F32)
        )
        for copy in (self.core, self.far_y, self.far_x, self.to_x, self.to_y, *self.along):
            copy.wait_send()


class Total:
    COPIES = 7

    def __init__(self, source, out, held, came, slots, send_sem, recv_sem, here):
        z, y, c, x = here
        sems = (send_sem, recv_sem)
        half = source.shape[0] // 2
        self.mine = pl.ds(pl.multiple_of(c * half, 8), half)
        theirs = pl.ds(pl.multiple_of((1 - c) * half, 8), half)
        self.source, self.held, self.came, self.slots, self.out = source, held, came, slots, out
        self.z = z
        twin = device(z, y, 1 - c, x)
        self.steps = [
            remote(source.at[theirs], came.at[0], sems, 0, twin),
            remote(held.at[0], came.at[1], sems, 1, device(z, y, c, 1 - x)),
            remote(held.at[1], came.at[2], sems, 2, device(z, 1 - y, c, x)),
        ]
        self.along = [
            remote(held.at[2], slots.at[z], sems, 2 + k, device((z + k) % NZ, y, c, x))
            for k in range(1, NZ)
        ]
        self.last = remote(out.at[self.mine], out.at[self.mine], sems, 6, twin)

    def begin(self):
        self.steps[0].start()

    def turn(self, step):
        self.steps[step].wait_recv()
        before = self.source[self.mine, :] if step == 0 else self.held[step - 1]
        self.held[step] = before + self.came[step]
        if step < 2:
            self.steps[step + 1].start()
        else:
            self.slots[self.z] = self.held[2]
            for copy in self.along:
                copy.start()

    def close(self):
        for copy in self.along:
            copy.wait_recv()
        self.out[self.mine, :] = self.slots[0] + self.slots[1] + self.slots[2] + self.slots[3]
        self.last.start()

    def finish(self):
        for copy in (*self.steps, *self.along):
            copy.wait_send()
        self.last.wait()


def near(z, y, c, x):
    return [
        device(z, y, c, 1 - x),
        device(z, 1 - y, c, x),
        device(z, y, 1 - c, x),
        *[device((z + k) % NZ, y, c, x) for k in range(1, NZ)],
    ]


def scatter_scratch(rows, width):
    half = width // 2
    return [
        pltpu.VMEM((NZ, 2, rows, width), BF),
        pltpu.VMEM((NZ, 2, rows, width), BF),
        pltpu.VMEM((2, rows, half), BF),
        pltpu.VMEM((2, rows, half), BF),
        pltpu.VMEM((NZ, rows, half), BF),
        pltpu.VMEM((NZ, rows, half), BF),
        pltpu.VMEM((3, rows, half), BF),
    ]


def total_scratch(shape):
    half = (shape[0] // 2,) + shape[1:]
    return [
        pltpu.VMEM((3,) + half, F32),
        pltpu.VMEM((3,) + half, F32),
        pltpu.VMEM((NZ,) + half, F32),
        pltpu.SemaphoreType.DMA((Total.COPIES,)),
        pltpu.SemaphoreType.DMA((Total.COPIES,)),
    ]


def piece_start(owner):
    return (owner * (GENOUT // 32)) // 128


FLAT = (GENOUT // 128) * MAXB


def unpack(taken, flat, wide, kernel):
    flat[...] = jnp.zeros_like(flat)
    used = COVER * MAXB
    for owner in range(32):
        first = piece_start(owner) * MAXB
        count = min(used, FLAT - first)
        piece = taken[owner // 8, (owner // 4) % 2, (owner // 2) % 2, owner % 2]
        flat[first : first + count, :] += piece.astype(F32)[:count]
    for pixel in range(PIX):
        for part in range(6):
            first = (pixel * 6 + part) * MAXB
            wide[part, pl.ds(pixel, MAXB, stride=PIX), :] = flat[first : first + MAXB, :]
    for part in range(6):
        kernel[:, part * 128 : (part + 1) * 128] = wide[part].astype(BF)


def pack(d_kernel, bias, pieces, wide, flat):
    for part in range(6):
        wide[part] = d_kernel[:, part * 128 : (part + 1) * 128]
        first = (PIX * 6 + part) * MAXB
        flat[first : first + MAXB, :] = bias[0:MAXB, part * 128 : (part + 1) * 128]
    flat[FLAT:, :] = jnp.zeros((flat.shape[0] - FLAT, 128), F32)
    for pixel in range(PIX):
        for part in range(6):
            first = (pixel * 6 + part) * MAXB
            flat[first : first + MAXB, :] = wide[part, pl.ds(pixel, MAXB, stride=PIX), :]
    for owner in range(32):
        first = piece_start(owner) * MAXB
        pieces[owner // 8, (owner // 4) % 2, (owner // 2) % 2, owner % 2] = flat[
            first : first + PIECE, :
        ].astype(BF)


def norm_rows_back(value, upstream, gain):
    normed, scale = standard(value)
    scaled = upstream * gain
    inside = (
        scaled
        - jnp.mean(scaled, axis=-1, keepdims=True)
        - normed * jnp.mean(scaled * normed, axis=-1, keepdims=True)
    )
    return scale * inside, column_sum(upstream * normed), column_sum(upstream)


def close_kernel(
    d_qkv, first, w_qkv, tokens, d_after, params, pixels, kernel, time_loc, late, b_grad,
    hidden, gen_shift, slope, codes, groups, bands,
    out_grad, in_grad, out_q, out_early, pixel_grad,
    d_tokens, grad_q, pieces, crossed, merged, taken, flat, wide, rows, source, early,
    x_send, x_recv, send_sem, recv_sem, local_sem, q_send, q_recv, *rest,
):
    here = z, y, c, x = spot()
    across = device(z, y, c, 1 - x)
    greet([where for _, where in group_peers(z, y, c, x)] + [across])
    scatter = Scatter(
        grad_q, *rest[10:17], out_q, (q_send, q_recv, local_sem), 0, here
    )
    begin = Total(early, out_early, *rest[0:5], here)
    total = Total(source, in_grad, *rest[5:10], here)
    gain = shift = jnp.zeros((1, D), F32)
    for start, count in BANDS:
        band = slice(start, start + count)
        upstream = nt_dot(d_qkv[band, :], w_qkv[...].reshape(D, 3 * D))
        d_norm, gain_part, shift_part = norm_rows_back(tokens[band, :], upstream, params[0:1, :])
        gain += gain_part
        shift += shift_part
        d_tokens[band, :] = (d_after[band, :] + d_norm).astype(BF)
    patches = d_tokens[0:TOK_DEV, :]
    d_kernel = inner_dot(pixels[...], patches)
    live = bands[groups[lax.axis_index("dp")]]
    band_at = lax.broadcasted_iota(jnp.int32, (16, D), 0)
    sums = column_sum(patches.astype(F32)) / live.astype(F32)
    pack(d_kernel, jnp.where(band_at < live, sums, 0.0), pieces, wide, flat)
    order = (2, 1, 3, 0)
    swaps = {}
    for dz in order:
        to = (z + dz) % NZ
        swaps[dz] = remote(
            pieces.at[to, :, :, 1 - x], crossed.at[to], (x_send, x_recv), dz, across
        )
    swaps[2].start()
    swaps[1].start()
    sends = []

    def merge(dz):
        to = (z + dz) % NZ
        swaps[dz].wait_recv()
        if dz in (2, 1):
            swaps[{2: 3, 1: 0}[dz]].start()
        for at_y in range(2):
            for at_c in range(2):
                merged[to, at_y, at_c] = (
                    pieces[to, at_y, at_c, x].astype(F32) + crossed[to, at_y, at_c].astype(F32)
                ).astype(BF)
        for dy in range(2):
            for dc in range(2):
                at_y, at_c = (y + dy) % 2, (c + dc) % 2
                if dz + dy + dc:
                    copy = remote(
                        merged.at[to, at_y, at_c],
                        taken.at[z, y, c],
                        (send_sem, recv_sem),
                        dz * 4 + dy * 2 + dc,
                        device(to, at_y, at_c, x),
                    )
                    copy.start()
                    sends.append(copy)
                else:
                    taken[z, y, c] = merged[z, y, c]

    def grad_third(third):
        part = slice(third * D, (third + 1) * D)
        grad_q[:, :, :, :, part] = (
            inner_dot(first[...], d_qkv[:, part]).astype(BF).reshape(NZ, 2, 2, -1, D)
        )

    grad_third(0)
    merge(2)
    grad_third(1)
    merge(1)
    grad_third(2)
    scatter.stage_a()
    merge(3)
    merge(0)
    extra = d_tokens[TOK_DEV:LIVE, :].astype(F32)
    stamps = jnp.concatenate([extra[2 * m + 1 : 2 * m + 2] for m in range(SLOTS)], axis=0)
    early[0:1, :] = extra[0:1] + extra[2:3] + extra[4:5] + extra[6:7]
    early[1:9, :] = lax.dot_general(
        time_loc[0],
        stamps,
        (((0,), (0,)), ((), ())),
        precision=lax.Precision.HIGHEST,
        preferred_element_type=F32,
    )
    early[9:16, :] = jnp.zeros((7, D), F32)
    early[16:24, :] = late[...]
    early[16:17, :] = gain
    early[17:18, :] = shift
    early[24:32, :] = b_grad[...]
    begin.begin()
    for start, count in BANDS[:2]:
        band = slice(start, start + count)
        pixel_grad[band, :] = nt_dot(d_tokens[band, :], kernel[...])
    scatter.stage_b()
    begin.turn(0)
    for start, count in BANDS[2:4]:
        band = slice(start, start + count)
        pixel_grad[band, :] = nt_dot(d_tokens[band, :], kernel[...])
    scatter.stage_c()
    begin.turn(1)
    for copy in sends:
        copy.wait_recv()
    for n in range(GROUPS):
        block = taken[n // 4, (n // 2) % 2, n % 2].astype(F32)
        for at in range(COVER):
            rows[at, n * MAXB : (n + 1) * MAXB, :] = block[at * MAXB : (at + 1) * MAXB]
    d_hidden = jnp.zeros((GROUPS * MAXB, GEN), F32)
    for at in range(COVER):
        d_hidden += nn_dot(rows[at].astype(BF), gen_shift[at * 128 : (at + 1) * 128, :])
    d_before = d_hidden * slope[...]
    source[0:GEN, :] = lax.dot_general(
        codes[...],
        d_before,
        (((0,), (0,)), ((), ())),
        precision=lax.Precision.HIGHEST,
        preferred_element_type=F32,
    )
    source[GEN:, :] = jnp.broadcast_to(column_sum(d_before), (source.shape[0] - GEN, GEN))
    total.begin()
    low = hidden[...].astype(BF)
    for at in range(COVER // 2):
        out_grad[at * 128 : (at + 1) * 128, :] = inner_dot(rows[at].astype(BF), low)
    total.turn(0)
    scatter.stage_d()
    for at in range(COVER // 2, COVER):
        out_grad[at * 128 : (at + 1) * 128, :] = inner_dot(rows[at].astype(BF), low)
    total.turn(1)
    total.turn(2)
    begin.turn(2)
    total.close()
    scatter.stage_e()
    begin.close()
    begin.finish()
    total.finish()
    for copy in (*sends, *swaps.values()):
        copy.wait_send()


def closing(operands, scalars):
    vmem = pl.BlockSpec(memory_space=pltpu.VMEM)
    smem = pl.BlockSpec(memory_space=pltpu.SMEM)
    small, early = (GEN + 16, GEN), (32, D)
    held = (NZ, 2, 2, PIECE, 128)
    _, _, _, rows, width = operands[2].shape
    return pl.pallas_call(
        close_kernel,
        in_specs=[vmem] * len(operands) + [smem] * len(scalars),
        out_specs=[vmem] * 5,
        out_shape=[
            jax.ShapeDtypeStruct((COVER * 128, GEN), F32),
            jax.ShapeDtypeStruct(small, F32),
            jax.ShapeDtypeStruct((rows, width // 2), F32),
            jax.ShapeDtypeStruct(early, F32),
            jax.ShapeDtypeStruct((TOK_DEV, MAXB * PIX), F32),
        ],
        scratch_shapes=[
            pltpu.VMEM((LIVE, D), BF),
            pltpu.VMEM(operands[2].shape, BF),
            pltpu.VMEM((NZ, 2, 2, 2, PIECE, 128), BF),
            pltpu.VMEM(held, BF),
            pltpu.VMEM(held, BF),
            pltpu.VMEM(held, BF),
            pltpu.VMEM((FLAT + 64, 128), F32),
            pltpu.VMEM((6, MAXB * PIX, 128), F32),
            pltpu.VMEM((COVER, GROUPS * MAXB, 128), F32),
            pltpu.VMEM(small, F32),
            pltpu.VMEM(early, F32),
            pltpu.SemaphoreType.DMA((4,)),
            pltpu.SemaphoreType.DMA((4,)),
            pltpu.SemaphoreType.DMA((16,)),
            pltpu.SemaphoreType.DMA((16,)),
            pltpu.SemaphoreType.DMA((1,)),
            pltpu.SemaphoreType.DMA((8,)),
            pltpu.SemaphoreType.DMA((8,)),
            *total_scratch(early),
            *total_scratch(small),
            *scatter_scratch(rows, width),
        ],
        compiler_params=pltpu.CompilerParams(
            collective_id=2, has_side_effects=True, vmem_limit_bytes=VMEM_ASK
        ),
    )(*operands, *scalars)


def tile_rows(source, first):
    if first + TILE <= LIVE:
        return source[first : first + TILE, :]
    part = source[first:LIVE, :]
    return jnp.concatenate([part, jnp.zeros((first + TILE - LIVE, 128), part.dtype)], axis=0)


def feed_kernel(
    tokens, mixed, top, w_out, vectors, w_up, w_down,
    layer_out, d_after, d_mixed, out_grad, rows, up_grad, down_grad, b_grad,
    second, second_turned, top_full, after, sum_out, sum_second, active, d_upper, proj,
):
    step = pl.program_id(0)

    @pl.when(step == 0)
    def _():
        for first, count in BANDS:
            band = slice(first, first + count)
            value = tokens[band, :] + (nn_dot(mixed[band, :], w_out[...]) + vectors[2:3, :])
            after[band, :] = value
            normed, _ = standard(value)
            put_rows(
                second, first, count, (normed * vectors[3:4, :] + vectors[4:5, :]).astype(BF)
            )
            put_rows(top_full, first, count, top[band, :])
        second_turned[...] = second[...].T
        sum_out[...] = jnp.zeros_like(sum_out)
        b_grad[...] = jnp.zeros_like(b_grad)
        sum_second[...] = jnp.zeros_like(sum_second)

    total = jnp.zeros((1, CHUNK), F32)
    for first, count in BANDS:
        count = -(-count // 16) * 16
        band = slice(first, first + count)
        upper = nn_dot(second[band, :], w_up[...]) + vectors[pl.ds(6 + step, 1), :]
        made, slope = gelu_parts(upper)
        made = made.astype(BF)
        active[band, :] = made
        back = (nt_dot(top_full[band, :], w_down[...]) * slope).astype(BF)
        d_upper[band, :] = back
        total += column_sum(back.astype(F32))
    b_grad[pl.ds(step, 1), :] = total
    sum_out[...] += nn_dot(active[...], w_down[...])
    sum_second[...] += nt_dot(d_upper[...], w_up[...])
    down_grad[...] = inner_dot(active[...], top_full[...]).astype(BF)
    up_grad[...] = nn_dot(second_turned[...], d_upper[...]).astype(BF)

    @pl.when(step == pl.num_programs(0) - 1)
    def _():
        gain = shift = bias = last = jnp.zeros((1, D), F32)
        for first, count in BANDS:
            band = slice(first, first + count)
            value = after[band, :]
            layer_out[band, :] = (value + sum_out[band, :] + vectors[5:6, :]).astype(BF)
            normed, scale = standard(value)
            upstream = sum_second[band, :]
            gain += column_sum(upstream * normed)
            shift += column_sum(upstream)
            scaled = upstream * vectors[3:4, :]
            inside = (
                scaled
                - jnp.mean(scaled, axis=-1, keepdims=True)
                - normed * jnp.mean(scaled * normed, axis=-1, keepdims=True)
            )
            grad_top = top[band, :].astype(F32)
            last += column_sum(grad_top)
            result = grad_top + scale * inside
            d_after[band, :] = result
            low = result.astype(BF)
            bias += column_sum(low.astype(F32))
            put_rows(proj, first, count, low)
            d_mixed[band, :] = nt_dot(low, w_out[...]).astype(BF)
        out_grad[...] = inner_dot(mixed[...], proj[0:LIVE, :]).astype(BF)
        rows[...] = jnp.concatenate([jnp.zeros((2, D), F32), bias, gain, shift, last, jnp.zeros((2, D), F32)], axis=0)


def feed(tokens, mixed, top, w_out, vectors, w_up, w_down):
    width = w_up.shape[1]

    def whole(*shape):
        return pl.BlockSpec(shape, lambda step: (0, 0))

    across = pl.BlockSpec((D, CHUNK), lambda step: (0, step))
    down = pl.BlockSpec((CHUNK, D), lambda step: (step, 0))
    block = whole(LIVE, D)
    return pl.pallas_call(
        feed_kernel,
        grid=(width // CHUNK,),
        in_specs=[block, block, block, whole(D, D), whole(16, D), across, down],
        out_specs=[block, block, block, whole(D, D), whole(8, D), across, down, whole(8, D)],
        out_shape=[
            jax.ShapeDtypeStruct((LIVE, D), BF),
            jax.ShapeDtypeStruct((LIVE, D), F32),
            jax.ShapeDtypeStruct((LIVE, D), BF),
            jax.ShapeDtypeStruct((D, D), BF),
            jax.ShapeDtypeStruct((8, D), F32),
            jax.ShapeDtypeStruct((D, width), BF),
            jax.ShapeDtypeStruct((width, D), BF),
            jax.ShapeDtypeStruct((8, D), F32),
        ],
        scratch_shapes=[
            pltpu.VMEM((ROWS, D), BF),
            pltpu.VMEM((D, ROWS), BF),
            pltpu.VMEM((ROWS, D), BF),
            pltpu.VMEM((LIVE, D), F32),
            pltpu.VMEM((ROWS, D), F32),
            pltpu.VMEM((ROWS, D), F32),
            pltpu.VMEM((ROWS, CHUNK), BF),
            pltpu.VMEM((ROWS, CHUNK), BF),
            pltpu.VMEM((ROWS, D), BF),
        ],
        compiler_params=pltpu.CompilerParams(vmem_limit_bytes=VMEM_ASK),
    )(tokens, mixed, top, w_out, vectors, w_up, w_down)


def three_parts(exact):
    high = exact.astype(BF)
    left = exact - high.astype(F32)
    middle = left.astype(BF)
    return high, middle, (left - middle.astype(F32)).astype(BF)


def attend_back_kernel(
    kind, q_ref, k_ref, v_ref, d_mixed, mixed, log_sum, go, gu, gd,
    out, out_o, out_u, out_d,
    mask_q, mask_k, keys, values, keys_turned, d_query, d_keys, d_values, send_sem, recv_sem, local_sem, *rest,
):
    pair, part = pl.program_id(0), pl.program_id(1)
    here = spot()
    o, u, d = [
        Scatter(
            whole, *rest[7 * at : 7 * at + 7], result, (send_sem, recv_sem, local_sem), 8 * at, here
        )
        for at, (whole, result) in enumerate(((go, out_o), (gu, out_u), (gd, out_d)))
    ]

    plan = {
        0: (lambda: greet(near(*here)), d.stage_a),
        3: (d.stage_b, u.stage_a),
        7: (d.stage_c, o.stage_a),
        13: (u.stage_b,),
        14: (d.stage_d,),
        17: (u.stage_c,),
        22: (d.stage_e,),
        23: (o.stage_b,),
        24: (u.stage_d,),
        25: (o.stage_c,),
        27: (o.stage_d,),
    }

    def transfers(tile):
        for slot, stages in plan.items():
            if slot % TILES == tile:

                @pl.when(pair == slot // TILES)
                def _():
                    for stage in stages:
                        stage()

    @pl.when((pair == 5) & (part == 2))
    def _():
        u.stage_e()
        o.stage_e()

    lane = lax.broadcasted_iota(jnp.int32, (TILE, 128), 1)
    sub = lax.broadcasted_iota(jnp.int32, (128, TILE), 0)

    def with_parts(exact, rest):
        a, b, c = three_parts(exact)
        return jnp.where(
            lane == SLOTS,
            a,
            jnp.where(lane == SLOTS + 1, b, jnp.where(lane == SLOTS + 2, c, rest)),
        )

    @pl.when(part == 0)
    def _():
        transfers(0)

        @pl.when(pair == 0)
        def _():
            mask_rows(kind[0], mask_q, mask_k)
            keys[:, 128:256] = mask_k[...]
            values[:, 128:256] = mask_k[...]

        keys[:, 0:128] = k_ref[0]
        values[:, 0:128] = v_ref[0]
        keys_turned[...] = keys[:, 0:128].T
        d_keys[...] = jnp.zeros_like(d_keys)
        d_values[...] = jnp.zeros_like(d_values)
        for tile in range(TILES):
            first = tile * TILE
            if tile:
                transfers(tile)
            both = q_ref[0, first : first + TILE, :] * BF(0.125)
            up = tile_rows(d_mixed, first)
            logs = log_sum[0, first : first + TILE, :]
            product = up.astype(F32) * tile_rows(mixed, first).astype(F32)
            marks = mask_q[first : first + TILE, :]
            turned = []
            for head in range(2):
                chosen = (lane < HEAD) == (head == 0)
                query = jnp.where(chosen, both, BF(0))
                upstream = jnp.where(chosen, up, BF(0))
                inside = jnp.sum(jnp.where(chosen, product, 0.0), axis=1, keepdims=True)
                wide_query = jnp.concatenate(
                    [query, with_parts(-logs[:, head * HEAD : head * HEAD + 1], marks)], axis=1
                )
                wide_up = jnp.concatenate(
                    [upstream, with_parts(-inside, jnp.zeros_like(marks))], axis=1
                )
                prob = jnp.exp(nt_dot(keys[...], wide_query))
                d_scores = (prob * nt_dot(values[...], wide_up)).astype(BF)
                d_values[...] += nn_dot(prob.astype(BF), upstream)
                d_keys[...] += nn_dot(d_scores, query)
                turned.append(nn_dot(keys_turned[...], d_scores))
            d_query[first : first + TILE, :] = (
                (jnp.where(sub < HEAD, *turned) * 0.125).T.astype(BF)
            )
        out[...] = d_query[0:LIVE, :]

    @pl.when(part == 1)
    def _():
        out[...] = d_keys[0:LIVE, :].astype(BF)

    @pl.when(part == 2)
    def _():
        out[...] = d_values[0:LIVE, :].astype(BF)


def attend_back(kind, qkv, d_mixed, mixed, log_sum, grads):
    def band(first):
        return pl.BlockSpec((LIVE, 128), lambda pair, part: (0, first + pair))

    def head(first):
        return pl.BlockSpec((1, ROWS, 128), lambda pair, part: (first + pair, 0, 0))

    shapes = [grad.shape[3:] for grad in grads]
    outs = [(rows, width // 2) for rows, width in shapes]
    return pl.pallas_call(
        attend_back_kernel,
        grid=(HEADS // 2, 3),
        in_specs=[
            pl.BlockSpec(memory_space=pltpu.SMEM),
            head(0), head(6), head(12), band(0), band(0), head(0),
        ]
        + [pl.BlockSpec(memory_space=pl.ANY)] * 3,
        out_specs=[pl.BlockSpec((LIVE, 128), lambda pair, part: (0, part * 6 + pair))]
        + [pl.BlockSpec(shape, lambda pair, part: (0, 0)) for shape in outs],
        out_shape=[
            jax.ShapeDtypeStruct((LIVE, 3 * D), BF),
            *[jax.ShapeDtypeStruct(shape, F32) for shape in outs],
        ],
        scratch_shapes=[
            pltpu.VMEM((ROWS, 128), BF),
            pltpu.VMEM((ROWS, 128), BF),
            pltpu.VMEM((ROWS, 256), BF),
            pltpu.VMEM((ROWS, 256), BF),
            pltpu.VMEM((128, ROWS), BF),
            pltpu.VMEM((ROWS, 128), BF),
            pltpu.VMEM((ROWS, 128), F32),
            pltpu.VMEM((ROWS, 128), F32),
            pltpu.SemaphoreType.DMA((24,)),
            pltpu.SemaphoreType.DMA((24,)),
            pltpu.SemaphoreType.DMA((3,)),
            *[entry for shape in shapes for entry in scatter_scratch(*shape)],
        ],
        compiler_params=pltpu.CompilerParams(
            collective_id=3, has_side_effects=True, vmem_limit_bytes=VMEM_ASK
        ),
    )(kind, qkv, qkv, qkv, d_mixed, mixed, log_sum, *grads)


def body_block(
    pixels,
    wave_table,
    band_count,
    wave_index,
    group_sensor,
    chip_kind,
    chip_gsd,
    time_loc,
    gen_in,
    gen_bias,
    gen_out,
    meta_weight,
    w_qkv,
    w_out,
    w_up,
    w_down,
    vectors,
    b_up,
    cotangent,
):
    group = lax.axis_index("dp")
    owner = group * 2 + lax.axis_index("fsdp")
    rows, up_rows = vectors.shape[0], b_up.shape[0]

    def steps(count, last):
        falling = 10000.0 ** -(np.arange(count) / last)
        return jnp.asarray(np.tile(np.concatenate([falling, falling]), (8, 1)), F32)

    gen_turned = gen_out.T
    (
        full_q, full_o, full_u, full_d, params, kernel, tokens_in, first, qkv, mixed, log_sum,
        gen_shift, hidden, slope, codes,
    ) = forward(
        (w_qkv, w_out, w_up, w_down),
        (
            pixels,
            vectors.T,
            b_up.reshape(1, -1),
            meta_weight,
            time_loc,
            gen_in,
            gen_bias.reshape(1, -1),
            gen_turned,
            steps(GEN // 2, GEN // 2),
            steps(D // 4, D // 4 - 1),
        ),
        (group_sensor, band_count, wave_index, wave_table, chip_kind, chip_gsd),
    )
    layer_out, d_after, d_mixed, w_out_grad, late, w_up_grad, w_down_grad, b_grad = feed(
        tokens_in,
        mixed,
        cotangent,
        full_o.reshape(D, D),
        params,
        full_u.reshape(D, -1),
        full_d.reshape(-1, D),
    )
    d_qkv, w_out_out, w_up_out, w_down_out = attend_back(
        chip_kind,
        qkv,
        d_mixed,
        mixed,
        log_sum,
        [
            grad.reshape(NZ, 2, 2, -1, grad.shape[1])
            for grad in (w_out_grad, w_up_grad, w_down_grad)
        ],
    )
    gen_out_wide, gen_small, w_qkv_out, summed, pixel_grad = closing(
        (
            d_qkv,
            first,
            full_q,
            tokens_in,
            d_after,
            params,
            pixels,
            kernel,
            time_loc,
            late,
            b_grad,
            hidden,
            gen_shift,
            slope,
            codes,
        ),
        (group_sensor, band_count),
    )
    width = gen_turned.shape[0]
    gen_out_grad = lax.dynamic_slice(
        gen_out_wide, ((owner * width) % 128, 0), (width, GEN)
    ).T
    vectors_out = lax.dynamic_slice(summed, (16, group * rows), (6, rows)).T
    b_up_out = lax.dynamic_slice(
        summed,
        (24 + group // (D // up_rows), (group % (D // up_rows)) * up_rows),
        (1, up_rows),
    ).reshape(-1)
    return (
        layer_out,
        pixel_grad,
        gen_small[:GEN],
        gen_small[GEN],
        gen_out_grad,
        summed[:9],
        w_qkv_out,
        w_out_out,
        w_up_out,
        w_down_out,
        vectors_out,
        b_up_out,
    )


def solution(mesh):
    fits = dict(mesh.shape) == {"dp": 16, "fsdp": 2}
    body = body_block if fits else body_general
    placed = (
        P(("dp", "fsdp"), None),
        P(),
        P(),
        P(),
        P(),
        P(("dp", "fsdp")),
        P(("dp", "fsdp"), None),
        P(("dp", "fsdp"), None, None),
        P(),
        P(),
        P(None, ("dp", "fsdp")),
        P(),
        P("dp", "fsdp"),
        P("dp", "fsdp"),
        P("dp", "fsdp"),
        P("dp", "fsdp"),
        P("dp", None),
        P("dp"),
        P(("dp", "fsdp"), None),
    )
    return jax.shard_map(
        body,
        mesh=mesh,
        in_specs=placed,
        out_specs=(
            P(("dp", "fsdp"), None),
            P(("dp", "fsdp"), None),
            P(),
            P(),
            P(None, ("dp", "fsdp")),
            P(),
            P("dp", "fsdp"),
            P("dp", "fsdp"),
            P("dp", "fsdp"),
            P("dp", "fsdp"),
            P("dp", None),
            P("dp"),
        ),
        check_vma=False,
    )
```

```python
import math

import jax
import jax.numpy as jnp
import numpy as np
from jax import lax
from jax.experimental import pallas as pl
from jax.experimental.pallas import tpu as pltpu
from jax.sharding import PartitionSpec as P

D = 768
HEADS = 12
HEAD = 64
GEN = 128
PIX = 64
MAXB = 10
SENSORS = 7
TOK_DEV = 1024
SLOTS = 4
GENOUT = 49920


def exact_dot(left, right):
    return jnp.dot(left, right, precision=lax.Precision.HIGHEST)


def inner_dot(left, right):
    return lax.dot_general(
        left, right, (((0,), (0,)), ((), ())), preferred_element_type=jnp.float32
    )


def outer_dot(left, right):
    return lax.dot_general(
        left, right, (((1,), (1,)), ((), ())), preferred_element_type=jnp.float32
    )


def gelu_exact(values):
    return jax.nn.gelu(values, approximate=False)


def gelu_slope(values, upstream):
    return jax.vjp(gelu_exact, values)[1](upstream)[0]


def table_lookup(indices, table):
    return jnp.sum(
        jnp.where(
            indices[:, None] == jnp.arange(table.shape[0], dtype=jnp.int32)[None, :],
            table[None, :],
            0.0,
        ),
        axis=1,
    )


def wave_code(wavelengths):
    half = GEN // 2
    omega = 1.0 / 10000.0 ** (jnp.arange(half, dtype=jnp.float32) / half)
    angle = (wavelengths * 1000.0)[:, None] * omega[None, :]
    return jnp.concatenate([jnp.sin(angle), jnp.cos(angle)], axis=1)


def place_code(kind_one, gsd_one):
    small = TOK_DEV // SLOTS
    index = jnp.arange(TOK_DEV, dtype=jnp.int32)
    within = jnp.where(kind_one == 1, index, index % small)
    side = jnp.where(kind_one == 1, math.isqrt(TOK_DEV), math.isqrt(small)).astype(jnp.int32)
    across = (within // side).astype(jnp.float32)
    along = (within % side).astype(jnp.float32)
    holder = jnp.where(kind_one == 1, 0, index // small)
    ground = (
        jnp.sum(
            jnp.where(
                holder[:, None] == jnp.arange(SLOTS, dtype=jnp.int32)[None, :], gsd_one[None, :], 0
            ),
            axis=1,
        ).astype(jnp.float32)
        / 10.0
    )
    quarter = D // 4
    omega = 1.0 / 10000.0 ** (jnp.arange(quarter, dtype=jnp.float32) / (quarter - 1))
    first = (across * ground)[:, None] * omega[None, :]
    second = (along * ground)[:, None] * omega[None, :]
    return jnp.concatenate(
        [jnp.sin(first), jnp.cos(first), jnp.sin(second), jnp.cos(second)], axis=1
    )


def segment_ids(kind_one):
    index = jnp.arange(TOK_DEV, dtype=jnp.int32)
    patches = jnp.where(kind_one == 1, 0, index // (TOK_DEV // SLOTS))
    extra = jnp.arange(2 * SLOTS, dtype=jnp.int32) // 2
    return jnp.concatenate([patches, extra])


def layer_norm(values, gain, shift):
    centred = values - jnp.mean(values, axis=-1, keepdims=True)
    scale = lax.rsqrt(jnp.mean(centred * centred, axis=-1, keepdims=True) + 1e-05)
    normed = centred * scale
    return (normed * gain + shift, normed, scale)


def norm_back(upstream, normed, scale, gain):
    gain_grad = jnp.sum(upstream * normed, axis=0)
    shift_grad = jnp.sum(upstream, axis=0)
    scaled = upstream * gain
    inside = (
        scaled
        - jnp.mean(scaled, axis=-1, keepdims=True)
        - normed * jnp.mean(scaled * normed, axis=-1, keepdims=True)
    )
    return (scale * inside, gain_grad, shift_grad)


def body_general(
    pixels,
    wave_table,
    band_count,
    wave_index,
    group_sensor,
    chip_kind,
    chip_gsd,
    time_loc,
    gen_in,
    gen_bias,
    gen_out,
    meta_weight,
    w_qkv,
    w_out,
    w_up,
    w_down,
    vectors,
    b_up,
    cotangent,
):
    half_type = jnp.bfloat16
    group = lax.axis_index("dp")
    sensor = jnp.sum(
        jnp.where(jnp.arange(group_sensor.shape[0], dtype=jnp.int32) == group, group_sensor, 0)
    )
    chosen_sensor = jnp.arange(SENSORS, dtype=jnp.int32) == sensor
    band_total = jnp.sum(jnp.where(chosen_sensor, band_count, 0))
    gen_in_full = gen_in.astype(jnp.float32)
    gen_bias_full = gen_bias.astype(jnp.float32)
    codes = wave_code(table_lookup(wave_index.reshape(-1), wave_table))
    before = exact_dot(codes, gen_in_full) + gen_bias_full
    hidden = gelu_exact(before).astype(half_type)
    shard_made = jnp.dot(hidden, gen_out, preferred_element_type=jnp.float32).astype(half_type)
    all_made = lax.all_gather(shard_made, ("dp", "fsdp"), axis=1, tiled=True)
    generated = lax.dynamic_slice_in_dim(all_made, sensor * MAXB, MAXB, 0)
    live_band = (jnp.arange(MAXB, dtype=jnp.int32) < band_total)[:, None]
    kernel = jnp.where(live_band, generated[:, : PIX * D], jnp.zeros((), half_type)).reshape(
        MAXB * PIX, D
    )
    band_float = band_total.astype(jnp.float32)
    embed_bias = (
        jnp.sum(jnp.where(live_band, generated[:, PIX * D :].astype(jnp.float32), 0.0), axis=0)
        / band_float
    )
    kind_one = chip_kind[0]
    patches = (
        jnp.dot(pixels, kernel, preferred_element_type=jnp.float32)
        + embed_bias
        + place_code(kind_one, chip_gsd[0])
    )
    meta_full = meta_weight.astype(jnp.float32)
    stamps = exact_dot(time_loc[0], meta_full[1:])
    classes = jnp.broadcast_to(meta_full[0], stamps.shape)
    extra = jnp.stack([classes, stamps], axis=1).reshape(2 * SLOTS, D)
    tokens_in = jnp.concatenate([patches, extra], axis=0)
    total_rows = tokens_in.shape[0]
    qkv_rows, out_rows, up_rows, down_rows, vectors_all, b_up_all = (
        lax.all_gather(w_qkv, "dp", axis=0, tiled=True),
        lax.all_gather(w_out, "dp", axis=0, tiled=True),
        lax.all_gather(w_up, "dp", axis=0, tiled=True),
        lax.all_gather(w_down, "dp", axis=0, tiled=True),
        lax.all_gather(vectors, "dp", axis=0, tiled=True),
        lax.all_gather(b_up, "dp", axis=0, tiled=True),
    )
    w_qkv_all, w_out_all, w_up_all, w_down_all = (
        lax.all_gather(qkv_rows, "fsdp", axis=1, tiled=True),
        lax.all_gather(out_rows, "fsdp", axis=1, tiled=True),
        lax.all_gather(up_rows, "fsdp", axis=1, tiled=True),
        lax.all_gather(down_rows, "fsdp", axis=1, tiled=True),
    )
    vector_full = vectors_all.astype(jnp.float32)
    b_up_full = b_up_all.astype(jnp.float32)
    first_norm, normed_one, scale_one = layer_norm(tokens_in, vector_full[:, 0], vector_full[:, 1])
    first = first_norm.astype(half_type)
    qkv = jnp.dot(first, w_qkv_all, preferred_element_type=jnp.float32).astype(half_type)
    query = qkv[:, :D].reshape(total_rows, HEADS, HEAD)
    keys = qkv[:, D : 2 * D].reshape(total_rows, HEADS, HEAD)
    values = qkv[:, 2 * D :].reshape(total_rows, HEADS, HEAD)
    segment = segment_ids(kind_one)
    same = (segment[:, None] == segment[None, :])[None]
    scores = jnp.einsum("qhd,khd->hqk", query, keys, preferred_element_type=jnp.float32) * HEAD ** (
        -0.5
    )
    scores = jnp.where(same, scores, -1e30)
    peak = jnp.max(scores, axis=-1, keepdims=True)
    expo = jnp.exp(scores - peak)
    totals = jnp.sum(expo, axis=-1, keepdims=True)
    prob_half = (expo / totals).astype(half_type)
    mixed = (
        jnp.einsum("hqk,khd->qhd", prob_half, values, preferred_element_type=jnp.float32)
        .reshape(total_rows, D)
        .astype(half_type)
    )
    after = tokens_in + (
        jnp.dot(mixed, w_out_all, preferred_element_type=jnp.float32) + vector_full[:, 2]
    )
    second_norm, normed_two, scale_two = layer_norm(after, vector_full[:, 3], vector_full[:, 4])
    second = second_norm.astype(half_type)
    upper = jnp.dot(second, w_up_all, preferred_element_type=jnp.float32) + b_up_full
    active = gelu_exact(upper).astype(half_type)
    layer_out = (
        after + jnp.dot(active, w_down_all, preferred_element_type=jnp.float32) + vector_full[:, 5]
    ).astype(half_type)
    grad_top = cotangent.astype(jnp.float32)
    w_down_grad = inner_dot(active, cotangent)
    down_bias_grad = jnp.sum(grad_top, axis=0)
    d_active = outer_dot(cotangent, w_down_all)
    d_upper = gelu_slope(upper, d_active).astype(half_type)
    w_up_grad = inner_dot(second, d_upper)
    b_up_grad = jnp.sum(d_upper.astype(jnp.float32), axis=0)
    d_second = outer_dot(d_upper, w_up_all)
    d_after_norm, gain_two_grad, shift_two_grad = norm_back(
        d_second, normed_two, scale_two, vector_full[:, 3]
    )
    d_after = grad_top + d_after_norm
    d_proj = d_after.astype(half_type)
    w_out_grad = inner_dot(mixed, d_proj)
    out_bias_grad = jnp.sum(d_proj.astype(jnp.float32), axis=0)
    d_mixed = outer_dot(d_proj, w_out_all).astype(half_type).reshape(total_rows, HEADS, HEAD)
    again = jnp.einsum("qhd,khd->hqk", query, keys, preferred_element_type=jnp.float32) * HEAD ** (
        -0.5
    )
    again = jnp.where(same, again, -1e30)
    prob_full = jnp.exp(again - peak) / totals
    recalled = prob_full.astype(half_type)
    d_values = jnp.einsum("hqk,qhd->khd", recalled, d_mixed, preferred_element_type=jnp.float32)
    d_prob = jnp.einsum("qhd,khd->hqk", d_mixed, values, preferred_element_type=jnp.float32)
    d_scores = prob_full * (d_prob - jnp.sum(d_prob * prob_full, axis=-1, keepdims=True))
    d_scores = jnp.where(same, d_scores, 0.0).astype(half_type)
    d_query = jnp.einsum(
        "hqk,khd->qhd", d_scores, keys, preferred_element_type=jnp.float32
    ) * HEAD ** (-0.5)
    d_keys = jnp.einsum(
        "hqk,qhd->khd", d_scores, query, preferred_element_type=jnp.float32
    ) * HEAD ** (-0.5)
    d_qkv = jnp.concatenate(
        [
            d_query.reshape(total_rows, D),
            d_keys.reshape(total_rows, D),
            d_values.reshape(total_rows, D),
        ],
        axis=1,
    ).astype(half_type)
    w_qkv_grad = inner_dot(first, d_qkv)
    d_first = outer_dot(d_qkv, w_qkv_all)
    d_tokens_norm, gain_one_grad, shift_one_grad = norm_back(
        d_first, normed_one, scale_one, vector_full[:, 0]
    )
    d_tokens = (d_after + d_tokens_norm).astype(half_type)
    vectors_grad = jnp.stack(
        [
            gain_one_grad,
            shift_one_grad,
            out_bias_grad,
            gain_two_grad,
            shift_two_grad,
            down_bias_grad,
        ],
        axis=1,
    )
    d_patches = d_tokens[:TOK_DEV]
    d_extra = d_tokens[TOK_DEV:].astype(jnp.float32).reshape(SLOTS, 2, D)
    pixel_grad = outer_dot(d_patches, kernel)
    class_grad = jnp.sum(d_extra[:, 0], axis=0)
    stamp_grad = exact_dot(time_loc[0].T, d_extra[:, 1])
    meta_part = jnp.concatenate([class_grad[None, :], stamp_grad], axis=0)
    d_kernel = inner_dot(pixels, d_patches).reshape(MAXB, PIX * D)
    d_kernel = jnp.where(live_band, d_kernel, 0.0)
    d_bias = jnp.sum(d_patches.astype(jnp.float32), axis=0) / band_float
    d_bias_rows = jnp.where(live_band, d_bias[None, :], 0.0)
    d_generated = jnp.concatenate([d_kernel, d_bias_rows], axis=1).astype(half_type)
    placed = jnp.where(
        chosen_sensor[:, None, None], d_generated.astype(jnp.float32)[None], 0.0
    ).reshape(SENSORS * MAXB, GENOUT)
    columns = lax.psum_scatter(placed, ("dp", "fsdp"), scatter_dimension=1, tiled=True)
    gen_out_grad = exact_dot(hidden.astype(jnp.float32).T, columns)
    d_hidden = exact_dot(columns, gen_out.astype(jnp.float32).T)
    d_before = gelu_slope(before, d_hidden)
    gen_in_part = exact_dot(codes.T, d_before)
    gen_bias_part = jnp.sum(d_before, axis=0)
    meta_grad, gen_in_grad, gen_bias_grad = lax.psum(
        (meta_part, gen_in_part, gen_bias_part), ("dp", "fsdp")
    )
    qkv_cols, out_cols, up_cols, down_cols = (
        lax.psum_scatter(
            w_qkv_grad.astype(jnp.bfloat16), "fsdp", scatter_dimension=1, tiled=True
        ).astype(jnp.float32),
        lax.psum_scatter(
            w_out_grad.astype(jnp.bfloat16), "fsdp", scatter_dimension=1, tiled=True
        ).astype(jnp.float32),
        lax.psum_scatter(
            w_up_grad.astype(jnp.bfloat16), "fsdp", scatter_dimension=1, tiled=True
        ).astype(jnp.float32),
        lax.psum_scatter(
            w_down_grad.astype(jnp.bfloat16), "fsdp", scatter_dimension=1, tiled=True
        ).astype(jnp.float32),
    )
    vectors_group, b_up_group = lax.psum((vectors_grad, b_up_grad), "fsdp")
    w_qkv_out, w_out_out, w_up_out, w_down_out, vectors_out, b_up_out = (
        lax.psum_scatter(
            qkv_cols.astype(jnp.bfloat16), "dp", scatter_dimension=0, tiled=True
        ).astype(jnp.float32),
        lax.psum_scatter(
            out_cols.astype(jnp.bfloat16), "dp", scatter_dimension=0, tiled=True
        ).astype(jnp.float32),
        lax.psum_scatter(
            up_cols.astype(jnp.bfloat16), "dp", scatter_dimension=0, tiled=True
        ).astype(jnp.float32),
        lax.psum_scatter(
            down_cols.astype(jnp.bfloat16), "dp", scatter_dimension=0, tiled=True
        ).astype(jnp.float32),
        lax.psum_scatter(
            vectors_group.astype(jnp.bfloat16), "dp", scatter_dimension=0, tiled=True
        ).astype(jnp.float32),
        lax.psum_scatter(
            b_up_group.astype(jnp.bfloat16), "dp", scatter_dimension=0, tiled=True
        ).astype(jnp.float32),
    )
    return (
        layer_out,
        pixel_grad,
        gen_in_grad,
        gen_bias_grad,
        gen_out_grad,
        meta_grad,
        w_qkv_out,
        w_out_out,
        w_up_out,
        w_down_out,
        vectors_out,
        b_up_out,
    )


LIVE = 1032
ROWS = 1040
TILE = 208
TILES = 5
NZ = 4
GROUPS = 16
PIECE = 144
COVER = 14
VMEM_ASK = 60 * 1024 * 1024
BF = jnp.bfloat16
F32 = jnp.float32


def nt_dot(left, right):
    return lax.dot_general(left, right, (((1,), (1,)), ((), ())), preferred_element_type=F32)


def nn_dot(left, right):
    return lax.dot_general(left, right, (((1,), (0,)), ((), ())), preferred_element_type=F32)


def spot():
    group = lax.axis_index("dp")
    return group // 4, (group // 2) % 2, group % 2, lax.axis_index("fsdp")


def device(z, y, c, x):
    return {"dp": z * 4 + y * 2 + c, "fsdp": x}


def remote(source, target, sems, slot, where):
    return pltpu.make_async_remote_copy(
        src_ref=source,
        dst_ref=target,
        send_sem=sems[0].at[slot],
        recv_sem=sems[1].at[slot],
        device_id=where,
        device_id_type=pl.DeviceIdType.MESH,
    )


def greet(others):
    barrier = pltpu.get_barrier_semaphore()
    for where in others:
        pl.semaphore_signal(
            barrier, inc=1, device_id=where, device_id_type=pl.DeviceIdType.MESH
        )
    pl.semaphore_wait(barrier, len(others))


def columns(ref, x):
    width = ref.shape[-1] // 2
    return pl.ds(pl.multiple_of(x * width, 128), width)


def group_peers(z, y, c, x):
    return [
        ((dz, dy, dc), device((z + dz) % NZ, (y + dy) % 2, (c + dc) % 2, x))
        for dz in range(NZ)
        for dy in range(2)
        for dc in range(2)
        if dz + dy + dc
    ]


CHUNK = 768
BANDS = ((0, 256), (256, 256), (512, 256), (768, 256), (1024, 8))


def gelu_parts(values):
    bell = jnp.exp(values * values * (-0.5))
    step = 1.0 / (1.0 + (0.3275911 * math.sqrt(0.5)) * jnp.abs(values))
    poly = 0.5 * 1.061405429 * step - 0.5 * 1.453152027
    poly = poly * step + 0.5 * 1.421413741
    poly = poly * step - 0.5 * 0.284496736
    poly = poly * step + 0.5 * 0.254829592
    tail = poly * step * bell
    below = jnp.where(values < 0.0, tail, 1.0 - tail)
    return values * below, below + values * bell * (1.0 / math.sqrt(2.0 * math.pi))


def standard(values):
    centred = values - jnp.mean(values, axis=-1, keepdims=True)
    scale = lax.rsqrt(jnp.mean(centred * centred, axis=-1, keepdims=True) + 1e-05)
    return centred * scale, scale


def column_sum(values):
    return jnp.sum(values, axis=0, keepdims=True)


def put_rows(target, first, count, values):
    if count % 16:
        values = jnp.concatenate(
            [values, jnp.zeros((16 - count % 16, values.shape[1]), values.dtype)], axis=0
        )
    target[first : first + values.shape[0], :] = values


class Gather:
    COPIES = 19

    def __init__(self, shard, whole, sems, local, first, lean, here):
        z, y, c, x = here
        self.lean = lean
        mine, other = columns(whole, x), columns(whole, 1 - x)
        across, beside, twin = device(z, y, c, 1 - x), device(z, 1 - y, c, x), device(z, y, 1 - c, x)
        target = whole.at[z, y, c, :, mine]
        self.local = pltpu.make_async_copy(shard, target, local)
        self.along = [
            remote(shard, target, sems, first + k - 1, device((z + k) % NZ, y, c, x))
            for k in range(1, NZ)
        ]
        self.to_x, self.to_y, self.far = [], [], []
        for k in range(NZ):
            at = (z + NZ - k) % NZ
            place = whole.at[at, y, c, :, mine]
            source = place if k else shard
            self.to_x.append(remote(source, place, sems, first + 3 + k, across))
            self.to_y.append(remote(source, place, sems, first + 7 + k, beside))
            if k < lean:
                place = whole.at[at, y, c, :, other]
                self.far.append(remote(place, place, sems, first + 11 + k, beside))
            else:
                place = whole.at[at, 1 - y, c, :, mine]
                self.far.append(remote(place, place, sems, first + 11 + k, across))
        self.core = []
        for step, part in enumerate(
            (
                whole.at[:, y, c, :, mine],
                whole.at[:, y, c, :, other],
                whole.at[:, 1 - y, c, :, mine],
                whole.at[:, 1 - y, c, :, other],
            )
        ):
            self.core.append(remote(part, part, sems, first + 15 + step, twin))

    def send_z(self):
        self.local.start()
        for copy in self.along:
            copy.start()

    def send_own(self):
        self.to_x[0].start()
        self.to_y[0].start()

    def pass_on(self):
        for k in range(1, NZ):
            self.along[k - 1].wait_recv()
            self.to_x[k].start()
            self.to_y[k].start()
        self.local.wait()
        self.core[0].start()

    def turn_corner(self):
        for k in range(NZ):
            (self.to_x if k < self.lean else self.to_y)[k].wait_recv()
            self.far[k].start()
        for k in range(self.lean, NZ):
            self.to_x[k].wait_recv()
        self.core[1].start()
        for k in range(self.lean):
            self.to_y[k].wait_recv()
        self.core[2].start()

    def share(self):
        for copy in self.far:
            copy.wait_recv()
        self.core[3].start()

    def receive(self):
        for copy in self.core:
            copy.wait_recv()

    def finish(self):
        for copy in (*self.along, *self.to_x, *self.to_y, *self.far, *self.core):
            copy.wait_send()


def make_small(vectors, b_up, held, small):
    group = lax.axis_index("dp")
    count, up_count = vectors.shape[1], b_up.shape[1]
    per_row = D // up_count
    held[...] = jnp.zeros_like(held)
    held[0:6, 0:count] = vectors[...].astype(F32)
    held[8:9, 0:up_count] = b_up[...].astype(F32)
    rows = pltpu.roll(held[0:8, :], group * count, 1)
    bias = pltpu.roll(held[8:16, :], (group % per_row) * up_count, 1)[0:1]
    row = lax.broadcasted_iota(jnp.int32, (8, D), 0)
    spot_at = 6 + group // per_row
    top = jnp.where(row < 6, rows, jnp.where(row == spot_at, bias, 0.0))
    small[...] = jnp.concatenate(
        [top, jnp.where(row + 8 == spot_at, bias, 0.0)], axis=0
    ).astype(BF)


def make_table(kind, ground, steps, table):
    wide = steps.shape[1]
    entry = lax.broadcasted_iota(jnp.int32, (64, wide), 0)
    lane = lax.broadcasted_iota(jnp.int32, (64, wide), 1)
    single = kind == 1
    chip = jnp.where(single, 0, entry // 16)
    step = jnp.where(single, entry, entry % 16).astype(F32)
    distance = jnp.zeros((64, wide), F32)
    for slot in range(SLOTS):
        distance = jnp.where(chip == slot, ground[0, slot].astype(F32), distance)
    angle = (step * (distance / 10.0)) * steps[0:1, :]
    exact = jnp.where(lane < wide // 2, jnp.sin(angle), jnp.cos(angle))
    for at, part in enumerate(three_parts(exact)):
        table[at * 64 : (at + 1) * 64, :] = part
    table[192:256, :] = jnp.zeros((64, wide), BF)


def make_pieces(
    groups, bands, waves, wave_table, steps, gen_in, gen_bias, gen_out,
    gen_shift, hidden, slope, codes, made, code_rows, rows, wide, angles,
):
    for wave in range(angles.shape[0]):
        angles[wave : wave + 1, :] = (wave_table[wave] * 1000.0) * steps[0:1, :]
    lane = lax.broadcasted_iota(jnp.int32, angles.shape, 1)
    angle = angles[...]
    angles[...] = jnp.where(lane < GEN // 2, jnp.sin(angle), jnp.cos(angle))
    for sensor in range(SENSORS):
        for band in range(MAXB):
            code_rows[sensor, band : band + 1, :] = angles[pl.ds(waves[sensor, band], 1), :]
        code_rows[sensor, MAXB:16, :] = jnp.zeros((16 - MAXB, GEN), F32)
    flat = code_rows[:, 0:16, :].reshape(SENSORS * 16, GEN)
    before = exact_dot(flat, gen_in[...].astype(F32)) + gen_bias[...].astype(F32)
    values, slopes = gelu_parts(before)
    band_at = lax.broadcasted_iota(jnp.int32, (16, GEN), 0)
    width = gen_out.shape[0]
    owner = lax.axis_index("dp") * 2 + lax.axis_index("fsdp")
    wide[...] = jnp.zeros_like(wide)
    wide[pl.ds(pl.multiple_of((owner * width) % 128, 8), width), :] = gen_out[...].astype(F32)
    gen_shift[...] = wide[...].astype(BF)
    kept = []
    for sensor in range(SENSORS):
        part = slice(sensor * 16, sensor * 16 + 16)
        live = band_at < bands[sensor]
        kept.append(jnp.where(live, values[part], 0.0))
        code_rows[sensor, 16:32, :] = kept[-1].astype(BF).astype(F32)
        code_rows[sensor, 32:48, :] = jnp.where(live, slopes[part], 0.0)
    lower = jnp.concatenate(kept, axis=0).astype(BF)
    for at in range(COVER):
        product = nt_dot(lower, gen_shift[at * 128 : (at + 1) * 128, :])
        for sensor in range(SENSORS):
            rows[sensor, at * MAXB : (at + 1) * MAXB, :] = product[
                sensor * 16 : sensor * 16 + MAXB
            ]
    rows[:, COVER * MAXB :, :] = jnp.zeros((SENSORS, PIECE - COVER * MAXB, 128), F32)
    for group in range(GROUPS):
        made[group // 4, (group // 2) % 2, group % 2] = rows[groups[group]].astype(BF)
    for group in range(GROUPS):
        own = code_rows[groups[group]]
        first = group * MAXB
        codes[first : first + MAXB, :] = own[0:MAXB]
        hidden[first : first + MAXB, :] = own[16 : 16 + MAXB]
        slope[first : first + MAXB, :] = own[32 : 32 + MAXB]


def mask_rows(kind, for_query, for_key):
    row = lax.broadcasted_iota(jnp.int32, (ROWS, 128), 0)
    lane = lax.broadcasted_iota(jnp.int32, (ROWS, 128), 1)
    patch = jnp.where(kind == 1, 0, row // (TOK_DEV // SLOTS))
    segment = jnp.where(row < TOK_DEV, patch, (row - TOK_DEV) // 2)
    hot = (lane == segment) & (row < LIVE)
    for_query[...] = jnp.where(hot, 1.0, 0.0).astype(BF)
    for_key[...] = jnp.where(
        lane < SLOTS, jnp.where(hot, 0.0, -1e30), jnp.where(lane < SLOTS + 3, 1.0, 0.0)
    ).astype(BF)


def attend_pair(pair, qkv, mask_q, mask_k, keys, values, mixed, log_sum):
    lane = lax.broadcasted_iota(jnp.int32, (TILE, 128), 1)
    lanes = pl.ds(pl.multiple_of(pair * 128, 128), 128)
    keys[:, 0:128] = qkv[6 + pair]
    keys[:, 128:256] = mask_k[...]
    values[:, 0:128] = qkv[12 + pair]
    for tile in range(TILES):
        first = tile * TILE
        both = qkv[pair, first : first + TILE, :] * BF(0.125)
        results, sums = [], []
        for head in range(2):
            query = jnp.where((lane < HEAD) == (head == 0), both, BF(0))
            scores = nt_dot(
                jnp.concatenate([query, mask_q[first : first + TILE, :]], axis=1), keys[...]
            )
            peak = jnp.max(scores, axis=1, keepdims=True)
            expo = jnp.exp(scores - peak).astype(BF)
            made = nn_dot(expo, values[...])
            totals = made[:, 128:256]
            results.append(made[:, 0:128] / totals)
            sums.append(peak + jnp.log(totals))
        count = min(TILE, LIVE - first)
        mixed[first : first + count, lanes] = jnp.where(lane < HEAD, *results)[:count].astype(BF)
        log_sum[pair, first : first + TILE, :] = jnp.where(lane < HEAD, *sums)


def forward_kernel(
    wq, wo, wu, wd, pixels, vectors, b_up, meta_weight, time_loc, gen_in, gen_bias, gen_out,
    wave_steps, place_steps,
    groups, bands, waves, wave_table, kind, ground,
    full_q, full_o, full_u, full_d, params, kernel, tokens, first, qkv, mixed, log_sum,
    gen_shift, hidden, slope, codes,
    made, code_rows, rows, roll, angles, small_held, small, table,
    taken, full_small, flat, wide, keys, values, mask_q, mask_k,
    w_send, w_recv, local_sem, s_send, s_recv, g_send, g_recv,
):
    here = z, y, c, x = spot()
    peers = group_peers(z, y, c, x)
    across = device(z, y, c, 1 - x)
    greet([where for _, where in peers] + [across])
    half = wd.shape[0] // 2
    gathers = q, o, u, d, e = [
        Gather(shard, whole, (w_send, w_recv), local_sem.at[step], Gather.COPIES * step, lean, here)
        for step, (shard, whole, lean) in enumerate(
            (
                (wq, full_q, 4),
                (wo, full_o, 2),
                (wu, full_u, 2),
                (wd.at[0:half], full_d.at[:, :, :, 0:half], 2),
                (wd.at[half : 2 * half], full_d.at[:, :, :, half : 2 * half], 2),
            )
        )
    ]
    s_sems = (s_send, s_recv)
    g_sems = (g_send, g_recv)
    q.send_z()
    for gather in gathers:
        gather.send_own()
    make_pieces(
        groups, bands, waves, wave_table, wave_steps, gen_in, gen_bias, gen_out,
        gen_shift, hidden, slope, codes, made, code_rows, rows, roll, angles,
    )
    make_small(vectors, b_up, small_held, small)
    mask_rows(kind[0], mask_q, mask_k)
    make_table(kind[0], ground, place_steps, table)
    values[:, 128:256] = jnp.ones((ROWS, 128), BF)
    q.pass_on()
    own_made = pltpu.make_async_copy(
        made.at[z, y, c], taken.at[z, y, c, x], local_sem.at[5]
    )
    own_made.start()
    sends = {}
    for (dz, dy, dc), where in peers:
        copy = remote(
            made.at[(z + dz) % NZ, (y + dy) % 2, (c + dc) % 2],
            taken.at[z, y, c, x],
            g_sems,
            dz * 4 + dy * 2 + dc,
            where,
        )
        copy.start()
        sends[dz, dy, dc] = copy
    own_small = pltpu.make_async_copy(small, full_small.at[z, y, c], local_sem.at[6])
    own_small.start()
    small_z = [
        remote(small, full_small.at[z, y, c], s_sems, k - 1, device((z + k) % NZ, y, c, x))
        for k in range(1, NZ)
    ]
    for copy in small_z:
        copy.start()
    q.turn_corner()
    own_made.wait()
    swaps = []
    for dz in range(NZ):
        for dy in range(2):
            for dc in range(2):
                if dz + dy + dc:
                    sends[dz, dy, dc].wait_recv()
        part = taken.at[(z + NZ - dz) % NZ, :, :, x]
        swap = remote(part, part, g_sems, 16 + dz, across)
        swap.start()
        swaps.append(swap)
    u.send_z()
    own_small.wait()
    for copy in small_z:
        copy.wait_recv()
    part = full_small.at[:, y, c]
    small_y = remote(part, part, s_sems, 3, device(z, 1 - y, c, x))
    small_y.start()
    q.share()
    for swap in swaps:
        swap.wait_recv()
    small_y.wait_recv()
    part = full_small.at[:, :, c]
    small_c = remote(part, part, s_sems, 4, device(z, y, 1 - c, x))
    small_c.start()
    u.pass_on()
    d.send_z()
    e.send_z()
    unpack(taken, flat, wide, kernel)
    bias = jnp.concatenate(
        [
            column_sum(flat[(PIX * 6 + part) * MAXB : (PIX * 6 + part + 1) * MAXB, :])
            for part in range(6)
        ],
        axis=1,
    ) / bands[groups[lax.axis_index("dp")]].astype(F32)
    single = kind[0] == 1
    for start, count in BANDS[:-1]:
        band = slice(start, start + count)
        made_rows = nn_dot(pixels[band, :], kernel[...])
        index = start + lax.broadcasted_iota(jnp.int32, (count, 256), 0)
        lane = lax.broadcasted_iota(jnp.int32, (count, 256), 1)
        spread = []
        for spots in (
            jnp.where(single, index // 32, index // 16),
            jnp.where(single, index % 32, index // 256 * 16 + index % 16),
        ):
            hot = (lane % 64 == spots) & (lane < 192)
            spread.append(nn_dot(jnp.where(hot, 1.0, 0.0).astype(BF), table[...]))
        tokens[band, :] = made_rows + bias + jnp.concatenate(spread, axis=1)
    small_c.wait_recv()
    params[...] = jnp.zeros_like(params)
    for n in range(GROUPS):
        params[...] += full_small[n // 4, (n // 2) % 2, n % 2].astype(F32)
    meta = meta_weight[...].astype(F32)
    stamps = exact_dot(time_loc[0], meta[1:])
    for slot in range(SLOTS):
        at = TOK_DEV + 2 * slot
        tokens[at : at + 1, :] = meta[0:1]
        tokens[at + 1 : at + 2, :] = stamps[slot : slot + 1]
    for start, count in BANDS:
        band = slice(start, start + count)
        normed, _ = standard(tokens[band, :])
        first[band, :] = (normed * params[0:1, :] + params[1:2, :]).astype(BF)
    q.receive()
    for start, count in BANDS:
        band = slice(start, start + count)
        for third in range(3):
            part = slice(third * D, (third + 1) * D)
            made_rows = nn_dot(
                first[band, :], full_q[:, :, :, :, part].reshape(D, D)
            ).astype(BF)
            for block in range(6):
                put_rows(
                    qkv.at[third * 6 + block],
                    start,
                    count,
                    made_rows[:, block * 128 : (block + 1) * 128],
                )

    def one_pair(pair, carry):
        @pl.when(pair == 0)
        def _():
            u.turn_corner()

        @pl.when(pair == 1)
        def _():
            d.pass_on()
            e.pass_on()
            o.send_z()

        @pl.when(pair == 2)
        def _():
            u.share()
            o.pass_on()

        @pl.when(pair == 3)
        def _():
            d.turn_corner()
            e.turn_corner()

        @pl.when(pair == 4)
        def _():
            o.turn_corner()
            d.share()

        @pl.when(pair == 5)
        def _():
            e.share()
            o.share()

        attend_pair(pair, qkv, mask_q, mask_k, keys, values, mixed, log_sum)
        return carry

    lax.fori_loop(0, HEADS // 2, one_pair, 0)
    for gather in (o, u, d, e):
        gather.receive()
    for gather in gathers:
        gather.finish()
    for copy in (*small_z, small_y, small_c, *sends.values(), *swaps):
        copy.wait_send()


def forward(shards, operands, scalars):
    anywhere = pl.BlockSpec(memory_space=pl.ANY)
    vmem = pl.BlockSpec(memory_space=pltpu.VMEM)
    smem = pl.BlockSpec(memory_space=pltpu.SMEM)
    blocks = GROUPS * MAXB
    outs = [
        jax.ShapeDtypeStruct((NZ, 2, 2, shard.shape[0], 2 * shard.shape[1]), BF) for shard in shards
    ]
    outs += [
        jax.ShapeDtypeStruct((16, D), F32),
        jax.ShapeDtypeStruct((MAXB * PIX, D), BF),
        jax.ShapeDtypeStruct((LIVE, D), F32),
        jax.ShapeDtypeStruct((LIVE, D), BF),
        jax.ShapeDtypeStruct((18, ROWS, 128), BF),
        jax.ShapeDtypeStruct((LIVE, D), BF),
        jax.ShapeDtypeStruct((HEADS // 2, ROWS, 128), F32),
        jax.ShapeDtypeStruct((COVER * 128, GEN), BF),
        jax.ShapeDtypeStruct((blocks, GEN), F32),
        jax.ShapeDtypeStruct((blocks, GEN), F32),
        jax.ShapeDtypeStruct((blocks, GEN), F32),
    ]
    return pl.pallas_call(
        forward_kernel,
        out_shape=outs,
        in_specs=[anywhere] * 4 + [vmem] * len(operands) + [smem] * len(scalars),
        out_specs=[vmem] + [anywhere] * 3 + [vmem] * 11,
        scratch_shapes=[
            pltpu.VMEM((NZ, 2, 2, PIECE, 128), BF),
            pltpu.VMEM((SENSORS, 48, GEN), F32),
            pltpu.VMEM((SENSORS, PIECE, 128), F32),
            pltpu.VMEM((COVER * 128, GEN), F32),
            pltpu.VMEM((scalars[3].shape[0], GEN), F32),
            pltpu.VMEM((16, D), F32),
            pltpu.VMEM((16, D), BF),
            pltpu.VMEM((256, D // 2), BF),
            pltpu.VMEM((NZ, 2, 2, 2, PIECE, 128), BF),
            pltpu.VMEM((NZ, 2, 2, 16, D), BF),
            pltpu.VMEM((FLAT, 128), F32),
            pltpu.VMEM((6, MAXB * PIX, 128), F32),
            pltpu.VMEM((ROWS, 256), BF),
            pltpu.VMEM((ROWS, 256), BF),
            pltpu.VMEM((ROWS, 128), BF),
            pltpu.VMEM((ROWS, 128), BF),
        ]
        + [pltpu.SemaphoreType.DMA((count,)) for count in (95, 95, 7, 5, 5, 20, 20)],
        compiler_params=pltpu.CompilerParams(
            collective_id=0, has_side_effects=True, vmem_limit_bytes=VMEM_ASK
        ),
    )(*shards, *operands, *scalars)


class Scatter:
    def __init__(self, whole, own, came, low, high, side_x, side_y, last, out, sems, first, here):
        z, y, c, x = here
        self.here, self.own, self.came, self.out = here, own, came, out
        self.low, self.high, self.side_x, self.side_y, self.last = low, high, side_x, side_y, last
        self.mine, self.other = columns(own, x), columns(own, 1 - x)
        mine, other = self.mine, self.other
        across, beside, twin = device(z, y, c, 1 - x), device(z, 1 - y, c, x), device(z, y, 1 - c, x)
        self.local = pltpu.make_async_copy(whole.at[:, :, c], own, sems[2].at[first // 8])
        self.core = remote(whole.at[:, :, 1 - c], came, sems, first, twin)
        self.far_y = remote(own.at[0:2, 1 - y, :, other], low, sems, first + 1, beside)
        self.far_x = remote(own.at[2:4, 1 - y, :, other], high, sems, first + 2, across)
        self.to_x = remote(own.at[:, y, :, other], side_x, sems, first + 3, across)
        self.to_y = remote(own.at[:, 1 - y, :, mine], side_y, sems, first + 4, beside)
        self.along = [
            remote(
                own.at[(z + k) % NZ, y, :, mine], last.at[k - 1], sems, first + 4 + k,
                device((z + k) % NZ, y, c, x),
            )
            for k in range(1, NZ)
        ]

    def stage_a(self):
        self.local.start()
        self.core.start()

    def stage_b(self):
        self.local.wait()
        self.core.wait_recv()
        for at_z in range(NZ):
            for at_y in range(2):
                self.own[at_z, at_y] = self.own[at_z, at_y] + self.came[at_z, at_y]
        self.far_y.start()
        self.far_x.start()

    def stage_c(self):
        _, y, _, _ = self.here
        self.far_y.wait_recv()
        for k in range(2):
            self.own[k, y, :, self.other] = self.own[k, y, :, self.other] + self.low[k]
        self.to_x.start()
        self.far_x.wait_recv()
        for k in range(2):
            self.own[2 + k, 1 - y, :, self.mine] = (
                self.own[2 + k, 1 - y, :, self.mine] + self.high[k]
            )
        self.to_y.start()

    def stage_d(self):
        _, y, _, _ = self.here
        self.to_x.wait_recv()
        self.to_y.wait_recv()
        for k in range(NZ):
            self.own[k, y, :, self.mine] = (
                self.own[k, y, :, self.mine].astype(F32)
                + self.side_x[k].astype(F32)
                + self.side_y[k].astype(F32)
            ).astype(BF)
        for copy in self.along:
            copy.start()

    def stage_e(self):
        z, y, _, _ = self.here
        for copy in self.along:
            copy.wait_recv()
        self.out[...] = (
            self.own[z, y, :, self.mine].astype(F32)
            + self.last[0].astype(F32)
            + self.last[1].astype(F32)
            + self.last[2].astype(F32)
        )
        for copy in (self.core, self.far_y, self.far_x, self.to_x, self.to_y, *self.along):
            copy.wait_send()


class Total:
    COPIES = 7

    def __init__(self, source, out, held, came, slots, send_sem, recv_sem, here):
        z, y, c, x = here
        sems = (send_sem, recv_sem)
        half = source.shape[0] // 2
        self.mine = pl.ds(pl.multiple_of(c * half, 8), half)
        theirs = pl.ds(pl.multiple_of((1 - c) * half, 8), half)
        self.source, self.held, self.came, self.slots, self.out = source, held, came, slots, out
        self.z = z
        twin = device(z, y, 1 - c, x)
        self.steps = [
            remote(source.at[theirs], came.at[0], sems, 0, twin),
            remote(held.at[0], came.at[1], sems, 1, device(z, y, c, 1 - x)),
            remote(held.at[1], came.at[2], sems, 2, device(z, 1 - y, c, x)),
        ]
        self.along = [
            remote(held.at[2], slots.at[z], sems, 2 + k, device((z + k) % NZ, y, c, x))
            for k in range(1, NZ)
        ]
        self.last = remote(out.at[self.mine], out.at[self.mine], sems, 6, twin)

    def begin(self):
        self.steps[0].start()

    def turn(self, step):
        self.steps[step].wait_recv()
        before = self.source[self.mine, :] if step == 0 else self.held[step - 1]
        self.held[step] = before + self.came[step]
        if step < 2:
            self.steps[step + 1].start()
        else:
            self.slots[self.z] = self.held[2]
            for copy in self.along:
                copy.start()

    def close(self):
        for copy in self.along:
            copy.wait_recv()
        self.out[self.mine, :] = self.slots[0] + self.slots[1] + self.slots[2] + self.slots[3]
        self.last.start()

    def finish(self):
        for copy in (*self.steps, *self.along):
            copy.wait_send()
        self.last.wait()


def near(z, y, c, x):
    return [
        device(z, y, c, 1 - x),
        device(z, 1 - y, c, x),
        device(z, y, 1 - c, x),
        *[device((z + k) % NZ, y, c, x) for k in range(1, NZ)],
    ]


def scatter_scratch(rows, width):
    half = width // 2
    return [
        pltpu.VMEM((NZ, 2, rows, width), BF),
        pltpu.VMEM((NZ, 2, rows, width), BF),
        pltpu.VMEM((2, rows, half), BF),
        pltpu.VMEM((2, rows, half), BF),
        pltpu.VMEM((NZ, rows, half), BF),
        pltpu.VMEM((NZ, rows, half), BF),
        pltpu.VMEM((3, rows, half), BF),
    ]


def total_scratch(shape):
    half = (shape[0] // 2,) + shape[1:]
    return [
        pltpu.VMEM((3,) + half, F32),
        pltpu.VMEM((3,) + half, F32),
        pltpu.VMEM((NZ,) + half, F32),
        pltpu.SemaphoreType.DMA((Total.COPIES,)),
        pltpu.SemaphoreType.DMA((Total.COPIES,)),
    ]


def piece_start(owner):
    return (owner * (GENOUT // 32)) // 128


FLAT = (GENOUT // 128) * MAXB


def unpack(taken, flat, wide, kernel):
    flat[...] = jnp.zeros_like(flat)
    used = COVER * MAXB
    for owner in range(32):
        first = piece_start(owner) * MAXB
        count = min(used, FLAT - first)
        piece = taken[owner // 8, (owner // 4) % 2, (owner // 2) % 2, owner % 2]
        flat[first : first + count, :] += piece.astype(F32)[:count]
    for pixel in range(PIX):
        for part in range(6):
            first = (pixel * 6 + part) * MAXB
            wide[part, pl.ds(pixel, MAXB, stride=PIX), :] = flat[first : first + MAXB, :]
    for part in range(6):
        kernel[:, part * 128 : (part + 1) * 128] = wide[part].astype(BF)


def pack(d_kernel, bias, pieces, wide, flat):
    for part in range(6):
        wide[part] = d_kernel[:, part * 128 : (part + 1) * 128]
        first = (PIX * 6 + part) * MAXB
        flat[first : first + MAXB, :] = bias[0:MAXB, part * 128 : (part + 1) * 128]
    flat[FLAT:, :] = jnp.zeros((flat.shape[0] - FLAT, 128), F32)
    for pixel in range(PIX):
        for part in range(6):
            first = (pixel * 6 + part) * MAXB
            flat[first : first + MAXB, :] = wide[part, pl.ds(pixel, MAXB, stride=PIX), :]
    for owner in range(32):
        first = piece_start(owner) * MAXB
        pieces[owner // 8, (owner // 4) % 2, (owner // 2) % 2, owner % 2] = flat[
            first : first + PIECE, :
        ].astype(BF)


def norm_rows_back(value, upstream, gain):
    normed, scale = standard(value)
    scaled = upstream * gain
    inside = (
        scaled
        - jnp.mean(scaled, axis=-1, keepdims=True)
        - normed * jnp.mean(scaled * normed, axis=-1, keepdims=True)
    )
    return scale * inside, column_sum(upstream * normed), column_sum(upstream)


def close_kernel(
    d_qkv, first, w_qkv, tokens, d_after, params, pixels, kernel, time_loc, late,
    hidden, gen_shift, slope, codes, groups, bands,
    out_gen, in_grad, in_bias, out_q, out_meta, out_vectors, out_up, pixel_grad,
    d_tokens, grad_q, pieces, crossed, merged, taken, flat, wide, rows, source, summed, out_grad,
    x_send, x_recv, send_sem, recv_sem, local_sem, q_send, q_recv, *rest,
):
    here = z, y, c, x = spot()
    across = device(z, y, c, 1 - x)
    greet([where for _, where in group_peers(z, y, c, x)] + [across])
    scatter = Scatter(
        grad_q, *rest[5:12], out_q, (q_send, q_recv, local_sem), 0, here
    )
    total = Total(source, summed, *rest[0:5], here)
    gain = shift = jnp.zeros((1, D), F32)
    for start, count in BANDS:
        band = slice(start, start + count)
        upstream = nt_dot(d_qkv[band, :], w_qkv[...].reshape(D, 3 * D))
        d_norm, gain_part, shift_part = norm_rows_back(tokens[band, :], upstream, params[0:1, :])
        gain += gain_part
        shift += shift_part
        d_tokens[band, :] = (d_after[band, :] + d_norm).astype(BF)
    patches = d_tokens[0:TOK_DEV, :]
    d_kernel = inner_dot(pixels[...], patches)
    live = bands[groups[lax.axis_index("dp")]]
    band_at = lax.broadcasted_iota(jnp.int32, (16, D), 0)
    sums = column_sum(patches.astype(F32)) / live.astype(F32)
    pack(d_kernel, jnp.where(band_at < live, sums, 0.0), pieces, wide, flat)
    order = (2, 1, 3, 0)
    swaps = {}
    for dz in order:
        to = (z + dz) % NZ
        swaps[dz] = remote(
            pieces.at[to, :, :, 1 - x], crossed.at[to], (x_send, x_recv), dz, across
        )
    swaps[2].start()
    swaps[1].start()
    sends = []

    def merge(dz):
        to = (z + dz) % NZ
        swaps[dz].wait_recv()
        if dz in (2, 1):
            swaps[{2: 3, 1: 0}[dz]].start()
        for at_y in range(2):
            for at_c in range(2):
                merged[to, at_y, at_c] = (
                    pieces[to, at_y, at_c, x].astype(F32) + crossed[to, at_y, at_c].astype(F32)
                ).astype(BF)
        for dy in range(2):
            for dc in range(2):
                at_y, at_c = (y + dy) % 2, (c + dc) % 2
                if dz + dy + dc:
                    copy = remote(
                        merged.at[to, at_y, at_c],
                        taken.at[z, y, c],
                        (send_sem, recv_sem),
                        dz * 4 + dy * 2 + dc,
                        device(to, at_y, at_c, x),
                    )
                    copy.start()
                    sends.append(copy)
                else:
                    taken[z, y, c] = merged[z, y, c]

    def grad_third(third):
        part = slice(third * D, (third + 1) * D)
        grad_q[:, :, :, :, part] = (
            inner_dot(first[...], d_qkv[:, part]).astype(BF).reshape(NZ, 2, 2, -1, D)
        )

    grad_third(0)
    merge(2)
    grad_third(1)
    merge(1)
    grad_third(2)
    scatter.stage_a()
    merge(3)
    merge(0)
    extra = d_tokens[TOK_DEV:LIVE, :].astype(F32)
    stamps = jnp.concatenate([extra[2 * m + 1 : 2 * m + 2] for m in range(SLOTS)], axis=0)
    first_rows = jnp.concatenate(
        [
            extra[0:1] + extra[2:3] + extra[4:5] + extra[6:7],
            lax.dot_general(
                time_loc[0],
                stamps,
                (((0,), (0,)), ((), ())),
                precision=lax.Precision.HIGHEST,
                preferred_element_type=F32,
            ),
            gain,
            shift,
            jnp.zeros((5, D), F32),
        ],
        axis=0,
    )
    meta_at = GEN + 16
    for part in range(6):
        source[meta_at + part * 16 : meta_at + part * 16 + 16, :] = first_rows[
            :, part * 128 : (part + 1) * 128
        ]
    for start, count in BANDS[:2]:
        band = slice(start, start + count)
        pixel_grad[band, :] = nt_dot(d_tokens[band, :], kernel[...])
    scatter.stage_b()
    for start, count in BANDS[2:4]:
        band = slice(start, start + count)
        pixel_grad[band, :] = nt_dot(d_tokens[band, :], kernel[...])
    scatter.stage_c()
    for copy in sends:
        copy.wait_recv()
    for n in range(GROUPS):
        block = taken[n // 4, (n // 2) % 2, n % 2].astype(F32)
        for at in range(COVER):
            rows[at, n * MAXB : (n + 1) * MAXB, :] = block[at * MAXB : (at + 1) * MAXB]
    d_hidden = jnp.zeros((GROUPS * MAXB, GEN), F32)
    for at in range(COVER):
        d_hidden += nn_dot(rows[at].astype(BF), gen_shift[at * 128 : (at + 1) * 128, :])
    d_before = d_hidden * slope[...]
    source[0:GEN, :] = lax.dot_general(
        codes[...],
        d_before,
        (((0,), (0,)), ((), ())),
        precision=lax.Precision.HIGHEST,
        preferred_element_type=F32,
    )
    source[GEN:meta_at, :] = jnp.broadcast_to(column_sum(d_before), (16, GEN))
    total.begin()
    low = hidden[...].astype(BF)
    for at in range(COVER // 2):
        out_grad[at * 128 : (at + 1) * 128, :] = inner_dot(rows[at].astype(BF), low)
    total.turn(0)
    scatter.stage_d()
    for at in range(COVER // 2, COVER):
        out_grad[at * 128 : (at + 1) * 128, :] = inner_dot(rows[at].astype(BF), low)
    total.turn(1)
    total.turn(2)
    width = out_gen.shape[0]
    group = lax.axis_index("dp")
    owner = group * 2 + x
    out_gen[...] = out_grad[pl.ds(pl.multiple_of((owner * width) % 128, 8), width), :]
    total.close()
    scatter.stage_e()
    total.finish()
    in_grad[...] = summed[0:GEN, :]
    in_bias[...] = summed[GEN : GEN + 1, :]
    all_rows = jnp.concatenate(
        [summed[meta_at + part * 16 : meta_at + part * 16 + 16, :] for part in range(6)], axis=1
    )
    out_meta[...] = all_rows[0:9]
    row = lax.broadcasted_iota(jnp.int32, (8, D), 0)
    count, up_count = out_vectors.shape[1], out_up.shape[1]
    per_row = D // up_count
    norms = jnp.where(
        row == 0, all_rows[9:10], jnp.where(row == 1, all_rows[10:11], late[0:8, :])
    )
    norms = pltpu.roll(norms, (GROUPS - group) % GROUPS * count, 1)
    out_vectors[...] = norms[0:6, 0:count]
    ups = pltpu.roll(late[8:16, :], (per_row - group % per_row) % per_row * up_count, 1)
    out_up[...] = column_sum(jnp.where(row == group // per_row, ups, 0.0))[:, 0:up_count]
    for copy in (*sends, *swaps.values()):
        copy.wait_send()


def closing(operands, scalars, sizes):
    vmem = pl.BlockSpec(memory_space=pltpu.VMEM)
    smem = pl.BlockSpec(memory_space=pltpu.SMEM)
    small = (GEN + 16 + 96, GEN)
    width_gen, rows_in, up_rows = sizes
    held = (NZ, 2, 2, PIECE, 128)
    _, _, _, rows, width = operands[2].shape
    return pl.pallas_call(
        close_kernel,
        in_specs=[vmem] * len(operands) + [smem] * len(scalars),
        out_specs=[vmem] * 8,
        out_shape=[
            jax.ShapeDtypeStruct((width_gen, GEN), F32),
            jax.ShapeDtypeStruct((GEN, GEN), F32),
            jax.ShapeDtypeStruct((1, GEN), F32),
            jax.ShapeDtypeStruct((rows, width // 2), F32),
            jax.ShapeDtypeStruct((9, D), F32),
            jax.ShapeDtypeStruct((6, rows_in), F32),
            jax.ShapeDtypeStruct((1, up_rows), F32),
            jax.ShapeDtypeStruct((TOK_DEV, MAXB * PIX), F32),
        ],
        scratch_shapes=[
            pltpu.VMEM((LIVE, D), BF),
            pltpu.VMEM(operands[2].shape, BF),
            pltpu.VMEM((NZ, 2, 2, 2, PIECE, 128), BF),
            pltpu.VMEM(held, BF),
            pltpu.VMEM(held, BF),
            pltpu.VMEM(held, BF),
            pltpu.VMEM((FLAT + 64, 128), F32),
            pltpu.VMEM((6, MAXB * PIX, 128), F32),
            pltpu.VMEM((COVER, GROUPS * MAXB, 128), F32),
            pltpu.VMEM(small, F32),
            pltpu.VMEM(small, F32),
            pltpu.VMEM((COVER * 128, GEN), F32),
            pltpu.SemaphoreType.DMA((4,)),
            pltpu.SemaphoreType.DMA((4,)),
            pltpu.SemaphoreType.DMA((16,)),
            pltpu.SemaphoreType.DMA((16,)),
            pltpu.SemaphoreType.DMA((1,)),
            pltpu.SemaphoreType.DMA((8,)),
            pltpu.SemaphoreType.DMA((8,)),
            *total_scratch(small),
            *scatter_scratch(rows, width),
        ],
        compiler_params=pltpu.CompilerParams(
            collective_id=2, has_side_effects=True, vmem_limit_bytes=VMEM_ASK
        ),
    )(*operands, *scalars)


def tile_rows(source, first):
    if first + TILE <= LIVE:
        return source[first : first + TILE, :]
    part = source[first:LIVE, :]
    return jnp.concatenate([part, jnp.zeros((first + TILE - LIVE, 128), part.dtype)], axis=0)


def feed_kernel(
    tokens, mixed, top, w_out, vectors, w_up, w_down,
    layer_out, d_after, d_mixed, out_grad, rows, up_grad, down_grad, b_grad,
    second, second_turned, top_full, after, sum_out, sum_second, active, d_upper, proj,
):
    step = pl.program_id(0)

    @pl.when(step == 0)
    def _():
        for first, count in BANDS:
            band = slice(first, first + count)
            value = tokens[band, :] + (nn_dot(mixed[band, :], w_out[...]) + vectors[2:3, :])
            after[band, :] = value
            normed, _ = standard(value)
            put_rows(
                second, first, count, (normed * vectors[3:4, :] + vectors[4:5, :]).astype(BF)
            )
            put_rows(top_full, first, count, top[band, :])
        second_turned[...] = second[...].T
        sum_out[...] = jnp.zeros_like(sum_out)
        b_grad[...] = jnp.zeros_like(b_grad)
        sum_second[...] = jnp.zeros_like(sum_second)

    total = jnp.zeros((1, CHUNK), F32)
    for first, count in BANDS:
        count = -(-count // 16) * 16
        band = slice(first, first + count)
        upper = nn_dot(second[band, :], w_up[...]) + vectors[pl.ds(6 + step, 1), :]
        made, slope = gelu_parts(upper)
        made = made.astype(BF)
        active[band, :] = made
        back = (nt_dot(top_full[band, :], w_down[...]) * slope).astype(BF)
        d_upper[band, :] = back
        total += column_sum(back.astype(F32))
    b_grad[pl.ds(step, 1), :] = total
    sum_out[...] += nn_dot(active[...], w_down[...])
    sum_second[...] += nt_dot(d_upper[...], w_up[...])
    down_grad[...] = inner_dot(active[...], top_full[...]).astype(BF)
    up_grad[...] = nn_dot(second_turned[...], d_upper[...]).astype(BF)

    @pl.when(step == pl.num_programs(0) - 1)
    def _():
        gain = shift = bias = last = jnp.zeros((1, D), F32)
        for first, count in BANDS:
            band = slice(first, first + count)
            value = after[band, :]
            layer_out[band, :] = (value + sum_out[band, :] + vectors[5:6, :]).astype(BF)
            normed, scale = standard(value)
            upstream = sum_second[band, :]
            gain += column_sum(upstream * normed)
            shift += column_sum(upstream)
            scaled = upstream * vectors[3:4, :]
            inside = (
                scaled
                - jnp.mean(scaled, axis=-1, keepdims=True)
                - normed * jnp.mean(scaled * normed, axis=-1, keepdims=True)
            )
            grad_top = top[band, :].astype(F32)
            last += column_sum(grad_top)
            result = grad_top + scale * inside
            d_after[band, :] = result
            low = result.astype(BF)
            bias += column_sum(low.astype(F32))
            put_rows(proj, first, count, low)
            d_mixed[band, :] = nt_dot(low, w_out[...]).astype(BF)
        out_grad[...] = inner_dot(mixed[...], proj[0:LIVE, :]).astype(BF)
        rows[...] = jnp.concatenate([jnp.zeros((2, D), F32), bias, gain, shift, last, jnp.zeros((2, D), F32)], axis=0)


def feed(tokens, mixed, top, w_out, vectors, w_up, w_down):
    width = w_up.shape[1]

    def whole(*shape):
        return pl.BlockSpec(shape, lambda step: (0, 0))

    across = pl.BlockSpec((D, CHUNK), lambda step: (0, step))
    down = pl.BlockSpec((CHUNK, D), lambda step: (step, 0))
    block = whole(LIVE, D)
    return pl.pallas_call(
        feed_kernel,
        grid=(width // CHUNK,),
        in_specs=[block, block, block, whole(D, D), whole(16, D), across, down],
        out_specs=[block, block, block, whole(D, D), whole(8, D), across, down, whole(8, D)],
        out_shape=[
            jax.ShapeDtypeStruct((LIVE, D), BF),
            jax.ShapeDtypeStruct((LIVE, D), F32),
            jax.ShapeDtypeStruct((LIVE, D), BF),
            jax.ShapeDtypeStruct((D, D), BF),
            jax.ShapeDtypeStruct((8, D), F32),
            jax.ShapeDtypeStruct((D, width), BF),
            jax.ShapeDtypeStruct((width, D), BF),
            jax.ShapeDtypeStruct((8, D), F32),
        ],
        scratch_shapes=[
            pltpu.VMEM((ROWS, D), BF),
            pltpu.VMEM((D, ROWS), BF),
            pltpu.VMEM((ROWS, D), BF),
            pltpu.VMEM((LIVE, D), F32),
            pltpu.VMEM((ROWS, D), F32),
            pltpu.VMEM((ROWS, D), F32),
            pltpu.VMEM((ROWS, CHUNK), BF),
            pltpu.VMEM((ROWS, CHUNK), BF),
            pltpu.VMEM((ROWS, D), BF),
        ],
        compiler_params=pltpu.CompilerParams(vmem_limit_bytes=VMEM_ASK),
    )(tokens, mixed, top, w_out, vectors, w_up, w_down)


def three_parts(exact):
    high = exact.astype(BF)
    left = exact - high.astype(F32)
    middle = left.astype(BF)
    return high, middle, (left - middle.astype(F32)).astype(BF)


def attend_back_kernel(
    kind, q_ref, k_ref, v_ref, d_mixed, mixed, log_sum, late, b_grad, go, gu, gd,
    out, out_o, out_u, out_d, out_late,
    mask_q, mask_k, keys, values, keys_turned, d_query, d_keys, d_values, send_sem, recv_sem, local_sem, *rest,
):
    pair, part = pl.program_id(0), pl.program_id(1)
    here = spot()
    half = out_d.shape[0] // 2
    wholes = (go, gu, gd.at[:, :, :, 0:half], gd.at[:, :, :, half : 2 * half])
    results = (out_o, out_u, out_d.at[0:half], out_d.at[half : 2 * half])
    o, u, d, e = [
        Scatter(
            whole, *rest[7 * at : 7 * at + 7], result, (send_sem, recv_sem, local_sem), 8 * at, here
        )
        for at, (whole, result) in enumerate(zip(wholes, results))
    ]
    late_rows, late_sum, *late_rest = rest[28:]
    total = Total(late_rows, late_sum, *late_rest, here)

    def begin_total():
        late_rows[0:8, :] = late[...]
        late_rows[8:16, :] = b_grad[...]
        total.begin()

    plan = {
        0: (lambda: greet(near(*here)), u.stage_a),
        1: (u.stage_b, d.stage_a),
        2: (e.stage_a, o.stage_a, begin_total),
        3: (u.stage_c,),
        4: (lambda: total.turn(0),),
        5: (d.stage_b,),
        6: (d.stage_c, u.stage_d, e.stage_b),
        7: (e.stage_c, lambda: total.turn(1)),
        8: (d.stage_d, o.stage_b),
        9: (e.stage_d, u.stage_e, o.stage_c, lambda: total.turn(2)),
        10: (o.stage_d, d.stage_e),
        11: (total.close,),
    }

    def transfers(half):
        for slot, stages in plan.items():
            if slot % 2 == half:

                @pl.when(pair == slot // 2)
                def _():
                    for stage in stages:
                        stage()

    @pl.when((pair == 5) & (part == 2))
    def _():
        e.stage_e()
        o.stage_e()
        total.finish()
        out_late[...] = late_sum[...]

    lane = lax.broadcasted_iota(jnp.int32, (TILE, 128), 1)
    sub = lax.broadcasted_iota(jnp.int32, (128, TILE), 0)

    def with_parts(exact, rest):
        a, b, c = three_parts(exact)
        return jnp.where(
            lane == SLOTS,
            a,
            jnp.where(lane == SLOTS + 1, b, jnp.where(lane == SLOTS + 2, c, rest)),
        )

    @pl.when(part == 0)
    def _():
        transfers(0)

        @pl.when(pair == 0)
        def _():
            mask_rows(kind[0], mask_q, mask_k)
            keys[:, 128:256] = mask_k[...]
            values[:, 128:256] = mask_k[...]

        keys[:, 0:128] = k_ref[0]
        values[:, 0:128] = v_ref[0]
        keys_turned[...] = keys[:, 0:128].T
        d_keys[...] = jnp.zeros_like(d_keys)
        d_values[...] = jnp.zeros_like(d_values)
        for tile in range(TILES):
            first = tile * TILE
            if tile == 3:
                transfers(1)
            both = q_ref[0, first : first + TILE, :] * BF(0.125)
            up = tile_rows(d_mixed, first)
            logs = log_sum[0, first : first + TILE, :]
            product = up.astype(F32) * tile_rows(mixed, first).astype(F32)
            marks = mask_q[first : first + TILE, :]
            turned = []
            for head in range(2):
                chosen = (lane < HEAD) == (head == 0)
                query = jnp.where(chosen, both, BF(0))
                upstream = jnp.where(chosen, up, BF(0))
                inside = jnp.sum(jnp.where(chosen, product, 0.0), axis=1, keepdims=True)
                wide_query = jnp.concatenate(
                    [query, with_parts(-logs[:, head * HEAD : head * HEAD + 1], marks)], axis=1
                )
                wide_up = jnp.concatenate(
                    [upstream, with_parts(-inside, jnp.zeros_like(marks))], axis=1
                )
                prob = jnp.exp(nt_dot(keys[...], wide_query))
                d_scores = (prob * nt_dot(values[...], wide_up)).astype(BF)
                d_values[...] += nn_dot(prob.astype(BF), upstream)
                d_keys[...] += nn_dot(d_scores, query)
                turned.append(nn_dot(keys_turned[...], d_scores))
            d_query[first : first + TILE, :] = (
                (jnp.where(sub < HEAD, *turned) * 0.125).T.astype(BF)
            )
        out[...] = d_query[0:LIVE, :]

    @pl.when(part == 1)
    def _():
        out[...] = d_keys[0:LIVE, :].astype(BF)

    @pl.when(part == 2)
    def _():
        out[...] = d_values[0:LIVE, :].astype(BF)


def attend_back(kind, qkv, d_mixed, mixed, log_sum, late, b_grad, grads):
    def band(first):
        return pl.BlockSpec((LIVE, 128), lambda pair, part: (0, first + pair))

    def row_block(count):
        return pl.BlockSpec((count, D), lambda pair, part: (0, 0))

    def head(first):
        return pl.BlockSpec((1, ROWS, 128), lambda pair, part: (first + pair, 0, 0))

    shapes = [grad.shape[3:] for grad in grads]
    outs = [(rows, width // 2) for rows, width in shapes]
    low = (shapes[2][0] // 2, shapes[2][1])
    parts = [*shapes[:2], low, low]
    return pl.pallas_call(
        attend_back_kernel,
        grid=(HEADS // 2, 3),
        in_specs=[
            pl.BlockSpec(memory_space=pltpu.SMEM),
            head(0), head(6), head(12), band(0), band(0), head(0), row_block(8), row_block(8),
        ]
        + [pl.BlockSpec(memory_space=pl.ANY)] * 3,
        out_specs=[pl.BlockSpec((LIVE, 128), lambda pair, part: (0, part * 6 + pair))]
        + [pl.BlockSpec(shape, lambda pair, part: (0, 0)) for shape in outs]
        + [row_block(16)],
        out_shape=[
            jax.ShapeDtypeStruct((LIVE, 3 * D), BF),
            *[jax.ShapeDtypeStruct(shape, F32) for shape in outs],
            jax.ShapeDtypeStruct((16, D), F32),
        ],
        scratch_shapes=[
            pltpu.VMEM((ROWS, 128), BF),
            pltpu.VMEM((ROWS, 128), BF),
            pltpu.VMEM((ROWS, 256), BF),
            pltpu.VMEM((ROWS, 256), BF),
            pltpu.VMEM((128, ROWS), BF),
            pltpu.VMEM((ROWS, 128), BF),
            pltpu.VMEM((ROWS, 128), F32),
            pltpu.VMEM((ROWS, 128), F32),
            pltpu.SemaphoreType.DMA((32,)),
            pltpu.SemaphoreType.DMA((32,)),
            pltpu.SemaphoreType.DMA((4,)),
            *[entry for shape in parts for entry in scatter_scratch(*shape)],
            pltpu.VMEM((16, D), F32),
            pltpu.VMEM((16, D), F32),
            *total_scratch((16, D)),
        ],
        compiler_params=pltpu.CompilerParams(
            collective_id=3, has_side_effects=True, vmem_limit_bytes=VMEM_ASK
        ),
    )(kind, qkv, qkv, qkv, d_mixed, mixed, log_sum, late, b_grad, *grads)


def body_block(
    pixels,
    wave_table,
    band_count,
    wave_index,
    group_sensor,
    chip_kind,
    chip_gsd,
    time_loc,
    gen_in,
    gen_bias,
    gen_out,
    meta_weight,
    w_qkv,
    w_out,
    w_up,
    w_down,
    vectors,
    b_up,
    cotangent,
):
    rows, up_rows = vectors.shape[0], b_up.shape[0]

    def steps(count, last):
        falling = 10000.0 ** -(np.arange(count) / last)
        return jnp.asarray(np.tile(np.concatenate([falling, falling]), (8, 1)), F32)

    gen_turned = gen_out.T
    (
        full_q, full_o, full_u, full_d, params, kernel, tokens_in, first, qkv, mixed, log_sum,
        gen_shift, hidden, slope, codes,
    ) = forward(
        (w_qkv, w_out, w_up, w_down),
        (
            pixels,
            vectors.T,
            b_up.reshape(1, -1),
            meta_weight,
            time_loc,
            gen_in,
            gen_bias.reshape(1, -1),
            gen_turned,
            steps(GEN // 2, GEN // 2),
            steps(D // 4, D // 4 - 1),
        ),
        (group_sensor, band_count, wave_index, wave_table, chip_kind, chip_gsd),
    )
    layer_out, d_after, d_mixed, w_out_grad, late, w_up_grad, w_down_grad, b_grad = feed(
        tokens_in,
        mixed,
        cotangent,
        full_o.reshape(D, D),
        params,
        full_u.reshape(D, -1),
        full_d.reshape(-1, D),
    )
    d_qkv, w_out_out, w_up_out, w_down_out, late_sum = attend_back(
        chip_kind,
        qkv,
        d_mixed,
        mixed,
        log_sum,
        late,
        b_grad,
        [
            grad.reshape(NZ, 2, 2, -1, grad.shape[1])
            for grad in (w_out_grad, w_up_grad, w_down_grad)
        ],
    )
    gen_out_grad, gen_in_grad, gen_bias_grad, w_qkv_out, meta_grad, vectors_out, b_up_out, pixel_grad = (
        closing(
            (
                d_qkv,
                first,
                full_q,
                tokens_in,
                d_after,
                params,
                pixels,
                kernel,
                time_loc,
                late_sum,
                hidden,
                gen_shift,
                slope,
                codes,
            ),
            (group_sensor, band_count),
            (gen_turned.shape[0], rows, up_rows),
        )
    )
    return (
        layer_out,
        pixel_grad,
        gen_in_grad,
        gen_bias_grad.reshape(-1),
        gen_out_grad.T,
        meta_grad,
        w_qkv_out,
        w_out_out,
        w_up_out,
        w_down_out,
        vectors_out.T,
        b_up_out.reshape(-1),
    )


def solution(mesh):
    fits = dict(mesh.shape) == {"dp": 16, "fsdp": 2}
    body = body_block if fits else body_general
    placed = (
        P(("dp", "fsdp"), None),
        P(),
        P(),
        P(),
        P(),
        P(("dp", "fsdp")),
        P(("dp", "fsdp"), None),
        P(("dp", "fsdp"), None, None),
        P(),
        P(),
        P(None, ("dp", "fsdp")),
        P(),
        P("dp", "fsdp"),
        P("dp", "fsdp"),
        P("dp", "fsdp"),
        P("dp", "fsdp"),
        P("dp", None),
        P("dp"),
        P(("dp", "fsdp"), None),
    )
    return jax.shard_map(
        body,
        mesh=mesh,
        in_specs=placed,
        out_specs=(
            P(("dp", "fsdp"), None),
            P(("dp", "fsdp"), None),
            P(),
            P(),
            P(None, ("dp", "fsdp")),
            P(),
            P("dp", "fsdp"),
            P("dp", "fsdp"),
            P("dp", "fsdp"),
            P("dp", "fsdp"),
            P("dp", None),
            P("dp"),
        ),
        check_vma=False,
    )
```

```python
import math

import jax
import jax.numpy as jnp
import numpy as np
from jax import lax
from jax.experimental import pallas as pl
from jax.experimental.pallas import tpu as pltpu
from jax.sharding import PartitionSpec as P

D = 768
HEADS = 12
HEAD = 64
GEN = 128
PIX = 64
MAXB = 10
SENSORS = 7
TOK_DEV = 1024
SLOTS = 4
GENOUT = 49920


def exact_dot(left, right):
    return jnp.dot(left, right, precision=lax.Precision.HIGHEST)


def inner_dot(left, right):
    return lax.dot_general(
        left, right, (((0,), (0,)), ((), ())), preferred_element_type=jnp.float32
    )


def outer_dot(left, right):
    return lax.dot_general(
        left, right, (((1,), (1,)), ((), ())), preferred_element_type=jnp.float32
    )


def gelu_exact(values):
    return jax.nn.gelu(values, approximate=False)


def gelu_slope(values, upstream):
    return jax.vjp(gelu_exact, values)[1](upstream)[0]


def table_lookup(indices, table):
    return jnp.sum(
        jnp.where(
            indices[:, None] == jnp.arange(table.shape[0], dtype=jnp.int32)[None, :],
            table[None, :],
            0.0,
        ),
        axis=1,
    )


def wave_code(wavelengths):
    half = GEN // 2
    omega = 1.0 / 10000.0 ** (jnp.arange(half, dtype=jnp.float32) / half)
    angle = (wavelengths * 1000.0)[:, None] * omega[None, :]
    return jnp.concatenate([jnp.sin(angle), jnp.cos(angle)], axis=1)


def place_code(kind_one, gsd_one):
    small = TOK_DEV // SLOTS
    index = jnp.arange(TOK_DEV, dtype=jnp.int32)
    within = jnp.where(kind_one == 1, index, index % small)
    side = jnp.where(kind_one == 1, math.isqrt(TOK_DEV), math.isqrt(small)).astype(jnp.int32)
    across = (within // side).astype(jnp.float32)
    along = (within % side).astype(jnp.float32)
    holder = jnp.where(kind_one == 1, 0, index // small)
    ground = (
        jnp.sum(
            jnp.where(
                holder[:, None] == jnp.arange(SLOTS, dtype=jnp.int32)[None, :], gsd_one[None, :], 0
            ),
            axis=1,
        ).astype(jnp.float32)
        / 10.0
    )
    quarter = D // 4
    omega = 1.0 / 10000.0 ** (jnp.arange(quarter, dtype=jnp.float32) / (quarter - 1))
    first = (across * ground)[:, None] * omega[None, :]
    second = (along * ground)[:, None] * omega[None, :]
    return jnp.concatenate(
        [jnp.sin(first), jnp.cos(first), jnp.sin(second), jnp.cos(second)], axis=1
    )


def segment_ids(kind_one):
    index = jnp.arange(TOK_DEV, dtype=jnp.int32)
    patches = jnp.where(kind_one == 1, 0, index // (TOK_DEV // SLOTS))
    extra = jnp.arange(2 * SLOTS, dtype=jnp.int32) // 2
    return jnp.concatenate([patches, extra])


def layer_norm(values, gain, shift):
    centred = values - jnp.mean(values, axis=-1, keepdims=True)
    scale = lax.rsqrt(jnp.mean(centred * centred, axis=-1, keepdims=True) + 1e-05)
    normed = centred * scale
    return (normed * gain + shift, normed, scale)


def norm_back(upstream, normed, scale, gain):
    gain_grad = jnp.sum(upstream * normed, axis=0)
    shift_grad = jnp.sum(upstream, axis=0)
    scaled = upstream * gain
    inside = (
        scaled
        - jnp.mean(scaled, axis=-1, keepdims=True)
        - normed * jnp.mean(scaled * normed, axis=-1, keepdims=True)
    )
    return (scale * inside, gain_grad, shift_grad)


def body_general(
    pixels,
    wave_table,
    band_count,
    wave_index,
    group_sensor,
    chip_kind,
    chip_gsd,
    time_loc,
    gen_in,
    gen_bias,
    gen_out,
    meta_weight,
    w_qkv,
    w_out,
    w_up,
    w_down,
    vectors,
    b_up,
    cotangent,
):
    half_type = jnp.bfloat16
    group = lax.axis_index("dp")
    sensor = jnp.sum(
        jnp.where(jnp.arange(group_sensor.shape[0], dtype=jnp.int32) == group, group_sensor, 0)
    )
    chosen_sensor = jnp.arange(SENSORS, dtype=jnp.int32) == sensor
    band_total = jnp.sum(jnp.where(chosen_sensor, band_count, 0))
    gen_in_full = gen_in.astype(jnp.float32)
    gen_bias_full = gen_bias.astype(jnp.float32)
    codes = wave_code(table_lookup(wave_index.reshape(-1), wave_table))
    before = exact_dot(codes, gen_in_full) + gen_bias_full
    hidden = gelu_exact(before).astype(half_type)
    shard_made = jnp.dot(hidden, gen_out, preferred_element_type=jnp.float32).astype(half_type)
    all_made = lax.all_gather(shard_made, ("dp", "fsdp"), axis=1, tiled=True)
    generated = lax.dynamic_slice_in_dim(all_made, sensor * MAXB, MAXB, 0)
    live_band = (jnp.arange(MAXB, dtype=jnp.int32) < band_total)[:, None]
    kernel = jnp.where(live_band, generated[:, : PIX * D], jnp.zeros((), half_type)).reshape(
        MAXB * PIX, D
    )
    band_float = band_total.astype(jnp.float32)
    embed_bias = (
        jnp.sum(jnp.where(live_band, generated[:, PIX * D :].astype(jnp.float32), 0.0), axis=0)
        / band_float
    )
    kind_one = chip_kind[0]
    patches = (
        jnp.dot(pixels, kernel, preferred_element_type=jnp.float32)
        + embed_bias
        + place_code(kind_one, chip_gsd[0])
    )
    meta_full = meta_weight.astype(jnp.float32)
    stamps = exact_dot(time_loc[0], meta_full[1:])
    classes = jnp.broadcast_to(meta_full[0], stamps.shape)
    extra = jnp.stack([classes, stamps], axis=1).reshape(2 * SLOTS, D)
    tokens_in = jnp.concatenate([patches, extra], axis=0)
    total_rows = tokens_in.shape[0]
    qkv_rows, out_rows, up_rows, down_rows, vectors_all, b_up_all = (
        lax.all_gather(w_qkv, "dp", axis=0, tiled=True),
        lax.all_gather(w_out, "dp", axis=0, tiled=True),
        lax.all_gather(w_up, "dp", axis=0, tiled=True),
        lax.all_gather(w_down, "dp", axis=0, tiled=True),
        lax.all_gather(vectors, "dp", axis=0, tiled=True),
        lax.all_gather(b_up, "dp", axis=0, tiled=True),
    )
    w_qkv_all, w_out_all, w_up_all, w_down_all = (
        lax.all_gather(qkv_rows, "fsdp", axis=1, tiled=True),
        lax.all_gather(out_rows, "fsdp", axis=1, tiled=True),
        lax.all_gather(up_rows, "fsdp", axis=1, tiled=True),
        lax.all_gather(down_rows, "fsdp", axis=1, tiled=True),
    )
    vector_full = vectors_all.astype(jnp.float32)
    b_up_full = b_up_all.astype(jnp.float32)
    first_norm, normed_one, scale_one = layer_norm(tokens_in, vector_full[:, 0], vector_full[:, 1])
    first = first_norm.astype(half_type)
    qkv = jnp.dot(first, w_qkv_all, preferred_element_type=jnp.float32).astype(half_type)
    query = qkv[:, :D].reshape(total_rows, HEADS, HEAD)
    keys = qkv[:, D : 2 * D].reshape(total_rows, HEADS, HEAD)
    values = qkv[:, 2 * D :].reshape(total_rows, HEADS, HEAD)
    segment = segment_ids(kind_one)
    same = (segment[:, None] == segment[None, :])[None]
    scores = jnp.einsum("qhd,khd->hqk", query, keys, preferred_element_type=jnp.float32) * HEAD ** (
        -0.5
    )
    scores = jnp.where(same, scores, -1e30)
    peak = jnp.max(scores, axis=-1, keepdims=True)
    expo = jnp.exp(scores - peak)
    totals = jnp.sum(expo, axis=-1, keepdims=True)
    prob_half = (expo / totals).astype(half_type)
    mixed = (
        jnp.einsum("hqk,khd->qhd", prob_half, values, preferred_element_type=jnp.float32)
        .reshape(total_rows, D)
        .astype(half_type)
    )
    after = tokens_in + (
        jnp.dot(mixed, w_out_all, preferred_element_type=jnp.float32) + vector_full[:, 2]
    )
    second_norm, normed_two, scale_two = layer_norm(after, vector_full[:, 3], vector_full[:, 4])
    second = second_norm.astype(half_type)
    upper = jnp.dot(second, w_up_all, preferred_element_type=jnp.float32) + b_up_full
    active = gelu_exact(upper).astype(half_type)
    layer_out = (
        after + jnp.dot(active, w_down_all, preferred_element_type=jnp.float32) + vector_full[:, 5]
    ).astype(half_type)
    grad_top = cotangent.astype(jnp.float32)
    w_down_grad = inner_dot(active, cotangent)
    down_bias_grad = jnp.sum(grad_top, axis=0)
    d_active = outer_dot(cotangent, w_down_all)
    d_upper = gelu_slope(upper, d_active).astype(half_type)
    w_up_grad = inner_dot(second, d_upper)
    b_up_grad = jnp.sum(d_upper.astype(jnp.float32), axis=0)
    d_second = outer_dot(d_upper, w_up_all)
    d_after_norm, gain_two_grad, shift_two_grad = norm_back(
        d_second, normed_two, scale_two, vector_full[:, 3]
    )
    d_after = grad_top + d_after_norm
    d_proj = d_after.astype(half_type)
    w_out_grad = inner_dot(mixed, d_proj)
    out_bias_grad = jnp.sum(d_proj.astype(jnp.float32), axis=0)
    d_mixed = outer_dot(d_proj, w_out_all).astype(half_type).reshape(total_rows, HEADS, HEAD)
    again = jnp.einsum("qhd,khd->hqk", query, keys, preferred_element_type=jnp.float32) * HEAD ** (
        -0.5
    )
    again = jnp.where(same, again, -1e30)
    prob_full = jnp.exp(again - peak) / totals
    recalled = prob_full.astype(half_type)
    d_values = jnp.einsum("hqk,qhd->khd", recalled, d_mixed, preferred_element_type=jnp.float32)
    d_prob = jnp.einsum("qhd,khd->hqk", d_mixed, values, preferred_element_type=jnp.float32)
    d_scores = prob_full * (d_prob - jnp.sum(d_prob * prob_full, axis=-1, keepdims=True))
    d_scores = jnp.where(same, d_scores, 0.0).astype(half_type)
    d_query = jnp.einsum(
        "hqk,khd->qhd", d_scores, keys, preferred_element_type=jnp.float32
    ) * HEAD ** (-0.5)
    d_keys = jnp.einsum(
        "hqk,qhd->khd", d_scores, query, preferred_element_type=jnp.float32
    ) * HEAD ** (-0.5)
    d_qkv = jnp.concatenate(
        [
            d_query.reshape(total_rows, D),
            d_keys.reshape(total_rows, D),
            d_values.reshape(total_rows, D),
        ],
        axis=1,
    ).astype(half_type)
    w_qkv_grad = inner_dot(first, d_qkv)
    d_first = outer_dot(d_qkv, w_qkv_all)
    d_tokens_norm, gain_one_grad, shift_one_grad = norm_back(
        d_first, normed_one, scale_one, vector_full[:, 0]
    )
    d_tokens = (d_after + d_tokens_norm).astype(half_type)
    vectors_grad = jnp.stack(
        [
            gain_one_grad,
            shift_one_grad,
            out_bias_grad,
            gain_two_grad,
            shift_two_grad,
            down_bias_grad,
        ],
        axis=1,
    )
    d_patches = d_tokens[:TOK_DEV]
    d_extra = d_tokens[TOK_DEV:].astype(jnp.float32).reshape(SLOTS, 2, D)
    pixel_grad = outer_dot(d_patches, kernel)
    class_grad = jnp.sum(d_extra[:, 0], axis=0)
    stamp_grad = exact_dot(time_loc[0].T, d_extra[:, 1])
    meta_part = jnp.concatenate([class_grad[None, :], stamp_grad], axis=0)
    d_kernel = inner_dot(pixels, d_patches).reshape(MAXB, PIX * D)
    d_kernel = jnp.where(live_band, d_kernel, 0.0)
    d_bias = jnp.sum(d_patches.astype(jnp.float32), axis=0) / band_float
    d_bias_rows = jnp.where(live_band, d_bias[None, :], 0.0)
    d_generated = jnp.concatenate([d_kernel, d_bias_rows], axis=1).astype(half_type)
    placed = jnp.where(
        chosen_sensor[:, None, None], d_generated.astype(jnp.float32)[None], 0.0
    ).reshape(SENSORS * MAXB, GENOUT)
    columns = lax.psum_scatter(placed, ("dp", "fsdp"), scatter_dimension=1, tiled=True)
    gen_out_grad = exact_dot(hidden.astype(jnp.float32).T, columns)
    d_hidden = exact_dot(columns, gen_out.astype(jnp.float32).T)
    d_before = gelu_slope(before, d_hidden)
    gen_in_part = exact_dot(codes.T, d_before)
    gen_bias_part = jnp.sum(d_before, axis=0)
    meta_grad, gen_in_grad, gen_bias_grad = lax.psum(
        (meta_part, gen_in_part, gen_bias_part), ("dp", "fsdp")
    )
    qkv_cols, out_cols, up_cols, down_cols = (
        lax.psum_scatter(
            w_qkv_grad.astype(jnp.bfloat16), "fsdp", scatter_dimension=1, tiled=True
        ).astype(jnp.float32),
        lax.psum_scatter(
            w_out_grad.astype(jnp.bfloat16), "fsdp", scatter_dimension=1, tiled=True
        ).astype(jnp.float32),
        lax.psum_scatter(
            w_up_grad.astype(jnp.bfloat16), "fsdp", scatter_dimension=1, tiled=True
        ).astype(jnp.float32),
        lax.psum_scatter(
            w_down_grad.astype(jnp.bfloat16), "fsdp", scatter_dimension=1, tiled=True
        ).astype(jnp.float32),
    )
    vectors_group, b_up_group = lax.psum((vectors_grad, b_up_grad), "fsdp")
    w_qkv_out, w_out_out, w_up_out, w_down_out, vectors_out, b_up_out = (
        lax.psum_scatter(
            qkv_cols.astype(jnp.bfloat16), "dp", scatter_dimension=0, tiled=True
        ).astype(jnp.float32),
        lax.psum_scatter(
            out_cols.astype(jnp.bfloat16), "dp", scatter_dimension=0, tiled=True
        ).astype(jnp.float32),
        lax.psum_scatter(
            up_cols.astype(jnp.bfloat16), "dp", scatter_dimension=0, tiled=True
        ).astype(jnp.float32),
        lax.psum_scatter(
            down_cols.astype(jnp.bfloat16), "dp", scatter_dimension=0, tiled=True
        ).astype(jnp.float32),
        lax.psum_scatter(
            vectors_group.astype(jnp.bfloat16), "dp", scatter_dimension=0, tiled=True
        ).astype(jnp.float32),
        lax.psum_scatter(
            b_up_group.astype(jnp.bfloat16), "dp", scatter_dimension=0, tiled=True
        ).astype(jnp.float32),
    )
    return (
        layer_out,
        pixel_grad,
        gen_in_grad,
        gen_bias_grad,
        gen_out_grad,
        meta_grad,
        w_qkv_out,
        w_out_out,
        w_up_out,
        w_down_out,
        vectors_out,
        b_up_out,
    )


LIVE = 1032
ROWS = 1040
TILE = 208
TILES = 5
WIDE = 520
NZ = 4
GROUPS = 16
PIECE = 144
COVER = 14
VMEM_ASK = 60 * 1024 * 1024
BF = jnp.bfloat16
F32 = jnp.float32


def nt_dot(left, right):
    return lax.dot_general(left, right, (((1,), (1,)), ((), ())), preferred_element_type=F32)


def nn_dot(left, right):
    return lax.dot_general(left, right, (((1,), (0,)), ((), ())), preferred_element_type=F32)


def spot():
    group = lax.axis_index("dp")
    return group // 4, (group // 2) % 2, group % 2, lax.axis_index("fsdp")


def device(z, y, c, x):
    return {"dp": z * 4 + y * 2 + c, "fsdp": x}


def remote(source, target, sems, slot, where):
    return pltpu.make_async_remote_copy(
        src_ref=source,
        dst_ref=target,
        send_sem=sems[0].at[slot],
        recv_sem=sems[1].at[slot],
        device_id=where,
        device_id_type=pl.DeviceIdType.MESH,
    )


def greet(others):
    barrier = pltpu.get_barrier_semaphore()
    for where in others:
        pl.semaphore_signal(
            barrier, inc=1, device_id=where, device_id_type=pl.DeviceIdType.MESH
        )
    pl.semaphore_wait(barrier, len(others))


def columns(ref, x):
    width = ref.shape[-1] // 2
    return pl.ds(pl.multiple_of(x * width, 128), width)


def group_peers(z, y, c, x):
    return [
        ((dz, dy, dc), device((z + dz) % NZ, (y + dy) % 2, (c + dc) % 2, x))
        for dz in range(NZ)
        for dy in range(2)
        for dc in range(2)
        if dz + dy + dc
    ]


CHUNK = 768
BANDS = ((0, 256), (256, 256), (512, 256), (768, 256), (1024, 8))


def gelu_parts(values):
    bell = jnp.exp(values * values * (-0.5))
    step = 1.0 / (1.0 + (0.3275911 * math.sqrt(0.5)) * jnp.abs(values))
    poly = 0.5 * 1.061405429 * step - 0.5 * 1.453152027
    poly = poly * step + 0.5 * 1.421413741
    poly = poly * step - 0.5 * 0.284496736
    poly = poly * step + 0.5 * 0.254829592
    tail = poly * step * bell
    below = jnp.where(values < 0.0, tail, 1.0 - tail)
    return values * below, below + values * bell * (1.0 / math.sqrt(2.0 * math.pi))


def standard(values):
    centred = values - jnp.mean(values, axis=-1, keepdims=True)
    scale = lax.rsqrt(jnp.mean(centred * centred, axis=-1, keepdims=True) + 1e-05)
    return centred * scale, scale


def column_sum(values):
    return jnp.sum(values, axis=0, keepdims=True)


def put_rows(target, first, count, values):
    if count % 16:
        values = jnp.concatenate(
            [values, jnp.zeros((16 - count % 16, values.shape[1]), values.dtype)], axis=0
        )
    target[first : first + values.shape[0], :] = values


class Gather:
    COPIES = 19

    def __init__(self, shard, whole, sems, local, first, lean, here):
        z, y, c, x = here
        self.lean = lean
        mine, other = columns(whole, x), columns(whole, 1 - x)
        across, beside, twin = device(z, y, c, 1 - x), device(z, 1 - y, c, x), device(z, y, 1 - c, x)
        target = whole.at[z, y, c, :, mine]
        self.local = pltpu.make_async_copy(shard, target, local)
        self.along = [
            remote(shard, target, sems, first + k - 1, device((z + k) % NZ, y, c, x))
            for k in range(1, NZ)
        ]
        self.to_x, self.to_y, self.far = [], [], []
        for k in range(NZ):
            at = (z + NZ - k) % NZ
            place = whole.at[at, y, c, :, mine]
            source = place if k else shard
            self.to_x.append(remote(source, place, sems, first + 3 + k, across))
            self.to_y.append(remote(source, place, sems, first + 7 + k, beside))
            if k < lean:
                place = whole.at[at, y, c, :, other]
                self.far.append(remote(place, place, sems, first + 11 + k, beside))
            else:
                place = whole.at[at, 1 - y, c, :, mine]
                self.far.append(remote(place, place, sems, first + 11 + k, across))
        self.core = []
        for step, part in enumerate(
            (
                whole.at[:, y, c, :, mine],
                whole.at[:, y, c, :, other],
                whole.at[:, 1 - y, c, :, mine],
                whole.at[:, 1 - y, c, :, other],
            )
        ):
            self.core.append(remote(part, part, sems, first + 15 + step, twin))

    def send_z(self):
        self.local.start()
        for copy in self.along:
            copy.start()

    def send_own(self):
        self.to_x[0].start()
        self.to_y[0].start()

    def pass_on(self):
        for k in range(1, NZ):
            self.along[k - 1].wait_recv()
            self.to_x[k].start()
            self.to_y[k].start()
        self.local.wait()
        self.core[0].start()

    def turn_corner(self):
        for k in range(NZ):
            (self.to_x if k < self.lean else self.to_y)[k].wait_recv()
            self.far[k].start()
        for k in range(self.lean, NZ):
            self.to_x[k].wait_recv()
        self.core[1].start()
        for k in range(self.lean):
            self.to_y[k].wait_recv()
        self.core[2].start()

    def share(self):
        for copy in self.far:
            copy.wait_recv()
        self.core[3].start()

    def receive(self):
        for copy in self.core:
            copy.wait_recv()

    def finish(self):
        for copy in (*self.along, *self.to_x, *self.to_y, *self.far, *self.core):
            copy.wait_send()


def make_small(vectors, b_up, held, small):
    group = lax.axis_index("dp")
    count, up_count = vectors.shape[1], b_up.shape[1]
    per_row = D // up_count
    held[...] = jnp.zeros_like(held)
    held[0:6, 0:count] = vectors[...].astype(F32)
    held[8:9, 0:up_count] = b_up[...].astype(F32)
    rows = pltpu.roll(held[0:8, :], group * count, 1)
    bias = pltpu.roll(held[8:16, :], (group % per_row) * up_count, 1)[0:1]
    row = lax.broadcasted_iota(jnp.int32, (8, D), 0)
    spot_at = 6 + group // per_row
    top = jnp.where(row < 6, rows, jnp.where(row == spot_at, bias, 0.0))
    small[...] = jnp.concatenate(
        [top, jnp.where(row + 8 == spot_at, bias, 0.0)], axis=0
    ).astype(BF)


def make_table(kind, ground, steps, table):
    wide = steps.shape[1]
    entry = lax.broadcasted_iota(jnp.int32, (64, wide), 0)
    lane = lax.broadcasted_iota(jnp.int32, (64, wide), 1)
    single = kind == 1
    chip = jnp.where(single, 0, entry // 16)
    step = jnp.where(single, entry, entry % 16).astype(F32)
    distance = jnp.zeros((64, wide), F32)
    for slot in range(SLOTS):
        distance = jnp.where(chip == slot, ground[0, slot].astype(F32), distance)
    angle = (step * (distance / 10.0)) * steps[0:1, :]
    exact = jnp.where(lane < wide // 2, jnp.sin(angle), jnp.cos(angle))
    for at, part in enumerate(three_parts(exact)):
        table[at * 64 : (at + 1) * 64, :] = part
    table[192:256, :] = jnp.zeros((64, wide), BF)


def make_pieces(
    groups, bands, waves, wave_table, steps, gen_in, gen_bias, gen_out,
    gen_shift, hidden, slope, codes, made, code_rows, rows, wide, angles,
):
    for wave in range(angles.shape[0]):
        angles[wave : wave + 1, :] = (wave_table[wave] * 1000.0) * steps[0:1, :]
    lane = lax.broadcasted_iota(jnp.int32, angles.shape, 1)
    angle = angles[...]
    angles[...] = jnp.where(lane < GEN // 2, jnp.sin(angle), jnp.cos(angle))
    for sensor in range(SENSORS):
        for band in range(MAXB):
            code_rows[sensor, band : band + 1, :] = angles[pl.ds(waves[sensor, band], 1), :]
        code_rows[sensor, MAXB:16, :] = jnp.zeros((16 - MAXB, GEN), F32)
    flat = code_rows[:, 0:16, :].reshape(SENSORS * 16, GEN)
    before = exact_dot(flat, gen_in[...].astype(F32)) + gen_bias[...].astype(F32)
    values, slopes = gelu_parts(before)
    band_at = lax.broadcasted_iota(jnp.int32, (16, GEN), 0)
    width = gen_out.shape[0]
    owner = lax.axis_index("dp") * 2 + lax.axis_index("fsdp")
    wide[...] = jnp.zeros_like(wide)
    wide[pl.ds(pl.multiple_of((owner * width) % 128, 8), width), :] = gen_out[...].astype(F32)
    gen_shift[...] = wide[...].astype(BF)
    kept = []
    for sensor in range(SENSORS):
        part = slice(sensor * 16, sensor * 16 + 16)
        live = band_at < bands[sensor]
        kept.append(jnp.where(live, values[part], 0.0))
        code_rows[sensor, 16:32, :] = kept[-1].astype(BF).astype(F32)
        code_rows[sensor, 32:48, :] = jnp.where(live, slopes[part], 0.0)
    lower = jnp.concatenate(kept, axis=0).astype(BF)
    for at in range(COVER):
        product = nt_dot(lower, gen_shift[at * 128 : (at + 1) * 128, :])
        for sensor in range(SENSORS):
            rows[sensor, at * MAXB : (at + 1) * MAXB, :] = product[
                sensor * 16 : sensor * 16 + MAXB
            ]
    rows[:, COVER * MAXB :, :] = jnp.zeros((SENSORS, PIECE - COVER * MAXB, 128), F32)
    for group in range(GROUPS):
        made[group // 4, (group // 2) % 2, group % 2] = rows[groups[group]].astype(BF)
    for group in range(GROUPS):
        own = code_rows[groups[group]]
        first = group * MAXB
        codes[first : first + MAXB, :] = own[0:MAXB]
        hidden[first : first + MAXB, :] = own[16 : 16 + MAXB]
        slope[first : first + MAXB, :] = own[32 : 32 + MAXB]


def mask_rows(kind, for_query, for_key):
    row = lax.broadcasted_iota(jnp.int32, (ROWS, 128), 0)
    lane = lax.broadcasted_iota(jnp.int32, (ROWS, 128), 1)
    patch = jnp.where(kind == 1, 0, row // (TOK_DEV // SLOTS))
    segment = jnp.where(row < TOK_DEV, patch, (row - TOK_DEV) // 2)
    hot = (lane == segment) & (row < LIVE)
    for_query[...] = jnp.where(hot, 1.0, 0.0).astype(BF)
    for_key[...] = jnp.where(
        lane < SLOTS, jnp.where(hot, 0.0, -1e30), jnp.where(lane < SLOTS + 3, 1.0, 0.0)
    ).astype(BF)


def attend_pair(pair, qkv, mask_q, mask_k, keys, values, mixed, log_sum):
    lane = lax.broadcasted_iota(jnp.int32, (WIDE, 128), 1)
    lanes = pl.ds(pl.multiple_of(pair * 128, 128), 128)
    keys[:, 0:128] = qkv[6 + pair]
    keys[:, 128:256] = mask_k[...]
    values[:, 0:128] = qkv[12 + pair]
    for tile in range((ROWS // WIDE)):
        first = tile * WIDE
        both = qkv[pair, first : first + WIDE, :] * BF(0.125)
        results, sums = [], []
        for head in range(2):
            query = jnp.where((lane < HEAD) == (head == 0), both, BF(0))
            scores = nt_dot(
                jnp.concatenate([query, mask_q[first : first + WIDE, :]], axis=1), keys[...]
            )
            peak = jnp.max(scores, axis=1, keepdims=True)
            expo = jnp.exp(scores - peak).astype(BF)
            made = nn_dot(expo, values[...])
            totals = made[:, 128:256]
            results.append(made[:, 0:128] / totals)
            sums.append(peak + jnp.log(totals))
        count = min(WIDE, LIVE - first)
        mixed[first : first + count, lanes] = jnp.where(lane < HEAD, *results)[:count].astype(BF)
        log_sum[pair, first : first + WIDE, :] = jnp.where(lane < HEAD, *sums)


def forward_kernel(
    wq, wo, wu, wd, pixels, vectors, b_up, meta_weight, time_loc, gen_in, gen_bias, gen_out,
    wave_steps, place_steps,
    groups, bands, waves, wave_table, kind, ground,
    full_q, full_o, full_u, full_d, params, kernel, tokens, first, qkv, mixed, log_sum,
    gen_shift, hidden, slope, codes,
    made, code_rows, rows, roll, angles, small_held, small, table,
    taken, full_small, flat, wide, keys, values, mask_q, mask_k,
    w_send, w_recv, local_sem, s_send, s_recv, g_send, g_recv,
):
    here = z, y, c, x = spot()
    peers = group_peers(z, y, c, x)
    across = device(z, y, c, 1 - x)
    greet([where for _, where in peers] + [across])
    half = wd.shape[0] // 2
    gathers = q, o, u, d, e = [
        Gather(shard, whole, (w_send, w_recv), local_sem.at[step], Gather.COPIES * step, lean, here)
        for step, (shard, whole, lean) in enumerate(
            (
                (wq, full_q, 4),
                (wo, full_o, 2),
                (wu, full_u, 2),
                (wd.at[0:half], full_d.at[:, :, :, 0:half], 2),
                (wd.at[half : 2 * half], full_d.at[:, :, :, half : 2 * half], 2),
            )
        )
    ]
    s_sems = (s_send, s_recv)
    g_sems = (g_send, g_recv)
    q.send_z()
    for gather in gathers:
        gather.send_own()
    make_pieces(
        groups, bands, waves, wave_table, wave_steps, gen_in, gen_bias, gen_out,
        gen_shift, hidden, slope, codes, made, code_rows, rows, roll, angles,
    )
    make_small(vectors, b_up, small_held, small)
    mask_rows(kind[0], mask_q, mask_k)
    make_table(kind[0], ground, place_steps, table)
    values[:, 128:256] = jnp.ones((ROWS, 128), BF)
    q.pass_on()
    own_made = pltpu.make_async_copy(
        made.at[z, y, c], taken.at[z, y, c, x], local_sem.at[5]
    )
    own_made.start()
    sends = {}
    for (dz, dy, dc), where in peers:
        copy = remote(
            made.at[(z + dz) % NZ, (y + dy) % 2, (c + dc) % 2],
            taken.at[z, y, c, x],
            g_sems,
            dz * 4 + dy * 2 + dc,
            where,
        )
        copy.start()
        sends[dz, dy, dc] = copy
    own_small = pltpu.make_async_copy(small, full_small.at[z, y, c], local_sem.at[6])
    own_small.start()
    small_z = [
        remote(small, full_small.at[z, y, c], s_sems, k - 1, device((z + k) % NZ, y, c, x))
        for k in range(1, NZ)
    ]
    for copy in small_z:
        copy.start()
    q.turn_corner()
    own_made.wait()
    swaps = []
    for dz in range(NZ):
        for dy in range(2):
            for dc in range(2):
                if dz + dy + dc:
                    sends[dz, dy, dc].wait_recv()
        part = taken.at[(z + NZ - dz) % NZ, :, :, x]
        swap = remote(part, part, g_sems, 16 + dz, across)
        swap.start()
        swaps.append(swap)
    u.send_z()
    own_small.wait()
    for copy in small_z:
        copy.wait_recv()
    part = full_small.at[:, y, c]
    small_y = remote(part, part, s_sems, 3, device(z, 1 - y, c, x))
    small_y.start()
    q.share()
    for swap in swaps:
        swap.wait_recv()
    small_y.wait_recv()
    part = full_small.at[:, :, c]
    small_c = remote(part, part, s_sems, 4, device(z, y, 1 - c, x))
    small_c.start()
    u.pass_on()
    d.send_z()
    e.send_z()
    unpack(taken, flat, wide, kernel)
    bias = jnp.concatenate(
        [
            column_sum(flat[(PIX * 6 + part) * MAXB : (PIX * 6 + part + 1) * MAXB, :])
            for part in range(6)
        ],
        axis=1,
    ) / bands[groups[lax.axis_index("dp")]].astype(F32)
    single = kind[0] == 1
    for start, count in BANDS[:-1]:
        band = slice(start, start + count)
        made_rows = nn_dot(pixels[band, :], kernel[...])
        index = start + lax.broadcasted_iota(jnp.int32, (count, 256), 0)
        lane = lax.broadcasted_iota(jnp.int32, (count, 256), 1)
        spread = []
        for spots in (
            jnp.where(single, index // 32, index // 16),
            jnp.where(single, index % 32, index // 256 * 16 + index % 16),
        ):
            hot = (lane % 64 == spots) & (lane < 192)
            spread.append(nn_dot(jnp.where(hot, 1.0, 0.0).astype(BF), table[...]))
        tokens[band, :] = made_rows + bias + jnp.concatenate(spread, axis=1)
    small_c.wait_recv()
    params[...] = jnp.zeros_like(params)
    for n in range(GROUPS):
        params[...] += full_small[n // 4, (n // 2) % 2, n % 2].astype(F32)
    meta = meta_weight[...].astype(F32)
    stamps = exact_dot(time_loc[0], meta[1:])
    for slot in range(SLOTS):
        at = TOK_DEV + 2 * slot
        tokens[at : at + 1, :] = meta[0:1]
        tokens[at + 1 : at + 2, :] = stamps[slot : slot + 1]
    for start, count in BANDS:
        band = slice(start, start + count)
        normed, _ = standard(tokens[band, :])
        first[band, :] = (normed * params[0:1, :] + params[1:2, :]).astype(BF)
    q.receive()
    for start, count in BANDS:
        band = slice(start, start + count)
        for third in range(3):
            part = slice(third * D, (third + 1) * D)
            made_rows = nn_dot(
                first[band, :], full_q[:, :, :, :, part].reshape(D, D)
            ).astype(BF)
            for block in range(6):
                put_rows(
                    qkv.at[third * 6 + block],
                    start,
                    count,
                    made_rows[:, block * 128 : (block + 1) * 128],
                )

    def one_pair(pair, carry):
        @pl.when(pair == 0)
        def _():
            u.turn_corner()

        @pl.when(pair == 1)
        def _():
            d.pass_on()
            e.pass_on()
            o.send_z()

        @pl.when(pair == 2)
        def _():
            u.share()
            o.pass_on()

        @pl.when(pair == 3)
        def _():
            d.turn_corner()
            e.turn_corner()

        @pl.when(pair == 4)
        def _():
            o.turn_corner()
            d.share()

        @pl.when(pair == 5)
        def _():
            e.share()
            o.share()

        attend_pair(pair, qkv, mask_q, mask_k, keys, values, mixed, log_sum)
        return carry

    lax.fori_loop(0, HEADS // 2, one_pair, 0)
    for gather in (o, u, d, e):
        gather.receive()
    for gather in gathers:
        gather.finish()
    for copy in (*small_z, small_y, small_c, *sends.values(), *swaps):
        copy.wait_send()


def forward(shards, operands, scalars):
    anywhere = pl.BlockSpec(memory_space=pl.ANY)
    vmem = pl.BlockSpec(memory_space=pltpu.VMEM)
    smem = pl.BlockSpec(memory_space=pltpu.SMEM)
    blocks = GROUPS * MAXB
    outs = [
        jax.ShapeDtypeStruct((NZ, 2, 2, shard.shape[0], 2 * shard.shape[1]), BF) for shard in shards
    ]
    outs += [
        jax.ShapeDtypeStruct((16, D), F32),
        jax.ShapeDtypeStruct((MAXB * PIX, D), BF),
        jax.ShapeDtypeStruct((LIVE, D), F32),
        jax.ShapeDtypeStruct((LIVE, D), BF),
        jax.ShapeDtypeStruct((18, ROWS, 128), BF),
        jax.ShapeDtypeStruct((LIVE, D), BF),
        jax.ShapeDtypeStruct((HEADS // 2, ROWS, 128), F32),
        jax.ShapeDtypeStruct((COVER * 128, GEN), BF),
        jax.ShapeDtypeStruct((blocks, GEN), F32),
        jax.ShapeDtypeStruct((blocks, GEN), F32),
        jax.ShapeDtypeStruct((blocks, GEN), F32),
    ]
    return pl.pallas_call(
        forward_kernel,
        out_shape=outs,
        in_specs=[anywhere] * 4 + [vmem] * len(operands) + [smem] * len(scalars),
        out_specs=[vmem] + [anywhere] * 3 + [vmem] * 11,
        scratch_shapes=[
            pltpu.VMEM((NZ, 2, 2, PIECE, 128), BF),
            pltpu.VMEM((SENSORS, 48, GEN), F32),
            pltpu.VMEM((SENSORS, PIECE, 128), F32),
            pltpu.VMEM((COVER * 128, GEN), F32),
            pltpu.VMEM((scalars[3].shape[0], GEN), F32),
            pltpu.VMEM((16, D), F32),
            pltpu.VMEM((16, D), BF),
            pltpu.VMEM((256, D // 2), BF),
            pltpu.VMEM((NZ, 2, 2, 2, PIECE, 128), BF),
            pltpu.VMEM((NZ, 2, 2, 16, D), BF),
            pltpu.VMEM((FLAT, 128), F32),
            pltpu.VMEM((6, MAXB * PIX, 128), F32),
            pltpu.VMEM((ROWS, 256), BF),
            pltpu.VMEM((ROWS, 256), BF),
            pltpu.VMEM((ROWS, 128), BF),
            pltpu.VMEM((ROWS, 128), BF),
        ]
        + [pltpu.SemaphoreType.DMA((count,)) for count in (95, 95, 7, 5, 5, 20, 20)],
        compiler_params=pltpu.CompilerParams(
            collective_id=0, has_side_effects=True, vmem_limit_bytes=VMEM_ASK
        ),
    )(*shards, *operands, *scalars)


class Scatter:
    def __init__(self, whole, own, came, low, high, side_x, side_y, last, out, sems, first, here):
        z, y, c, x = here
        self.here, self.own, self.came, self.out = here, own, came, out
        self.low, self.high, self.side_x, self.side_y, self.last = low, high, side_x, side_y, last
        self.mine, self.other = columns(own, x), columns(own, 1 - x)
        mine, other = self.mine, self.other
        across, beside, twin = device(z, y, c, 1 - x), device(z, 1 - y, c, x), device(z, y, 1 - c, x)
        self.local = pltpu.make_async_copy(whole.at[:, :, c], own, sems[2].at[first // 8])
        self.core = remote(whole.at[:, :, 1 - c], came, sems, first, twin)
        self.far_y = remote(own.at[0:2, 1 - y, :, other], low, sems, first + 1, beside)
        self.far_x = remote(own.at[2:4, 1 - y, :, other], high, sems, first + 2, across)
        self.to_x = remote(own.at[:, y, :, other], side_x, sems, first + 3, across)
        self.to_y = remote(own.at[:, 1 - y, :, mine], side_y, sems, first + 4, beside)
        self.along = [
            remote(
                own.at[(z + k) % NZ, y, :, mine], last.at[k - 1], sems, first + 4 + k,
                device((z + k) % NZ, y, c, x),
            )
            for k in range(1, NZ)
        ]

    def stage_a(self):
        self.local.start()
        self.core.start()

    def stage_b(self):
        self.local.wait()
        self.core.wait_recv()
        for at_z in range(NZ):
            for at_y in range(2):
                self.own[at_z, at_y] = self.own[at_z, at_y] + self.came[at_z, at_y]
        self.far_y.start()
        self.far_x.start()

    def stage_c(self):
        _, y, _, _ = self.here
        self.far_y.wait_recv()
        for k in range(2):
            self.own[k, y, :, self.other] = self.own[k, y, :, self.other] + self.low[k]
        self.to_x.start()
        self.far_x.wait_recv()
        for k in range(2):
            self.own[2 + k, 1 - y, :, self.mine] = (
                self.own[2 + k, 1 - y, :, self.mine] + self.high[k]
            )
        self.to_y.start()

    def stage_d(self):
        _, y, _, _ = self.here
        self.to_x.wait_recv()
        self.to_y.wait_recv()
        for k in range(NZ):
            self.own[k, y, :, self.mine] = (
                self.own[k, y, :, self.mine].astype(F32)
                + self.side_x[k].astype(F32)
                + self.side_y[k].astype(F32)
            ).astype(BF)
        for copy in self.along:
            copy.start()

    def stage_e(self):
        z, y, _, _ = self.here
        for copy in self.along:
            copy.wait_recv()
        self.out[...] = (
            self.own[z, y, :, self.mine].astype(F32)
            + self.last[0].astype(F32)
            + self.last[1].astype(F32)
            + self.last[2].astype(F32)
        )
        for copy in (self.core, self.far_y, self.far_x, self.to_x, self.to_y, *self.along):
            copy.wait_send()


class Total:
    COPIES = 7

    def __init__(self, source, out, held, came, slots, send_sem, recv_sem, here):
        z, y, c, x = here
        sems = (send_sem, recv_sem)
        half = source.shape[0] // 2
        self.mine = pl.ds(pl.multiple_of(c * half, 8), half)
        theirs = pl.ds(pl.multiple_of((1 - c) * half, 8), half)
        self.source, self.held, self.came, self.slots, self.out = source, held, came, slots, out
        self.z = z
        twin = device(z, y, 1 - c, x)
        self.steps = [
            remote(source.at[theirs], came.at[0], sems, 0, twin),
            remote(held.at[0], came.at[1], sems, 1, device(z, y, c, 1 - x)),
            remote(held.at[1], came.at[2], sems, 2, device(z, 1 - y, c, x)),
        ]
        self.along = [
            remote(held.at[2], slots.at[z], sems, 2 + k, device((z + k) % NZ, y, c, x))
            for k in range(1, NZ)
        ]
        self.last = remote(out.at[self.mine], out.at[self.mine], sems, 6, twin)

    def begin(self):
        self.steps[0].start()

    def turn(self, step):
        self.steps[step].wait_recv()
        before = self.source[self.mine, :] if step == 0 else self.held[step - 1]
        self.held[step] = before + self.came[step]
        if step < 2:
            self.steps[step + 1].start()
        else:
            self.slots[self.z] = self.held[2]
            for copy in self.along:
                copy.start()

    def close(self):
        for copy in self.along:
            copy.wait_recv()
        self.out[self.mine, :] = self.slots[0] + self.slots[1] + self.slots[2] + self.slots[3]
        self.last.start()

    def finish(self):
        for copy in (*self.steps, *self.along):
            copy.wait_send()
        self.last.wait()


def near(z, y, c, x):
    return [
        device(z, y, c, 1 - x),
        device(z, 1 - y, c, x),
        device(z, y, 1 - c, x),
        *[device((z + k) % NZ, y, c, x) for k in range(1, NZ)],
    ]


def scatter_scratch(rows, width):
    half = width // 2
    return [
        pltpu.VMEM((NZ, 2, rows, width), BF),
        pltpu.VMEM((NZ, 2, rows, width), BF),
        pltpu.VMEM((2, rows, half), BF),
        pltpu.VMEM((2, rows, half), BF),
        pltpu.VMEM((NZ, rows, half), BF),
        pltpu.VMEM((NZ, rows, half), BF),
        pltpu.VMEM((3, rows, half), BF),
    ]


def total_scratch(shape):
    half = (shape[0] // 2,) + shape[1:]
    return [
        pltpu.VMEM((3,) + half, F32),
        pltpu.VMEM((3,) + half, F32),
        pltpu.VMEM((NZ,) + half, F32),
        pltpu.SemaphoreType.DMA((Total.COPIES,)),
        pltpu.SemaphoreType.DMA((Total.COPIES,)),
    ]


def piece_start(owner):
    return (owner * (GENOUT // 32)) // 128


FLAT = (GENOUT // 128) * MAXB


def unpack(taken, flat, wide, kernel):
    flat[...] = jnp.zeros_like(flat)
    used = COVER * MAXB
    for owner in range(32):
        first = piece_start(owner) * MAXB
        count = min(used, FLAT - first)
        piece = taken[owner // 8, (owner // 4) % 2, (owner // 2) % 2, owner % 2]
        flat[first : first + count, :] += piece.astype(F32)[:count]
    for pixel in range(PIX):
        for part in range(6):
            first = (pixel * 6 + part) * MAXB
            wide[part, pl.ds(pixel, MAXB, stride=PIX), :] = flat[first : first + MAXB, :]
    for part in range(6):
        kernel[:, part * 128 : (part + 1) * 128] = wide[part].astype(BF)


def pack(d_kernel, bias, pieces, wide, flat):
    for part in range(6):
        wide[part] = d_kernel[:, part * 128 : (part + 1) * 128]
        first = (PIX * 6 + part) * MAXB
        flat[first : first + MAXB, :] = bias[0:MAXB, part * 128 : (part + 1) * 128]
    flat[FLAT:, :] = jnp.zeros((flat.shape[0] - FLAT, 128), F32)
    for pixel in range(PIX):
        for part in range(6):
            first = (pixel * 6 + part) * MAXB
            flat[first : first + MAXB, :] = wide[part, pl.ds(pixel, MAXB, stride=PIX), :]
    for owner in range(32):
        first = piece_start(owner) * MAXB
        pieces[owner // 8, (owner // 4) % 2, (owner // 2) % 2, owner % 2] = flat[
            first : first + PIECE, :
        ].astype(BF)


def norm_rows_back(value, upstream, gain):
    normed, scale = standard(value)
    scaled = upstream * gain
    inside = (
        scaled
        - jnp.mean(scaled, axis=-1, keepdims=True)
        - normed * jnp.mean(scaled * normed, axis=-1, keepdims=True)
    )
    return scale * inside, column_sum(upstream * normed), column_sum(upstream)


def close_kernel(
    d_qkv, first, w_qkv, tokens, d_after, params, pixels, kernel, time_loc, late,
    hidden, gen_shift, slope, codes, groups, bands,
    out_gen, in_grad, in_bias, out_q, out_meta, out_vectors, out_up, pixel_grad,
    d_tokens, grad_q, pieces, crossed, merged, taken, flat, wide, rows, source, summed, out_grad,
    x_send, x_recv, send_sem, recv_sem, local_sem, q_send, q_recv, *rest,
):
    here = z, y, c, x = spot()
    across = device(z, y, c, 1 - x)
    greet([where for _, where in group_peers(z, y, c, x)] + [across])
    scatter = Scatter(
        grad_q, *rest[5:12], out_q, (q_send, q_recv, local_sem), 0, here
    )
    total = Total(source, summed, *rest[0:5], here)
    gain = shift = jnp.zeros((1, D), F32)
    for start, count in BANDS:
        band = slice(start, start + count)
        upstream = nt_dot(d_qkv[band, :], w_qkv[...].reshape(D, 3 * D))
        d_norm, gain_part, shift_part = norm_rows_back(tokens[band, :], upstream, params[0:1, :])
        gain += gain_part
        shift += shift_part
        d_tokens[band, :] = (d_after[band, :] + d_norm).astype(BF)
    patches = d_tokens[0:TOK_DEV, :]
    d_kernel = inner_dot(pixels[...], patches)
    live = bands[groups[lax.axis_index("dp")]]
    band_at = lax.broadcasted_iota(jnp.int32, (16, D), 0)
    sums = column_sum(patches.astype(F32)) / live.astype(F32)
    pack(d_kernel, jnp.where(band_at < live, sums, 0.0), pieces, wide, flat)
    order = (2, 1, 3, 0)
    swaps = {}
    for dz in order:
        to = (z + dz) % NZ
        swaps[dz] = remote(
            pieces.at[to, :, :, 1 - x], crossed.at[to], (x_send, x_recv), dz, across
        )
    swaps[2].start()
    swaps[1].start()
    sends = []

    def merge(dz):
        to = (z + dz) % NZ
        swaps[dz].wait_recv()
        if dz in (2, 1):
            swaps[{2: 3, 1: 0}[dz]].start()
        for at_y in range(2):
            for at_c in range(2):
                merged[to, at_y, at_c] = (
                    pieces[to, at_y, at_c, x].astype(F32) + crossed[to, at_y, at_c].astype(F32)
                ).astype(BF)
        for dy in range(2):
            for dc in range(2):
                at_y, at_c = (y + dy) % 2, (c + dc) % 2
                if dz + dy + dc:
                    copy = remote(
                        merged.at[to, at_y, at_c],
                        taken.at[z, y, c],
                        (send_sem, recv_sem),
                        dz * 4 + dy * 2 + dc,
                        device(to, at_y, at_c, x),
                    )
                    copy.start()
                    sends.append(copy)
                else:
                    taken[z, y, c] = merged[z, y, c]

    def grad_third(third):
        part = slice(third * D, (third + 1) * D)
        grad_q[:, :, :, :, part] = (
            inner_dot(first[...], d_qkv[:, part]).astype(BF).reshape(NZ, 2, 2, -1, D)
        )

    grad_third(0)
    merge(2)
    grad_third(1)
    merge(1)
    grad_third(2)
    scatter.stage_a()
    merge(3)
    merge(0)
    extra = d_tokens[TOK_DEV:LIVE, :].astype(F32)
    stamps = jnp.concatenate([extra[2 * m + 1 : 2 * m + 2] for m in range(SLOTS)], axis=0)
    first_rows = jnp.concatenate(
        [
            extra[0:1] + extra[2:3] + extra[4:5] + extra[6:7],
            lax.dot_general(
                time_loc[0],
                stamps,
                (((0,), (0,)), ((), ())),
                precision=lax.Precision.HIGHEST,
                preferred_element_type=F32,
            ),
            gain,
            shift,
            jnp.zeros((5, D), F32),
        ],
        axis=0,
    )
    meta_at = GEN + 16
    for part in range(6):
        source[meta_at + part * 16 : meta_at + part * 16 + 16, :] = first_rows[
            :, part * 128 : (part + 1) * 128
        ]
    for start, count in BANDS[:2]:
        band = slice(start, start + count)
        pixel_grad[band, :] = nt_dot(d_tokens[band, :], kernel[...])
    scatter.stage_b()
    for start, count in BANDS[2:4]:
        band = slice(start, start + count)
        pixel_grad[band, :] = nt_dot(d_tokens[band, :], kernel[...])
    scatter.stage_c()
    for copy in sends:
        copy.wait_recv()
    for n in range(GROUPS):
        block = taken[n // 4, (n // 2) % 2, n % 2].astype(F32)
        for at in range(COVER):
            rows[at, n * MAXB : (n + 1) * MAXB, :] = block[at * MAXB : (at + 1) * MAXB]
    d_hidden = jnp.zeros((GROUPS * MAXB, GEN), F32)
    for at in range(COVER):
        d_hidden += nn_dot(rows[at].astype(BF), gen_shift[at * 128 : (at + 1) * 128, :])
    d_before = d_hidden * slope[...]
    source[0:GEN, :] = lax.dot_general(
        codes[...],
        d_before,
        (((0,), (0,)), ((), ())),
        precision=lax.Precision.HIGHEST,
        preferred_element_type=F32,
    )
    source[GEN:meta_at, :] = jnp.broadcast_to(column_sum(d_before), (16, GEN))
    total.begin()
    low = hidden[...].astype(BF)
    for at in range(COVER // 2):
        out_grad[at * 128 : (at + 1) * 128, :] = inner_dot(rows[at].astype(BF), low)
    total.turn(0)
    scatter.stage_d()
    for at in range(COVER // 2, COVER):
        out_grad[at * 128 : (at + 1) * 128, :] = inner_dot(rows[at].astype(BF), low)
    total.turn(1)
    total.turn(2)
    width = out_gen.shape[0]
    group = lax.axis_index("dp")
    owner = group * 2 + x
    out_gen[...] = out_grad[pl.ds(pl.multiple_of((owner * width) % 128, 8), width), :]
    total.close()
    scatter.stage_e()
    total.finish()
    in_grad[...] = summed[0:GEN, :]
    in_bias[...] = summed[GEN : GEN + 1, :]
    all_rows = jnp.concatenate(
        [summed[meta_at + part * 16 : meta_at + part * 16 + 16, :] for part in range(6)], axis=1
    )
    out_meta[...] = all_rows[0:9]
    row = lax.broadcasted_iota(jnp.int32, (8, D), 0)
    count, up_count = out_vectors.shape[1], out_up.shape[1]
    per_row = D // up_count
    norms = jnp.where(
        row == 0, all_rows[9:10], jnp.where(row == 1, all_rows[10:11], late[0:8, :])
    )
    norms = pltpu.roll(norms, (GROUPS - group) % GROUPS * count, 1)
    out_vectors[...] = norms[0:6, 0:count]
    ups = pltpu.roll(late[8:16, :], (per_row - group % per_row) % per_row * up_count, 1)
    out_up[...] = column_sum(jnp.where(row == group // per_row, ups, 0.0))[:, 0:up_count]
    for copy in (*sends, *swaps.values()):
        copy.wait_send()


def closing(operands, scalars, sizes):
    vmem = pl.BlockSpec(memory_space=pltpu.VMEM)
    smem = pl.BlockSpec(memory_space=pltpu.SMEM)
    small = (GEN + 16 + 96, GEN)
    width_gen, rows_in, up_rows = sizes
    held = (NZ, 2, 2, PIECE, 128)
    _, _, _, rows, width = operands[2].shape
    return pl.pallas_call(
        close_kernel,
        in_specs=[vmem] * len(operands) + [smem] * len(scalars),
        out_specs=[vmem] * 8,
        out_shape=[
            jax.ShapeDtypeStruct((width_gen, GEN), F32),
            jax.ShapeDtypeStruct((GEN, GEN), F32),
            jax.ShapeDtypeStruct((1, GEN), F32),
            jax.ShapeDtypeStruct((rows, width // 2), F32),
            jax.ShapeDtypeStruct((9, D), F32),
            jax.ShapeDtypeStruct((6, rows_in), F32),
            jax.ShapeDtypeStruct((1, up_rows), F32),
            jax.ShapeDtypeStruct((TOK_DEV, MAXB * PIX), F32),
        ],
        scratch_shapes=[
            pltpu.VMEM((LIVE, D), BF),
            pltpu.VMEM(operands[2].shape, BF),
            pltpu.VMEM((NZ, 2, 2, 2, PIECE, 128), BF),
            pltpu.VMEM(held, BF),
            pltpu.VMEM(held, BF),
            pltpu.VMEM(held, BF),
            pltpu.VMEM((FLAT + 64, 128), F32),
            pltpu.VMEM((6, MAXB * PIX, 128), F32),
            pltpu.VMEM((COVER, GROUPS * MAXB, 128), F32),
            pltpu.VMEM(small, F32),
            pltpu.VMEM(small, F32),
            pltpu.VMEM((COVER * 128, GEN), F32),
            pltpu.SemaphoreType.DMA((4,)),
            pltpu.SemaphoreType.DMA((4,)),
            pltpu.SemaphoreType.DMA((16,)),
            pltpu.SemaphoreType.DMA((16,)),
            pltpu.SemaphoreType.DMA((1,)),
            pltpu.SemaphoreType.DMA((8,)),
            pltpu.SemaphoreType.DMA((8,)),
            *total_scratch(small),
            *scatter_scratch(rows, width),
        ],
        compiler_params=pltpu.CompilerParams(
            collective_id=2, has_side_effects=True, vmem_limit_bytes=VMEM_ASK
        ),
    )(*operands, *scalars)


def tile_rows(source, first):
    if first + TILE <= LIVE:
        return source[first : first + TILE, :]
    part = source[first:LIVE, :]
    return jnp.concatenate([part, jnp.zeros((first + TILE - LIVE, 128), part.dtype)], axis=0)


def feed_kernel(
    tokens, mixed, top, w_out, vectors, w_up, w_down,
    layer_out, d_after, d_mixed, out_grad, rows, up_grad, down_grad, b_grad,
    second, second_turned, top_full, after, sum_out, sum_second, active, d_upper, proj,
):
    step = pl.program_id(0)

    @pl.when(step == 0)
    def _():
        for first, count in BANDS:
            band = slice(first, first + count)
            value = tokens[band, :] + (nn_dot(mixed[band, :], w_out[...]) + vectors[2:3, :])
            after[band, :] = value
            normed, _ = standard(value)
            put_rows(
                second, first, count, (normed * vectors[3:4, :] + vectors[4:5, :]).astype(BF)
            )
            put_rows(top_full, first, count, top[band, :])
        second_turned[...] = second[...].T
        sum_out[...] = jnp.zeros_like(sum_out)
        b_grad[...] = jnp.zeros_like(b_grad)
        sum_second[...] = jnp.zeros_like(sum_second)

    total = jnp.zeros((1, CHUNK), F32)
    for first, count in BANDS:
        count = -(-count // 16) * 16
        band = slice(first, first + count)
        upper = nn_dot(second[band, :], w_up[...]) + vectors[pl.ds(6 + step, 1), :]
        made, slope = gelu_parts(upper)
        made = made.astype(BF)
        active[band, :] = made
        back = (nt_dot(top_full[band, :], w_down[...]) * slope).astype(BF)
        d_upper[band, :] = back
        total += column_sum(back.astype(F32))
    b_grad[pl.ds(step, 1), :] = total
    sum_out[...] += nn_dot(active[...], w_down[...])
    sum_second[...] += nt_dot(d_upper[...], w_up[...])
    down_grad[...] = inner_dot(active[...], top_full[...]).astype(BF)
    up_grad[...] = nn_dot(second_turned[...], d_upper[...]).astype(BF)

    @pl.when(step == pl.num_programs(0) - 1)
    def _():
        gain = shift = bias = last = jnp.zeros((1, D), F32)
        for first, count in BANDS:
            band = slice(first, first + count)
            value = after[band, :]
            layer_out[band, :] = (value + sum_out[band, :] + vectors[5:6, :]).astype(BF)
            normed, scale = standard(value)
            upstream = sum_second[band, :]
            gain += column_sum(upstream * normed)
            shift += column_sum(upstream)
            scaled = upstream * vectors[3:4, :]
            inside = (
                scaled
                - jnp.mean(scaled, axis=-1, keepdims=True)
                - normed * jnp.mean(scaled * normed, axis=-1, keepdims=True)
            )
            grad_top = top[band, :].astype(F32)
            last += column_sum(grad_top)
            result = grad_top + scale * inside
            d_after[band, :] = result
            low = result.astype(BF)
            bias += column_sum(low.astype(F32))
            put_rows(proj, first, count, low)
            d_mixed[band, :] = nt_dot(low, w_out[...]).astype(BF)
        out_grad[...] = inner_dot(mixed[...], proj[0:LIVE, :]).astype(BF)
        rows[...] = jnp.concatenate([jnp.zeros((2, D), F32), bias, gain, shift, last, jnp.zeros((2, D), F32)], axis=0)


def feed(tokens, mixed, top, w_out, vectors, w_up, w_down):
    width = w_up.shape[1]

    def whole(*shape):
        return pl.BlockSpec(shape, lambda step: (0, 0))

    across = pl.BlockSpec((D, CHUNK), lambda step: (0, step))
    down = pl.BlockSpec((CHUNK, D), lambda step: (step, 0))
    block = whole(LIVE, D)
    return pl.pallas_call(
        feed_kernel,
        grid=(width // CHUNK,),
        in_specs=[block, block, block, whole(D, D), whole(16, D), across, down],
        out_specs=[block, block, block, whole(D, D), whole(8, D), across, down, whole(8, D)],
        out_shape=[
            jax.ShapeDtypeStruct((LIVE, D), BF),
            jax.ShapeDtypeStruct((LIVE, D), F32),
            jax.ShapeDtypeStruct((LIVE, D), BF),
            jax.ShapeDtypeStruct((D, D), BF),
            jax.ShapeDtypeStruct((8, D), F32),
            jax.ShapeDtypeStruct((D, width), BF),
            jax.ShapeDtypeStruct((width, D), BF),
            jax.ShapeDtypeStruct((8, D), F32),
        ],
        scratch_shapes=[
            pltpu.VMEM((ROWS, D), BF),
            pltpu.VMEM((D, ROWS), BF),
            pltpu.VMEM((ROWS, D), BF),
            pltpu.VMEM((LIVE, D), F32),
            pltpu.VMEM((ROWS, D), F32),
            pltpu.VMEM((ROWS, D), F32),
            pltpu.VMEM((ROWS, CHUNK), BF),
            pltpu.VMEM((ROWS, CHUNK), BF),
            pltpu.VMEM((ROWS, D), BF),
        ],
        compiler_params=pltpu.CompilerParams(vmem_limit_bytes=VMEM_ASK),
    )(tokens, mixed, top, w_out, vectors, w_up, w_down)


def three_parts(exact):
    high = exact.astype(BF)
    left = exact - high.astype(F32)
    middle = left.astype(BF)
    return high, middle, (left - middle.astype(F32)).astype(BF)


def attend_back_kernel(
    kind, q_ref, k_ref, v_ref, d_mixed, mixed, log_sum, late, b_grad, go, gu, gd,
    out, out_o, out_u, out_d, out_late,
    mask_q, mask_k, keys, values, keys_turned, d_query, d_keys, d_values, send_sem, recv_sem, local_sem, *rest,
):
    pair, part = pl.program_id(0), pl.program_id(1)
    here = spot()
    half = out_d.shape[0] // 2
    wholes = (go, gu, gd.at[:, :, :, 0:half], gd.at[:, :, :, half : 2 * half])
    results = (out_o, out_u, out_d.at[0:half], out_d.at[half : 2 * half])
    o, u, d, e = [
        Scatter(
            whole, *rest[7 * at : 7 * at + 7], result, (send_sem, recv_sem, local_sem), 8 * at, here
        )
        for at, (whole, result) in enumerate(zip(wholes, results))
    ]
    late_rows, late_sum, *late_rest = rest[28:]
    total = Total(late_rows, late_sum, *late_rest, here)

    def begin_total():
        late_rows[0:8, :] = late[...]
        late_rows[8:16, :] = b_grad[...]
        total.begin()

    plan = {
        0: (lambda: greet(near(*here)), u.stage_a),
        1: (u.stage_b, d.stage_a),
        2: (e.stage_a, o.stage_a, begin_total),
        3: (u.stage_c,),
        4: (lambda: total.turn(0),),
        5: (d.stage_b,),
        6: (d.stage_c, u.stage_d, e.stage_b),
        7: (e.stage_c, lambda: total.turn(1)),
        8: (d.stage_d, o.stage_b),
        9: (e.stage_d, u.stage_e, o.stage_c, lambda: total.turn(2)),
        10: (o.stage_d, d.stage_e),
        11: (total.close,),
    }

    def transfers(half):
        for slot, stages in plan.items():
            if slot % 2 == half:

                @pl.when(pair == slot // 2)
                def _():
                    for stage in stages:
                        stage()

    @pl.when((pair == 5) & (part == 2))
    def _():
        e.stage_e()
        o.stage_e()
        total.finish()
        out_late[...] = late_sum[...]

    lane = lax.broadcasted_iota(jnp.int32, (TILE, 128), 1)
    sub = lax.broadcasted_iota(jnp.int32, (128, TILE), 0)

    def with_parts(exact, rest):
        a, b, c = three_parts(exact)
        return jnp.where(
            lane == SLOTS,
            a,
            jnp.where(lane == SLOTS + 1, b, jnp.where(lane == SLOTS + 2, c, rest)),
        )

    @pl.when(part == 0)
    def _():
        transfers(0)

        @pl.when(pair == 0)
        def _():
            mask_rows(kind[0], mask_q, mask_k)
            keys[:, 128:256] = mask_k[...]
            values[:, 128:256] = mask_k[...]

        keys[:, 0:128] = k_ref[0]
        values[:, 0:128] = v_ref[0]
        keys_turned[...] = keys[:, 0:128].T
        d_keys[...] = jnp.zeros_like(d_keys)
        d_values[...] = jnp.zeros_like(d_values)
        for tile in range(TILES):
            first = tile * TILE
            if tile == 3:
                transfers(1)
            both = q_ref[0, first : first + TILE, :] * BF(0.125)
            up = tile_rows(d_mixed, first)
            logs = log_sum[0, first : first + TILE, :]
            product = up.astype(F32) * tile_rows(mixed, first).astype(F32)
            marks = mask_q[first : first + TILE, :]
            turned = []
            for head in range(2):
                chosen = (lane < HEAD) == (head == 0)
                query = jnp.where(chosen, both, BF(0))
                upstream = jnp.where(chosen, up, BF(0))
                inside = jnp.sum(jnp.where(chosen, product, 0.0), axis=1, keepdims=True)
                wide_query = jnp.concatenate(
                    [query, with_parts(-logs[:, head * HEAD : head * HEAD + 1], marks)], axis=1
                )
                wide_up = jnp.concatenate(
                    [upstream, with_parts(-inside, jnp.zeros_like(marks))], axis=1
                )
                prob = jnp.exp(nt_dot(keys[...], wide_query))
                d_scores = (prob * nt_dot(values[...], wide_up)).astype(BF)
                d_values[...] += nn_dot(prob.astype(BF), upstream)
                d_keys[...] += nn_dot(d_scores, query)
                turned.append(nn_dot(keys_turned[...], d_scores))
            d_query[first : first + TILE, :] = (
                (jnp.where(sub < HEAD, *turned) * 0.125).T.astype(BF)
            )
        out[...] = d_query[0:LIVE, :]

    @pl.when(part == 1)
    def _():
        out[...] = d_keys[0:LIVE, :].astype(BF)

    @pl.when(part == 2)
    def _():
        out[...] = d_values[0:LIVE, :].astype(BF)


def attend_back(kind, qkv, d_mixed, mixed, log_sum, late, b_grad, grads):
    def band(first):
        return pl.BlockSpec((LIVE, 128), lambda pair, part: (0, first + pair))

    def row_block(count):
        return pl.BlockSpec((count, D), lambda pair, part: (0, 0))

    def head(first):
        return pl.BlockSpec((1, ROWS, 128), lambda pair, part: (first + pair, 0, 0))

    shapes = [grad.shape[3:] for grad in grads]
    outs = [(rows, width // 2) for rows, width in shapes]
    low = (shapes[2][0] // 2, shapes[2][1])
    parts = [*shapes[:2], low, low]
    return pl.pallas_call(
        attend_back_kernel,
        grid=(HEADS // 2, 3),
        in_specs=[
            pl.BlockSpec(memory_space=pltpu.SMEM),
            head(0), head(6), head(12), band(0), band(0), head(0), row_block(8), row_block(8),
        ]
        + [pl.BlockSpec(memory_space=pl.ANY)] * 3,
        out_specs=[pl.BlockSpec((LIVE, 128), lambda pair, part: (0, part * 6 + pair))]
        + [pl.BlockSpec(shape, lambda pair, part: (0, 0)) for shape in outs]
        + [row_block(16)],
        out_shape=[
            jax.ShapeDtypeStruct((LIVE, 3 * D), BF),
            *[jax.ShapeDtypeStruct(shape, F32) for shape in outs],
            jax.ShapeDtypeStruct((16, D), F32),
        ],
        scratch_shapes=[
            pltpu.VMEM((ROWS, 128), BF),
            pltpu.VMEM((ROWS, 128), BF),
            pltpu.VMEM((ROWS, 256), BF),
            pltpu.VMEM((ROWS, 256), BF),
            pltpu.VMEM((128, ROWS), BF),
            pltpu.VMEM((ROWS, 128), BF),
            pltpu.VMEM((ROWS, 128), F32),
            pltpu.VMEM((ROWS, 128), F32),
            pltpu.SemaphoreType.DMA((32,)),
            pltpu.SemaphoreType.DMA((32,)),
            pltpu.SemaphoreType.DMA((4,)),
            *[entry for shape in parts for entry in scatter_scratch(*shape)],
            pltpu.VMEM((16, D), F32),
            pltpu.VMEM((16, D), F32),
            *total_scratch((16, D)),
        ],
        compiler_params=pltpu.CompilerParams(
            collective_id=3, has_side_effects=True, vmem_limit_bytes=VMEM_ASK
        ),
    )(kind, qkv, qkv, qkv, d_mixed, mixed, log_sum, late, b_grad, *grads)


def body_block(
    pixels,
    wave_table,
    band_count,
    wave_index,
    group_sensor,
    chip_kind,
    chip_gsd,
    time_loc,
    gen_in,
    gen_bias,
    gen_out,
    meta_weight,
    w_qkv,
    w_out,
    w_up,
    w_down,
    vectors,
    b_up,
    cotangent,
):
    rows, up_rows = vectors.shape[0], b_up.shape[0]

    def steps(count, last):
        falling = 10000.0 ** -(np.arange(count) / last)
        return jnp.asarray(np.tile(np.concatenate([falling, falling]), (8, 1)), F32)

    gen_turned = gen_out.T
    (
        full_q, full_o, full_u, full_d, params, kernel, tokens_in, first, qkv, mixed, log_sum,
        gen_shift, hidden, slope, codes,
    ) = forward(
        (w_qkv, w_out, w_up, w_down),
        (
            pixels,
            vectors.T,
            b_up.reshape(1, -1),
            meta_weight,
            time_loc,
            gen_in,
            gen_bias.reshape(1, -1),
            gen_turned,
            steps(GEN // 2, GEN // 2),
            steps(D // 4, D // 4 - 1),
        ),
        (group_sensor, band_count, wave_index, wave_table, chip_kind, chip_gsd),
    )
    layer_out, d_after, d_mixed, w_out_grad, late, w_up_grad, w_down_grad, b_grad = feed(
        tokens_in,
        mixed,
        cotangent,
        full_o.reshape(D, D),
        params,
        full_u.reshape(D, -1),
        full_d.reshape(-1, D),
    )
    d_qkv, w_out_out, w_up_out, w_down_out, late_sum = attend_back(
        chip_kind,
        qkv,
        d_mixed,
        mixed,
        log_sum,
        late,
        b_grad,
        [
            grad.reshape(NZ, 2, 2, -1, grad.shape[1])
            for grad in (w_out_grad, w_up_grad, w_down_grad)
        ],
    )
    gen_out_grad, gen_in_grad, gen_bias_grad, w_qkv_out, meta_grad, vectors_out, b_up_out, pixel_grad = (
        closing(
            (
                d_qkv,
                first,
                full_q,
                tokens_in,
                d_after,
                params,
                pixels,
                kernel,
                time_loc,
                late_sum,
                hidden,
                gen_shift,
                slope,
                codes,
            ),
            (group_sensor, band_count),
            (gen_turned.shape[0], rows, up_rows),
        )
    )
    return (
        layer_out,
        pixel_grad,
        gen_in_grad,
        gen_bias_grad.reshape(-1),
        gen_out_grad.T,
        meta_grad,
        w_qkv_out,
        w_out_out,
        w_up_out,
        w_down_out,
        vectors_out.T,
        b_up_out.reshape(-1),
    )


def solution(mesh):
    fits = dict(mesh.shape) == {"dp": 16, "fsdp": 2}
    body = body_block if fits else body_general
    placed = (
        P(("dp", "fsdp"), None),
        P(),
        P(),
        P(),
        P(),
        P(("dp", "fsdp")),
        P(("dp", "fsdp"), None),
        P(("dp", "fsdp"), None, None),
        P(),
        P(),
        P(None, ("dp", "fsdp")),
        P(),
        P("dp", "fsdp"),
        P("dp", "fsdp"),
        P("dp", "fsdp"),
        P("dp", "fsdp"),
        P("dp", None),
        P("dp"),
        P(("dp", "fsdp"), None),
    )
    return jax.shard_map(
        body,
        mesh=mesh,
        in_specs=placed,
        out_specs=(
            P(("dp", "fsdp"), None),
            P(("dp", "fsdp"), None),
            P(),
            P(),
            P(None, ("dp", "fsdp")),
            P(),
            P("dp", "fsdp"),
            P("dp", "fsdp"),
            P("dp", "fsdp"),
            P("dp", "fsdp"),
            P("dp", None),
            P("dp"),
        ),
        check_vma=False,
    )
```

```python
import math

import jax
import jax.numpy as jnp
import numpy as np
from jax import lax
from jax.experimental import pallas as pl
from jax.experimental.pallas import tpu as pltpu
from jax.sharding import PartitionSpec as P

D = 768
HEADS = 12
HEAD = 64
GEN = 128
PIX = 64
MAXB = 10
SENSORS = 7
TOK_DEV = 1024
SLOTS = 4
GENOUT = 49920


def exact_dot(left, right):
    return jnp.dot(left, right, precision=lax.Precision.HIGHEST)


def inner_dot(left, right):
    return lax.dot_general(
        left, right, (((0,), (0,)), ((), ())), preferred_element_type=jnp.float32
    )


def outer_dot(left, right):
    return lax.dot_general(
        left, right, (((1,), (1,)), ((), ())), preferred_element_type=jnp.float32
    )


def gelu_exact(values):
    return jax.nn.gelu(values, approximate=False)


def gelu_slope(values, upstream):
    return jax.vjp(gelu_exact, values)[1](upstream)[0]


def table_lookup(indices, table):
    return jnp.sum(
        jnp.where(
            indices[:, None] == jnp.arange(table.shape[0], dtype=jnp.int32)[None, :],
            table[None, :],
            0.0,
        ),
        axis=1,
    )


def wave_code(wavelengths):
    half = GEN // 2
    omega = 1.0 / 10000.0 ** (jnp.arange(half, dtype=jnp.float32) / half)
    angle = (wavelengths * 1000.0)[:, None] * omega[None, :]
    return jnp.concatenate([jnp.sin(angle), jnp.cos(angle)], axis=1)


def place_code(kind_one, gsd_one):
    small = TOK_DEV // SLOTS
    index = jnp.arange(TOK_DEV, dtype=jnp.int32)
    within = jnp.where(kind_one == 1, index, index % small)
    side = jnp.where(kind_one == 1, math.isqrt(TOK_DEV), math.isqrt(small)).astype(jnp.int32)
    across = (within // side).astype(jnp.float32)
    along = (within % side).astype(jnp.float32)
    holder = jnp.where(kind_one == 1, 0, index // small)
    ground = (
        jnp.sum(
            jnp.where(
                holder[:, None] == jnp.arange(SLOTS, dtype=jnp.int32)[None, :], gsd_one[None, :], 0
            ),
            axis=1,
        ).astype(jnp.float32)
        / 10.0
    )
    quarter = D // 4
    omega = 1.0 / 10000.0 ** (jnp.arange(quarter, dtype=jnp.float32) / (quarter - 1))
    first = (across * ground)[:, None] * omega[None, :]
    second = (along * ground)[:, None] * omega[None, :]
    return jnp.concatenate(
        [jnp.sin(first), jnp.cos(first), jnp.sin(second), jnp.cos(second)], axis=1
    )


def segment_ids(kind_one):
    index = jnp.arange(TOK_DEV, dtype=jnp.int32)
    patches = jnp.where(kind_one == 1, 0, index // (TOK_DEV // SLOTS))
    extra = jnp.arange(2 * SLOTS, dtype=jnp.int32) // 2
    return jnp.concatenate([patches, extra])


def layer_norm(values, gain, shift):
    centred = values - jnp.mean(values, axis=-1, keepdims=True)
    scale = lax.rsqrt(jnp.mean(centred * centred, axis=-1, keepdims=True) + 1e-05)
    normed = centred * scale
    return (normed * gain + shift, normed, scale)


def norm_back(upstream, normed, scale, gain):
    gain_grad = jnp.sum(upstream * normed, axis=0)
    shift_grad = jnp.sum(upstream, axis=0)
    scaled = upstream * gain
    inside = (
        scaled
        - jnp.mean(scaled, axis=-1, keepdims=True)
        - normed * jnp.mean(scaled * normed, axis=-1, keepdims=True)
    )
    return (scale * inside, gain_grad, shift_grad)


def body_general(
    pixels,
    wave_table,
    band_count,
    wave_index,
    group_sensor,
    chip_kind,
    chip_gsd,
    time_loc,
    gen_in,
    gen_bias,
    gen_out,
    meta_weight,
    w_qkv,
    w_out,
    w_up,
    w_down,
    vectors,
    b_up,
    cotangent,
):
    half_type = jnp.bfloat16
    group = lax.axis_index("dp")
    sensor = jnp.sum(
        jnp.where(jnp.arange(group_sensor.shape[0], dtype=jnp.int32) == group, group_sensor, 0)
    )
    chosen_sensor = jnp.arange(SENSORS, dtype=jnp.int32) == sensor
    band_total = jnp.sum(jnp.where(chosen_sensor, band_count, 0))
    gen_in_full = gen_in.astype(jnp.float32)
    gen_bias_full = gen_bias.astype(jnp.float32)
    codes = wave_code(table_lookup(wave_index.reshape(-1), wave_table))
    before = exact_dot(codes, gen_in_full) + gen_bias_full
    hidden = gelu_exact(before).astype(half_type)
    shard_made = jnp.dot(hidden, gen_out, preferred_element_type=jnp.float32).astype(half_type)
    all_made = lax.all_gather(shard_made, ("dp", "fsdp"), axis=1, tiled=True)
    generated = lax.dynamic_slice_in_dim(all_made, sensor * MAXB, MAXB, 0)
    live_band = (jnp.arange(MAXB, dtype=jnp.int32) < band_total)[:, None]
    kernel = jnp.where(live_band, generated[:, : PIX * D], jnp.zeros((), half_type)).reshape(
        MAXB * PIX, D
    )
    band_float = band_total.astype(jnp.float32)
    embed_bias = (
        jnp.sum(jnp.where(live_band, generated[:, PIX * D :].astype(jnp.float32), 0.0), axis=0)
        / band_float
    )
    kind_one = chip_kind[0]
    patches = (
        jnp.dot(pixels, kernel, preferred_element_type=jnp.float32)
        + embed_bias
        + place_code(kind_one, chip_gsd[0])
    )
    meta_full = meta_weight.astype(jnp.float32)
    stamps = exact_dot(time_loc[0], meta_full[1:])
    classes = jnp.broadcast_to(meta_full[0], stamps.shape)
    extra = jnp.stack([classes, stamps], axis=1).reshape(2 * SLOTS, D)
    tokens_in = jnp.concatenate([patches, extra], axis=0)
    total_rows = tokens_in.shape[0]
    qkv_rows, out_rows, up_rows, down_rows, vectors_all, b_up_all = (
        lax.all_gather(w_qkv, "dp", axis=0, tiled=True),
        lax.all_gather(w_out, "dp", axis=0, tiled=True),
        lax.all_gather(w_up, "dp", axis=0, tiled=True),
        lax.all_gather(w_down, "dp", axis=0, tiled=True),
        lax.all_gather(vectors, "dp", axis=0, tiled=True),
        lax.all_gather(b_up, "dp", axis=0, tiled=True),
    )
    w_qkv_all, w_out_all, w_up_all, w_down_all = (
        lax.all_gather(qkv_rows, "fsdp", axis=1, tiled=True),
        lax.all_gather(out_rows, "fsdp", axis=1, tiled=True),
        lax.all_gather(up_rows, "fsdp", axis=1, tiled=True),
        lax.all_gather(down_rows, "fsdp", axis=1, tiled=True),
    )
    vector_full = vectors_all.astype(jnp.float32)
    b_up_full = b_up_all.astype(jnp.float32)
    first_norm, normed_one, scale_one = layer_norm(tokens_in, vector_full[:, 0], vector_full[:, 1])
    first = first_norm.astype(half_type)
    qkv = jnp.dot(first, w_qkv_all, preferred_element_type=jnp.float32).astype(half_type)
    query = qkv[:, :D].reshape(total_rows, HEADS, HEAD)
    keys = qkv[:, D : 2 * D].reshape(total_rows, HEADS, HEAD)
    values = qkv[:, 2 * D :].reshape(total_rows, HEADS, HEAD)
    segment = segment_ids(kind_one)
    same = (segment[:, None] == segment[None, :])[None]
    scores = jnp.einsum("qhd,khd->hqk", query, keys, preferred_element_type=jnp.float32) * HEAD ** (
        -0.5
    )
    scores = jnp.where(same, scores, -1e30)
    peak = jnp.max(scores, axis=-1, keepdims=True)
    expo = jnp.exp(scores - peak)
    totals = jnp.sum(expo, axis=-1, keepdims=True)
    prob_half = (expo / totals).astype(half_type)
    mixed = (
        jnp.einsum("hqk,khd->qhd", prob_half, values, preferred_element_type=jnp.float32)
        .reshape(total_rows, D)
        .astype(half_type)
    )
    after = tokens_in + (
        jnp.dot(mixed, w_out_all, preferred_element_type=jnp.float32) + vector_full[:, 2]
    )
    second_norm, normed_two, scale_two = layer_norm(after, vector_full[:, 3], vector_full[:, 4])
    second = second_norm.astype(half_type)
    upper = jnp.dot(second, w_up_all, preferred_element_type=jnp.float32) + b_up_full
    active = gelu_exact(upper).astype(half_type)
    layer_out = (
        after + jnp.dot(active, w_down_all, preferred_element_type=jnp.float32) + vector_full[:, 5]
    ).astype(half_type)
    grad_top = cotangent.astype(jnp.float32)
    w_down_grad = inner_dot(active, cotangent)
    down_bias_grad = jnp.sum(grad_top, axis=0)
    d_active = outer_dot(cotangent, w_down_all)
    d_upper = gelu_slope(upper, d_active).astype(half_type)
    w_up_grad = inner_dot(second, d_upper)
    b_up_grad = jnp.sum(d_upper.astype(jnp.float32), axis=0)
    d_second = outer_dot(d_upper, w_up_all)
    d_after_norm, gain_two_grad, shift_two_grad = norm_back(
        d_second, normed_two, scale_two, vector_full[:, 3]
    )
    d_after = grad_top + d_after_norm
    d_proj = d_after.astype(half_type)
    w_out_grad = inner_dot(mixed, d_proj)
    out_bias_grad = jnp.sum(d_proj.astype(jnp.float32), axis=0)
    d_mixed = outer_dot(d_proj, w_out_all).astype(half_type).reshape(total_rows, HEADS, HEAD)
    again = jnp.einsum("qhd,khd->hqk", query, keys, preferred_element_type=jnp.float32) * HEAD ** (
        -0.5
    )
    again = jnp.where(same, again, -1e30)
    prob_full = jnp.exp(again - peak) / totals
    recalled = prob_full.astype(half_type)
    d_values = jnp.einsum("hqk,qhd->khd", recalled, d_mixed, preferred_element_type=jnp.float32)
    d_prob = jnp.einsum("qhd,khd->hqk", d_mixed, values, preferred_element_type=jnp.float32)
    d_scores = prob_full * (d_prob - jnp.sum(d_prob * prob_full, axis=-1, keepdims=True))
    d_scores = jnp.where(same, d_scores, 0.0).astype(half_type)
    d_query = jnp.einsum(
        "hqk,khd->qhd", d_scores, keys, preferred_element_type=jnp.float32
    ) * HEAD ** (-0.5)
    d_keys = jnp.einsum(
        "hqk,qhd->khd", d_scores, query, preferred_element_type=jnp.float32
    ) * HEAD ** (-0.5)
    d_qkv = jnp.concatenate(
        [
            d_query.reshape(total_rows, D),
            d_keys.reshape(total_rows, D),
            d_values.reshape(total_rows, D),
        ],
        axis=1,
    ).astype(half_type)
    w_qkv_grad = inner_dot(first, d_qkv)
    d_first = outer_dot(d_qkv, w_qkv_all)
    d_tokens_norm, gain_one_grad, shift_one_grad = norm_back(
        d_first, normed_one, scale_one, vector_full[:, 0]
    )
    d_tokens = (d_after + d_tokens_norm).astype(half_type)
    vectors_grad = jnp.stack(
        [
            gain_one_grad,
            shift_one_grad,
            out_bias_grad,
            gain_two_grad,
            shift_two_grad,
            down_bias_grad,
        ],
        axis=1,
    )
    d_patches = d_tokens[:TOK_DEV]
    d_extra = d_tokens[TOK_DEV:].astype(jnp.float32).reshape(SLOTS, 2, D)
    pixel_grad = outer_dot(d_patches, kernel)
    class_grad = jnp.sum(d_extra[:, 0], axis=0)
    stamp_grad = exact_dot(time_loc[0].T, d_extra[:, 1])
    meta_part = jnp.concatenate([class_grad[None, :], stamp_grad], axis=0)
    d_kernel = inner_dot(pixels, d_patches).reshape(MAXB, PIX * D)
    d_kernel = jnp.where(live_band, d_kernel, 0.0)
    d_bias = jnp.sum(d_patches.astype(jnp.float32), axis=0) / band_float
    d_bias_rows = jnp.where(live_band, d_bias[None, :], 0.0)
    d_generated = jnp.concatenate([d_kernel, d_bias_rows], axis=1).astype(half_type)
    placed = jnp.where(
        chosen_sensor[:, None, None], d_generated.astype(jnp.float32)[None], 0.0
    ).reshape(SENSORS * MAXB, GENOUT)
    columns = lax.psum_scatter(placed, ("dp", "fsdp"), scatter_dimension=1, tiled=True)
    gen_out_grad = exact_dot(hidden.astype(jnp.float32).T, columns)
    d_hidden = exact_dot(columns, gen_out.astype(jnp.float32).T)
    d_before = gelu_slope(before, d_hidden)
    gen_in_part = exact_dot(codes.T, d_before)
    gen_bias_part = jnp.sum(d_before, axis=0)
    meta_grad, gen_in_grad, gen_bias_grad = lax.psum(
        (meta_part, gen_in_part, gen_bias_part), ("dp", "fsdp")
    )
    qkv_cols, out_cols, up_cols, down_cols = (
        lax.psum_scatter(
            w_qkv_grad.astype(jnp.bfloat16), "fsdp", scatter_dimension=1, tiled=True
        ).astype(jnp.float32),
        lax.psum_scatter(
            w_out_grad.astype(jnp.bfloat16), "fsdp", scatter_dimension=1, tiled=True
        ).astype(jnp.float32),
        lax.psum_scatter(
            w_up_grad.astype(jnp.bfloat16), "fsdp", scatter_dimension=1, tiled=True
        ).astype(jnp.float32),
        lax.psum_scatter(
            w_down_grad.astype(jnp.bfloat16), "fsdp", scatter_dimension=1, tiled=True
        ).astype(jnp.float32),
    )
    vectors_group, b_up_group = lax.psum((vectors_grad, b_up_grad), "fsdp")
    w_qkv_out, w_out_out, w_up_out, w_down_out, vectors_out, b_up_out = (
        lax.psum_scatter(
            qkv_cols.astype(jnp.bfloat16), "dp", scatter_dimension=0, tiled=True
        ).astype(jnp.float32),
        lax.psum_scatter(
            out_cols.astype(jnp.bfloat16), "dp", scatter_dimension=0, tiled=True
        ).astype(jnp.float32),
        lax.psum_scatter(
            up_cols.astype(jnp.bfloat16), "dp", scatter_dimension=0, tiled=True
        ).astype(jnp.float32),
        lax.psum_scatter(
            down_cols.astype(jnp.bfloat16), "dp", scatter_dimension=0, tiled=True
        ).astype(jnp.float32),
        lax.psum_scatter(
            vectors_group.astype(jnp.bfloat16), "dp", scatter_dimension=0, tiled=True
        ).astype(jnp.float32),
        lax.psum_scatter(
            b_up_group.astype(jnp.bfloat16), "dp", scatter_dimension=0, tiled=True
        ).astype(jnp.float32),
    )
    return (
        layer_out,
        pixel_grad,
        gen_in_grad,
        gen_bias_grad,
        gen_out_grad,
        meta_grad,
        w_qkv_out,
        w_out_out,
        w_up_out,
        w_down_out,
        vectors_out,
        b_up_out,
    )


LIVE = 1032
ROWS = 1040
TILE = 208
TILES = 5
WIDE = 520
NZ = 4
GROUPS = 16
PIECE = 144
COVER = 14
VMEM_ASK = 60 * 1024 * 1024
BF = jnp.bfloat16
F32 = jnp.float32


def nt_dot(left, right):
    return lax.dot_general(left, right, (((1,), (1,)), ((), ())), preferred_element_type=F32)


def nn_dot(left, right):
    return lax.dot_general(left, right, (((1,), (0,)), ((), ())), preferred_element_type=F32)


def spot():
    group = lax.axis_index("dp")
    return group // 4, (group // 2) % 2, group % 2, lax.axis_index("fsdp")


def device(z, y, c, x):
    return {"dp": z * 4 + y * 2 + c, "fsdp": x}


def remote(source, target, sems, slot, where):
    return pltpu.make_async_remote_copy(
        src_ref=source,
        dst_ref=target,
        send_sem=sems[0].at[slot],
        recv_sem=sems[1].at[slot],
        device_id=where,
        device_id_type=pl.DeviceIdType.MESH,
    )


def greet(others):
    barrier = pltpu.get_barrier_semaphore()
    for where in others:
        pl.semaphore_signal(
            barrier, inc=1, device_id=where, device_id_type=pl.DeviceIdType.MESH
        )
    pl.semaphore_wait(barrier, len(others))


def columns(ref, x):
    width = ref.shape[-1] // 2
    return pl.ds(pl.multiple_of(x * width, 128), width)


def group_peers(z, y, c, x):
    return [
        ((dz, dy, dc), device((z + dz) % NZ, (y + dy) % 2, (c + dc) % 2, x))
        for dz in range(NZ)
        for dy in range(2)
        for dc in range(2)
        if dz + dy + dc
    ]


CHUNK = 768
BANDS = ((0, 256), (256, 256), (512, 256), (768, 256), (1024, 8))


def gelu_parts(values):
    bell = jnp.exp(values * values * (-0.5))
    step = 1.0 / (1.0 + (0.3275911 * math.sqrt(0.5)) * jnp.abs(values))
    poly = 0.5 * 1.061405429 * step - 0.5 * 1.453152027
    poly = poly * step + 0.5 * 1.421413741
    poly = poly * step - 0.5 * 0.284496736
    poly = poly * step + 0.5 * 0.254829592
    tail = poly * step * bell
    below = jnp.where(values < 0.0, tail, 1.0 - tail)
    return values * below, below + values * bell * (1.0 / math.sqrt(2.0 * math.pi))


def standard(values):
    centred = values - jnp.mean(values, axis=-1, keepdims=True)
    scale = lax.rsqrt(jnp.mean(centred * centred, axis=-1, keepdims=True) + 1e-05)
    return centred * scale, scale


def column_sum(values):
    return jnp.sum(values, axis=0, keepdims=True)


def put_rows(target, first, count, values):
    if count % 16:
        values = jnp.concatenate(
            [values, jnp.zeros((16 - count % 16, values.shape[1]), values.dtype)], axis=0
        )
    target[first : first + values.shape[0], :] = values


class Gather:
    COPIES = 19

    def __init__(self, shard, whole, sems, local, first, lean, here):
        z, y, c, x = here
        self.lean = lean
        mine, other = columns(whole, x), columns(whole, 1 - x)
        across, beside, twin = device(z, y, c, 1 - x), device(z, 1 - y, c, x), device(z, y, 1 - c, x)
        target = whole.at[z, y, c, :, mine]
        self.local = pltpu.make_async_copy(shard, target, local)
        self.along = [
            remote(shard, target, sems, first + k - 1, device((z + k) % NZ, y, c, x))
            for k in range(1, NZ)
        ]
        self.to_x, self.to_y, self.far = [], [], []
        for k in range(NZ):
            at = (z + NZ - k) % NZ
            place = whole.at[at, y, c, :, mine]
            source = place if k else shard
            self.to_x.append(remote(source, place, sems, first + 3 + k, across))
            self.to_y.append(remote(source, place, sems, first + 7 + k, beside))
            if k < lean:
                place = whole.at[at, y, c, :, other]
                self.far.append(remote(place, place, sems, first + 11 + k, beside))
            else:
                place = whole.at[at, 1 - y, c, :, mine]
                self.far.append(remote(place, place, sems, first + 11 + k, across))
        self.core = []
        for step, part in enumerate(
            (
                whole.at[:, y, c, :, mine],
                whole.at[:, y, c, :, other],
                whole.at[:, 1 - y, c, :, mine],
                whole.at[:, 1 - y, c, :, other],
            )
        ):
            self.core.append(remote(part, part, sems, first + 15 + step, twin))

    def send_z(self):
        self.local.start()
        for copy in self.along:
            copy.start()

    def send_own(self):
        self.to_x[0].start()
        self.to_y[0].start()

    def pass_on(self):
        for k in range(1, NZ):
            self.along[k - 1].wait_recv()
            self.to_x[k].start()
            self.to_y[k].start()
        self.local.wait()
        self.core[0].start()

    def turn_corner(self):
        for k in range(NZ):
            (self.to_x if k < self.lean else self.to_y)[k].wait_recv()
            self.far[k].start()
        for k in range(self.lean, NZ):
            self.to_x[k].wait_recv()
        self.core[1].start()
        for k in range(self.lean):
            self.to_y[k].wait_recv()
        self.core[2].start()

    def share(self):
        for copy in self.far:
            copy.wait_recv()
        self.core[3].start()

    def receive(self):
        for copy in self.core:
            copy.wait_recv()

    def finish(self):
        for copy in (*self.along, *self.to_x, *self.to_y, *self.far, *self.core):
            copy.wait_send()


def make_small(vectors, b_up, held, small):
    group = lax.axis_index("dp")
    count, up_count = vectors.shape[1], b_up.shape[0]
    per_row = D // up_count
    held[...] = jnp.zeros_like(held)
    held[0:6, 0:count] = vectors[...].astype(F32)
    held[8:9, 0:up_count] = b_up[...].astype(F32).reshape(1, up_count)
    rows = pltpu.roll(held[0:8, :], group * count, 1)
    bias = pltpu.roll(held[8:16, :], (group % per_row) * up_count, 1)[0:1]
    row = lax.broadcasted_iota(jnp.int32, (8, D), 0)
    spot_at = 6 + group // per_row
    top = jnp.where(row < 6, rows, jnp.where(row == spot_at, bias, 0.0))
    small[...] = jnp.concatenate(
        [top, jnp.where(row + 8 == spot_at, bias, 0.0)], axis=0
    ).astype(BF)


def make_table(kind, ground, steps, table):
    wide = steps.shape[1]
    entry = lax.broadcasted_iota(jnp.int32, (64, wide), 0)
    lane = lax.broadcasted_iota(jnp.int32, (64, wide), 1)
    single = kind == 1
    chip = jnp.where(single, 0, entry // 16)
    step = jnp.where(single, entry, entry % 16).astype(F32)
    distance = jnp.zeros((64, wide), F32)
    for slot in range(SLOTS):
        distance = jnp.where(chip == slot, ground[0, slot].astype(F32), distance)
    angle = (step * (distance / 10.0)) * steps[0:1, :]
    exact = jnp.where(lane < wide // 2, jnp.sin(angle), jnp.cos(angle))
    for at, part in enumerate(three_parts(exact)):
        table[at * 64 : (at + 1) * 64, :] = part
    table[192:256, :] = jnp.zeros((64, wide), BF)


def make_pieces(
    groups, bands, waves, wave_table, steps, gen_in, gen_bias, gen_out,
    gen_shift, hidden, slope, codes, made, code_rows, rows, wide, angles,
):
    for wave in range(angles.shape[0]):
        angles[wave : wave + 1, :] = (wave_table[wave] * 1000.0) * steps[0:1, :]
    lane = lax.broadcasted_iota(jnp.int32, angles.shape, 1)
    angle = angles[...]
    angles[...] = jnp.where(lane < GEN // 2, jnp.sin(angle), jnp.cos(angle))
    for sensor in range(SENSORS):
        for band in range(MAXB):
            code_rows[sensor, band : band + 1, :] = angles[pl.ds(waves[sensor, band], 1), :]
        code_rows[sensor, MAXB:16, :] = jnp.zeros((16 - MAXB, GEN), F32)
    flat = code_rows[:, 0:16, :].reshape(SENSORS * 16, GEN)
    before = exact_dot(flat, gen_in[...].astype(F32)) + gen_bias[...].astype(F32)
    values, slopes = gelu_parts(before)
    band_at = lax.broadcasted_iota(jnp.int32, (16, GEN), 0)
    width = gen_out.shape[0]
    owner = lax.axis_index("dp") * 2 + lax.axis_index("fsdp")
    wide[...] = jnp.zeros_like(wide)
    wide[pl.ds(pl.multiple_of((owner * width) % 128, 8), width), :] = gen_out[...].astype(F32)
    gen_shift[...] = wide[...].astype(BF)
    kept = []
    for sensor in range(SENSORS):
        part = slice(sensor * 16, sensor * 16 + 16)
        live = band_at < bands[sensor]
        kept.append(jnp.where(live, values[part], 0.0))
        code_rows[sensor, 16:32, :] = kept[-1].astype(BF).astype(F32)
        code_rows[sensor, 32:48, :] = jnp.where(live, slopes[part], 0.0)
    lower = jnp.concatenate(kept, axis=0).astype(BF)
    for at in range(COVER):
        product = nt_dot(lower, gen_shift[at * 128 : (at + 1) * 128, :])
        for sensor in range(SENSORS):
            rows[sensor, at * MAXB : (at + 1) * MAXB, :] = product[
                sensor * 16 : sensor * 16 + MAXB
            ]
    rows[:, COVER * MAXB :, :] = jnp.zeros((SENSORS, PIECE - COVER * MAXB, 128), F32)
    for group in range(GROUPS):
        made[group // 4, (group // 2) % 2, group % 2] = rows[groups[group]].astype(BF)
    for group in range(GROUPS):
        own = code_rows[groups[group]]
        first = group * MAXB
        codes[first : first + MAXB, :] = own[0:MAXB]
        hidden[first : first + MAXB, :] = own[16 : 16 + MAXB]
        slope[first : first + MAXB, :] = own[32 : 32 + MAXB]


def mask_rows(kind, for_query, for_key):
    row = lax.broadcasted_iota(jnp.int32, (ROWS, 128), 0)
    lane = lax.broadcasted_iota(jnp.int32, (ROWS, 128), 1)
    patch = jnp.where(kind == 1, 0, row // (TOK_DEV // SLOTS))
    segment = jnp.where(row < TOK_DEV, patch, (row - TOK_DEV) // 2)
    hot = (lane == segment) & (row < LIVE)
    for_query[...] = jnp.where(hot, 1.0, 0.0).astype(BF)
    for_key[...] = jnp.where(
        lane < SLOTS, jnp.where(hot, 0.0, -1e30), jnp.where(lane < SLOTS + 3, 1.0, 0.0)
    ).astype(BF)


def attend_pair(pair, qkv, mask_q, mask_k, keys, values, mixed, log_sum):
    lane = lax.broadcasted_iota(jnp.int32, (WIDE, 128), 1)
    lanes = pl.ds(pl.multiple_of(pair * 128, 128), 128)
    keys[:, 0:128] = qkv[6 + pair]
    keys[:, 128:256] = mask_k[...]
    values[:, 0:128] = qkv[12 + pair]
    for tile in range((ROWS // WIDE)):
        first = tile * WIDE
        both = qkv[pair, first : first + WIDE, :] * BF(0.125)
        results, sums = [], []
        for head in range(2):
            query = jnp.where((lane < HEAD) == (head == 0), both, BF(0))
            scores = nt_dot(
                jnp.concatenate([query, mask_q[first : first + WIDE, :]], axis=1), keys[...]
            )
            peak = jnp.max(scores, axis=1, keepdims=True)
            expo = jnp.exp(scores - peak).astype(BF)
            made = nn_dot(expo, values[...])
            totals = made[:, 128:256]
            results.append(made[:, 0:128] / totals)
            sums.append(peak + jnp.log(totals))
        count = min(WIDE, LIVE - first)
        mixed[first : first + count, lanes] = jnp.where(lane < HEAD, *results)[:count].astype(BF)
        log_sum[pair, first : first + WIDE, :] = jnp.where(lane < HEAD, *sums)


def forward_kernel(
    wq, wo, wu, wd, pixels, vectors, b_up, meta_weight, time_loc, gen_in, gen_bias, gen_out,
    wave_steps, place_steps,
    groups, bands, waves, wave_table, kind, ground,
    full_q, full_o, full_u, full_d, params, kernel, tokens, first, qkv, mixed, log_sum,
    gen_shift, hidden, slope, codes,
    made, code_rows, rows, roll, angles, small_held, small, table,
    taken, full_small, flat, wide, keys, values, mask_q, mask_k,
    w_send, w_recv, local_sem, s_send, s_recv, g_send, g_recv,
):
    here = z, y, c, x = spot()
    peers = group_peers(z, y, c, x)
    across = device(z, y, c, 1 - x)
    greet([where for _, where in peers] + [across])
    half = wd.shape[0] // 2
    gathers = q, o, u, d, e = [
        Gather(shard, whole, (w_send, w_recv), local_sem.at[step], Gather.COPIES * step, lean, here)
        for step, (shard, whole, lean) in enumerate(
            (
                (wq, full_q, 4),
                (wo, full_o, 2),
                (wu, full_u, 2),
                (wd.at[0:half], full_d.at[:, :, :, 0:half], 2),
                (wd.at[half : 2 * half], full_d.at[:, :, :, half : 2 * half], 2),
            )
        )
    ]
    s_sems = (s_send, s_recv)
    g_sems = (g_send, g_recv)
    q.send_z()
    for gather in gathers:
        gather.send_own()
    make_pieces(
        groups, bands, waves, wave_table, wave_steps, gen_in, gen_bias, gen_out,
        gen_shift, hidden, slope, codes, made, code_rows, rows, roll, angles,
    )
    make_small(vectors, b_up, small_held, small)
    mask_rows(kind[0], mask_q, mask_k)
    make_table(kind[0], ground, place_steps, table)
    values[:, 128:256] = jnp.ones((ROWS, 128), BF)
    q.pass_on()
    own_made = pltpu.make_async_copy(
        made.at[z, y, c], taken.at[z, y, c, x], local_sem.at[5]
    )
    own_made.start()
    sends = {}
    for (dz, dy, dc), where in peers:
        copy = remote(
            made.at[(z + dz) % NZ, (y + dy) % 2, (c + dc) % 2],
            taken.at[z, y, c, x],
            g_sems,
            dz * 4 + dy * 2 + dc,
            where,
        )
        copy.start()
        sends[dz, dy, dc] = copy
    own_small = pltpu.make_async_copy(small, full_small.at[z, y, c], local_sem.at[6])
    own_small.start()
    small_z = [
        remote(small, full_small.at[z, y, c], s_sems, k - 1, device((z + k) % NZ, y, c, x))
        for k in range(1, NZ)
    ]
    for copy in small_z:
        copy.start()
    q.turn_corner()
    own_made.wait()
    swaps = []
    for dz in range(NZ):
        for dy in range(2):
            for dc in range(2):
                if dz + dy + dc:
                    sends[dz, dy, dc].wait_recv()
        part = taken.at[(z + NZ - dz) % NZ, :, :, x]
        swap = remote(part, part, g_sems, 16 + dz, across)
        swap.start()
        swaps.append(swap)
    u.send_z()
    own_small.wait()
    for copy in small_z:
        copy.wait_recv()
    part = full_small.at[:, y, c]
    small_y = remote(part, part, s_sems, 3, device(z, 1 - y, c, x))
    small_y.start()
    q.share()
    for swap in swaps:
        swap.wait_recv()
    small_y.wait_recv()
    part = full_small.at[:, :, c]
    small_c = remote(part, part, s_sems, 4, device(z, y, 1 - c, x))
    small_c.start()
    u.pass_on()
    d.send_z()
    e.send_z()
    unpack(taken, flat, wide, kernel)
    bias = jnp.concatenate(
        [
            column_sum(flat[(PIX * 6 + part) * MAXB : (PIX * 6 + part + 1) * MAXB, :])
            for part in range(6)
        ],
        axis=1,
    ) / bands[groups[lax.axis_index("dp")]].astype(F32)
    single = kind[0] == 1
    for start, count in BANDS[:-1]:
        band = slice(start, start + count)
        made_rows = nn_dot(pixels[band, :], kernel[...])
        index = start + lax.broadcasted_iota(jnp.int32, (count, 256), 0)
        lane = lax.broadcasted_iota(jnp.int32, (count, 256), 1)
        spread = []
        for spots in (
            jnp.where(single, index // 32, index // 16),
            jnp.where(single, index % 32, index // 256 * 16 + index % 16),
        ):
            hot = (lane % 64 == spots) & (lane < 192)
            spread.append(nn_dot(jnp.where(hot, 1.0, 0.0).astype(BF), table[...]))
        tokens[band, :] = made_rows + bias + jnp.concatenate(spread, axis=1)
    small_c.wait_recv()
    params[...] = jnp.zeros_like(params)
    for n in range(GROUPS):
        params[...] += full_small[n // 4, (n // 2) % 2, n % 2].astype(F32)
    meta = meta_weight[...].astype(F32)
    stamps = exact_dot(time_loc[0], meta[1:])
    for slot in range(SLOTS):
        at = TOK_DEV + 2 * slot
        tokens[at : at + 1, :] = meta[0:1]
        tokens[at + 1 : at + 2, :] = stamps[slot : slot + 1]
    for start, count in BANDS:
        band = slice(start, start + count)
        normed, _ = standard(tokens[band, :])
        first[band, :] = (normed * params[0:1, :] + params[1:2, :]).astype(BF)
    q.receive()
    for start, count in BANDS:
        band = slice(start, start + count)
        for third in range(3):
            part = slice(third * D, (third + 1) * D)
            made_rows = nn_dot(
                first[band, :], full_q[:, :, :, :, part].reshape(D, D)
            ).astype(BF)
            for block in range(6):
                put_rows(
                    qkv.at[third * 6 + block],
                    start,
                    count,
                    made_rows[:, block * 128 : (block + 1) * 128],
                )

    def one_pair(pair, carry):
        @pl.when(pair == 0)
        def _():
            u.turn_corner()

        @pl.when(pair == 1)
        def _():
            d.pass_on()
            e.pass_on()
            o.send_z()

        @pl.when(pair == 2)
        def _():
            u.share()
            o.pass_on()

        @pl.when(pair == 3)
        def _():
            d.turn_corner()
            e.turn_corner()

        @pl.when(pair == 4)
        def _():
            o.turn_corner()
            d.share()

        @pl.when(pair == 5)
        def _():
            e.share()
            o.share()

        attend_pair(pair, qkv, mask_q, mask_k, keys, values, mixed, log_sum)
        return carry

    lax.fori_loop(0, HEADS // 2, one_pair, 0)
    for gather in (o, u, d, e):
        gather.receive()
    for gather in gathers:
        gather.finish()
    for copy in (*small_z, small_y, small_c, *sends.values(), *swaps):
        copy.wait_send()


def forward(shards, operands, scalars):
    anywhere = pl.BlockSpec(memory_space=pl.ANY)
    vmem = pl.BlockSpec(memory_space=pltpu.VMEM)
    smem = pl.BlockSpec(memory_space=pltpu.SMEM)
    blocks = GROUPS * MAXB
    outs = [
        jax.ShapeDtypeStruct((NZ, 2, 2, shard.shape[0], 2 * shard.shape[1]), BF) for shard in shards
    ]
    outs += [
        jax.ShapeDtypeStruct((16, D), F32),
        jax.ShapeDtypeStruct((MAXB * PIX, D), BF),
        jax.ShapeDtypeStruct((LIVE, D), F32),
        jax.ShapeDtypeStruct((LIVE, D), BF),
        jax.ShapeDtypeStruct((18, ROWS, 128), BF),
        jax.ShapeDtypeStruct((LIVE, D), BF),
        jax.ShapeDtypeStruct((HEADS // 2, ROWS, 128), F32),
        jax.ShapeDtypeStruct((COVER * 128, GEN), BF),
        jax.ShapeDtypeStruct((blocks, GEN), F32),
        jax.ShapeDtypeStruct((blocks, GEN), F32),
        jax.ShapeDtypeStruct((blocks, GEN), F32),
    ]
    return pl.pallas_call(
        forward_kernel,
        out_shape=outs,
        in_specs=[anywhere] * 4 + [vmem] * len(operands) + [smem] * len(scalars),
        out_specs=[vmem] + [anywhere] * 3 + [vmem] * 11,
        scratch_shapes=[
            pltpu.VMEM((NZ, 2, 2, PIECE, 128), BF),
            pltpu.VMEM((SENSORS, 48, GEN), F32),
            pltpu.VMEM((SENSORS, PIECE, 128), F32),
            pltpu.VMEM((COVER * 128, GEN), F32),
            pltpu.VMEM((scalars[3].shape[0], GEN), F32),
            pltpu.VMEM((16, D), F32),
            pltpu.VMEM((16, D), BF),
            pltpu.VMEM((256, D // 2), BF),
            pltpu.VMEM((NZ, 2, 2, 2, PIECE, 128), BF),
            pltpu.VMEM((NZ, 2, 2, 16, D), BF),
            pltpu.VMEM((FLAT, 128), F32),
            pltpu.VMEM((6, MAXB * PIX, 128), F32),
            pltpu.VMEM((ROWS, 256), BF),
            pltpu.VMEM((ROWS, 256), BF),
            pltpu.VMEM((ROWS, 128), BF),
            pltpu.VMEM((ROWS, 128), BF),
        ]
        + [pltpu.SemaphoreType.DMA((count,)) for count in (95, 95, 7, 5, 5, 20, 20)],
        compiler_params=pltpu.CompilerParams(
            collective_id=0, has_side_effects=True, vmem_limit_bytes=VMEM_ASK
        ),
    )(*shards, *operands, *scalars)


class Scatter:
    def __init__(self, whole, own, came, low, high, side_x, side_y, last, out, sems, first, here):
        z, y, c, x = here
        self.here, self.own, self.came, self.out = here, own, came, out
        self.low, self.high, self.side_x, self.side_y, self.last = low, high, side_x, side_y, last
        self.mine, self.other = columns(own, x), columns(own, 1 - x)
        mine, other = self.mine, self.other
        across, beside, twin = device(z, y, c, 1 - x), device(z, 1 - y, c, x), device(z, y, 1 - c, x)
        self.local = pltpu.make_async_copy(whole.at[:, :, c], own, sems[2].at[first // 8])
        self.core = remote(whole.at[:, :, 1 - c], came, sems, first, twin)
        self.far_y = remote(own.at[0:2, 1 - y, :, other], low, sems, first + 1, beside)
        self.far_x = remote(own.at[2:4, 1 - y, :, other], high, sems, first + 2, across)
        self.to_x = remote(own.at[:, y, :, other], side_x, sems, first + 3, across)
        self.to_y = remote(own.at[:, 1 - y, :, mine], side_y, sems, first + 4, beside)
        self.along = [
            remote(
                own.at[(z + k) % NZ, y, :, mine], last.at[k - 1], sems, first + 4 + k,
                device((z + k) % NZ, y, c, x),
            )
            for k in range(1, NZ)
        ]

    def stage_a(self):
        self.local.start()
        self.core.start()

    def stage_b(self):
        self.local.wait()
        self.core.wait_recv()
        for at_z in range(NZ):
            for at_y in range(2):
                self.own[at_z, at_y] = self.own[at_z, at_y] + self.came[at_z, at_y]
        self.far_y.start()
        self.far_x.start()

    def stage_c(self):
        _, y, _, _ = self.here
        self.far_y.wait_recv()
        for k in range(2):
            self.own[k, y, :, self.other] = self.own[k, y, :, self.other] + self.low[k]
        self.to_x.start()
        self.far_x.wait_recv()
        for k in range(2):
            self.own[2 + k, 1 - y, :, self.mine] = (
                self.own[2 + k, 1 - y, :, self.mine] + self.high[k]
            )
        self.to_y.start()

    def stage_d(self):
        _, y, _, _ = self.here
        self.to_x.wait_recv()
        self.to_y.wait_recv()
        for k in range(NZ):
            self.own[k, y, :, self.mine] = (
                self.own[k, y, :, self.mine].astype(F32)
                + self.side_x[k].astype(F32)
                + self.side_y[k].astype(F32)
            ).astype(BF)
        for copy in self.along:
            copy.start()

    def stage_e(self):
        z, y, _, _ = self.here
        for copy in self.along:
            copy.wait_recv()
        self.out[...] = (
            self.own[z, y, :, self.mine].astype(F32)
            + self.last[0].astype(F32)
            + self.last[1].astype(F32)
            + self.last[2].astype(F32)
        )
        for copy in (self.core, self.far_y, self.far_x, self.to_x, self.to_y, *self.along):
            copy.wait_send()


class Total:
    COPIES = 7

    def __init__(self, source, out, held, came, slots, send_sem, recv_sem, here):
        z, y, c, x = here
        sems = (send_sem, recv_sem)
        half = source.shape[0] // 2
        self.mine = pl.ds(pl.multiple_of(c * half, 8), half)
        theirs = pl.ds(pl.multiple_of((1 - c) * half, 8), half)
        self.source, self.held, self.came, self.slots, self.out = source, held, came, slots, out
        self.z = z
        twin = device(z, y, 1 - c, x)
        self.steps = [
            remote(source.at[theirs], came.at[0], sems, 0, twin),
            remote(held.at[0], came.at[1], sems, 1, device(z, y, c, 1 - x)),
            remote(held.at[1], came.at[2], sems, 2, device(z, 1 - y, c, x)),
        ]
        self.along = [
            remote(held.at[2], slots.at[z], sems, 2 + k, device((z + k) % NZ, y, c, x))
            for k in range(1, NZ)
        ]
        self.last = remote(out.at[self.mine], out.at[self.mine], sems, 6, twin)

    def begin(self):
        self.steps[0].start()

    def turn(self, step):
        self.steps[step].wait_recv()
        before = self.source[self.mine, :] if step == 0 else self.held[step - 1]
        self.held[step] = before + self.came[step]
        if step < 2:
            self.steps[step + 1].start()
        else:
            self.slots[self.z] = self.held[2]
            for copy in self.along:
                copy.start()

    def close(self):
        for copy in self.along:
            copy.wait_recv()
        self.out[self.mine, :] = self.slots[0] + self.slots[1] + self.slots[2] + self.slots[3]
        self.last.start()

    def finish(self):
        for copy in (*self.steps, *self.along):
            copy.wait_send()
        self.last.wait()


def near(z, y, c, x):
    return [
        device(z, y, c, 1 - x),
        device(z, 1 - y, c, x),
        device(z, y, 1 - c, x),
        *[device((z + k) % NZ, y, c, x) for k in range(1, NZ)],
    ]


def scatter_scratch(rows, width):
    half = width // 2
    return [
        pltpu.VMEM((NZ, 2, rows, width), BF),
        pltpu.VMEM((NZ, 2, rows, width), BF),
        pltpu.VMEM((2, rows, half), BF),
        pltpu.VMEM((2, rows, half), BF),
        pltpu.VMEM((NZ, rows, half), BF),
        pltpu.VMEM((NZ, rows, half), BF),
        pltpu.VMEM((3, rows, half), BF),
    ]


def total_scratch(shape):
    half = (shape[0] // 2,) + shape[1:]
    return [
        pltpu.VMEM((3,) + half, F32),
        pltpu.VMEM((3,) + half, F32),
        pltpu.VMEM((NZ,) + half, F32),
        pltpu.SemaphoreType.DMA((Total.COPIES,)),
        pltpu.SemaphoreType.DMA((Total.COPIES,)),
    ]


def piece_start(owner):
    return (owner * (GENOUT // 32)) // 128


FLAT = (GENOUT // 128) * MAXB


def unpack(taken, flat, wide, kernel):
    flat[...] = jnp.zeros_like(flat)
    used = COVER * MAXB
    for owner in range(32):
        first = piece_start(owner) * MAXB
        count = min(used, FLAT - first)
        piece = taken[owner // 8, (owner // 4) % 2, (owner // 2) % 2, owner % 2]
        flat[first : first + count, :] += piece.astype(F32)[:count]
    for pixel in range(PIX):
        for part in range(6):
            first = (pixel * 6 + part) * MAXB
            wide[part, pl.ds(pixel, MAXB, stride=PIX), :] = flat[first : first + MAXB, :]
    for part in range(6):
        kernel[:, part * 128 : (part + 1) * 128] = wide[part].astype(BF)


def pack(d_kernel, bias, pieces, wide, flat):
    for part in range(6):
        wide[part] = d_kernel[:, part * 128 : (part + 1) * 128]
        first = (PIX * 6 + part) * MAXB
        flat[first : first + MAXB, :] = bias[0:MAXB, part * 128 : (part + 1) * 128]
    flat[FLAT:, :] = jnp.zeros((flat.shape[0] - FLAT, 128), F32)
    for pixel in range(PIX):
        for part in range(6):
            first = (pixel * 6 + part) * MAXB
            flat[first : first + MAXB, :] = wide[part, pl.ds(pixel, MAXB, stride=PIX), :]
    for owner in range(32):
        first = piece_start(owner) * MAXB
        pieces[owner // 8, (owner // 4) % 2, (owner // 2) % 2, owner % 2] = flat[
            first : first + PIECE, :
        ].astype(BF)


def norm_rows_back(value, upstream, gain):
    normed, scale = standard(value)
    scaled = upstream * gain
    inside = (
        scaled
        - jnp.mean(scaled, axis=-1, keepdims=True)
        - normed * jnp.mean(scaled * normed, axis=-1, keepdims=True)
    )
    return scale * inside, column_sum(upstream * normed), column_sum(upstream)


def close_kernel(
    d_qkv, first, w_qkv, tokens, d_after, params, pixels, kernel, time_loc, late,
    hidden, gen_shift, slope, codes, groups, bands,
    out_gen, in_grad, in_bias, out_q, out_meta, out_vectors, out_up, pixel_grad,
    d_tokens, grad_q, pieces, crossed, merged, taken, flat, wide, rows, source, summed, out_grad,
    x_send, x_recv, send_sem, recv_sem, local_sem, q_send, q_recv, *rest,
):
    here = z, y, c, x = spot()
    across = device(z, y, c, 1 - x)
    greet([where for _, where in group_peers(z, y, c, x)] + [across])
    scatter = Scatter(
        grad_q, *rest[5:12], out_q, (q_send, q_recv, local_sem), 0, here
    )
    total = Total(source, summed, *rest[0:5], here)
    gain = shift = jnp.zeros((1, D), F32)
    for start, count in BANDS:
        band = slice(start, start + count)
        upstream = nt_dot(d_qkv[band, :], w_qkv[...].reshape(D, 3 * D))
        d_norm, gain_part, shift_part = norm_rows_back(tokens[band, :], upstream, params[0:1, :])
        gain += gain_part
        shift += shift_part
        d_tokens[band, :] = (d_after[band, :] + d_norm).astype(BF)
    patches = d_tokens[0:TOK_DEV, :]
    d_kernel = inner_dot(pixels[...], patches)
    live = bands[groups[lax.axis_index("dp")]]
    band_at = lax.broadcasted_iota(jnp.int32, (16, D), 0)
    sums = column_sum(patches.astype(F32)) / live.astype(F32)
    pack(d_kernel, jnp.where(band_at < live, sums, 0.0), pieces, wide, flat)
    order = (2, 1, 3, 0)
    swaps = {}
    for dz in order:
        to = (z + dz) % NZ
        swaps[dz] = remote(
            pieces.at[to, :, :, 1 - x], crossed.at[to], (x_send, x_recv), dz, across
        )
    swaps[2].start()
    swaps[1].start()
    sends = []

    def merge(dz):
        to = (z + dz) % NZ
        swaps[dz].wait_recv()
        if dz in (2, 1):
            swaps[{2: 3, 1: 0}[dz]].start()
        for at_y in range(2):
            for at_c in range(2):
                merged[to, at_y, at_c] = (
                    pieces[to, at_y, at_c, x].astype(F32) + crossed[to, at_y, at_c].astype(F32)
                ).astype(BF)
        for dy in range(2):
            for dc in range(2):
                at_y, at_c = (y + dy) % 2, (c + dc) % 2
                if dz + dy + dc:
                    copy = remote(
                        merged.at[to, at_y, at_c],
                        taken.at[z, y, c],
                        (send_sem, recv_sem),
                        dz * 4 + dy * 2 + dc,
                        device(to, at_y, at_c, x),
                    )
                    copy.start()
                    sends.append(copy)
                else:
                    taken[z, y, c] = merged[z, y, c]

    def grad_third(third):
        part = slice(third * D, (third + 1) * D)
        grad_q[:, :, :, :, part] = (
            inner_dot(first[...], d_qkv[:, part]).astype(BF).reshape(NZ, 2, 2, -1, D)
        )

    grad_third(0)
    merge(2)
    grad_third(1)
    merge(1)
    grad_third(2)
    scatter.stage_a()
    merge(3)
    merge(0)
    extra = d_tokens[TOK_DEV:LIVE, :].astype(F32)
    stamps = jnp.concatenate([extra[2 * m + 1 : 2 * m + 2] for m in range(SLOTS)], axis=0)
    first_rows = jnp.concatenate(
        [
            extra[0:1] + extra[2:3] + extra[4:5] + extra[6:7],
            lax.dot_general(
                time_loc[0],
                stamps,
                (((0,), (0,)), ((), ())),
                precision=lax.Precision.HIGHEST,
                preferred_element_type=F32,
            ),
            gain,
            shift,
            jnp.zeros((5, D), F32),
        ],
        axis=0,
    )
    meta_at = GEN + 16
    for part in range(6):
        source[meta_at + part * 16 : meta_at + part * 16 + 16, :] = first_rows[
            :, part * 128 : (part + 1) * 128
        ]
    for start, count in BANDS[:2]:
        band = slice(start, start + count)
        pixel_grad[band, :] = nt_dot(d_tokens[band, :], kernel[...])
    scatter.stage_b()
    for start, count in BANDS[2:4]:
        band = slice(start, start + count)
        pixel_grad[band, :] = nt_dot(d_tokens[band, :], kernel[...])
    scatter.stage_c()
    for copy in sends:
        copy.wait_recv()
    for n in range(GROUPS):
        block = taken[n // 4, (n // 2) % 2, n % 2].astype(F32)
        for at in range(COVER):
            rows[at, n * MAXB : (n + 1) * MAXB, :] = block[at * MAXB : (at + 1) * MAXB]
    d_hidden = jnp.zeros((GROUPS * MAXB, GEN), F32)
    for at in range(COVER):
        d_hidden += nn_dot(rows[at].astype(BF), gen_shift[at * 128 : (at + 1) * 128, :])
    d_before = d_hidden * slope[...]
    source[0:GEN, :] = lax.dot_general(
        codes[...],
        d_before,
        (((0,), (0,)), ((), ())),
        precision=lax.Precision.HIGHEST,
        preferred_element_type=F32,
    )
    source[GEN:meta_at, :] = jnp.broadcast_to(column_sum(d_before), (16, GEN))
    total.begin()
    low = hidden[...].astype(BF)
    for at in range(COVER // 2):
        out_grad[at * 128 : (at + 1) * 128, :] = inner_dot(rows[at].astype(BF), low)
    total.turn(0)
    scatter.stage_d()
    for at in range(COVER // 2, COVER):
        out_grad[at * 128 : (at + 1) * 128, :] = inner_dot(rows[at].astype(BF), low)
    total.turn(1)
    total.turn(2)
    width = out_gen.shape[0]
    group = lax.axis_index("dp")
    owner = group * 2 + x
    out_gen[...] = out_grad[pl.ds(pl.multiple_of((owner * width) % 128, 8), width), :]
    total.close()
    scatter.stage_e()
    total.finish()
    in_grad[...] = summed[0:GEN, :]
    in_bias[...] = summed[GEN : GEN + 1, :]
    all_rows = jnp.concatenate(
        [summed[meta_at + part * 16 : meta_at + part * 16 + 16, :] for part in range(6)], axis=1
    )
    out_meta[...] = all_rows[0:9]
    row = lax.broadcasted_iota(jnp.int32, (8, D), 0)
    count, up_count = out_vectors.shape[1], out_up.shape[1]
    per_row = D // up_count
    norms = jnp.where(
        row == 0, all_rows[9:10], jnp.where(row == 1, all_rows[10:11], late[0:8, :])
    )
    norms = pltpu.roll(norms, (GROUPS - group) % GROUPS * count, 1)
    out_vectors[...] = norms[0:6, 0:count]
    ups = pltpu.roll(late[8:16, :], (per_row - group % per_row) % per_row * up_count, 1)
    out_up[...] = column_sum(jnp.where(row == group // per_row, ups, 0.0))[:, 0:up_count]
    for copy in (*sends, *swaps.values()):
        copy.wait_send()


def closing(operands, scalars, sizes):
    vmem = pl.BlockSpec(memory_space=pltpu.VMEM)
    smem = pl.BlockSpec(memory_space=pltpu.SMEM)
    small = (GEN + 16 + 96, GEN)
    width_gen, rows_in, up_rows = sizes
    held = (NZ, 2, 2, PIECE, 128)
    _, _, _, rows, width = operands[2].shape
    return pl.pallas_call(
        close_kernel,
        in_specs=[vmem] * len(operands) + [smem] * len(scalars),
        out_specs=[vmem] * 8,
        out_shape=[
            jax.ShapeDtypeStruct((width_gen, GEN), F32),
            jax.ShapeDtypeStruct((GEN, GEN), F32),
            jax.ShapeDtypeStruct((1, GEN), F32),
            jax.ShapeDtypeStruct((rows, width // 2), F32),
            jax.ShapeDtypeStruct((9, D), F32),
            jax.ShapeDtypeStruct((6, rows_in), F32),
            jax.ShapeDtypeStruct((1, up_rows), F32),
            jax.ShapeDtypeStruct((TOK_DEV, MAXB * PIX), F32),
        ],
        scratch_shapes=[
            pltpu.VMEM((LIVE, D), BF),
            pltpu.VMEM(operands[2].shape, BF),
            pltpu.VMEM((NZ, 2, 2, 2, PIECE, 128), BF),
            pltpu.VMEM(held, BF),
            pltpu.VMEM(held, BF),
            pltpu.VMEM(held, BF),
            pltpu.VMEM((FLAT + 64, 128), F32),
            pltpu.VMEM((6, MAXB * PIX, 128), F32),
            pltpu.VMEM((COVER, GROUPS * MAXB, 128), F32),
            pltpu.VMEM(small, F32),
            pltpu.VMEM(small, F32),
            pltpu.VMEM((COVER * 128, GEN), F32),
            pltpu.SemaphoreType.DMA((4,)),
            pltpu.SemaphoreType.DMA((4,)),
            pltpu.SemaphoreType.DMA((16,)),
            pltpu.SemaphoreType.DMA((16,)),
            pltpu.SemaphoreType.DMA((1,)),
            pltpu.SemaphoreType.DMA((8,)),
            pltpu.SemaphoreType.DMA((8,)),
            *total_scratch(small),
            *scatter_scratch(rows, width),
        ],
        compiler_params=pltpu.CompilerParams(
            collective_id=2, has_side_effects=True, vmem_limit_bytes=VMEM_ASK
        ),
    )(*operands, *scalars)


def tile_rows(source, first):
    if first + TILE <= LIVE:
        return source[first : first + TILE, :]
    part = source[first:LIVE, :]
    return jnp.concatenate([part, jnp.zeros((first + TILE - LIVE, 128), part.dtype)], axis=0)


def feed_kernel(
    tokens, mixed, top, w_out, vectors, w_up, w_down,
    layer_out, d_after, d_mixed, out_grad, rows, up_grad, down_grad, b_grad,
    second, second_turned, top_full, after, sum_out, sum_second, active, d_upper, proj, wide_up, wide_back,
):
    step = pl.program_id(0)

    @pl.when(step == 0)
    def _():
        for first, count in BANDS:
            band = slice(first, first + count)
            value = tokens[band, :] + (nn_dot(mixed[band, :], w_out[...]) + vectors[2:3, :])
            after[band, :] = value
            normed, _ = standard(value)
            put_rows(
                second, first, count, (normed * vectors[3:4, :] + vectors[4:5, :]).astype(BF)
            )
            put_rows(top_full, first, count, top[band, :])
        second_turned[...] = second[...].T
        sum_out[...] = jnp.zeros_like(sum_out)
        b_grad[...] = jnp.zeros_like(b_grad)
        sum_second[...] = jnp.zeros_like(sum_second)

    wide_up[...] = nn_dot(second[...], w_up[...])
    wide_back[...] = nt_dot(top_full[...], w_down[...])
    total = jnp.zeros((1, CHUNK), F32)
    for first, count in BANDS:
        count = -(-count // 16) * 16
        band = slice(first, first + count)
        upper = wide_up[band, :] + vectors[pl.ds(6 + step, 1), :]
        made, slope = gelu_parts(upper)
        made = made.astype(BF)
        active[band, :] = made
        back = (wide_back[band, :] * slope).astype(BF)
        d_upper[band, :] = back
        total += column_sum(back.astype(F32))
    b_grad[pl.ds(step, 1), :] = total
    sum_out[...] += nn_dot(active[...], w_down[...])
    sum_second[...] += nt_dot(d_upper[...], w_up[...])
    down_grad[...] = inner_dot(active[...], top_full[...]).astype(BF)
    up_grad[...] = nn_dot(second_turned[...], d_upper[...]).astype(BF)

    @pl.when(step == pl.num_programs(0) - 1)
    def _():
        gain = shift = bias = last = jnp.zeros((1, D), F32)
        for first, count in BANDS:
            band = slice(first, first + count)
            value = after[band, :]
            layer_out[band, :] = (value + sum_out[band, :] + vectors[5:6, :]).astype(BF)
            normed, scale = standard(value)
            upstream = sum_second[band, :]
            gain += column_sum(upstream * normed)
            shift += column_sum(upstream)
            scaled = upstream * vectors[3:4, :]
            inside = (
                scaled
                - jnp.mean(scaled, axis=-1, keepdims=True)
                - normed * jnp.mean(scaled * normed, axis=-1, keepdims=True)
            )
            grad_top = top[band, :].astype(F32)
            last += column_sum(grad_top)
            result = grad_top + scale * inside
            d_after[band, :] = result
            low = result.astype(BF)
            bias += column_sum(low.astype(F32))
            put_rows(proj, first, count, low)
            d_mixed[band, :] = nt_dot(low, w_out[...]).astype(BF)
        out_grad[...] = inner_dot(mixed[...], proj[0:LIVE, :]).astype(BF)
        rows[...] = jnp.concatenate([jnp.zeros((2, D), F32), bias, gain, shift, last, jnp.zeros((2, D), F32)], axis=0)


def feed(tokens, mixed, top, w_out, vectors, w_up, w_down):
    width = w_up.shape[1]

    def whole(*shape):
        return pl.BlockSpec(shape, lambda step: (0, 0), pipeline_mode=pl.Buffered(1))

    across = pl.BlockSpec((D, CHUNK), lambda step: (0, step))
    down = pl.BlockSpec((CHUNK, D), lambda step: (step, 0))
    block = whole(LIVE, D)
    return pl.pallas_call(
        feed_kernel,
        grid=(width // CHUNK,),
        in_specs=[block, block, block, whole(D, D), whole(16, D), across, down],
        out_specs=[pl.BlockSpec((LIVE, D), lambda step: (0, 0))] * 3 + [pl.BlockSpec((D, D), lambda step: (0, 0)), pl.BlockSpec((8, D), lambda step: (0, 0)), across, down, pl.BlockSpec((8, D), lambda step: (0, 0))],
        out_shape=[
            jax.ShapeDtypeStruct((LIVE, D), BF),
            jax.ShapeDtypeStruct((LIVE, D), F32),
            jax.ShapeDtypeStruct((LIVE, D), BF),
            jax.ShapeDtypeStruct((D, D), BF),
            jax.ShapeDtypeStruct((8, D), F32),
            jax.ShapeDtypeStruct((D, width), BF),
            jax.ShapeDtypeStruct((width, D), BF),
            jax.ShapeDtypeStruct((8, D), F32),
        ],
        scratch_shapes=[
            pltpu.VMEM((ROWS, D), BF),
            pltpu.VMEM((D, ROWS), BF),
            pltpu.VMEM((ROWS, D), BF),
            pltpu.VMEM((LIVE, D), F32),
            pltpu.VMEM((ROWS, D), F32),
            pltpu.VMEM((ROWS, D), F32),
            pltpu.VMEM((ROWS, CHUNK), BF),
            pltpu.VMEM((ROWS, CHUNK), BF),
            pltpu.VMEM((ROWS, D), BF),
            pltpu.VMEM((ROWS, CHUNK), F32),
            pltpu.VMEM((ROWS, CHUNK), F32),
        ],
        compiler_params=pltpu.CompilerParams(vmem_limit_bytes=VMEM_ASK),
    )(tokens, mixed, top, w_out, vectors, w_up, w_down)


def three_parts(exact):
    high = exact.astype(BF)
    left = exact - high.astype(F32)
    middle = left.astype(BF)
    return high, middle, (left - middle.astype(F32)).astype(BF)


def attend_back_kernel(
    kind, q_ref, k_ref, v_ref, d_mixed, mixed, log_sum, late, b_grad, go, gu, gd,
    out, out_o, out_u, out_d, out_late,
    mask_q, mask_k, keys, values, keys_turned, d_query, d_keys, d_values, send_sem, recv_sem, local_sem, *rest,
):
    pair, part = pl.program_id(0), pl.program_id(1)
    here = spot()
    half = out_d.shape[0] // 2
    wholes = (go, gu, gd.at[:, :, :, 0:half], gd.at[:, :, :, half : 2 * half])
    results = (out_o, out_u, out_d.at[0:half], out_d.at[half : 2 * half])
    o, u, d, e = [
        Scatter(
            whole, *rest[7 * at : 7 * at + 7], result, (send_sem, recv_sem, local_sem), 8 * at, here
        )
        for at, (whole, result) in enumerate(zip(wholes, results))
    ]
    late_rows, late_sum, *late_rest = rest[28:]
    total = Total(late_rows, late_sum, *late_rest, here)

    def begin_total():
        late_rows[0:8, :] = late[...]
        late_rows[8:16, :] = b_grad[...]
        total.begin()

    plan = {
        0: (lambda: greet(near(*here)), u.stage_a),
        1: (u.stage_b, d.stage_a),
        2: (e.stage_a, o.stage_a, begin_total),
        3: (u.stage_c,),
        4: (lambda: total.turn(0),),
        5: (d.stage_b,),
        6: (d.stage_c, u.stage_d, e.stage_b),
        7: (e.stage_c, lambda: total.turn(1)),
        8: (d.stage_d, o.stage_b),
        9: (e.stage_d, u.stage_e, o.stage_c, lambda: total.turn(2)),
        10: (o.stage_d, d.stage_e),
        11: (total.close,),
    }

    def transfers(half):
        for slot, stages in plan.items():
            if slot % 2 == half:

                @pl.when(pair == slot // 2)
                def _():
                    for stage in stages:
                        stage()

    @pl.when((pair == 5) & (part == 2))
    def _():
        e.stage_e()
        o.stage_e()
        total.finish()
        out_late[...] = late_sum[...]

    lane = lax.broadcasted_iota(jnp.int32, (TILE, 128), 1)
    sub = lax.broadcasted_iota(jnp.int32, (128, TILE), 0)

    def with_parts(exact, rest):
        a, b, c = three_parts(exact)
        return jnp.where(
            lane == SLOTS,
            a,
            jnp.where(lane == SLOTS + 1, b, jnp.where(lane == SLOTS + 2, c, rest)),
        )

    @pl.when(part == 0)
    def _():
        transfers(0)

        @pl.when(pair == 0)
        def _():
            mask_rows(kind[0], mask_q, mask_k)
            keys[:, 128:256] = mask_k[...]
            values[:, 128:256] = mask_k[...]

        keys[:, 0:128] = k_ref[0]
        values[:, 0:128] = v_ref[0]
        keys_turned[...] = keys[:, 0:128].T
        d_keys[...] = jnp.zeros_like(d_keys)
        d_values[...] = jnp.zeros_like(d_values)
        for tile in range(TILES):
            first = tile * TILE
            if tile == 3:
                transfers(1)
            both = q_ref[0, first : first + TILE, :] * BF(0.125)
            up = tile_rows(d_mixed, first)
            logs = log_sum[0, first : first + TILE, :]
            product = up.astype(F32) * tile_rows(mixed, first).astype(F32)
            marks = mask_q[first : first + TILE, :]
            turned = []
            for head in range(2):
                chosen = (lane < HEAD) == (head == 0)
                query = jnp.where(chosen, both, BF(0))
                upstream = jnp.where(chosen, up, BF(0))
                inside = jnp.sum(jnp.where(chosen, product, 0.0), axis=1, keepdims=True)
                wide_query = jnp.concatenate(
                    [query, with_parts(-logs[:, head * HEAD : head * HEAD + 1], marks)], axis=1
                )
                wide_up = jnp.concatenate(
                    [upstream, with_parts(-inside, jnp.zeros_like(marks))], axis=1
                )
                prob = jnp.exp(nt_dot(keys[...], wide_query))
                d_scores = (prob * nt_dot(values[...], wide_up)).astype(BF)
                d_values[...] += nn_dot(prob.astype(BF), upstream)
                d_keys[...] += nn_dot(d_scores, query)
                turned.append(nn_dot(keys_turned[...], d_scores))
            d_query[first : first + TILE, :] = (
                (jnp.where(sub < HEAD, *turned) * 0.125).T.astype(BF)
            )
        out[...] = d_query[0:LIVE, :]

    @pl.when(part == 1)
    def _():
        out[...] = d_keys[0:LIVE, :].astype(BF)

    @pl.when(part == 2)
    def _():
        out[...] = d_values[0:LIVE, :].astype(BF)


def attend_back(kind, qkv, d_mixed, mixed, log_sum, late, b_grad, grads):
    def band(first):
        return pl.BlockSpec((LIVE, 128), lambda pair, part: (0, first + pair))

    def row_block(count):
        return pl.BlockSpec((count, D), lambda pair, part: (0, 0))

    def head(first):
        return pl.BlockSpec((1, ROWS, 128), lambda pair, part: (first + pair, 0, 0))

    shapes = [grad.shape[3:] for grad in grads]
    outs = [(rows, width // 2) for rows, width in shapes]
    low = (shapes[2][0] // 2, shapes[2][1])
    parts = [*shapes[:2], low, low]
    return pl.pallas_call(
        attend_back_kernel,
        grid=(HEADS // 2, 3),
        in_specs=[
            pl.BlockSpec(memory_space=pltpu.SMEM),
            head(0), head(6), head(12), band(0), band(0), head(0), row_block(8), row_block(8),
        ]
        + [pl.BlockSpec(memory_space=pl.ANY)] * 3,
        out_specs=[pl.BlockSpec((LIVE, 128), lambda pair, part: (0, part * 6 + pair))]
        + [pl.BlockSpec(shape, lambda pair, part: (0, 0)) for shape in outs]
        + [row_block(16)],
        out_shape=[
            jax.ShapeDtypeStruct((LIVE, 3 * D), BF),
            *[jax.ShapeDtypeStruct(shape, F32) for shape in outs],
            jax.ShapeDtypeStruct((16, D), F32),
        ],
        scratch_shapes=[
            pltpu.VMEM((ROWS, 128), BF),
            pltpu.VMEM((ROWS, 128), BF),
            pltpu.VMEM((ROWS, 256), BF),
            pltpu.VMEM((ROWS, 256), BF),
            pltpu.VMEM((128, ROWS), BF),
            pltpu.VMEM((ROWS, 128), BF),
            pltpu.VMEM((ROWS, 128), F32),
            pltpu.VMEM((ROWS, 128), F32),
            pltpu.SemaphoreType.DMA((32,)),
            pltpu.SemaphoreType.DMA((32,)),
            pltpu.SemaphoreType.DMA((4,)),
            *[entry for shape in parts for entry in scatter_scratch(*shape)],
            pltpu.VMEM((16, D), F32),
            pltpu.VMEM((16, D), F32),
            *total_scratch((16, D)),
        ],
        compiler_params=pltpu.CompilerParams(
            collective_id=3, has_side_effects=True, vmem_limit_bytes=VMEM_ASK
        ),
    )(kind, qkv, qkv, qkv, d_mixed, mixed, log_sum, late, b_grad, *grads)


def body_block(
    pixels,
    wave_table,
    band_count,
    wave_index,
    group_sensor,
    chip_kind,
    chip_gsd,
    time_loc,
    gen_in,
    gen_bias,
    gen_out,
    meta_weight,
    w_qkv,
    w_out,
    w_up,
    w_down,
    vectors,
    b_up,
    cotangent,
):
    rows, up_rows = vectors.shape[0], b_up.shape[0]

    def steps(count, last):
        falling = 10000.0 ** -(np.arange(count) / last)
        return jnp.asarray(np.tile(np.concatenate([falling, falling]), (8, 1)), F32)

    gen_turned = gen_out.T
    (
        full_q, full_o, full_u, full_d, params, kernel, tokens_in, first, qkv, mixed, log_sum,
        gen_shift, hidden, slope, codes,
    ) = forward(
        (w_qkv, w_out, w_up, w_down),
        (
            pixels,
            vectors.T,
            b_up,
            meta_weight,
            time_loc,
            gen_in,
            gen_bias.reshape(1, -1),
            gen_turned,
            steps(GEN // 2, GEN // 2),
            steps(D // 4, D // 4 - 1),
        ),
        (group_sensor, band_count, wave_index, wave_table, chip_kind, chip_gsd),
    )
    layer_out, d_after, d_mixed, w_out_grad, late, w_up_grad, w_down_grad, b_grad = feed(
        tokens_in,
        mixed,
        cotangent,
        full_o.reshape(D, D),
        params,
        full_u.reshape(D, -1),
        full_d.reshape(-1, D),
    )
    d_qkv, w_out_out, w_up_out, w_down_out, late_sum = attend_back(
        chip_kind,
        qkv,
        d_mixed,
        mixed,
        log_sum,
        late,
        b_grad,
        [
            grad.reshape(NZ, 2, 2, -1, grad.shape[1])
            for grad in (w_out_grad, w_up_grad, w_down_grad)
        ],
    )
    gen_out_grad, gen_in_grad, gen_bias_grad, w_qkv_out, meta_grad, vectors_out, b_up_out, pixel_grad = (
        closing(
            (
                d_qkv,
                first,
                full_q,
                tokens_in,
                d_after,
                params,
                pixels,
                kernel,
                time_loc,
                late_sum,
                hidden,
                gen_shift,
                slope,
                codes,
            ),
            (group_sensor, band_count),
            (gen_turned.shape[0], rows, up_rows),
        )
    )
    return (
        layer_out,
        pixel_grad,
        gen_in_grad,
        gen_bias_grad.reshape(-1),
        gen_out_grad.T,
        meta_grad,
        w_qkv_out,
        w_out_out,
        w_up_out,
        w_down_out,
        vectors_out.T,
        b_up_out.reshape(-1),
    )


def solution(mesh):
    fits = dict(mesh.shape) == {"dp": 16, "fsdp": 2}
    body = body_block if fits else body_general
    placed = (
        P(("dp", "fsdp"), None),
        P(),
        P(),
        P(),
        P(),
        P(("dp", "fsdp")),
        P(("dp", "fsdp"), None),
        P(("dp", "fsdp"), None, None),
        P(),
        P(),
        P(None, ("dp", "fsdp")),
        P(),
        P("dp", "fsdp"),
        P("dp", "fsdp"),
        P("dp", "fsdp"),
        P("dp", "fsdp"),
        P("dp", None),
        P("dp"),
        P(("dp", "fsdp"), None),
    )
    return jax.shard_map(
        body,
        mesh=mesh,
        in_specs=placed,
        out_specs=(
            P(("dp", "fsdp"), None),
            P(("dp", "fsdp"), None),
            P(),
            P(),
            P(None, ("dp", "fsdp")),
            P(),
            P("dp", "fsdp"),
            P("dp", "fsdp"),
            P("dp", "fsdp"),
            P("dp", "fsdp"),
            P("dp", None),
            P("dp"),
        ),
        check_vma=False,
    )
```

```python
import math

import jax
import jax.numpy as jnp
import numpy as np
from jax import lax
from jax.experimental import pallas as pl
from jax.experimental.pallas import tpu as pltpu
from jax.sharding import PartitionSpec as P

D = 768
HEADS = 12
HEAD = 64
GEN = 128
PIX = 64
MAXB = 10
SENSORS = 7
TOK_DEV = 1024
SLOTS = 4
GENOUT = 49920


def exact_dot(left, right):
    return jnp.dot(left, right, precision=lax.Precision.HIGHEST)


def inner_dot(left, right):
    return lax.dot_general(
        left, right, (((0,), (0,)), ((), ())), preferred_element_type=jnp.float32
    )


def outer_dot(left, right):
    return lax.dot_general(
        left, right, (((1,), (1,)), ((), ())), preferred_element_type=jnp.float32
    )


def gelu_exact(values):
    return jax.nn.gelu(values, approximate=False)


def gelu_slope(values, upstream):
    return jax.vjp(gelu_exact, values)[1](upstream)[0]


def table_lookup(indices, table):
    return jnp.sum(
        jnp.where(
            indices[:, None] == jnp.arange(table.shape[0], dtype=jnp.int32)[None, :],
            table[None, :],
            0.0,
        ),
        axis=1,
    )


def wave_code(wavelengths):
    half = GEN // 2
    omega = 1.0 / 10000.0 ** (jnp.arange(half, dtype=jnp.float32) / half)
    angle = (wavelengths * 1000.0)[:, None] * omega[None, :]
    return jnp.concatenate([jnp.sin(angle), jnp.cos(angle)], axis=1)


def place_code(kind_one, gsd_one):
    small = TOK_DEV // SLOTS
    index = jnp.arange(TOK_DEV, dtype=jnp.int32)
    within = jnp.where(kind_one == 1, index, index % small)
    side = jnp.where(kind_one == 1, math.isqrt(TOK_DEV), math.isqrt(small)).astype(jnp.int32)
    across = (within // side).astype(jnp.float32)
    along = (within % side).astype(jnp.float32)
    holder = jnp.where(kind_one == 1, 0, index // small)
    ground = (
        jnp.sum(
            jnp.where(
                holder[:, None] == jnp.arange(SLOTS, dtype=jnp.int32)[None, :], gsd_one[None, :], 0
            ),
            axis=1,
        ).astype(jnp.float32)
        / 10.0
    )
    quarter = D // 4
    omega = 1.0 / 10000.0 ** (jnp.arange(quarter, dtype=jnp.float32) / (quarter - 1))
    first = (across * ground)[:, None] * omega[None, :]
    second = (along * ground)[:, None] * omega[None, :]
    return jnp.concatenate(
        [jnp.sin(first), jnp.cos(first), jnp.sin(second), jnp.cos(second)], axis=1
    )


def segment_ids(kind_one):
    index = jnp.arange(TOK_DEV, dtype=jnp.int32)
    patches = jnp.where(kind_one == 1, 0, index // (TOK_DEV // SLOTS))
    extra = jnp.arange(2 * SLOTS, dtype=jnp.int32) // 2
    return jnp.concatenate([patches, extra])


def layer_norm(values, gain, shift):
    centred = values - jnp.mean(values, axis=-1, keepdims=True)
    scale = lax.rsqrt(jnp.mean(centred * centred, axis=-1, keepdims=True) + 1e-05)
    normed = centred * scale
    return (normed * gain + shift, normed, scale)


def norm_back(upstream, normed, scale, gain):
    gain_grad = jnp.sum(upstream * normed, axis=0)
    shift_grad = jnp.sum(upstream, axis=0)
    scaled = upstream * gain
    inside = (
        scaled
        - jnp.mean(scaled, axis=-1, keepdims=True)
        - normed * jnp.mean(scaled * normed, axis=-1, keepdims=True)
    )
    return (scale * inside, gain_grad, shift_grad)


def body_general(
    pixels,
    wave_table,
    band_count,
    wave_index,
    group_sensor,
    chip_kind,
    chip_gsd,
    time_loc,
    gen_in,
    gen_bias,
    gen_out,
    meta_weight,
    w_qkv,
    w_out,
    w_up,
    w_down,
    vectors,
    b_up,
    cotangent,
):
    half_type = jnp.bfloat16
    group = lax.axis_index("dp")
    sensor = jnp.sum(
        jnp.where(jnp.arange(group_sensor.shape[0], dtype=jnp.int32) == group, group_sensor, 0)
    )
    chosen_sensor = jnp.arange(SENSORS, dtype=jnp.int32) == sensor
    band_total = jnp.sum(jnp.where(chosen_sensor, band_count, 0))
    gen_in_full = gen_in.astype(jnp.float32)
    gen_bias_full = gen_bias.astype(jnp.float32)
    codes = wave_code(table_lookup(wave_index.reshape(-1), wave_table))
    before = exact_dot(codes, gen_in_full) + gen_bias_full
    hidden = gelu_exact(before).astype(half_type)
    shard_made = jnp.dot(hidden, gen_out, preferred_element_type=jnp.float32).astype(half_type)
    all_made = lax.all_gather(shard_made, ("dp", "fsdp"), axis=1, tiled=True)
    generated = lax.dynamic_slice_in_dim(all_made, sensor * MAXB, MAXB, 0)
    live_band = (jnp.arange(MAXB, dtype=jnp.int32) < band_total)[:, None]
    kernel = jnp.where(live_band, generated[:, : PIX * D], jnp.zeros((), half_type)).reshape(
        MAXB * PIX, D
    )
    band_float = band_total.astype(jnp.float32)
    embed_bias = (
        jnp.sum(jnp.where(live_band, generated[:, PIX * D :].astype(jnp.float32), 0.0), axis=0)
        / band_float
    )
    kind_one = chip_kind[0]
    patches = (
        jnp.dot(pixels, kernel, preferred_element_type=jnp.float32)
        + embed_bias
        + place_code(kind_one, chip_gsd[0])
    )
    meta_full = meta_weight.astype(jnp.float32)
    stamps = exact_dot(time_loc[0], meta_full[1:])
    classes = jnp.broadcast_to(meta_full[0], stamps.shape)
    extra = jnp.stack([classes, stamps], axis=1).reshape(2 * SLOTS, D)
    tokens_in = jnp.concatenate([patches, extra], axis=0)
    total_rows = tokens_in.shape[0]
    qkv_rows, out_rows, up_rows, down_rows, vectors_all, b_up_all = (
        lax.all_gather(w_qkv, "dp", axis=0, tiled=True),
        lax.all_gather(w_out, "dp", axis=0, tiled=True),
        lax.all_gather(w_up, "dp", axis=0, tiled=True),
        lax.all_gather(w_down, "dp", axis=0, tiled=True),
        lax.all_gather(vectors, "dp", axis=0, tiled=True),
        lax.all_gather(b_up, "dp", axis=0, tiled=True),
    )
    w_qkv_all, w_out_all, w_up_all, w_down_all = (
        lax.all_gather(qkv_rows, "fsdp", axis=1, tiled=True),
        lax.all_gather(out_rows, "fsdp", axis=1, tiled=True),
        lax.all_gather(up_rows, "fsdp", axis=1, tiled=True),
        lax.all_gather(down_rows, "fsdp", axis=1, tiled=True),
    )
    vector_full = vectors_all.astype(jnp.float32)
    b_up_full = b_up_all.astype(jnp.float32)
    first_norm, normed_one, scale_one = layer_norm(tokens_in, vector_full[:, 0], vector_full[:, 1])
    first = first_norm.astype(half_type)
    qkv = jnp.dot(first, w_qkv_all, preferred_element_type=jnp.float32).astype(half_type)
    query = qkv[:, :D].reshape(total_rows, HEADS, HEAD)
    keys = qkv[:, D : 2 * D].reshape(total_rows, HEADS, HEAD)
    values = qkv[:, 2 * D :].reshape(total_rows, HEADS, HEAD)
    segment = segment_ids(kind_one)
    same = (segment[:, None] == segment[None, :])[None]
    scores = jnp.einsum("qhd,khd->hqk", query, keys, preferred_element_type=jnp.float32) * HEAD ** (
        -0.5
    )
    scores = jnp.where(same, scores, -1e30)
    peak = jnp.max(scores, axis=-1, keepdims=True)
    expo = jnp.exp(scores - peak)
    totals = jnp.sum(expo, axis=-1, keepdims=True)
    prob_half = (expo / totals).astype(half_type)
    mixed = (
        jnp.einsum("hqk,khd->qhd", prob_half, values, preferred_element_type=jnp.float32)
        .reshape(total_rows, D)
        .astype(half_type)
    )
    after = tokens_in + (
        jnp.dot(mixed, w_out_all, preferred_element_type=jnp.float32) + vector_full[:, 2]
    )
    second_norm, normed_two, scale_two = layer_norm(after, vector_full[:, 3], vector_full[:, 4])
    second = second_norm.astype(half_type)
    upper = jnp.dot(second, w_up_all, preferred_element_type=jnp.float32) + b_up_full
    active = gelu_exact(upper).astype(half_type)
    layer_out = (
        after + jnp.dot(active, w_down_all, preferred_element_type=jnp.float32) + vector_full[:, 5]
    ).astype(half_type)
    grad_top = cotangent.astype(jnp.float32)
    w_down_grad = inner_dot(active, cotangent)
    down_bias_grad = jnp.sum(grad_top, axis=0)
    d_active = outer_dot(cotangent, w_down_all)
    d_upper = gelu_slope(upper, d_active).astype(half_type)
    w_up_grad = inner_dot(second, d_upper)
    b_up_grad = jnp.sum(d_upper.astype(jnp.float32), axis=0)
    d_second = outer_dot(d_upper, w_up_all)
    d_after_norm, gain_two_grad, shift_two_grad = norm_back(
        d_second, normed_two, scale_two, vector_full[:, 3]
    )
    d_after = grad_top + d_after_norm
    d_proj = d_after.astype(half_type)
    w_out_grad = inner_dot(mixed, d_proj)
    out_bias_grad = jnp.sum(d_proj.astype(jnp.float32), axis=0)
    d_mixed = outer_dot(d_proj, w_out_all).astype(half_type).reshape(total_rows, HEADS, HEAD)
    again = jnp.einsum("qhd,khd->hqk", query, keys, preferred_element_type=jnp.float32) * HEAD ** (
        -0.5
    )
    again = jnp.where(same, again, -1e30)
    prob_full = jnp.exp(again - peak) / totals
    recalled = prob_full.astype(half_type)
    d_values = jnp.einsum("hqk,qhd->khd", recalled, d_mixed, preferred_element_type=jnp.float32)
    d_prob = jnp.einsum("qhd,khd->hqk", d_mixed, values, preferred_element_type=jnp.float32)
    d_scores = prob_full * (d_prob - jnp.sum(d_prob * prob_full, axis=-1, keepdims=True))
    d_scores = jnp.where(same, d_scores, 0.0).astype(half_type)
    d_query = jnp.einsum(
        "hqk,khd->qhd", d_scores, keys, preferred_element_type=jnp.float32
    ) * HEAD ** (-0.5)
    d_keys = jnp.einsum(
        "hqk,qhd->khd", d_scores, query, preferred_element_type=jnp.float32
    ) * HEAD ** (-0.5)
    d_qkv = jnp.concatenate(
        [
            d_query.reshape(total_rows, D),
            d_keys.reshape(total_rows, D),
            d_values.reshape(total_rows, D),
        ],
        axis=1,
    ).astype(half_type)
    w_qkv_grad = inner_dot(first, d_qkv)
    d_first = outer_dot(d_qkv, w_qkv_all)
    d_tokens_norm, gain_one_grad, shift_one_grad = norm_back(
        d_first, normed_one, scale_one, vector_full[:, 0]
    )
    d_tokens = (d_after + d_tokens_norm).astype(half_type)
    vectors_grad = jnp.stack(
        [
            gain_one_grad,
            shift_one_grad,
            out_bias_grad,
            gain_two_grad,
            shift_two_grad,
            down_bias_grad,
        ],
        axis=1,
    )
    d_patches = d_tokens[:TOK_DEV]
    d_extra = d_tokens[TOK_DEV:].astype(jnp.float32).reshape(SLOTS, 2, D)
    pixel_grad = outer_dot(d_patches, kernel)
    class_grad = jnp.sum(d_extra[:, 0], axis=0)
    stamp_grad = exact_dot(time_loc[0].T, d_extra[:, 1])
    meta_part = jnp.concatenate([class_grad[None, :], stamp_grad], axis=0)
    d_kernel = inner_dot(pixels, d_patches).reshape(MAXB, PIX * D)
    d_kernel = jnp.where(live_band, d_kernel, 0.0)
    d_bias = jnp.sum(d_patches.astype(jnp.float32), axis=0) / band_float
    d_bias_rows = jnp.where(live_band, d_bias[None, :], 0.0)
    d_generated = jnp.concatenate([d_kernel, d_bias_rows], axis=1).astype(half_type)
    placed = jnp.where(
        chosen_sensor[:, None, None], d_generated.astype(jnp.float32)[None], 0.0
    ).reshape(SENSORS * MAXB, GENOUT)
    columns = lax.psum_scatter(placed, ("dp", "fsdp"), scatter_dimension=1, tiled=True)
    gen_out_grad = exact_dot(hidden.astype(jnp.float32).T, columns)
    d_hidden = exact_dot(columns, gen_out.astype(jnp.float32).T)
    d_before = gelu_slope(before, d_hidden)
    gen_in_part = exact_dot(codes.T, d_before)
    gen_bias_part = jnp.sum(d_before, axis=0)
    meta_grad, gen_in_grad, gen_bias_grad = lax.psum(
        (meta_part, gen_in_part, gen_bias_part), ("dp", "fsdp")
    )
    qkv_cols, out_cols, up_cols, down_cols = (
        lax.psum_scatter(
            w_qkv_grad.astype(jnp.bfloat16), "fsdp", scatter_dimension=1, tiled=True
        ).astype(jnp.float32),
        lax.psum_scatter(
            w_out_grad.astype(jnp.bfloat16), "fsdp", scatter_dimension=1, tiled=True
        ).astype(jnp.float32),
        lax.psum_scatter(
            w_up_grad.astype(jnp.bfloat16), "fsdp", scatter_dimension=1, tiled=True
        ).astype(jnp.float32),
        lax.psum_scatter(
            w_down_grad.astype(jnp.bfloat16), "fsdp", scatter_dimension=1, tiled=True
        ).astype(jnp.float32),
    )
    vectors_group, b_up_group = lax.psum((vectors_grad, b_up_grad), "fsdp")
    w_qkv_out, w_out_out, w_up_out, w_down_out, vectors_out, b_up_out = (
        lax.psum_scatter(
            qkv_cols.astype(jnp.bfloat16), "dp", scatter_dimension=0, tiled=True
        ).astype(jnp.float32),
        lax.psum_scatter(
            out_cols.astype(jnp.bfloat16), "dp", scatter_dimension=0, tiled=True
        ).astype(jnp.float32),
        lax.psum_scatter(
            up_cols.astype(jnp.bfloat16), "dp", scatter_dimension=0, tiled=True
        ).astype(jnp.float32),
        lax.psum_scatter(
            down_cols.astype(jnp.bfloat16), "dp", scatter_dimension=0, tiled=True
        ).astype(jnp.float32),
        lax.psum_scatter(
            vectors_group.astype(jnp.bfloat16), "dp", scatter_dimension=0, tiled=True
        ).astype(jnp.float32),
        lax.psum_scatter(
            b_up_group.astype(jnp.bfloat16), "dp", scatter_dimension=0, tiled=True
        ).astype(jnp.float32),
    )
    return (
        layer_out,
        pixel_grad,
        gen_in_grad,
        gen_bias_grad,
        gen_out_grad,
        meta_grad,
        w_qkv_out,
        w_out_out,
        w_up_out,
        w_down_out,
        vectors_out,
        b_up_out,
    )


LIVE = 1032
ROWS = 1040
TILE = 208
TILES = 5
WIDE = 520
NZ = 4
GROUPS = 16
PIECE = 144
COVER = 14
VMEM_ASK = 60 * 1024 * 1024
BF = jnp.bfloat16
F32 = jnp.float32


def nt_dot(left, right):
    return lax.dot_general(left, right, (((1,), (1,)), ((), ())), preferred_element_type=F32)


def nn_dot(left, right):
    return lax.dot_general(left, right, (((1,), (0,)), ((), ())), preferred_element_type=F32)


def spot():
    group = lax.axis_index("dp")
    return group // 4, (group // 2) % 2, group % 2, lax.axis_index("fsdp")


def device(z, y, c, x):
    return {"dp": z * 4 + y * 2 + c, "fsdp": x}


def remote(source, target, sems, slot, where):
    return pltpu.make_async_remote_copy(
        src_ref=source,
        dst_ref=target,
        send_sem=sems[0].at[slot],
        recv_sem=sems[1].at[slot],
        device_id=where,
        device_id_type=pl.DeviceIdType.MESH,
    )


def greet(others):
    barrier = pltpu.get_barrier_semaphore()
    for where in others:
        pl.semaphore_signal(
            barrier, inc=1, device_id=where, device_id_type=pl.DeviceIdType.MESH
        )
    pl.semaphore_wait(barrier, len(others))


def columns(ref, x):
    width = ref.shape[-1] // 2
    return pl.ds(pl.multiple_of(x * width, 128), width)


def group_peers(z, y, c, x):
    return [
        ((dz, dy, dc), device((z + dz) % NZ, (y + dy) % 2, (c + dc) % 2, x))
        for dz in range(NZ)
        for dy in range(2)
        for dc in range(2)
        if dz + dy + dc
    ]


CHUNK = 768
BANDS = ((0, 256), (256, 256), (512, 256), (768, 256), (1024, 8))


def gelu_parts(values):
    bell = jnp.exp(values * values * (-0.5))
    step = 1.0 / (1.0 + (0.3275911 * math.sqrt(0.5)) * jnp.abs(values))
    poly = 0.5 * 1.061405429 * step - 0.5 * 1.453152027
    poly = poly * step + 0.5 * 1.421413741
    poly = poly * step - 0.5 * 0.284496736
    poly = poly * step + 0.5 * 0.254829592
    tail = poly * step * bell
    below = jnp.where(values < 0.0, tail, 1.0 - tail)
    return values * below, below + values * bell * (1.0 / math.sqrt(2.0 * math.pi))


def standard(values):
    centred = values - jnp.mean(values, axis=-1, keepdims=True)
    scale = lax.rsqrt(jnp.mean(centred * centred, axis=-1, keepdims=True) + 1e-05)
    return centred * scale, scale


def column_sum(values):
    return jnp.sum(values, axis=0, keepdims=True)


def put_rows(target, first, count, values):
    if count % 16:
        values = jnp.concatenate(
            [values, jnp.zeros((16 - count % 16, values.shape[1]), values.dtype)], axis=0
        )
    target[first : first + values.shape[0], :] = values


class Gather:
    COPIES = 19

    def __init__(self, shard, whole, sems, local, first, lean, here):
        z, y, c, x = here
        self.lean = lean
        mine, other = columns(whole, x), columns(whole, 1 - x)
        across, beside, twin = device(z, y, c, 1 - x), device(z, 1 - y, c, x), device(z, y, 1 - c, x)
        target = whole.at[z, y, c, :, mine]
        self.local = pltpu.make_async_copy(shard, target, local)
        self.along = [
            remote(shard, target, sems, first + k - 1, device((z + k) % NZ, y, c, x))
            for k in range(1, NZ)
        ]
        self.to_x, self.to_y, self.far = [], [], []
        for k in range(NZ):
            at = (z + NZ - k) % NZ
            place = whole.at[at, y, c, :, mine]
            source = place if k else shard
            self.to_x.append(remote(source, place, sems, first + 3 + k, across))
            self.to_y.append(remote(source, place, sems, first + 7 + k, beside))
            if k < lean:
                place = whole.at[at, y, c, :, other]
                self.far.append(remote(place, place, sems, first + 11 + k, beside))
            else:
                place = whole.at[at, 1 - y, c, :, mine]
                self.far.append(remote(place, place, sems, first + 11 + k, across))
        self.core = []
        for step, part in enumerate(
            (
                whole.at[:, y, c, :, mine],
                whole.at[:, y, c, :, other],
                whole.at[:, 1 - y, c, :, mine],
                whole.at[:, 1 - y, c, :, other],
            )
        ):
            self.core.append(remote(part, part, sems, first + 15 + step, twin))

    def send_z(self):
        self.local.start()
        for copy in self.along:
            copy.start()

    def send_own(self):
        self.to_x[0].start()
        self.to_y[0].start()

    def pass_on(self):
        for k in range(1, NZ):
            self.along[k - 1].wait_recv()
            self.to_x[k].start()
            self.to_y[k].start()
        self.local.wait()
        self.core[0].start()

    def turn_corner(self):
        for k in range(NZ):
            (self.to_x if k < self.lean else self.to_y)[k].wait_recv()
            self.far[k].start()
        for k in range(self.lean, NZ):
            self.to_x[k].wait_recv()
        self.core[1].start()
        for k in range(self.lean):
            self.to_y[k].wait_recv()
        self.core[2].start()

    def share(self):
        for copy in self.far:
            copy.wait_recv()
        self.core[3].start()

    def receive(self):
        for copy in self.core:
            copy.wait_recv()

    def finish(self):
        for copy in (*self.along, *self.to_x, *self.to_y, *self.far, *self.core):
            copy.wait_send()


def make_small(vectors, b_up, held, small):
    group = lax.axis_index("dp")
    count, up_count = vectors.shape[1], b_up.shape[0]
    per_row = D // up_count
    held[...] = jnp.zeros_like(held)
    held[0:6, 0:count] = vectors[...].astype(F32)
    held[8:9, 0:up_count] = b_up[...].astype(F32).reshape(1, up_count)
    rows = pltpu.roll(held[0:8, :], group * count, 1)
    bias = pltpu.roll(held[8:16, :], (group % per_row) * up_count, 1)[0:1]
    row = lax.broadcasted_iota(jnp.int32, (8, D), 0)
    spot_at = 6 + group // per_row
    top = jnp.where(row < 6, rows, jnp.where(row == spot_at, bias, 0.0))
    small[...] = jnp.concatenate(
        [top, jnp.where(row + 8 == spot_at, bias, 0.0)], axis=0
    ).astype(BF)


def make_table(kind, ground, steps, table):
    wide = steps.shape[1]
    entry = lax.broadcasted_iota(jnp.int32, (64, wide), 0)
    lane = lax.broadcasted_iota(jnp.int32, (64, wide), 1)
    single = kind == 1
    chip = jnp.where(single, 0, entry // 16)
    step = jnp.where(single, entry, entry % 16).astype(F32)
    distance = jnp.zeros((64, wide), F32)
    for slot in range(SLOTS):
        distance = jnp.where(chip == slot, ground[0, slot].astype(F32), distance)
    angle = (step * (distance / 10.0)) * steps[0:1, :]
    exact = jnp.where(lane < wide // 2, jnp.sin(angle), jnp.cos(angle))
    for at, part in enumerate(three_parts(exact)):
        table[at * 64 : (at + 1) * 64, :] = part
    table[192:256, :] = jnp.zeros((64, wide), BF)


def make_pieces(
    groups, bands, waves, wave_table, steps, gen_in, gen_bias, gen_out,
    gen_shift, hidden, slope, codes, made, code_rows, rows, wide, angles,
):
    for wave in range(angles.shape[0]):
        angles[wave : wave + 1, :] = (wave_table[wave] * 1000.0) * steps[0:1, :]
    lane = lax.broadcasted_iota(jnp.int32, angles.shape, 1)
    angle = angles[...]
    angles[...] = jnp.where(lane < GEN // 2, jnp.sin(angle), jnp.cos(angle))
    for sensor in range(SENSORS):
        for band in range(MAXB):
            code_rows[sensor, band : band + 1, :] = angles[pl.ds(waves[sensor, band], 1), :]
        code_rows[sensor, MAXB:16, :] = jnp.zeros((16 - MAXB, GEN), F32)
    flat = code_rows[:, 0:16, :].reshape(SENSORS * 16, GEN)
    before = exact_dot(flat, gen_in[...].astype(F32)) + gen_bias[...].astype(F32)
    values, slopes = gelu_parts(before)
    band_at = lax.broadcasted_iota(jnp.int32, (16, GEN), 0)
    width = gen_out.shape[0]
    owner = lax.axis_index("dp") * 2 + lax.axis_index("fsdp")
    wide[...] = jnp.zeros_like(wide)
    wide[pl.ds(pl.multiple_of((owner * width) % 128, 8), width), :] = gen_out[...].astype(F32)
    gen_shift[...] = wide[...].astype(BF)
    kept = []
    for sensor in range(SENSORS):
        part = slice(sensor * 16, sensor * 16 + 16)
        live = band_at < bands[sensor]
        kept.append(jnp.where(live, values[part], 0.0))
        code_rows[sensor, 16:32, :] = kept[-1].astype(BF).astype(F32)
        code_rows[sensor, 32:48, :] = jnp.where(live, slopes[part], 0.0)
    lower = jnp.concatenate(kept, axis=0).astype(BF)
    for at in range(COVER):
        product = nt_dot(lower, gen_shift[at * 128 : (at + 1) * 128, :])
        for sensor in range(SENSORS):
            rows[sensor, at * MAXB : (at + 1) * MAXB, :] = product[
                sensor * 16 : sensor * 16 + MAXB
            ]
    rows[:, COVER * MAXB :, :] = jnp.zeros((SENSORS, PIECE - COVER * MAXB, 128), F32)
    for group in range(GROUPS):
        made[group // 4, (group // 2) % 2, group % 2] = rows[groups[group]].astype(BF)
    for group in range(GROUPS):
        own = code_rows[groups[group]]
        first = group * MAXB
        codes[first : first + MAXB, :] = own[0:MAXB]
        hidden[first : first + MAXB, :] = own[16 : 16 + MAXB]
        slope[first : first + MAXB, :] = own[32 : 32 + MAXB]


def mask_rows(kind, for_query, for_key):
    row = lax.broadcasted_iota(jnp.int32, (ROWS, 128), 0)
    lane = lax.broadcasted_iota(jnp.int32, (ROWS, 128), 1)
    patch = jnp.where(kind == 1, 0, row // (TOK_DEV // SLOTS))
    segment = jnp.where(row < TOK_DEV, patch, (row - TOK_DEV) // 2)
    hot = (lane == segment) & (row < LIVE)
    for_query[...] = jnp.where(hot, 1.0, 0.0).astype(BF)
    for_key[...] = jnp.where(
        lane < SLOTS, jnp.where(hot, 0.0, -1e30), jnp.where(lane < SLOTS + 3, 1.0, 0.0)
    ).astype(BF)


def attend_pair(pair, qkv, mask_q, mask_k, keys, values, mixed, log_sum):
    lane = lax.broadcasted_iota(jnp.int32, (WIDE, 128), 1)
    lanes = pl.ds(pl.multiple_of(pair * 128, 128), 128)
    keys[:, 0:128] = qkv[6 + pair]
    keys[:, 128:256] = mask_k[...]
    values[:, 0:128] = qkv[12 + pair]
    for tile in range((ROWS // WIDE)):
        first = tile * WIDE
        both = qkv[pair, first : first + WIDE, :] * BF(0.125)
        results, sums = [], []
        for head in range(2):
            query = jnp.where((lane < HEAD) == (head == 0), both, BF(0))
            scores = nt_dot(
                jnp.concatenate([query, mask_q[first : first + WIDE, :]], axis=1), keys[...]
            )
            peak = jnp.max(scores, axis=1, keepdims=True)
            expo = jnp.exp(scores - peak).astype(BF)
            made = nn_dot(expo, values[...])
            totals = made[:, 128:256]
            results.append(made[:, 0:128] / totals)
            sums.append(peak + jnp.log(totals))
        count = min(WIDE, LIVE - first)
        mixed[first : first + count, lanes] = jnp.where(lane < HEAD, *results)[:count].astype(BF)
        log_sum[pair, first : first + WIDE, :] = jnp.where(lane < HEAD, *sums)


def forward_kernel(
    wq, wo, wu, wd, pixels, vectors, b_up, meta_weight, time_loc, gen_in, gen_bias, gen_out,
    wave_steps, place_steps,
    groups, bands, waves, wave_table, kind, ground,
    full_q, full_o, full_u, full_d, params, kernel, tokens, first, qkv, mixed, log_sum,
    gen_shift, hidden, slope, codes,
    made, code_rows, rows, roll, angles, small_held, small, table,
    taken, full_small, flat, wide, keys, values, mask_q, mask_k,
    w_send, w_recv, local_sem, s_send, s_recv, g_send, g_recv,
):
    here = z, y, c, x = spot()
    peers = group_peers(z, y, c, x)
    across = device(z, y, c, 1 - x)
    greet([where for _, where in peers] + [across])
    half = wd.shape[0] // 2
    gathers = q, o, u, d, e = [
        Gather(shard, whole, (w_send, w_recv), local_sem.at[step], Gather.COPIES * step, lean, here)
        for step, (shard, whole, lean) in enumerate(
            (
                (wq, full_q, 4),
                (wo, full_o, 2),
                (wu, full_u, 2),
                (wd.at[0:half], full_d.at[:, :, :, 0:half], 2),
                (wd.at[half : 2 * half], full_d.at[:, :, :, half : 2 * half], 2),
            )
        )
    ]
    s_sems = (s_send, s_recv)
    g_sems = (g_send, g_recv)
    q.send_z()
    for gather in gathers:
        gather.send_own()
    make_pieces(
        groups, bands, waves, wave_table, wave_steps, gen_in, gen_bias, gen_out,
        gen_shift, hidden, slope, codes, made, code_rows, rows, roll, angles,
    )
    make_small(vectors, b_up, small_held, small)
    mask_rows(kind[0], mask_q, mask_k)
    make_table(kind[0], ground, place_steps, table)
    values[:, 128:256] = jnp.ones((ROWS, 128), BF)
    q.pass_on()
    own_made = pltpu.make_async_copy(
        made.at[z, y, c], taken.at[z, y, c, x], local_sem.at[5]
    )
    own_made.start()
    sends = {}
    for (dz, dy, dc), where in peers:
        copy = remote(
            made.at[(z + dz) % NZ, (y + dy) % 2, (c + dc) % 2],
            taken.at[z, y, c, x],
            g_sems,
            dz * 4 + dy * 2 + dc,
            where,
        )
        copy.start()
        sends[dz, dy, dc] = copy
    own_small = pltpu.make_async_copy(small, full_small.at[z, y, c], local_sem.at[6])
    own_small.start()
    small_z = [
        remote(small, full_small.at[z, y, c], s_sems, k - 1, device((z + k) % NZ, y, c, x))
        for k in range(1, NZ)
    ]
    for copy in small_z:
        copy.start()
    q.turn_corner()
    own_made.wait()
    swaps = []
    for dz in range(NZ):
        for dy in range(2):
            for dc in range(2):
                if dz + dy + dc:
                    sends[dz, dy, dc].wait_recv()
        part = taken.at[(z + NZ - dz) % NZ, :, :, x]
        swap = remote(part, part, g_sems, 16 + dz, across)
        swap.start()
        swaps.append(swap)
    u.send_z()
    own_small.wait()
    for copy in small_z:
        copy.wait_recv()
    part = full_small.at[:, y, c]
    small_y = remote(part, part, s_sems, 3, device(z, 1 - y, c, x))
    small_y.start()
    q.share()
    for swap in swaps:
        swap.wait_recv()
    small_y.wait_recv()
    part = full_small.at[:, :, c]
    small_c = remote(part, part, s_sems, 4, device(z, y, 1 - c, x))
    small_c.start()
    u.pass_on()
    d.send_z()
    e.send_z()
    o.send_z()
    unpack(taken, flat, wide, kernel)
    bias = jnp.concatenate(
        [
            column_sum(flat[(PIX * 6 + part) * MAXB : (PIX * 6 + part + 1) * MAXB, :])
            for part in range(6)
        ],
        axis=1,
    ) / bands[groups[lax.axis_index("dp")]].astype(F32)
    single = kind[0] == 1
    for start, count in BANDS[:-1]:
        band = slice(start, start + count)
        made_rows = nn_dot(pixels[band, :], kernel[...])
        index = start + lax.broadcasted_iota(jnp.int32, (count, 256), 0)
        lane = lax.broadcasted_iota(jnp.int32, (count, 256), 1)
        spread = []
        for spots in (
            jnp.where(single, index // 32, index // 16),
            jnp.where(single, index % 32, index // 256 * 16 + index % 16),
        ):
            hot = (lane % 64 == spots) & (lane < 192)
            spread.append(nn_dot(jnp.where(hot, 1.0, 0.0).astype(BF), table[...]))
        tokens[band, :] = made_rows + bias + jnp.concatenate(spread, axis=1)
    small_c.wait_recv()
    params[...] = jnp.zeros_like(params)
    for n in range(GROUPS):
        params[...] += full_small[n // 4, (n // 2) % 2, n % 2].astype(F32)
    meta = meta_weight[...].astype(F32)
    stamps = exact_dot(time_loc[0], meta[1:])
    for slot in range(SLOTS):
        at = TOK_DEV + 2 * slot
        tokens[at : at + 1, :] = meta[0:1]
        tokens[at + 1 : at + 2, :] = stamps[slot : slot + 1]
    for start, count in BANDS:
        band = slice(start, start + count)
        normed, _ = standard(tokens[band, :])
        first[band, :] = (normed * params[0:1, :] + params[1:2, :]).astype(BF)
    q.receive()
    for start, count in BANDS:
        band = slice(start, start + count)
        for third in range(3):
            part = slice(third * D, (third + 1) * D)
            made_rows = nn_dot(
                first[band, :], full_q[:, :, :, :, part].reshape(D, D)
            ).astype(BF)
            for block in range(6):
                put_rows(
                    qkv.at[third * 6 + block],
                    start,
                    count,
                    made_rows[:, block * 128 : (block + 1) * 128],
                )

    def one_pair(pair, carry):
        @pl.when(pair == 0)
        def _():
            u.turn_corner()

        @pl.when(pair == 1)
        def _():
            d.pass_on()
            e.pass_on()

        @pl.when(pair == 2)
        def _():
            u.share()
            o.pass_on()

        @pl.when(pair == 3)
        def _():
            d.turn_corner()
            e.turn_corner()

        @pl.when(pair == 4)
        def _():
            o.turn_corner()
            d.share()

        @pl.when(pair == 5)
        def _():
            e.share()
            o.share()

        attend_pair(pair, qkv, mask_q, mask_k, keys, values, mixed, log_sum)
        return carry

    lax.fori_loop(0, HEADS // 2, one_pair, 0)
    for gather in (o, u, d, e):
        gather.receive()
    for gather in gathers:
        gather.finish()
    for copy in (*small_z, small_y, small_c, *sends.values(), *swaps):
        copy.wait_send()


def forward(shards, operands, scalars):
    anywhere = pl.BlockSpec(memory_space=pl.ANY)
    vmem = pl.BlockSpec(memory_space=pltpu.VMEM)
    smem = pl.BlockSpec(memory_space=pltpu.SMEM)
    blocks = GROUPS * MAXB
    outs = [
        jax.ShapeDtypeStruct((NZ, 2, 2, shard.shape[0], 2 * shard.shape[1]), BF) for shard in shards
    ]
    outs += [
        jax.ShapeDtypeStruct((16, D), F32),
        jax.ShapeDtypeStruct((MAXB * PIX, D), BF),
        jax.ShapeDtypeStruct((LIVE, D), F32),
        jax.ShapeDtypeStruct((LIVE, D), BF),
        jax.ShapeDtypeStruct((18, ROWS, 128), BF),
        jax.ShapeDtypeStruct((LIVE, D), BF),
        jax.ShapeDtypeStruct((HEADS // 2, ROWS, 128), F32),
        jax.ShapeDtypeStruct((COVER * 128, GEN), BF),
        jax.ShapeDtypeStruct((blocks, GEN), F32),
        jax.ShapeDtypeStruct((blocks, GEN), F32),
        jax.ShapeDtypeStruct((blocks, GEN), F32),
    ]
    return pl.pallas_call(
        forward_kernel,
        out_shape=outs,
        in_specs=[anywhere] * 4 + [vmem] * len(operands) + [smem] * len(scalars),
        out_specs=[vmem] + [anywhere] * 3 + [vmem] * 11,
        scratch_shapes=[
            pltpu.VMEM((NZ, 2, 2, PIECE, 128), BF),
            pltpu.VMEM((SENSORS, 48, GEN), F32),
            pltpu.VMEM((SENSORS, PIECE, 128), F32),
            pltpu.VMEM((COVER * 128, GEN), F32),
            pltpu.VMEM((scalars[3].shape[0], GEN), F32),
            pltpu.VMEM((16, D), F32),
            pltpu.VMEM((16, D), BF),
            pltpu.VMEM((256, D // 2), BF),
            pltpu.VMEM((NZ, 2, 2, 2, PIECE, 128), BF),
            pltpu.VMEM((NZ, 2, 2, 16, D), BF),
            pltpu.VMEM((FLAT, 128), F32),
            pltpu.VMEM((6, MAXB * PIX, 128), F32),
            pltpu.VMEM((ROWS, 256), BF),
            pltpu.VMEM((ROWS, 256), BF),
            pltpu.VMEM((ROWS, 128), BF),
            pltpu.VMEM((ROWS, 128), BF),
        ]
        + [pltpu.SemaphoreType.DMA((count,)) for count in (95, 95, 7, 5, 5, 20, 20)],
        compiler_params=pltpu.CompilerParams(
            collective_id=0, has_side_effects=True, vmem_limit_bytes=VMEM_ASK
        ),
    )(*shards, *operands, *scalars)


class Scatter:
    def __init__(self, whole, own, came, low, high, side_x, side_y, last, out, sems, first, here):
        z, y, c, x = here
        self.here, self.own, self.came, self.out = here, own, came, out
        self.low, self.high, self.side_x, self.side_y, self.last = low, high, side_x, side_y, last
        self.mine, self.other = columns(own, x), columns(own, 1 - x)
        mine, other = self.mine, self.other
        across, beside, twin = device(z, y, c, 1 - x), device(z, 1 - y, c, x), device(z, y, 1 - c, x)
        self.local = pltpu.make_async_copy(whole.at[:, :, c], own, sems[2].at[first // 8])
        self.core = remote(whole.at[:, :, 1 - c], came, sems, first, twin)
        self.far_y = remote(own.at[0:2, 1 - y, :, other], low, sems, first + 1, beside)
        self.far_x = remote(own.at[2:4, 1 - y, :, other], high, sems, first + 2, across)
        self.to_x = remote(own.at[:, y, :, other], side_x, sems, first + 3, across)
        self.to_y = remote(own.at[:, 1 - y, :, mine], side_y, sems, first + 4, beside)
        self.along = [
            remote(
                own.at[(z + k) % NZ, y, :, mine], last.at[k - 1], sems, first + 4 + k,
                device((z + k) % NZ, y, c, x),
            )
            for k in range(1, NZ)
        ]

    def stage_a(self):
        self.local.start()
        self.core.start()

    def stage_b(self):
        self.local.wait()
        self.core.wait_recv()
        for at_z in range(NZ):
            for at_y in range(2):
                self.own[at_z, at_y] = self.own[at_z, at_y] + self.came[at_z, at_y]
        self.far_y.start()
        self.far_x.start()

    def stage_c(self):
        _, y, _, _ = self.here
        self.far_y.wait_recv()
        for k in range(2):
            self.own[k, y, :, self.other] = self.own[k, y, :, self.other] + self.low[k]
        self.to_x.start()
        self.far_x.wait_recv()
        for k in range(2):
            self.own[2 + k, 1 - y, :, self.mine] = (
                self.own[2 + k, 1 - y, :, self.mine] + self.high[k]
            )
        self.to_y.start()

    def stage_d(self):
        _, y, _, _ = self.here
        self.to_x.wait_recv()
        self.to_y.wait_recv()
        for k in range(NZ):
            self.own[k, y, :, self.mine] = (
                self.own[k, y, :, self.mine].astype(F32)
                + self.side_x[k].astype(F32)
                + self.side_y[k].astype(F32)
            ).astype(BF)
        for copy in self.along:
            copy.start()

    def stage_e(self):
        z, y, _, _ = self.here
        for copy in self.along:
            copy.wait_recv()
        self.out[...] = (
            self.own[z, y, :, self.mine].astype(F32)
            + self.last[0].astype(F32)
            + self.last[1].astype(F32)
            + self.last[2].astype(F32)
        )
        for copy in (self.core, self.far_y, self.far_x, self.to_x, self.to_y, *self.along):
            copy.wait_send()


class Total:
    COPIES = 7

    def __init__(self, source, out, held, came, slots, send_sem, recv_sem, here):
        z, y, c, x = here
        sems = (send_sem, recv_sem)
        half = source.shape[0] // 2
        self.mine = pl.ds(pl.multiple_of(c * half, 8), half)
        theirs = pl.ds(pl.multiple_of((1 - c) * half, 8), half)
        self.source, self.held, self.came, self.slots, self.out = source, held, came, slots, out
        self.z = z
        twin = device(z, y, 1 - c, x)
        self.steps = [
            remote(source.at[theirs], came.at[0], sems, 0, twin),
            remote(held.at[0], came.at[1], sems, 1, device(z, y, c, 1 - x)),
            remote(held.at[1], came.at[2], sems, 2, device(z, 1 - y, c, x)),
        ]
        self.along = [
            remote(held.at[2], slots.at[z], sems, 2 + k, device((z + k) % NZ, y, c, x))
            for k in range(1, NZ)
        ]
        self.last = remote(out.at[self.mine], out.at[self.mine], sems, 6, twin)

    def begin(self):
        self.steps[0].start()

    def turn(self, step):
        self.steps[step].wait_recv()
        before = self.source[self.mine, :] if step == 0 else self.held[step - 1]
        self.held[step] = before + self.came[step]
        if step < 2:
            self.steps[step + 1].start()
        else:
            self.slots[self.z] = self.held[2]
            for copy in self.along:
                copy.start()

    def close(self):
        for copy in self.along:
            copy.wait_recv()
        self.out[self.mine, :] = self.slots[0] + self.slots[1] + self.slots[2] + self.slots[3]
        self.last.start()

    def finish(self):
        for copy in (*self.steps, *self.along):
            copy.wait_send()
        self.last.wait()


def near(z, y, c, x):
    return [
        device(z, y, c, 1 - x),
        device(z, 1 - y, c, x),
        device(z, y, 1 - c, x),
        *[device((z + k) % NZ, y, c, x) for k in range(1, NZ)],
    ]


def scatter_scratch(rows, width):
    half = width // 2
    return [
        pltpu.VMEM((NZ, 2, rows, width), BF),
        pltpu.VMEM((NZ, 2, rows, width), BF),
        pltpu.VMEM((2, rows, half), BF),
        pltpu.VMEM((2, rows, half), BF),
        pltpu.VMEM((NZ, rows, half), BF),
        pltpu.VMEM((NZ, rows, half), BF),
        pltpu.VMEM((3, rows, half), BF),
    ]


def total_scratch(shape):
    half = (shape[0] // 2,) + shape[1:]
    return [
        pltpu.VMEM((3,) + half, F32),
        pltpu.VMEM((3,) + half, F32),
        pltpu.VMEM((NZ,) + half, F32),
        pltpu.SemaphoreType.DMA((Total.COPIES,)),
        pltpu.SemaphoreType.DMA((Total.COPIES,)),
    ]


def piece_start(owner):
    return (owner * (GENOUT // 32)) // 128


FLAT = (GENOUT // 128) * MAXB


def unpack(taken, flat, wide, kernel):
    flat[...] = jnp.zeros_like(flat)
    used = COVER * MAXB
    for owner in range(32):
        first = piece_start(owner) * MAXB
        count = min(used, FLAT - first)
        piece = taken[owner // 8, (owner // 4) % 2, (owner // 2) % 2, owner % 2]
        flat[first : first + count, :] += piece.astype(F32)[:count]
    for pixel in range(PIX):
        for part in range(6):
            first = (pixel * 6 + part) * MAXB
            wide[part, pl.ds(pixel, MAXB, stride=PIX), :] = flat[first : first + MAXB, :]
    for part in range(6):
        kernel[:, part * 128 : (part + 1) * 128] = wide[part].astype(BF)


def pack(d_kernel, bias, pieces, wide, flat):
    for part in range(6):
        wide[part] = d_kernel[:, part * 128 : (part + 1) * 128]
        first = (PIX * 6 + part) * MAXB
        flat[first : first + MAXB, :] = bias[0:MAXB, part * 128 : (part + 1) * 128]
    flat[FLAT:, :] = jnp.zeros((flat.shape[0] - FLAT, 128), F32)
    for pixel in range(PIX):
        for part in range(6):
            first = (pixel * 6 + part) * MAXB
            flat[first : first + MAXB, :] = wide[part, pl.ds(pixel, MAXB, stride=PIX), :]
    for owner in range(32):
        first = piece_start(owner) * MAXB
        pieces[owner // 8, (owner // 4) % 2, (owner // 2) % 2, owner % 2] = flat[
            first : first + PIECE, :
        ].astype(BF)


def norm_rows_back(value, upstream, gain):
    normed, scale = standard(value)
    scaled = upstream * gain
    inside = (
        scaled
        - jnp.mean(scaled, axis=-1, keepdims=True)
        - normed * jnp.mean(scaled * normed, axis=-1, keepdims=True)
    )
    return scale * inside, column_sum(upstream * normed), column_sum(upstream)


def close_kernel(
    d_qkv, first, w_qkv, tokens, d_after, params, pixels, kernel, time_loc, late,
    hidden, gen_shift, slope, codes, groups, bands,
    out_gen, in_grad, in_bias, out_q, out_meta, out_vectors, out_up, pixel_grad,
    d_tokens, grad_q, pieces, crossed, merged, taken, flat, wide, rows, source, summed, out_grad,
    x_send, x_recv, send_sem, recv_sem, local_sem, q_send, q_recv, *rest,
):
    here = z, y, c, x = spot()
    across = device(z, y, c, 1 - x)
    greet([where for _, where in group_peers(z, y, c, x)] + [across])
    scatter = Scatter(
        grad_q, *rest[5:12], out_q, (q_send, q_recv, local_sem), 0, here
    )
    total = Total(source, summed, *rest[0:5], here)
    gain = shift = jnp.zeros((1, D), F32)
    for start, count in BANDS:
        band = slice(start, start + count)
        upstream = nt_dot(d_qkv[band, :], w_qkv[...].reshape(D, 3 * D))
        d_norm, gain_part, shift_part = norm_rows_back(tokens[band, :], upstream, params[0:1, :])
        gain += gain_part
        shift += shift_part
        d_tokens[band, :] = (d_after[band, :] + d_norm).astype(BF)
    patches = d_tokens[0:TOK_DEV, :]
    d_kernel = inner_dot(pixels[...], patches)
    live = bands[groups[lax.axis_index("dp")]]
    band_at = lax.broadcasted_iota(jnp.int32, (16, D), 0)
    sums = column_sum(patches.astype(F32)) / live.astype(F32)
    pack(d_kernel, jnp.where(band_at < live, sums, 0.0), pieces, wide, flat)
    order = (2, 1, 3, 0)
    swaps = {}
    for dz in order:
        to = (z + dz) % NZ
        swaps[dz] = remote(
            pieces.at[to, :, :, 1 - x], crossed.at[to], (x_send, x_recv), dz, across
        )
    swaps[2].start()
    swaps[1].start()
    sends = []

    def merge(dz):
        to = (z + dz) % NZ
        swaps[dz].wait_recv()
        if dz in (2, 1):
            swaps[{2: 3, 1: 0}[dz]].start()
        for at_y in range(2):
            for at_c in range(2):
                merged[to, at_y, at_c] = (
                    pieces[to, at_y, at_c, x].astype(F32) + crossed[to, at_y, at_c].astype(F32)
                ).astype(BF)
        for dy in range(2):
            for dc in range(2):
                at_y, at_c = (y + dy) % 2, (c + dc) % 2
                if dz + dy + dc:
                    copy = remote(
                        merged.at[to, at_y, at_c],
                        taken.at[z, y, c],
                        (send_sem, recv_sem),
                        dz * 4 + dy * 2 + dc,
                        device(to, at_y, at_c, x),
                    )
                    copy.start()
                    sends.append(copy)
                else:
                    taken[z, y, c] = merged[z, y, c]

    def grad_third(third):
        part = slice(third * D, (third + 1) * D)
        grad_q[:, :, :, :, part] = (
            inner_dot(first[...], d_qkv[:, part]).astype(BF).reshape(NZ, 2, 2, -1, D)
        )

    grad_third(0)
    merge(2)
    grad_third(1)
    merge(1)
    grad_third(2)
    scatter.stage_a()
    merge(3)
    merge(0)
    extra = d_tokens[TOK_DEV:LIVE, :].astype(F32)
    stamps = jnp.concatenate([extra[2 * m + 1 : 2 * m + 2] for m in range(SLOTS)], axis=0)
    first_rows = jnp.concatenate(
        [
            extra[0:1] + extra[2:3] + extra[4:5] + extra[6:7],
            lax.dot_general(
                time_loc[0],
                stamps,
                (((0,), (0,)), ((), ())),
                precision=lax.Precision.HIGHEST,
                preferred_element_type=F32,
            ),
            gain,
            shift,
            jnp.zeros((5, D), F32),
        ],
        axis=0,
    )
    meta_at = GEN + 16
    for part in range(6):
        source[meta_at + part * 16 : meta_at + part * 16 + 16, :] = first_rows[
            :, part * 128 : (part + 1) * 128
        ]
    for start, count in BANDS[:2]:
        band = slice(start, start + count)
        pixel_grad[band, :] = nt_dot(d_tokens[band, :], kernel[...])
    scatter.stage_b()
    for start, count in BANDS[2:4]:
        band = slice(start, start + count)
        pixel_grad[band, :] = nt_dot(d_tokens[band, :], kernel[...])
    scatter.stage_c()
    for copy in sends:
        copy.wait_recv()
    for n in range(GROUPS):
        block = taken[n // 4, (n // 2) % 2, n % 2].astype(F32)
        for at in range(COVER):
            rows[at, n * MAXB : (n + 1) * MAXB, :] = block[at * MAXB : (at + 1) * MAXB]
    d_hidden = jnp.zeros((GROUPS * MAXB, GEN), F32)
    for at in range(COVER):
        d_hidden += nn_dot(rows[at].astype(BF), gen_shift[at * 128 : (at + 1) * 128, :])
    d_before = d_hidden * slope[...]
    source[0:GEN, :] = lax.dot_general(
        codes[...],
        d_before,
        (((0,), (0,)), ((), ())),
        precision=lax.Precision.HIGHEST,
        preferred_element_type=F32,
    )
    source[GEN:meta_at, :] = jnp.broadcast_to(column_sum(d_before), (16, GEN))
    total.begin()
    low = hidden[...].astype(BF)
    for at in range(COVER // 2):
        out_grad[at * 128 : (at + 1) * 128, :] = inner_dot(rows[at].astype(BF), low)
    total.turn(0)
    scatter.stage_d()
    for at in range(COVER // 2, COVER):
        out_grad[at * 128 : (at + 1) * 128, :] = inner_dot(rows[at].astype(BF), low)
    total.turn(1)
    total.turn(2)
    width = out_gen.shape[0]
    group = lax.axis_index("dp")
    owner = group * 2 + x
    out_gen[...] = out_grad[pl.ds(pl.multiple_of((owner * width) % 128, 8), width), :]
    total.close()
    scatter.stage_e()
    total.finish()
    in_grad[...] = summed[0:GEN, :]
    in_bias[...] = summed[GEN : GEN + 1, :]
    all_rows = jnp.concatenate(
        [summed[meta_at + part * 16 : meta_at + part * 16 + 16, :] for part in range(6)], axis=1
    )
    out_meta[...] = all_rows[0:9]
    row = lax.broadcasted_iota(jnp.int32, (8, D), 0)
    count, up_count = out_vectors.shape[1], out_up.shape[1]
    per_row = D // up_count
    norms = jnp.where(
        row == 0, all_rows[9:10], jnp.where(row == 1, all_rows[10:11], late[0:8, :])
    )
    norms = pltpu.roll(norms, (GROUPS - group) % GROUPS * count, 1)
    out_vectors[...] = norms[0:6, 0:count]
    ups = pltpu.roll(late[8:16, :], (per_row - group % per_row) % per_row * up_count, 1)
    out_up[...] = column_sum(jnp.where(row == group // per_row, ups, 0.0))[:, 0:up_count]
    for copy in (*sends, *swaps.values()):
        copy.wait_send()


def closing(operands, scalars, sizes):
    vmem = pl.BlockSpec(memory_space=pltpu.VMEM)
    smem = pl.BlockSpec(memory_space=pltpu.SMEM)
    small = (GEN + 16 + 96, GEN)
    width_gen, rows_in, up_rows = sizes
    held = (NZ, 2, 2, PIECE, 128)
    _, _, _, rows, width = operands[2].shape
    return pl.pallas_call(
        close_kernel,
        in_specs=[vmem] * len(operands) + [smem] * len(scalars),
        out_specs=[vmem] * 8,
        out_shape=[
            jax.ShapeDtypeStruct((width_gen, GEN), F32),
            jax.ShapeDtypeStruct((GEN, GEN), F32),
            jax.ShapeDtypeStruct((1, GEN), F32),
            jax.ShapeDtypeStruct((rows, width // 2), F32),
            jax.ShapeDtypeStruct((9, D), F32),
            jax.ShapeDtypeStruct((6, rows_in), F32),
            jax.ShapeDtypeStruct((1, up_rows), F32),
            jax.ShapeDtypeStruct((TOK_DEV, MAXB * PIX), F32),
        ],
        scratch_shapes=[
            pltpu.VMEM((LIVE, D), BF),
            pltpu.VMEM(operands[2].shape, BF),
            pltpu.VMEM((NZ, 2, 2, 2, PIECE, 128), BF),
            pltpu.VMEM(held, BF),
            pltpu.VMEM(held, BF),
            pltpu.VMEM(held, BF),
            pltpu.VMEM((FLAT + 64, 128), F32),
            pltpu.VMEM((6, MAXB * PIX, 128), F32),
            pltpu.VMEM((COVER, GROUPS * MAXB, 128), F32),
            pltpu.VMEM(small, F32),
            pltpu.VMEM(small, F32),
            pltpu.VMEM((COVER * 128, GEN), F32),
            pltpu.SemaphoreType.DMA((4,)),
            pltpu.SemaphoreType.DMA((4,)),
            pltpu.SemaphoreType.DMA((16,)),
            pltpu.SemaphoreType.DMA((16,)),
            pltpu.SemaphoreType.DMA((1,)),
            pltpu.SemaphoreType.DMA((8,)),
            pltpu.SemaphoreType.DMA((8,)),
            *total_scratch(small),
            *scatter_scratch(rows, width),
        ],
        compiler_params=pltpu.CompilerParams(
            collective_id=2, has_side_effects=True, vmem_limit_bytes=VMEM_ASK
        ),
    )(*operands, *scalars)


def tile_rows(source, first):
    if first + TILE <= LIVE:
        return source[first : first + TILE, :]
    part = source[first:LIVE, :]
    return jnp.concatenate([part, jnp.zeros((first + TILE - LIVE, 128), part.dtype)], axis=0)


def feed_kernel(
    tokens, mixed, top, w_out, vectors, w_up, w_down,
    layer_out, d_after, d_mixed, out_grad, rows, up_grad, down_grad, b_grad,
    second, second_turned, top_full, after, sum_out, sum_second, active, d_upper, proj, wide_up, wide_back,
):
    step = pl.program_id(0)

    @pl.when(step == 0)
    def _():
        for first, count in BANDS:
            band = slice(first, first + count)
            value = tokens[band, :] + (nn_dot(mixed[band, :], w_out[...]) + vectors[2:3, :])
            after[band, :] = value
            normed, _ = standard(value)
            put_rows(
                second, first, count, (normed * vectors[3:4, :] + vectors[4:5, :]).astype(BF)
            )
            put_rows(top_full, first, count, top[band, :])
        second_turned[...] = second[...].T
        sum_out[...] = jnp.zeros_like(sum_out)
        b_grad[...] = jnp.zeros_like(b_grad)
        sum_second[...] = jnp.zeros_like(sum_second)

    wide_up[...] = nn_dot(second[...], w_up[...])
    wide_back[...] = nt_dot(top_full[...], w_down[...])
    total = jnp.zeros((1, CHUNK), F32)
    for first, count in BANDS:
        count = -(-count // 16) * 16
        band = slice(first, first + count)
        upper = wide_up[band, :] + vectors[pl.ds(6 + step, 1), :]
        made, slope = gelu_parts(upper)
        made = made.astype(BF)
        active[band, :] = made
        back = (wide_back[band, :] * slope).astype(BF)
        d_upper[band, :] = back
        total += column_sum(back.astype(F32))
    b_grad[pl.ds(step, 1), :] = total
    sum_out[...] += nn_dot(active[...], w_down[...])
    sum_second[...] += nt_dot(d_upper[...], w_up[...])
    down_grad[...] = inner_dot(active[...], top_full[...]).astype(BF)
    up_grad[...] = nn_dot(second_turned[...], d_upper[...]).astype(BF)

    @pl.when(step == pl.num_programs(0) - 1)
    def _():
        gain = shift = bias = last = jnp.zeros((1, D), F32)
        for first, count in BANDS:
            band = slice(first, first + count)
            value = after[band, :]
            layer_out[band, :] = (value + sum_out[band, :] + vectors[5:6, :]).astype(BF)
            normed, scale = standard(value)
            upstream = sum_second[band, :]
            gain += column_sum(upstream * normed)
            shift += column_sum(upstream)
            scaled = upstream * vectors[3:4, :]
            inside = (
                scaled
                - jnp.mean(scaled, axis=-1, keepdims=True)
                - normed * jnp.mean(scaled * normed, axis=-1, keepdims=True)
            )
            grad_top = top[band, :].astype(F32)
            last += column_sum(grad_top)
            result = grad_top + scale * inside
            d_after[band, :] = result
            low = result.astype(BF)
            bias += column_sum(low.astype(F32))
            put_rows(proj, first, count, low)
            d_mixed[band, :] = nt_dot(low, w_out[...]).astype(BF)
        out_grad[...] = inner_dot(mixed[...], proj[0:LIVE, :]).astype(BF)
        rows[...] = jnp.concatenate([jnp.zeros((2, D), F32), bias, gain, shift, last, jnp.zeros((2, D), F32)], axis=0)


def feed(tokens, mixed, top, w_out, vectors, w_up, w_down):
    width = w_up.shape[1]

    def whole(*shape):
        return pl.BlockSpec(shape, lambda step: (0, 0), pipeline_mode=pl.Buffered(1))

    across = pl.BlockSpec((D, CHUNK), lambda step: (0, step))
    down = pl.BlockSpec((CHUNK, D), lambda step: (step, 0))
    block = whole(LIVE, D)
    return pl.pallas_call(
        feed_kernel,
        grid=(width // CHUNK,),
        in_specs=[block, block, block, whole(D, D), whole(16, D), across, down],
        out_specs=[pl.BlockSpec((LIVE, D), lambda step: (0, 0))] * 3 + [pl.BlockSpec((D, D), lambda step: (0, 0)), pl.BlockSpec((8, D), lambda step: (0, 0)), across, down, pl.BlockSpec((8, D), lambda step: (0, 0))],
        out_shape=[
            jax.ShapeDtypeStruct((LIVE, D), BF),
            jax.ShapeDtypeStruct((LIVE, D), F32),
            jax.ShapeDtypeStruct((LIVE, D), BF),
            jax.ShapeDtypeStruct((D, D), BF),
            jax.ShapeDtypeStruct((8, D), F32),
            jax.ShapeDtypeStruct((D, width), BF),
            jax.ShapeDtypeStruct((width, D), BF),
            jax.ShapeDtypeStruct((8, D), F32),
        ],
        scratch_shapes=[
            pltpu.VMEM((ROWS, D), BF),
            pltpu.VMEM((D, ROWS), BF),
            pltpu.VMEM((ROWS, D), BF),
            pltpu.VMEM((LIVE, D), F32),
            pltpu.VMEM((ROWS, D), F32),
            pltpu.VMEM((ROWS, D), F32),
            pltpu.VMEM((ROWS, CHUNK), BF),
            pltpu.VMEM((ROWS, CHUNK), BF),
            pltpu.VMEM((ROWS, D), BF),
            pltpu.VMEM((ROWS, CHUNK), F32),
            pltpu.VMEM((ROWS, CHUNK), F32),
        ],
        compiler_params=pltpu.CompilerParams(vmem_limit_bytes=VMEM_ASK),
    )(tokens, mixed, top, w_out, vectors, w_up, w_down)


def three_parts(exact):
    high = exact.astype(BF)
    left = exact - high.astype(F32)
    middle = left.astype(BF)
    return high, middle, (left - middle.astype(F32)).astype(BF)


def attend_back_kernel(
    kind, q_ref, k_ref, v_ref, d_mixed, mixed, log_sum, late, b_grad, go, gu, gd,
    out, out_o, out_u, out_d, out_late,
    mask_q, mask_k, keys, values, keys_turned, d_query, d_keys, d_values, send_sem, recv_sem, local_sem, *rest,
):
    pair, part = pl.program_id(0), pl.program_id(1)
    here = spot()
    half = out_d.shape[0] // 2
    wholes = (go, gu, gd.at[:, :, :, 0:half], gd.at[:, :, :, half : 2 * half])
    results = (out_o, out_u, out_d.at[0:half], out_d.at[half : 2 * half])
    o, u, d, e = [
        Scatter(
            whole, *rest[7 * at : 7 * at + 7], result, (send_sem, recv_sem, local_sem), 8 * at, here
        )
        for at, (whole, result) in enumerate(zip(wholes, results))
    ]
    late_rows, late_sum, *late_rest = rest[28:]
    total = Total(late_rows, late_sum, *late_rest, here)

    def begin_total():
        late_rows[0:8, :] = late[...]
        late_rows[8:16, :] = b_grad[...]
        total.begin()

    plan = {
        0: (lambda: greet(near(*here)), u.stage_a),
        1: (u.stage_b, d.stage_a),
        2: (e.stage_a, o.stage_a, begin_total),
        3: (u.stage_c,),
        4: (lambda: total.turn(0),),
        5: (d.stage_b,),
        6: (d.stage_c, u.stage_d, e.stage_b),
        7: (e.stage_c, lambda: total.turn(1)),
        8: (d.stage_d, o.stage_b),
        9: (e.stage_d, u.stage_e, o.stage_c, lambda: total.turn(2)),
        10: (o.stage_d, d.stage_e),
        11: (total.close,),
    }

    def transfers(half):
        for slot, stages in plan.items():
            if slot % 2 == half:

                @pl.when(pair == slot // 2)
                def _():
                    for stage in stages:
                        stage()

    @pl.when((pair == 5) & (part == 2))
    def _():
        e.stage_e()
        o.stage_e()
        total.finish()
        out_late[...] = late_sum[...]

    lane = lax.broadcasted_iota(jnp.int32, (TILE, 128), 1)
    sub = lax.broadcasted_iota(jnp.int32, (128, TILE), 0)

    def with_parts(exact, rest):
        a, b, c = three_parts(exact)
        return jnp.where(
            lane == SLOTS,
            a,
            jnp.where(lane == SLOTS + 1, b, jnp.where(lane == SLOTS + 2, c, rest)),
        )

    @pl.when(part == 0)
    def _():
        transfers(0)

        @pl.when(pair == 0)
        def _():
            mask_rows(kind[0], mask_q, mask_k)
            keys[:, 128:256] = mask_k[...]
            values[:, 128:256] = mask_k[...]

        keys[:, 0:128] = k_ref[0]
        values[:, 0:128] = v_ref[0]
        keys_turned[...] = keys[:, 0:128].T
        d_keys[...] = jnp.zeros_like(d_keys)
        d_values[...] = jnp.zeros_like(d_values)
        for tile in range(TILES):
            first = tile * TILE
            if tile == 3:
                transfers(1)
            both = q_ref[0, first : first + TILE, :] * BF(0.125)
            up = tile_rows(d_mixed, first)
            logs = log_sum[0, first : first + TILE, :]
            product = up.astype(F32) * tile_rows(mixed, first).astype(F32)
            marks = mask_q[first : first + TILE, :]
            turned = []
            for head in range(2):
                chosen = (lane < HEAD) == (head == 0)
                query = jnp.where(chosen, both, BF(0))
                upstream = jnp.where(chosen, up, BF(0))
                inside = jnp.sum(jnp.where(chosen, product, 0.0), axis=1, keepdims=True)
                wide_query = jnp.concatenate(
                    [query, with_parts(-logs[:, head * HEAD : head * HEAD + 1], marks)], axis=1
                )
                wide_up = jnp.concatenate(
                    [upstream, with_parts(-inside, jnp.zeros_like(marks))], axis=1
                )
                prob = jnp.exp(nt_dot(keys[...], wide_query))
                d_scores = (prob * nt_dot(values[...], wide_up)).astype(BF)
                d_values[...] += nn_dot(prob.astype(BF), upstream)
                d_keys[...] += nn_dot(d_scores, query)
                turned.append(nn_dot(keys_turned[...], d_scores))
            d_query[first : first + TILE, :] = (
                (jnp.where(sub < HEAD, *turned) * 0.125).T.astype(BF)
            )
        out[...] = d_query[0:LIVE, :]

    @pl.when(part == 1)
    def _():
        out[...] = d_keys[0:LIVE, :].astype(BF)

    @pl.when(part == 2)
    def _():
        out[...] = d_values[0:LIVE, :].astype(BF)


def attend_back(kind, qkv, d_mixed, mixed, log_sum, late, b_grad, grads):
    def band(first):
        return pl.BlockSpec((LIVE, 128), lambda pair, part: (0, first + pair))

    def row_block(count):
        return pl.BlockSpec((count, D), lambda pair, part: (0, 0))

    def head(first):
        return pl.BlockSpec((1, ROWS, 128), lambda pair, part: (first + pair, 0, 0))

    shapes = [grad.shape[3:] for grad in grads]
    outs = [(rows, width // 2) for rows, width in shapes]
    low = (shapes[2][0] // 2, shapes[2][1])
    parts = [*shapes[:2], low, low]
    return pl.pallas_call(
        attend_back_kernel,
        grid=(HEADS // 2, 3),
        in_specs=[
            pl.BlockSpec(memory_space=pltpu.SMEM),
            head(0), head(6), head(12), band(0), band(0), head(0), row_block(8), row_block(8),
        ]
        + [pl.BlockSpec(memory_space=pl.ANY)] * 3,
        out_specs=[pl.BlockSpec((LIVE, 128), lambda pair, part: (0, part * 6 + pair))]
        + [pl.BlockSpec(shape, lambda pair, part: (0, 0)) for shape in outs]
        + [row_block(16)],
        out_shape=[
            jax.ShapeDtypeStruct((LIVE, 3 * D), BF),
            *[jax.ShapeDtypeStruct(shape, F32) for shape in outs],
            jax.ShapeDtypeStruct((16, D), F32),
        ],
        scratch_shapes=[
            pltpu.VMEM((ROWS, 128), BF),
            pltpu.VMEM((ROWS, 128), BF),
            pltpu.VMEM((ROWS, 256), BF),
            pltpu.VMEM((ROWS, 256), BF),
            pltpu.VMEM((128, ROWS), BF),
            pltpu.VMEM((ROWS, 128), BF),
            pltpu.VMEM((ROWS, 128), F32),
            pltpu.VMEM((ROWS, 128), F32),
            pltpu.SemaphoreType.DMA((32,)),
            pltpu.SemaphoreType.DMA((32,)),
            pltpu.SemaphoreType.DMA((4,)),
            *[entry for shape in parts for entry in scatter_scratch(*shape)],
            pltpu.VMEM((16, D), F32),
            pltpu.VMEM((16, D), F32),
            *total_scratch((16, D)),
        ],
        compiler_params=pltpu.CompilerParams(
            collective_id=3, has_side_effects=True, vmem_limit_bytes=VMEM_ASK
        ),
    )(kind, qkv, qkv, qkv, d_mixed, mixed, log_sum, late, b_grad, *grads)


def body_block(
    pixels,
    wave_table,
    band_count,
    wave_index,
    group_sensor,
    chip_kind,
    chip_gsd,
    time_loc,
    gen_in,
    gen_bias,
    gen_out,
    meta_weight,
    w_qkv,
    w_out,
    w_up,
    w_down,
    vectors,
    b_up,
    cotangent,
):
    rows, up_rows = vectors.shape[0], b_up.shape[0]

    def steps(count, last):
        falling = 10000.0 ** -(np.arange(count) / last)
        return jnp.asarray(np.tile(np.concatenate([falling, falling]), (8, 1)), F32)

    gen_turned = gen_out.T
    (
        full_q, full_o, full_u, full_d, params, kernel, tokens_in, first, qkv, mixed, log_sum,
        gen_shift, hidden, slope, codes,
    ) = forward(
        (w_qkv, w_out, w_up, w_down),
        (
            pixels,
            vectors.T,
            b_up,
            meta_weight,
            time_loc,
            gen_in,
            gen_bias.reshape(1, -1),
            gen_turned,
            steps(GEN // 2, GEN // 2),
            steps(D // 4, D // 4 - 1),
        ),
        (group_sensor, band_count, wave_index, wave_table, chip_kind, chip_gsd),
    )
    layer_out, d_after, d_mixed, w_out_grad, late, w_up_grad, w_down_grad, b_grad = feed(
        tokens_in,
        mixed,
        cotangent,
        full_o.reshape(D, D),
        params,
        full_u.reshape(D, -1),
        full_d.reshape(-1, D),
    )
    d_qkv, w_out_out, w_up_out, w_down_out, late_sum = attend_back(
        chip_kind,
        qkv,
        d_mixed,
        mixed,
        log_sum,
        late,
        b_grad,
        [
            grad.reshape(NZ, 2, 2, -1, grad.shape[1])
            for grad in (w_out_grad, w_up_grad, w_down_grad)
        ],
    )
    gen_out_grad, gen_in_grad, gen_bias_grad, w_qkv_out, meta_grad, vectors_out, b_up_out, pixel_grad = (
        closing(
            (
                d_qkv,
                first,
                full_q,
                tokens_in,
                d_after,
                params,
                pixels,
                kernel,
                time_loc,
                late_sum,
                hidden,
                gen_shift,
                slope,
                codes,
            ),
            (group_sensor, band_count),
            (gen_turned.shape[0], rows, up_rows),
        )
    )
    return (
        layer_out,
        pixel_grad,
        gen_in_grad,
        gen_bias_grad.reshape(-1),
        gen_out_grad.T,
        meta_grad,
        w_qkv_out,
        w_out_out,
        w_up_out,
        w_down_out,
        vectors_out.T,
        b_up_out.reshape(-1),
    )


def solution(mesh):
    fits = dict(mesh.shape) == {"dp": 16, "fsdp": 2}
    body = body_block if fits else body_general
    placed = (
        P(("dp", "fsdp"), None),
        P(),
        P(),
        P(),
        P(),
        P(("dp", "fsdp")),
        P(("dp", "fsdp"), None),
        P(("dp", "fsdp"), None, None),
        P(),
        P(),
        P(None, ("dp", "fsdp")),
        P(),
        P("dp", "fsdp"),
        P("dp", "fsdp"),
        P("dp", "fsdp"),
        P("dp", "fsdp"),
        P("dp", None),
        P("dp"),
        P(("dp", "fsdp"), None),
    )
    return jax.shard_map(
        body,
        mesh=mesh,
        in_specs=placed,
        out_specs=(
            P(("dp", "fsdp"), None),
            P(("dp", "fsdp"), None),
            P(),
            P(),
            P(None, ("dp", "fsdp")),
            P(),
            P("dp", "fsdp"),
            P("dp", "fsdp"),
            P("dp", "fsdp"),
            P("dp", "fsdp"),
            P("dp", None),
            P("dp"),
        ),
        check_vma=False,
    )
```
